32 devices in a mesh: rep: 4 (over y, x), shard: 8 (over z, core).
Axes of the slice: x: 2, y: 2, z: 4, core: 2. Of those that a mesh axis runs over, the one named last changes fastest.
Arguments:
- tokens: bfloat16 [8192, 1024], P(('rep', 'shard')), may hold values from -6 to 6
- segments: int32 [8192], P('rep'), may hold values from 0 to 2047, as said below
- enc_states: bfloat16 [2048, 1024], P(('rep', 'shard')), may hold values from -6 to 6
- enc_lengths: int32 [4], P('rep'), may hold values from 128 to 512, as said below
- cotangent: bfloat16 [8192, 1024], P(('rep', 'shard')), may hold values from -6 to 6
- self_qkv: bfloat16 [1024, 3072], P('shard'), may hold values from -0.1875 to 0.1875
- self_out: bfloat16 [1024, 1024], P('shard'), may hold values from -3 to 3
- cross_query: bfloat16 [1024, 1024], P('shard'), may hold values from -0.1875 to 0.1875
- cross_memory: bfloat16 [1024, 2048], P('shard'), may hold values from -0.1875 to 0.1875
- cross_out: bfloat16 [1024, 1024], P('shard'), may hold values from -2 to 2
- expand_weight: bfloat16 [1024, 8192], P('shard'), may hold values from -0.1875 to 0.1875
- shrink_weight: bfloat16 [8192, 1024], P('shard'), may hold values from -0.0625 to 0.0625
- norm_gain: bfloat16 [3, 1024], P(None, 'shard'), may hold values from 0.5 to 1.5
- norm_bias: bfloat16 [3, 1024], P(None, 'shard'), may hold values from -2 to 2
- proj_bias: bfloat16 [7, 1024], P(None, 'shard'), may hold values from -2 to 2
- expand_bias: bfloat16 [8192], P('shard'), may hold values from -2 to 2
Outputs:
- output: bfloat16 [8192, 1024], P(('rep', 'shard'))
- tokens_grad: float32 [8192, 1024], P(('rep', 'shard'))
- enc_grad: float32 [2048, 1024], P(('rep', 'shard'))
- self_qkv_grad: float32 [1024, 3072], P('shard')
- self_out_grad: float32 [1024, 1024], P('shard')
- cross_query_grad: float32 [1024, 1024], P('shard')
- cross_memory_grad: float32 [1024, 2048], P('shard')
- cross_out_grad: float32 [1024, 1024], P('shard')
- expand_grad: float32 [1024, 8192], P('shard')
- shrink_grad: float32 [8192, 1024], P('shard')
- gain_grad: float32 [3, 1024], P(None, 'shard')
- shift_grad: float32 [3, 1024], P(None, 'shard')
- proj_bias_grad: float32 [7, 1024], P(None, 'shard')
- expand_bias_grad: float32 [8192], P('shard')
The draws below stay inside these ranges and needn't reach their ends.
Inputs may be any that keep to these rules, and one draw needn't show every extreme that they name: `segments`: within each sequence of 2048 tokens the ids start at 0 and never fall, and its last token is a document of its own with id 2048 - 1; among the 1 sequence of each index of rep, one holds a document that starts within its first 256 tokens and ends within its last 256. `enc_lengths`: some sequence has all 512 states valid.
All inputs are finite; a program needn't handle non-finite values.
Results may differ from the reference program's by a relative error of at most 0.025.
Values may be sent and summed in bfloat16 or wider, within the bound.
No kernel may reach another device: no remote copies, remote signals or barrier semaphores. Data moves between devices by JAX's collectives and lax.ppermute only.
A program may use at most 256 MiB of HBM per device.

```python
import jax
import jax.numpy as jnp
from jax import lax

D = 1024
H = 16
HD = 64
FF = 8192
ENC = 512
TOK_DEV = 256
SEQ = 2048
SEQ_GROUP = 1
NSEQ = 4
TOKENS = 8192
ENC_ROWS = 2048


def draw_segments(key, part):
    key = jax.random.fold_in(key, 11)
    rate_key, cut_key, pick_key, start_key, finish_key = jax.random.split(key, 5)
    region_count = 8
    region_rows = SEQ // region_count
    exponent = jax.random.randint(rate_key, (NSEQ, region_count), 3, 12)
    limits = jnp.repeat(jnp.left_shift(jnp.ones_like(exponent), exponent), region_rows, axis=1)
    cut_flags = jax.random.randint(cut_key, (NSEQ, SEQ), 0, limits) == 0
    chosen = jax.random.randint(pick_key, (NSEQ // SEQ_GROUP,), 0, SEQ_GROUP)
    spanning = jnp.arange(NSEQ, dtype=jnp.int32) % SEQ_GROUP == jnp.repeat(chosen, SEQ_GROUP)
    start_place = jax.random.randint(start_key, (NSEQ, 1), 1, TOK_DEV)
    finish = jax.random.randint(finish_key, (NSEQ, 1), SEQ - TOK_DEV + 1, SEQ)
    places = jnp.arange(SEQ, dtype=jnp.int32)[None, :]
    inside = (places > start_place) & (places < finish)
    forced = (places == start_place) | (places == finish)
    spanning_flags = cut_flags & jnp.logical_not(inside) | forced
    cut_flags = jnp.where(spanning[:, None], spanning_flags, cut_flags)
    cut_flags = cut_flags & (places > 0)
    ids = jnp.cumsum(cut_flags.astype(jnp.int32), axis=1)
    ids = jnp.where(places == SEQ - 1, SEQ - 1, ids)
    return ids.reshape(TOKENS).astype(jnp.int32)


def draw_enc_lengths(key, part):
    key = jax.random.fold_in(key, 23)
    value_key, pick_key = jax.random.split(key)
    lengths = jax.random.randint(value_key, (NSEQ,), ENC // 4, ENC + 1)
    chosen = jax.random.randint(pick_key, (), 0, NSEQ)
    lengths = lengths.at[chosen].set(ENC)
    return lengths.at[(chosen + 1) % NSEQ].set(ENC // 4)


def levels(stream_key, shape, cuts, least, top_value):
    level = 1.0
    for position, shards_of in cuts:
        heights = jax.random.uniform(jax.random.fold_in(jax.random.fold_in(stream_key, 6), position), (shards_of,), jnp.float32, least / len(cuts), top_value / len(cuts))
        level = level * jnp.repeat(jnp.exp(heights), shape[position] // shards_of).reshape((-1,) + (1,) * (len(shape) - 1 - position))
    return level


def gaussian(rng, dims, width, bound, cuts=(), kind=jnp.bfloat16):
    entries = width * jax.random.normal(rng, dims, jnp.float32)
    if cuts:
        entries = entries * levels(rng, dims, cuts, -0.22, 0.18)
    return jnp.clip(entries, -bound, bound).astype(kind)


def setup_inputs(seed: int = 0) -> dict:
    arg_keys = jax.random.split(jax.random.key(seed), 17)
    return {
        "tokens": gaussian(arg_keys[0], (TOKENS, D), 1.0, 6.0, ((0, 32),)),
        "segments": draw_segments(jax.random.fold_in(arg_keys[16], 71), 0),
        "enc_states": gaussian(arg_keys[2], (ENC_ROWS, D), 1.0, 6.0, ((0, 32),)),
        "enc_lengths": draw_enc_lengths(jax.random.fold_in(arg_keys[16], 71), 0),
        "cotangent": gaussian(arg_keys[4], (TOKENS, D), 1.0, 6.0, ((0, 32),)),
        "self_qkv": gaussian(arg_keys[5], (D, 3 * D), D ** -0.5, 0.1875, ((0, 8),)),
        "self_out": gaussian(arg_keys[6], (D, D), (max(D // 256, 1)) ** -0.5, 3.0, ((0, 8),)),
        "cross_query": gaussian(arg_keys[7], (D, D), D ** -0.5, 0.1875, ((0, 8),)),
        "cross_memory": gaussian(arg_keys[8], (D, 2 * D), D ** -0.5, 0.1875, ((0, 8),)),
        "cross_out": gaussian(arg_keys[9], (D, D), (max(D // 128, 1)) ** -0.5, 2.0, ((0, 8),)),
        "expand_weight": gaussian(arg_keys[10], (D, FF), D ** -0.5, 0.1875, ((0, 8),)),
        "shrink_weight": gaussian(arg_keys[11], (FF, D), FF ** -0.5, 0.0625, ((0, 8),)),
        "norm_gain": jnp.clip(1.0 + 0.1 * jax.random.normal(arg_keys[12], (3, D), jnp.float32), 0.5, 1.5).astype(jnp.bfloat16),
        "norm_bias": gaussian(arg_keys[13], (3, D), 0.3, 2.0, ((1, 8),)),
        "proj_bias": gaussian(arg_keys[14], (7, D), 0.3, 2.0, ((1, 8),)),
        "expand_bias": gaussian(arg_keys[15], (FF,), 0.3, 2.0, ((0, 8),)),
    }


EPS = 1e-05
NEGATIVE = -1e+30
HIGH = lax.Precision.HIGHEST

@jax.custom_vjp
def low(v):
    return lax.optimization_barrier(v.astype(jnp.bfloat16)).astype(jnp.float32)

@jax.custom_vjp
def low_back(v):
    return v

def low_keep(v):
    return (low(v), None)

def low_pass(kept, grad):
    return (grad,)

def back_keep(v):
    return (v, None)

def back_low(kept, grad):
    return (low(grad),)
low.defvjp(low_keep, low_pass)
low_back.defvjp(back_keep, back_low)

def matmul(left, right):
    return jnp.dot(left, right, precision=HIGH)

def rounded_both(values):
    return low_back(low(values))

def norm_apply(rows, gain, shift):
    mean_rows = lax.optimization_barrier(jnp.mean(rows, axis=-1, keepdims=True))
    centered = rows - mean_rows
    inverse = lax.rsqrt(lax.optimization_barrier(jnp.mean(centered * centered, axis=-1, keepdims=True)) + EPS)
    return centered * inverse * gain + shift

def masked_softmax(scores, keep_mask):
    top_rows = lax.optimization_barrier(jnp.max(jnp.where(keep_mask, scores, NEGATIVE), axis=-1, keepdims=True))
    expo_rows = jnp.exp(jnp.where(keep_mask, scores - top_rows, NEGATIVE))
    return expo_rows / lax.optimization_barrier(jnp.sum(expo_rows, axis=-1, keepdims=True))

def sequence_layer(seq_tokens, seq_memory, seq_segments, seq_length, params):
    attn_in, attn_proj, query_in, memory_in, cross_proj, expand_full, shrink_full, gain_rows, shift_rows, bias_rows, hidden_bias = params
    token_count = seq_tokens.shape[0]
    score_scale = HD ** (-0.5)
    block_rows = min(512, token_count)
    block_ids = jnp.arange(token_count // block_rows, dtype=jnp.int32)
    positions = jnp.arange(token_count, dtype=jnp.int32)
    input_one = low(norm_apply(seq_tokens, gain_rows[0], shift_rows[0]))
    projected = matmul(input_one, attn_in)
    query = rounded_both(projected[:, :D] + bias_rows[0]).reshape(token_count, H, HD)
    key_rows = rounded_both(projected[:, D:2 * D]).reshape(token_count, H, HD)
    value_rows = rounded_both(projected[:, 2 * D:] + bias_rows[1]).reshape(token_count, H, HD)

    def self_block(index):
        first_row = index * block_rows
        query_part = lax.dynamic_slice_in_dim(query, first_row, block_rows, 0)
        query_pos = lax.dynamic_slice_in_dim(positions, first_row, block_rows, 0)
        query_seg = lax.dynamic_slice_in_dim(seq_segments, first_row, block_rows, 0)
        keep_mask = (positions[None, :] <= query_pos[:, None]) & (seq_segments[None, :] == query_seg[:, None])
        scores = low_back(jnp.einsum('qhd,khd->hqk', query_part, key_rows, precision=HIGH) * score_scale)
        probs = low(masked_softmax(scores, keep_mask[None]))
        return jnp.einsum('hqk,khd->qhd', probs, value_rows, precision=HIGH)
    attended = lax.map(jax.checkpoint(self_block), block_ids)
    attended = rounded_both(attended.reshape(token_count, D))
    hidden_one = seq_tokens + low_back(matmul(attended, attn_proj) + bias_rows[2])
    input_two = low(norm_apply(hidden_one, gain_rows[1], shift_rows[1]))
    cross_q = rounded_both(matmul(input_two, query_in) + bias_rows[3]).reshape(token_count, H, HD)
    memory_rows = matmul(seq_memory, memory_in)
    memory_key = rounded_both(memory_rows[:, :D]).reshape(ENC, H, HD)
    memory_value = rounded_both(memory_rows[:, D:] + bias_rows[4]).reshape(ENC, H, HD)
    memory_keep = (jnp.arange(ENC, dtype=jnp.int32) < seq_length)[None, None, :]

    def cross_block(index):
        query_part = lax.dynamic_slice_in_dim(cross_q, index * block_rows, block_rows, 0)
        scores = low_back(jnp.einsum('qhd,khd->hqk', query_part, memory_key, precision=HIGH) * score_scale)
        probs = low(masked_softmax(scores, memory_keep))
        return jnp.einsum('hqk,khd->qhd', probs, memory_value, precision=HIGH)
    context = lax.map(jax.checkpoint(cross_block), block_ids)
    context = rounded_both(context.reshape(token_count, D))
    hidden_two = hidden_one + low_back(matmul(context, cross_proj) + bias_rows[5])
    input_three = low(norm_apply(hidden_two, gain_rows[2], shift_rows[2]))
    pre_act = low_back(matmul(input_three, expand_full) + hidden_bias)
    activated = low(jax.nn.gelu(pre_act, approximate=True))
    return hidden_two + low_back(matmul(activated, shrink_full) + bias_rows[6])

def reference(tokens, segments, enc_states, enc_lengths, cotangent, self_qkv, self_out, cross_query, cross_memory, cross_out, expand_weight, shrink_weight, norm_gain, norm_bias, proj_bias, expand_bias):
    params = tuple((item.astype(jnp.float32) for item in (self_qkv, self_out, cross_query, cross_memory, cross_out, expand_weight, shrink_weight, norm_gain, norm_bias, proj_bias, expand_bias)))
    inputs = tokens.astype(jnp.float32).reshape(NSEQ, SEQ, D)
    memory = enc_states.astype(jnp.float32).reshape(NSEQ, ENC, D)
    segment_rows = segments.reshape(NSEQ, SEQ)

    def forward(inputs_now, memory_now, params_now):

        def one_sequence(item):
            return jax.checkpoint(sequence_layer)(item[0], item[1], item[2], item[3], params_now)
        return lax.map(one_sequence, (inputs_now, memory_now, segment_rows, enc_lengths))
    result, pullback = jax.vjp(forward, inputs, memory, params)
    grad_inputs, grad_memory, grad_params = pullback(cotangent.astype(jnp.float32).reshape(NSEQ, SEQ, D))
    return (result.reshape(TOKENS, D).astype(jnp.bfloat16), grad_inputs.reshape(TOKENS, D), grad_memory.reshape(ENC_ROWS, D), grad_params[0], grad_params[1], grad_params[2], grad_params[3], grad_params[4], grad_params[5], grad_params[6], grad_params[7], grad_params[8], grad_params[9], grad_params[10])
```

```python
import jax
import jax.numpy as jnp
from jax import lax
from jax.experimental import pallas as pl
from jax.experimental.pallas import tpu as pltpu
from jax.sharding import PartitionSpec as P

D = 1024
H = 16
HD = 64
SEQ = 2048
PAIR = 2 * HD

EPS = 1e-05
NEGATIVE = -1e30
SCALE = HD**-0.5
BLOCK = 512


def norm_apply(rows, gain, shift):
    mean_rows = jnp.mean(rows, axis=-1, keepdims=True)
    centered = rows - mean_rows
    inverse = lax.rsqrt(jnp.mean(centered * centered, axis=-1, keepdims=True) + EPS)
    return centered * inverse * gain + shift


def gelu_apply(values):
    return jax.nn.gelu(values, approximate=True)


def column_sums(rows):
    return jnp.sum(rows, axis=0, dtype=jnp.float32)


def low(values):
    return values.astype(jnp.bfloat16)


def dot(left, right):
    return jnp.dot(left, right, preferred_element_type=jnp.float32)


def dot_nt(left, right):
    return lax.dot_general(left, right, (((1,), (1,)), ((), ())), preferred_element_type=jnp.float32)


def dot_tn(left, right):
    return lax.dot_general(left, right, (((0,), (0,)), ((), ())), preferred_element_type=jnp.float32)


def head_halves(rows, scale=None):
    lane = lax.broadcasted_iota(jnp.int32, rows.shape, 1)
    if scale is not None:
        rows = rows * jnp.asarray(scale, rows.dtype)
    zero = jnp.zeros_like(rows)
    return jnp.where(lane < HD, rows, zero), jnp.where(lane < HD, zero, rows)


def self_forward_kernel(ends, q_ref, k_ref, v_ref, seg_col, seg_row, low_ref, full_ref, lse_ref):
    step = pl.program_id(0)
    rows = q_ref.shape[0]
    queries = head_halves(q_ref[...], SCALE)
    query_seg = seg_col[...]
    last_seg = ends[1, step]

    def piece(index, state, masked, diagonal):
        keys = k_ref[pl.ds(index * rows, rows), :]
        values = v_ref[pl.ds(index * rows, rows), :]
        keep = None
        if masked:
            keep = seg_row[:, pl.ds(index * rows, rows)] == query_seg
            if diagonal:
                key_pos = lax.broadcasted_iota(jnp.int32, (rows, rows), 1)
                query_pos = lax.broadcasted_iota(jnp.int32, (rows, rows), 0)
                keep = keep & (key_pos <= query_pos)
        after = []
        for head in range(2):
            top, total, acc = state[head]
            scores = dot_nt(queries[head], keys)
            if masked:
                scores = jnp.where(keep, scores, NEGATIVE)
            top_new = jnp.maximum(top, jnp.max(scores, axis=1, keepdims=True))
            expo = jnp.exp(scores - top_new)
            fade = jnp.exp(top - top_new)
            after.append(
                (
                    top_new,
                    total * fade + jnp.sum(expo, axis=1, keepdims=True),
                    acc * fade + dot(low(expo), values),
                )
            )
        return tuple(after)

    def before(index, state):
        return lax.cond(
            ends[0, index] == last_seg,
            lambda s: piece(index, s, False, False),
            lambda s: piece(index, s, True, False),
            state,
        )

    blank = (
        jnp.full((rows, 1), NEGATIVE, jnp.float32),
        jnp.zeros((rows, 1), jnp.float32),
        jnp.zeros((rows, PAIR), jnp.float32),
    )
    state = lax.fori_loop(0, step, before, (blank, blank))
    state = piece(step, state, True, True)
    lane = lax.broadcasted_iota(jnp.int32, (rows, PAIR), 1)
    joined = jnp.where(lane < HD, state[0][2] / state[0][1], state[1][2] / state[1][1])
    full_ref[...] = joined
    low_ref[...] = low(joined)
    lse_ref[:, 0:1] = state[0][0] + jnp.log(state[0][1])
    lse_ref[:, 1:2] = state[1][0] + jnp.log(state[1][1])


def block_ends(segments, rows):
    return jnp.stack([segments[::rows], segments[rows - 1 :: rows]])


def self_forward(qkv, segments):
    count = qkv.shape[0]
    rows = BLOCK
    col = segments[:, None]
    row = segments[None, :]
    grid_spec = pltpu.PrefetchScalarGridSpec(
        num_scalar_prefetch=1,
        grid=(count // rows,),
        in_specs=[
            pl.BlockSpec((rows, PAIR), lambda i, e: (i, 0)),
            pl.BlockSpec((count, PAIR), lambda i, e: (0, 1)),
            pl.BlockSpec((count, PAIR), lambda i, e: (0, 2)),
            pl.BlockSpec((rows, 1), lambda i, e: (i, 0)),
            pl.BlockSpec((1, count), lambda i, e: (0, 0)),
        ],
        out_specs=[
            pl.BlockSpec((rows, PAIR), lambda i, e: (i, 0)),
            pl.BlockSpec((rows, PAIR), lambda i, e: (i, 0)),
            pl.BlockSpec((rows, 2), lambda i, e: (i, 0)),
        ],
    )
    return pl.pallas_call(
        self_forward_kernel,
        grid_spec=grid_spec,
        out_shape=(
            jax.ShapeDtypeStruct((count, PAIR), jnp.bfloat16),
            jax.ShapeDtypeStruct((count, PAIR), jnp.float32),
            jax.ShapeDtypeStruct((count, 2), jnp.float32),
        ),
        compiler_params=pltpu.CompilerParams(vmem_limit_bytes=40 * 2**20),
        cost_estimate=pl.CostEstimate(
            flops=4 * count * count * PAIR, bytes_accessed=8 * count * PAIR, transcendentals=count * count
        ),
    )(block_ends(segments, rows), qkv, qkv, qkv, col, row)


def self_backward_kernel(
    ends, q_ref, k_ref, v_ref, go_ref, lse_ref, delta_ref, seg_col, seg_row, grad_ref, acc_q, acc_k, acc_v
):
    step = pl.program_id(0)
    blocks = pl.num_programs(0)
    rows = k_ref.shape[0]

    @pl.when(step == 0)
    def _():
        acc_q[...] = jnp.zeros_like(acc_q)

    keys = k_ref[...]
    values = v_ref[...]
    key_halves = head_halves(keys, SCALE)
    key_seg = seg_col[...]
    first_seg = ends[0, step]

    def piece(index, masked, diagonal):
        place = pl.ds(pl.multiple_of(index * rows, rows), rows)
        queries = head_halves(q_ref[place, :], SCALE)
        grads = head_halves(go_ref[place, :])
        keep = None
        if masked:
            keep = seg_row[:, place] == key_seg
            if diagonal:
                key_pos = lax.broadcasted_iota(jnp.int32, (rows, rows), 0)
                query_pos = lax.broadcasted_iota(jnp.int32, (rows, rows), 1)
                keep = keep & (key_pos <= query_pos)
        sum_q = sum_k = sum_v = None
        for head in range(2):
            scores = dot_nt(keys, queries[head])
            probs = jnp.exp(scores - lse_ref[head : head + 1, place])
            if masked:
                probs = jnp.where(keep, probs, 0.0)
            part_v = dot(low(probs), grads[head])
            grad_probs = dot_nt(values, grads[head])
            grad_scores = low(probs * (grad_probs - delta_ref[head : head + 1, place]))
            part_k = dot(grad_scores, queries[head])
            part_q = dot_tn(grad_scores, key_halves[head])
            sum_q = part_q if sum_q is None else sum_q + part_q
            sum_k = part_k if sum_k is None else sum_k + part_k
            sum_v = part_v if sum_v is None else sum_v + part_v
        acc_q[place, :] += sum_q
        if diagonal:
            acc_k[...] = sum_k
            acc_v[...] = sum_v
        else:
            acc_k[...] += sum_k
            acc_v[...] += sum_v

    piece(step, True, True)

    @pl.loop(step + 1, blocks)
    def _(index):
        whole = ends[1, index] == first_seg

        @pl.when(whole)
        def _():
            piece(index, False, False)

        @pl.when(jnp.logical_not(whole))
        def _():
            piece(index, True, False)

    own = pl.ds(pl.multiple_of(step * rows, rows), rows)
    grad_ref[own, 0:PAIR] = low(acc_q[own, :])
    grad_ref[own, PAIR : 2 * PAIR] = low(acc_k[...])
    grad_ref[own, 2 * PAIR : 3 * PAIR] = low(acc_v[...])


def self_backward(qkv, grad_att, lse, delta, segments):
    count = qkv.shape[0]
    rows = BLOCK
    col = segments[:, None]
    row = segments[None, :]
    whole = lambda i, e: (0, 0)
    grid_spec = pltpu.PrefetchScalarGridSpec(
        num_scalar_prefetch=1,
        grid=(count // rows,),
        in_specs=[
            pl.BlockSpec((count, PAIR), whole),
            pl.BlockSpec((rows, PAIR), lambda i, e: (i, 1)),
            pl.BlockSpec((rows, PAIR), lambda i, e: (i, 2)),
            pl.BlockSpec((count, PAIR), whole),
            pl.BlockSpec((2, count), whole),
            pl.BlockSpec((2, count), whole),
            pl.BlockSpec((rows, 1), lambda i, e: (i, 0)),
            pl.BlockSpec((1, count), whole),
        ],
        out_specs=pl.BlockSpec((count, 3 * PAIR), whole),
        scratch_shapes=[
            pltpu.VMEM((count, PAIR), jnp.float32),
            pltpu.VMEM((rows, PAIR), jnp.float32),
            pltpu.VMEM((rows, PAIR), jnp.float32),
        ],
    )
    return pl.pallas_call(
        self_backward_kernel,
        grid_spec=grid_spec,
        out_shape=jax.ShapeDtypeStruct((count, 3 * PAIR), jnp.bfloat16),
        compiler_params=pltpu.CompilerParams(vmem_limit_bytes=40 * 2**20),
        cost_estimate=pl.CostEstimate(
            flops=10 * count * count * PAIR, bytes_accessed=14 * count * PAIR, transcendentals=count * count
        ),
    )(block_ends(segments, rows), qkv, qkv, qkv, grad_att, lse, delta, col, row)


def cross_forward_kernel(length, q_ref, m_ref, out_ref):
    queries = head_halves(q_ref[...], SCALE)
    keys = m_ref[:, :PAIR]
    values = m_ref[:, PAIR:]
    shape = (q_ref.shape[0], m_ref.shape[0])
    keep = lax.broadcasted_iota(jnp.int32, shape, 1) < length[0]
    parts = []
    for head in range(2):
        scores = jnp.where(keep, dot_nt(queries[head], keys), NEGATIVE)
        expo = jnp.exp(scores - jnp.max(scores, axis=1, keepdims=True))
        parts.append(dot(low(expo), values) / jnp.sum(expo, axis=1, keepdims=True))
    lane = lax.broadcasted_iota(jnp.int32, parts[0].shape, 1)
    out_ref[...] = low(jnp.where(lane < HD, parts[0], parts[1]))


def cross_forward(queries, memory, length):
    count, states = queries.shape[0], memory.shape[0]
    grid_spec = pltpu.PrefetchScalarGridSpec(
        num_scalar_prefetch=1,
        grid=(D // PAIR,),
        in_specs=[
            pl.BlockSpec((count, PAIR), lambda i, e: (0, i)),
            pl.BlockSpec((states, 2 * PAIR), lambda i, e: (0, i)),
        ],
        out_specs=pl.BlockSpec((count, PAIR), lambda i, e: (0, i)),
    )
    return pl.pallas_call(
        cross_forward_kernel,
        grid_spec=grid_spec,
        out_shape=jax.ShapeDtypeStruct((count, D), jnp.bfloat16),
        cost_estimate=pl.CostEstimate(
            flops=8 * count * states * D, bytes_accessed=4 * count * D + 4 * states * D, transcendentals=count * states * H
        ),
    )(length, queries, memory)


def cross_backward_kernel(length, q_ref, m_ref, g_ref, dq_ref, dm_ref):
    queries = head_halves(q_ref[...], SCALE)
    grads = head_halves(g_ref[...])
    keys = m_ref[:, :PAIR]
    values = m_ref[:, PAIR:]
    key_halves = head_halves(keys, SCALE)
    shape = (m_ref.shape[0], q_ref.shape[0])
    keep = lax.broadcasted_iota(jnp.int32, shape, 0) < length[0]
    sum_q = sum_k = sum_v = None
    for head in range(2):
        scores = jnp.where(keep, dot_nt(keys, queries[head]), NEGATIVE)
        expo = jnp.exp(scores - jnp.max(scores, axis=0, keepdims=True))
        probs = expo * (1.0 / jnp.sum(expo, axis=0, keepdims=True))
        part_v = dot(low(probs), grads[head])
        grad_probs = dot_nt(values, grads[head])
        inner = jnp.sum(probs * grad_probs, axis=0, keepdims=True)
        grad_scores = low(probs * (grad_probs - inner))
        part_k = dot(grad_scores, queries[head])
        part_q = dot_tn(grad_scores, key_halves[head])
        sum_q = part_q if sum_q is None else sum_q + part_q
        sum_k = part_k if sum_k is None else sum_k + part_k
        sum_v = part_v if sum_v is None else sum_v + part_v
    dq_ref[...] = low(sum_q)
    dm_ref[:, :PAIR] = low(sum_k)
    dm_ref[:, PAIR:] = low(sum_v)


def cross_backward(queries, memory, grads, length):
    count, states = queries.shape[0], memory.shape[0]
    grid_spec = pltpu.PrefetchScalarGridSpec(
        num_scalar_prefetch=1,
        grid=(D // PAIR,),
        in_specs=[
            pl.BlockSpec((count, PAIR), lambda i, e: (0, i)),
            pl.BlockSpec((states, 2 * PAIR), lambda i, e: (0, i)),
            pl.BlockSpec((count, PAIR), lambda i, e: (0, i)),
        ],
        out_specs=[
            pl.BlockSpec((count, PAIR), lambda i, e: (0, i)),
            pl.BlockSpec((states, 2 * PAIR), lambda i, e: (0, i)),
        ],
    )
    return pl.pallas_call(
        cross_backward_kernel,
        grid_spec=grid_spec,
        out_shape=(
            jax.ShapeDtypeStruct((count, D), jnp.bfloat16),
            jax.ShapeDtypeStruct((states, 2 * D), jnp.bfloat16),
        ),
        cost_estimate=pl.CostEstimate(
            flops=20 * count * states * D, bytes_accessed=6 * count * D + 8 * states * D, transcendentals=count * states * H
        ),
    )(length, queries, memory, grads)


def shards(
    tokens,
    segments,
    enc_states,
    enc_lengths,
    cotangent,
    self_qkv,
    self_out,
    cross_query,
    cross_memory,
    cross_out,
    expand_weight,
    shrink_weight,
    norm_gain,
    norm_bias,
    proj_bias,
    expand_bias,
):
    row_count = tokens.shape[0]
    span = SEQ // row_count
    width = D // span
    count = lax.axis_size("shard")
    shard_pos = lax.axis_index("shard")
    local_pos = shard_pos % span
    local_seq = shard_pos // span
    groups = None
    if count != span:
        groups = [[g * span + i for i in range(span)] for g in range(count // span)]
    weight_rows = self_qkv.shape[0]
    hidden = expand_bias.shape[0]

    def gather(value, groups=None):
        return lax.all_gather(value, "shard", axis=0, tiled=True, axis_index_groups=groups)

    def scatter(value, groups=None):
        return lax.psum_scatter(value, "shard", scatter_dimension=0, tiled=True, axis_index_groups=groups)

    def swap(value):
        return lax.all_to_all(value, "shard", 0, 0, tiled=True)

    tokens_all = gather(tokens, groups)
    blocks = self_qkv.reshape(weight_rows, 3, span, width).transpose(2, 0, 1, 3)
    blocks = jnp.tile(blocks.reshape(span, weight_rows, 3 * width), (count // span, 1, 1))
    qkv_weight = swap(blocks).reshape(D, 3 * width)
    small = jnp.concatenate([norm_gain, norm_bias, proj_bias], axis=0)
    small_all = lax.all_gather(small, "shard", axis=1, tiled=True).astype(jnp.float32)
    gain_rows, shift_rows, bias_rows = small_all[:3], small_all[3:6], small_all[6:]
    memory_weight = cross_memory.reshape(weight_rows, 2, span, width).transpose(0, 2, 1, 3)
    memory_weight = memory_weight.reshape(weight_rows, 2 * D)
    pack = gather(jnp.concatenate([self_out, cross_query, cross_out, memory_weight], axis=1))
    attn_proj, query_in, cross_proj = pack[:, :D], pack[:, D : 2 * D], pack[:, 2 * D : 3 * D]
    memory_in = pack[:, 3 * D :]
    expand_local = swap(expand_weight.reshape(weight_rows, count, hidden).transpose(1, 0, 2)).reshape(D, hidden)

    seq_segments = lax.dynamic_slice_in_dim(segments, local_seq * SEQ, SEQ)
    x_all = tokens_all.astype(jnp.float32)
    input_one_all = low(norm_apply(x_all, gain_rows[0], shift_rows[0]))
    own_bias = lax.dynamic_slice_in_dim(bias_rows[:2], local_pos * width, width, axis=1)
    qkv_bias = jnp.concatenate([own_bias[0], jnp.zeros((width,), jnp.float32), own_bias[1]])
    qkv = low(dot(input_one_all, qkv_weight) + qkv_bias)
    att_low, att_full, lse = self_forward(qkv, seq_segments)
    attended = lax.all_to_all(att_low, "shard", 0, 1, tiled=True, axis_index_groups=groups)

    pair_bias = bias_rows[4].reshape(span, width)
    pair_bias = jnp.stack([jnp.zeros_like(pair_bias), pair_bias], axis=1).reshape(2 * D)
    memory_own = low(dot(enc_states, memory_in) + pair_bias)
    memory_all = gather(memory_own, groups)
    enc_count = lax.dynamic_slice_in_dim(enc_lengths, local_seq, 1)

    residual_in = tokens.astype(jnp.float32)
    hidden_one = residual_in + dot(attended, attn_proj) + bias_rows[2]
    input_two = low(norm_apply(hidden_one, gain_rows[1], shift_rows[1]))
    cross_q = low(dot(input_two, query_in) + bias_rows[3])
    context = cross_forward(cross_q, memory_all, enc_count)
    hidden_two = hidden_one + dot(context, cross_proj) + bias_rows[5]
    input_three = low(norm_apply(hidden_two, gain_rows[2], shift_rows[2]))

    grad_all = gather(cotangent)
    input_three_all = gather(input_three)
    pre_act = dot(input_three_all, expand_local) + expand_bias.astype(jnp.float32)
    act = low(gelu_apply(pre_act))
    grad_act = dot_nt(grad_all, shrink_weight)
    grad_pre = low(jax.vjp(gelu_apply, pre_act)[1](grad_act)[0])
    grad_in_three = scatter(low(dot_nt(grad_pre, expand_local))).astype(jnp.float32)
    result = hidden_two + scatter(low(dot(act, shrink_weight))).astype(jnp.float32) + bias_rows[6]
    grad_shrink = dot_tn(act, grad_all)
    grad_expand = dot_tn(input_three_all, grad_pre)
    grad_hidden_bias = column_sums(grad_pre)

    grad_out = cotangent.astype(jnp.float32)
    norm_three = jax.vjp(norm_apply, hidden_two, gain_rows[2], shift_rows[2])[1](grad_in_three)
    grad_two = grad_out + norm_three[0]
    grad_two_low = low(grad_two)
    grad_cross_proj = dot_tn(context, grad_two_low)
    grad_context = low(dot_nt(grad_two_low, cross_proj))
    grad_cross_q, memory_part = cross_backward(cross_q, memory_all, grad_context, enc_count)
    mem_grads = scatter(memory_part, groups)
    grad_memory = dot_tn(enc_states, mem_grads)
    grad_enc = dot_nt(mem_grads, memory_in)
    grad_query_in = dot_tn(input_two, grad_cross_q)
    grad_in_two = dot_nt(grad_cross_q, query_in)
    norm_two = jax.vjp(norm_apply, hidden_one, gain_rows[1], shift_rows[1])[1](grad_in_two)
    grad_one = grad_two + norm_two[0]
    grad_one_low = low(grad_one)
    grad_attn_proj = dot_tn(attended, grad_one_low)
    grad_attn = low(dot_nt(grad_one_low, attn_proj))

    grad_att_heads = lax.all_to_all(grad_attn, "shard", 1, 0, tiled=True, axis_index_groups=groups)
    delta = jnp.sum((grad_att_heads.astype(jnp.float32) * att_full).reshape(SEQ, 2, HD), axis=-1).T
    grad_qkv = self_backward(qkv, grad_att_heads, lse.T, delta, seq_segments)
    grad_in_one = scatter(low(dot_nt(grad_qkv, qkv_weight)), groups).astype(jnp.float32)
    grad_attn_in = low(dot_tn(input_one_all, grad_qkv))
    norm_one = jax.vjp(norm_apply, residual_in, gain_rows[0], shift_rows[0])[1](grad_in_one)
    grad_tokens = grad_one + norm_one[0]

    qkv_sums = column_sums(grad_qkv)
    zero_row = jnp.zeros((D,), jnp.float32)
    bias_zero = lax.dynamic_update_slice_in_dim(zero_row, qkv_sums[:width], local_pos * width, 0)
    bias_one = lax.dynamic_update_slice_in_dim(zero_row, qkv_sums[2 * width :], local_pos * width, 0)
    memory_sums = column_sums(mem_grads).reshape(span, 2, width)[:, 1].reshape(D)
    small_grads = jnp.stack(
        [
            norm_one[1],
            norm_two[1],
            norm_three[1],
            norm_one[2],
            norm_two[2],
            norm_three[2],
            bias_zero,
            bias_one,
            column_sums(grad_one_low),
            column_sums(grad_cross_q),
            memory_sums,
            column_sums(grad_two_low),
            column_sums(cotangent),
        ]
    )
    small_count = small_grads.shape[0]
    shard_width = D // count
    pack_width = 5 * D
    extra = 8
    small_rows = low(small_grads).reshape(small_count, count, shard_width).transpose(1, 0, 2)
    small_rows = small_rows.reshape(count, small_count * shard_width)
    small_rows = jnp.pad(small_rows, ((0, 0), (0, extra * pack_width - small_count * shard_width)))
    small_rows = small_rows.reshape(count, extra, pack_width)
    grad_pack = low(jnp.concatenate([grad_attn_proj, grad_query_in, grad_cross_proj, grad_memory], axis=1))
    grad_pack = jnp.concatenate([grad_pack.reshape(count, weight_rows, pack_width), small_rows], axis=1)
    owned_pack = scatter(grad_pack.reshape(count * (weight_rows + extra), pack_width))
    owned_qkv = swap(grad_attn_in.reshape(count, weight_rows, 3 * width))
    owned_qkv = owned_qkv.astype(jnp.float32).reshape(count // span, span, weight_rows, 3 * width)
    owned_qkv = low(jnp.sum(owned_qkv, axis=0))
    owned_expand = swap(low(grad_expand).reshape(count, weight_rows, hidden))
    total_shrink, total_hidden_bias = lax.psum((low(grad_shrink), low(grad_hidden_bias)), "rep")
    total_expand = lax.psum(owned_expand, "rep")
    total_pack, total_qkv = lax.psum((owned_pack, owned_qkv), "rep")
    total_expand = total_expand.transpose(1, 0, 2).reshape(weight_rows, count * hidden)
    total_qkv = total_qkv.reshape(span, weight_rows, 3, width).transpose(1, 2, 0, 3)
    total_qkv = total_qkv.reshape(weight_rows, 3 * D)
    total_memory = total_pack[:weight_rows, 3 * D :].reshape(weight_rows, span, 2, width)
    total_memory = total_memory.transpose(0, 2, 1, 3).reshape(weight_rows, 2 * D)
    total_small = total_pack[weight_rows:].reshape(-1)[: small_count * shard_width]
    total_small = total_small.reshape(small_count, shard_width)

    def wide(value):
        return value.astype(jnp.float32)

    return (
        low(result),
        grad_tokens,
        grad_enc,
        wide(total_qkv),
        wide(total_pack[:weight_rows, :D]),
        wide(total_pack[:weight_rows, D : 2 * D]),
        wide(total_memory),
        wide(total_pack[:weight_rows, 2 * D : 3 * D]),
        wide(total_expand),
        wide(total_shrink),
        wide(total_small[:3]),
        wide(total_small[3:6]),
        wide(total_small[6:]),
        wide(total_hidden_bias),
    )


def solution(mesh):
    return jax.shard_map(
        shards,
        mesh=mesh,
        in_specs=(
            P(("rep", "shard"), None),
            P("rep"),
            P(("rep", "shard"), None),
            P("rep"),
            P(("rep", "shard"), None),
            P("shard", None),
            P("shard", None),
            P("shard", None),
            P("shard", None),
            P("shard", None),
            P("shard", None),
            P("shard", None),
            P(None, "shard"),
            P(None, "shard"),
            P(None, "shard"),
            P("shard"),
        ),
        out_specs=(
            P(("rep", "shard"), None),
            P(("rep", "shard"), None),
            P(("rep", "shard"), None),
            P("shard", None),
            P("shard", None),
            P("shard", None),
            P("shard", None),
            P("shard", None),
            P("shard", None),
            P("shard", None),
            P(None, "shard"),
            P(None, "shard"),
            P(None, "shard"),
            P("shard"),
        ),
        check_vma=False,
    )
```

```python
import jax
import jax.numpy as jnp
from jax import lax
from jax.experimental import pallas as pl
from jax.experimental.pallas import tpu as pltpu
from jax.sharding import PartitionSpec as P

D = 1024
H = 16
HD = 64
SEQ = 2048
PAIR = 2 * HD

EPS = 1e-05
NEGATIVE = -1e30
SCALE = HD**-0.5
BLOCK = 512


def norm_apply(rows, gain, shift):
    mean_rows = jnp.mean(rows, axis=-1, keepdims=True)
    centered = rows - mean_rows
    inverse = lax.rsqrt(jnp.mean(centered * centered, axis=-1, keepdims=True) + EPS)
    return centered * inverse * gain + shift


def gelu_apply(values):
    return jax.nn.gelu(values, approximate=True)


def column_sums(rows):
    return jnp.sum(rows, axis=0, dtype=jnp.float32)


def low(values):
    return values.astype(jnp.bfloat16)


def dot(left, right):
    return jnp.dot(left, right, preferred_element_type=jnp.float32)


def dot_nt(left, right):
    return lax.dot_general(left, right, (((1,), (1,)), ((), ())), preferred_element_type=jnp.float32)


def dot_tn(left, right):
    return lax.dot_general(left, right, (((0,), (0,)), ((), ())), preferred_element_type=jnp.float32)


def head_halves(rows, scale=None):
    lane = lax.broadcasted_iota(jnp.int32, rows.shape, 1)
    if scale is not None:
        rows = rows * jnp.asarray(scale, rows.dtype)
    zero = jnp.zeros_like(rows)
    return jnp.where(lane < HD, rows, zero), jnp.where(lane < HD, zero, rows)


def self_forward_kernel(ends, q_ref, k_ref, v_ref, seg_col, seg_row, low_ref, full_ref, lse_ref):
    step = pl.program_id(0)
    rows = q_ref.shape[0]
    queries = head_halves(q_ref[...], SCALE)
    query_seg = seg_col[...]
    last_seg = ends[1, step]

    def piece(index, state, masked, diagonal):
        keys = k_ref[pl.ds(index * rows, rows), :]
        values = v_ref[pl.ds(index * rows, rows), :]
        keep = None
        if masked:
            keep = seg_row[:, pl.ds(index * rows, rows)] == query_seg
            if diagonal:
                key_pos = lax.broadcasted_iota(jnp.int32, (rows, rows), 1)
                query_pos = lax.broadcasted_iota(jnp.int32, (rows, rows), 0)
                keep = keep & (key_pos <= query_pos)
        after = []
        for head in range(2):
            top, total, acc = state[head]
            scores = dot_nt(queries[head], keys)
            if masked:
                scores = jnp.where(keep, scores, NEGATIVE)
            top_new = jnp.maximum(top, jnp.max(scores, axis=1, keepdims=True))
            expo = jnp.exp(scores - top_new)
            fade = jnp.exp(top - top_new)
            after.append(
                (
                    top_new,
                    total * fade + jnp.sum(expo, axis=1, keepdims=True),
                    acc * fade + dot(low(expo), values),
                )
            )
        return tuple(after)

    def before(index, state):
        return lax.cond(
            ends[0, index] == last_seg,
            lambda s: piece(index, s, False, False),
            lambda s: piece(index, s, True, False),
            state,
        )

    blank = (
        jnp.full((rows, 1), NEGATIVE, jnp.float32),
        jnp.zeros((rows, 1), jnp.float32),
        jnp.zeros((rows, PAIR), jnp.float32),
    )
    state = lax.fori_loop(0, step, before, (blank, blank))
    state = piece(step, state, True, True)
    lane = lax.broadcasted_iota(jnp.int32, (rows, PAIR), 1)
    joined = jnp.where(lane < HD, state[0][2] / state[0][1], state[1][2] / state[1][1])
    full_ref[...] = joined
    low_ref[...] = low(joined)
    lse_ref[:, 0:1] = state[0][0] + jnp.log(state[0][1])
    lse_ref[:, 1:2] = state[1][0] + jnp.log(state[1][1])


def block_ends(segments, rows):
    return jnp.stack([segments[::rows], segments[rows - 1 :: rows]])


def self_forward(qkv, segments):
    count = qkv.shape[0]
    rows = BLOCK
    col = segments[:, None]
    row = segments[None, :]
    grid_spec = pltpu.PrefetchScalarGridSpec(
        num_scalar_prefetch=1,
        grid=(count // rows,),
        in_specs=[
            pl.BlockSpec((rows, PAIR), lambda i, e: (i, 0)),
            pl.BlockSpec((count, PAIR), lambda i, e: (0, 1)),
            pl.BlockSpec((count, PAIR), lambda i, e: (0, 2)),
            pl.BlockSpec((rows, 1), lambda i, e: (i, 0)),
            pl.BlockSpec((1, count), lambda i, e: (0, 0)),
        ],
        out_specs=[
            pl.BlockSpec((rows, PAIR), lambda i, e: (i, 0)),
            pl.BlockSpec((rows, PAIR), lambda i, e: (i, 0)),
            pl.BlockSpec((rows, 2), lambda i, e: (i, 0)),
        ],
    )
    return pl.pallas_call(
        self_forward_kernel,
        grid_spec=grid_spec,
        out_shape=(
            jax.ShapeDtypeStruct((count, PAIR), jnp.bfloat16),
            jax.ShapeDtypeStruct((count, PAIR), jnp.float32),
            jax.ShapeDtypeStruct((count, 2), jnp.float32),
        ),
        compiler_params=pltpu.CompilerParams(vmem_limit_bytes=40 * 2**20),
        cost_estimate=pl.CostEstimate(
            flops=4 * count * count * PAIR, bytes_accessed=8 * count * PAIR, transcendentals=count * count
        ),
    )(block_ends(segments, rows), qkv, qkv, qkv, col, row)


def self_backward_kernel(
    ends, q_ref, k_ref, v_ref, go_ref, lse_ref, delta_ref, seg_col, seg_row, grad_ref, acc_q, acc_k, acc_v
):
    step = pl.program_id(0)
    blocks = pl.num_programs(0)
    rows = k_ref.shape[0]

    @pl.when(step == 0)
    def _():
        acc_q[...] = jnp.zeros_like(acc_q)

    keys = k_ref[...]
    values = v_ref[...]
    key_halves = head_halves(keys, SCALE)
    key_seg = seg_col[...]
    first_seg = ends[0, step]

    def piece(index, masked, diagonal):
        place = pl.ds(pl.multiple_of(index * rows, rows), rows)
        queries = head_halves(q_ref[place, :], SCALE)
        grads = head_halves(go_ref[place, :])
        keep = None
        if masked:
            keep = seg_row[:, place] == key_seg
            if diagonal:
                key_pos = lax.broadcasted_iota(jnp.int32, (rows, rows), 0)
                query_pos = lax.broadcasted_iota(jnp.int32, (rows, rows), 1)
                keep = keep & (key_pos <= query_pos)
        sum_q = sum_k = sum_v = None
        for head in range(2):
            scores = dot_nt(keys, queries[head])
            probs = jnp.exp(scores - lse_ref[head : head + 1, place])
            if masked:
                probs = jnp.where(keep, probs, 0.0)
            part_v = dot(low(probs), grads[head])
            grad_probs = dot_nt(values, grads[head])
            grad_scores = low(probs * (grad_probs - delta_ref[head : head + 1, place]))
            part_k = dot(grad_scores, queries[head])
            part_q = dot_tn(grad_scores, key_halves[head])
            sum_q = part_q if sum_q is None else sum_q + part_q
            sum_k = part_k if sum_k is None else sum_k + part_k
            sum_v = part_v if sum_v is None else sum_v + part_v
        acc_q[place, :] += sum_q
        if diagonal:
            acc_k[...] = sum_k
            acc_v[...] = sum_v
        else:
            acc_k[...] += sum_k
            acc_v[...] += sum_v

    piece(step, True, True)

    @pl.loop(step + 1, blocks)
    def _(index):
        whole = ends[1, index] == first_seg

        @pl.when(whole)
        def _():
            piece(index, False, False)

        @pl.when(jnp.logical_not(whole))
        def _():
            piece(index, True, False)

    own = pl.ds(pl.multiple_of(step * rows, rows), rows)
    grad_ref[own, 0:PAIR] = low(acc_q[own, :])
    grad_ref[own, PAIR : 2 * PAIR] = low(acc_k[...])
    grad_ref[own, 2 * PAIR : 3 * PAIR] = low(acc_v[...])


def self_backward(qkv, grad_att, lse, delta, segments):
    count = qkv.shape[0]
    rows = BLOCK
    col = segments[:, None]
    row = segments[None, :]
    whole = lambda i, e: (0, 0)
    grid_spec = pltpu.PrefetchScalarGridSpec(
        num_scalar_prefetch=1,
        grid=(count // rows,),
        in_specs=[
            pl.BlockSpec((count, PAIR), whole),
            pl.BlockSpec((rows, PAIR), lambda i, e: (i, 1)),
            pl.BlockSpec((rows, PAIR), lambda i, e: (i, 2)),
            pl.BlockSpec((count, PAIR), whole),
            pl.BlockSpec((2, count), whole),
            pl.BlockSpec((2, count), whole),
            pl.BlockSpec((rows, 1), lambda i, e: (i, 0)),
            pl.BlockSpec((1, count), whole),
        ],
        out_specs=pl.BlockSpec((count, 3 * PAIR), whole),
        scratch_shapes=[
            pltpu.VMEM((count, PAIR), jnp.float32),
            pltpu.VMEM((rows, PAIR), jnp.float32),
            pltpu.VMEM((rows, PAIR), jnp.float32),
        ],
    )
    return pl.pallas_call(
        self_backward_kernel,
        grid_spec=grid_spec,
        out_shape=jax.ShapeDtypeStruct((count, 3 * PAIR), jnp.bfloat16),
        compiler_params=pltpu.CompilerParams(vmem_limit_bytes=40 * 2**20),
        cost_estimate=pl.CostEstimate(
            flops=10 * count * count * PAIR, bytes_accessed=14 * count * PAIR, transcendentals=count * count
        ),
    )(block_ends(segments, rows), qkv, qkv, qkv, grad_att, lse, delta, col, row)


def cross_forward_kernel(length, q_ref, m_ref, out_ref):
    queries = head_halves(q_ref[...], SCALE)
    keys = m_ref[:, :PAIR]
    values = m_ref[:, PAIR:]
    shape = (q_ref.shape[0], m_ref.shape[0])
    keep = lax.broadcasted_iota(jnp.int32, shape, 1) < length[0]
    parts = []
    for head in range(2):
        scores = jnp.where(keep, dot_nt(queries[head], keys), NEGATIVE)
        expo = jnp.exp(scores - jnp.max(scores, axis=1, keepdims=True))
        parts.append(dot(low(expo), values) / jnp.sum(expo, axis=1, keepdims=True))
    lane = lax.broadcasted_iota(jnp.int32, parts[0].shape, 1)
    out_ref[...] = low(jnp.where(lane < HD, parts[0], parts[1]))


def cross_forward(queries, memory, length):
    count, states = queries.shape[0], memory.shape[0] // (D // PAIR)
    grid_spec = pltpu.PrefetchScalarGridSpec(
        num_scalar_prefetch=1,
        grid=(D // PAIR,),
        in_specs=[
            pl.BlockSpec((count, PAIR), lambda i, e: (0, i)),
            pl.BlockSpec((states, 2 * PAIR), lambda i, e: (i, 0)),
        ],
        out_specs=pl.BlockSpec((count, PAIR), lambda i, e: (0, i)),
    )
    return pl.pallas_call(
        cross_forward_kernel,
        grid_spec=grid_spec,
        out_shape=jax.ShapeDtypeStruct((count, D), jnp.bfloat16),
        cost_estimate=pl.CostEstimate(
            flops=8 * count * states * D, bytes_accessed=4 * count * D + 4 * states * D, transcendentals=count * states * H
        ),
    )(length, queries, memory)


def cross_backward_kernel(length, q_ref, m_ref, g_ref, dq_ref, dm_ref):
    queries = head_halves(q_ref[...], SCALE)
    grads = head_halves(g_ref[...])
    keys = m_ref[:, :PAIR]
    values = m_ref[:, PAIR:]
    key_halves = head_halves(keys, SCALE)
    shape = (m_ref.shape[0], q_ref.shape[0])
    keep = lax.broadcasted_iota(jnp.int32, shape, 0) < length[0]
    sum_q = sum_k = sum_v = None
    for head in range(2):
        scores = jnp.where(keep, dot_nt(keys, queries[head]), NEGATIVE)
        expo = jnp.exp(scores - jnp.max(scores, axis=0, keepdims=True))
        probs = expo * (1.0 / jnp.sum(expo, axis=0, keepdims=True))
        part_v = dot(low(probs), grads[head])
        grad_probs = dot_nt(values, grads[head])
        inner = jnp.sum(probs * grad_probs, axis=0, keepdims=True)
        grad_scores = low(probs * (grad_probs - inner))
        part_k = dot(grad_scores, queries[head])
        part_q = dot_tn(grad_scores, key_halves[head])
        sum_q = part_q if sum_q is None else sum_q + part_q
        sum_k = part_k if sum_k is None else sum_k + part_k
        sum_v = part_v if sum_v is None else sum_v + part_v
    dq_ref[...] = low(sum_q)
    dm_ref[:, :PAIR] = low(sum_k)
    dm_ref[:, PAIR:] = low(sum_v)


def cross_backward(queries, memory, grads, length):
    count, states = queries.shape[0], memory.shape[0] // (D // PAIR)
    grid_spec = pltpu.PrefetchScalarGridSpec(
        num_scalar_prefetch=1,
        grid=(D // PAIR,),
        in_specs=[
            pl.BlockSpec((count, PAIR), lambda i, e: (0, i)),
            pl.BlockSpec((states, 2 * PAIR), lambda i, e: (i, 0)),
            pl.BlockSpec((count, PAIR), lambda i, e: (0, i)),
        ],
        out_specs=[
            pl.BlockSpec((count, PAIR), lambda i, e: (0, i)),
            pl.BlockSpec((states, 2 * PAIR), lambda i, e: (i, 0)),
        ],
    )
    return pl.pallas_call(
        cross_backward_kernel,
        grid_spec=grid_spec,
        out_shape=(
            jax.ShapeDtypeStruct((count, D), jnp.bfloat16),
            jax.ShapeDtypeStruct((states * (D // PAIR), 2 * PAIR), jnp.bfloat16),
        ),
        cost_estimate=pl.CostEstimate(
            flops=20 * count * states * D, bytes_accessed=6 * count * D + 8 * states * D, transcendentals=count * states * H
        ),
    )(length, queries, memory, grads)


def rep_send(value, step):
    size = lax.axis_size("rep")
    return lax.ppermute(value, "rep", [(i, i ^ step) for i in range(size)])


def rep_gather(value, axis):
    size, me = lax.axis_size("rep"), lax.axis_index("rep")
    parts = [value] + [rep_send(value, step) for step in range(1, size)]
    shape = value.shape[:axis] + (size,) + value.shape[axis:]
    out = jnp.zeros(shape, value.dtype)
    for step, part in enumerate(parts):
        out = lax.dynamic_update_slice_in_dim(out, jnp.expand_dims(part, axis), me ^ step, axis)
    return out


def rep_reduce(parts, axis):
    size, me = lax.axis_size("rep"), lax.axis_index("rep")

    def pick(step):
        return lax.dynamic_index_in_dim(parts, me ^ step, axis, keepdims=False)

    total = pick(0).astype(jnp.float32)
    for step in range(1, size):
        total = total + rep_send(low(pick(step)), step).astype(jnp.float32)
    return low(total)


def core_send(value):
    size = lax.axis_size("shard")
    return lax.ppermute(value, "shard", [(i, i ^ 1) for i in range(size)])


def line_send(value, step):
    size = lax.axis_size("shard")
    return lax.ppermute(value, "shard", [(i, (i + 2 * step) % size) for i in range(size)])


def gather_weights(piece):
    kinds, rows, columns = piece.shape
    chips = lax.axis_size("shard") // 2
    chip, core = lax.axis_index("shard") // 2, lax.axis_index("shard") % 2
    line = jnp.zeros((kinds, chips, rows, columns), piece.dtype)
    for step in range(chips):
        part = line_send(piece, step) if step else piece
        line = lax.dynamic_update_slice_in_dim(line, part[:, None], (chip - step) % chips, 1)
    plane = rep_gather(line, 2)
    other = core_send(plane)
    full = jnp.zeros((kinds, chips, 2) + plane.shape[2:], piece.dtype)
    full = lax.dynamic_update_slice_in_dim(full, plane[:, :, None], core, 2)
    full = lax.dynamic_update_slice_in_dim(full, other[:, :, None], 1 - core, 2)
    return full.reshape(kinds, D, columns)


def reduce_weights(grads):
    kinds = len(grads)
    size = lax.axis_size("rep")
    chips = lax.axis_size("shard") // 2
    chip, core = lax.axis_index("shard") // 2, lax.axis_index("shard") % 2
    rows = D // (2 * chips * size)
    stack = jnp.stack([low(g) for g in grads]).reshape(kinds, chips, 2, size, rows, D)
    mine = lax.dynamic_index_in_dim(stack, core, 2, keepdims=False)
    theirs = lax.dynamic_index_in_dim(stack, 1 - core, 2, keepdims=False)
    both = low(mine.astype(jnp.float32) + core_send(theirs).astype(jnp.float32))
    line = rep_reduce(both, 2)
    total = lax.dynamic_index_in_dim(line, chip, 1, keepdims=False).astype(jnp.float32)
    for step in range(1, chips):
        part = lax.dynamic_index_in_dim(line, (chip + step) % chips, 1, keepdims=False)
        total = total + line_send(part, step).astype(jnp.float32)
    return rep_gather(low(total), 1).reshape(kinds, size * rows, D).astype(jnp.float32)


def shards(
    tokens,
    segments,
    enc_states,
    enc_lengths,
    cotangent,
    self_qkv,
    self_out,
    cross_query,
    cross_memory,
    cross_out,
    expand_weight,
    shrink_weight,
    norm_gain,
    norm_bias,
    proj_bias,
    expand_bias,
):
    row_count, enc_rows = tokens.shape[0], enc_states.shape[0]
    span = SEQ // row_count
    width = D // span
    count = lax.axis_size("shard")
    size = lax.axis_size("rep")
    rep_pos = lax.axis_index("rep")
    shard_pos = lax.axis_index("shard")
    local_pos = shard_pos % span
    local_seq = shard_pos // span
    groups = None
    if count != span:
        groups = [[g * span + i for i in range(span)] for g in range(count // span)]
    weight_rows = self_qkv.shape[0]
    part_rows = weight_rows // size
    hidden = expand_bias.shape[0]
    shard_width = norm_gain.shape[1]

    def gather(value, groups=None):
        return lax.all_gather(value, "shard", axis=0, tiled=True, axis_index_groups=groups)

    def scatter(value, groups=None):
        return lax.psum_scatter(value, "shard", scatter_dimension=0, tiled=True, axis_index_groups=groups)

    def swap(value):
        return lax.all_to_all(value, "shard", 0, 0, tiled=True)

    def own_part(weight):
        return lax.dynamic_slice_in_dim(weight, rep_pos * part_rows, part_rows, axis=0)

    def by_pairs(weight, kinds):
        blocks = weight.reshape(part_rows, kinds, span, width).transpose(2, 0, 1, 3)
        return blocks.reshape(span, part_rows, kinds * width)

    rows_all = gather(jnp.concatenate([tokens, enc_states], axis=0), groups)
    rows_all = rows_all.reshape(span, row_count + enc_rows, D)
    blocks = jnp.concatenate([by_pairs(own_part(self_qkv), 3), by_pairs(own_part(cross_memory), 2)], axis=2)
    blocks = jnp.tile(blocks, (count // span, 1, 1))
    small = jnp.concatenate([norm_gain, norm_bias, proj_bias], axis=0)
    small_count = small.shape[0]
    small = jnp.pad(small, ((0, 16 - small_count), (0, 5 * width - shard_width)))
    blocks = jnp.concatenate([blocks, jnp.broadcast_to(small, (count,) + small.shape)], axis=1)
    swapped = swap(blocks)
    small_all = swapped[:, part_rows : part_rows + small_count, :shard_width].astype(jnp.float32)
    small_all = small_all.transpose(1, 0, 2).reshape(small_count, D)
    gain_rows, shift_rows, bias_rows = small_all[:3], small_all[3:6], small_all[6:]
    head_weight = rep_gather(swapped[:, :part_rows], 1).reshape(D, 5 * width)
    qkv_weight, memory_weight = head_weight[:, : 3 * width], head_weight[:, 3 * width :]
    plain = gather_weights(jnp.stack([own_part(self_out), own_part(cross_query), own_part(cross_out)]))
    attn_proj, query_in, cross_proj = plain[0], plain[1], plain[2]
    expand_part = own_part(expand_weight).reshape(part_rows, count, hidden).transpose(1, 0, 2)
    expand_local = rep_gather(swap(expand_part), 1).reshape(D, hidden)

    seq_segments = lax.dynamic_slice_in_dim(segments, local_seq * SEQ, SEQ)
    x_all = rows_all[:, :row_count].astype(jnp.float32)
    input_one_all = low(norm_apply(x_all, gain_rows[0], shift_rows[0])).reshape(SEQ, D)
    own_bias = lax.dynamic_slice_in_dim(bias_rows, local_pos * width, width, axis=1)
    zero_bias = jnp.zeros((width,), jnp.float32)
    qkv = low(dot(input_one_all, qkv_weight) + jnp.concatenate([own_bias[0], zero_bias, own_bias[1]]))
    att_low, att_full, lse = self_forward(qkv, seq_segments)
    attended = lax.all_to_all(att_low, "shard", 0, 1, tiled=True, axis_index_groups=groups)

    enc_all = rows_all[:, row_count:].reshape(span * enc_rows, D)
    memory_pair = low(dot(enc_all, memory_weight) + jnp.concatenate([zero_bias, own_bias[4]]))
    memory_all = gather(memory_pair, groups)
    enc_count = lax.dynamic_slice_in_dim(enc_lengths, local_seq, 1)

    residual_in = tokens.astype(jnp.float32)
    hidden_one = residual_in + dot(attended, attn_proj) + bias_rows[2]
    input_two = low(norm_apply(hidden_one, gain_rows[1], shift_rows[1]))
    cross_q = low(dot(input_two, query_in) + bias_rows[3])
    context = cross_forward(cross_q, memory_all, enc_count)
    hidden_two = hidden_one + dot(context, cross_proj) + bias_rows[5]
    input_three = low(norm_apply(hidden_two, gain_rows[2], shift_rows[2]))

    grad_all = gather(cotangent)
    input_three_all = gather(input_three)
    pre_act = dot(input_three_all, expand_local) + expand_bias.astype(jnp.float32)
    act = low(gelu_apply(pre_act))
    grad_act = dot_nt(grad_all, shrink_weight)
    grad_pre = low(jax.vjp(gelu_apply, pre_act)[1](grad_act)[0])
    grad_in_three = scatter(low(dot_nt(grad_pre, expand_local))).astype(jnp.float32)
    result = hidden_two + scatter(low(dot(act, shrink_weight))).astype(jnp.float32) + bias_rows[6]
    grad_shrink = dot_tn(act, grad_all)
    grad_expand = dot_tn(input_three_all, grad_pre)
    grad_hidden_bias = column_sums(grad_pre)
    total_shrink = rep_gather(rep_reduce(low(grad_shrink).reshape(size, hidden // size, D), 0), 0)
    own_expand = swap(rep_reduce(low(grad_expand).reshape(count, size, part_rows, hidden), 1))
    total_expand = rep_gather(own_expand.transpose(1, 0, 2).reshape(part_rows, count * hidden), 0)

    grad_out = cotangent.astype(jnp.float32)
    norm_three = jax.vjp(norm_apply, hidden_two, gain_rows[2], shift_rows[2])[1](grad_in_three)
    grad_two = grad_out + norm_three[0]
    grad_two_low = low(grad_two)
    grad_cross_proj = dot_tn(context, grad_two_low)
    grad_context = low(dot_nt(grad_two_low, cross_proj))
    grad_cross_q, memory_part = cross_backward(cross_q, memory_all, grad_context, enc_count)
    mem_grads = scatter(memory_part, groups)
    grad_memory = dot_tn(enc_all, mem_grads)
    grad_enc = scatter(low(dot_nt(mem_grads, memory_weight)), groups).astype(jnp.float32)
    grad_query_in = dot_tn(input_two, grad_cross_q)
    grad_in_two = dot_nt(grad_cross_q, query_in)
    norm_two = jax.vjp(norm_apply, hidden_one, gain_rows[1], shift_rows[1])[1](grad_in_two)
    grad_one = grad_two + norm_two[0]
    grad_one_low = low(grad_one)
    grad_attn_proj = dot_tn(attended, grad_one_low)
    grad_attn = low(dot_nt(grad_one_low, attn_proj))
    total_query, total_cross = reduce_weights([grad_query_in, grad_cross_proj])
    (total_proj,) = reduce_weights([grad_attn_proj])

    grad_att_heads = lax.all_to_all(grad_attn, "shard", 1, 0, tiled=True, axis_index_groups=groups)
    delta = jnp.sum((grad_att_heads.astype(jnp.float32) * att_full).reshape(SEQ, 2, HD), axis=-1).T
    grad_qkv = self_backward(qkv, grad_att_heads, lse.T, delta, seq_segments)
    grad_in_one = scatter(low(dot_nt(grad_qkv, qkv_weight)), groups).astype(jnp.float32)
    grad_attn_in = dot_tn(input_one_all, grad_qkv)
    norm_one = jax.vjp(norm_apply, residual_in, gain_rows[0], shift_rows[0])[1](grad_in_one)
    grad_tokens = grad_one + norm_one[0]

    heads_grad = low(jnp.concatenate([grad_attn_in, grad_memory], axis=1))
    own_heads = swap(rep_reduce(heads_grad.reshape(count, size, part_rows, 5 * width), 1))
    own_heads = own_heads.reshape(count // span, span, part_rows, 5 * width)
    own_heads = own_heads[0] if count == span else low(jnp.sum(own_heads.astype(jnp.float32), axis=0))
    total_heads = rep_gather(own_heads.transpose(1, 0, 2), 0).reshape(weight_rows, span, 5, width)
    total_heads = total_heads.transpose(0, 2, 1, 3).reshape(weight_rows, 5 * D).astype(jnp.float32)

    qkv_sums = column_sums(grad_qkv)
    zero_row = jnp.zeros((D,), jnp.float32)

    def at_own(values):
        return lax.dynamic_update_slice_in_dim(zero_row, values, local_pos * width, 0)

    small_grads = jnp.stack(
        [
            norm_one[1],
            norm_two[1],
            norm_three[1],
            norm_one[2],
            norm_two[2],
            norm_three[2],
            at_own(qkv_sums[:width]),
            at_own(qkv_sums[2 * width :]),
            column_sums(grad_one_low),
            column_sums(grad_cross_q),
            at_own(column_sums(mem_grads)[width:]),
            column_sums(grad_two_low),
            column_sums(cotangent),
        ]
    )
    small_grads = small_grads.reshape(small_count, count, shard_width).transpose(1, 0, 2)
    hidden_rows = hidden // shard_width
    hidden_grads = jnp.zeros((count, hidden_rows, shard_width), jnp.float32)
    hidden_grads = lax.dynamic_update_slice_in_dim(
        hidden_grads, grad_hidden_bias.reshape(1, hidden_rows, shard_width), shard_pos, 0
    )
    small_grads = low(jnp.concatenate([small_grads, hidden_grads], axis=1))
    small_grads = jnp.broadcast_to(small_grads, (size,) + small_grads.shape)
    small_grads = small_grads.reshape((size * count,) + small_grads.shape[2:])
    small_grads = lax.all_to_all(small_grads, ("rep", "shard"), 0, 0, tiled=True)
    total_small = jnp.sum(small_grads.astype(jnp.float32), axis=0)

    return (
        low(result),
        grad_tokens,
        grad_enc,
        total_heads[:, : 3 * D],
        total_proj,
        total_query,
        total_heads[:, 3 * D :],
        total_cross,
        total_expand.reshape(weight_rows, count * hidden).astype(jnp.float32),
        total_shrink.reshape(hidden, D).astype(jnp.float32),
        total_small[:3],
        total_small[3:6],
        total_small[6:small_count],
        total_small[small_count:].reshape(hidden),
    )


def solution(mesh):
    return jax.shard_map(
        shards,
        mesh=mesh,
        in_specs=(
            P(("rep", "shard"), None),
            P("rep"),
            P(("rep", "shard"), None),
            P("rep"),
            P(("rep", "shard"), None),
            P("shard", None),
            P("shard", None),
            P("shard", None),
            P("shard", None),
            P("shard", None),
            P("shard", None),
            P("shard", None),
            P(None, "shard"),
            P(None, "shard"),
            P(None, "shard"),
            P("shard"),
        ),
        out_specs=(
            P(("rep", "shard"), None),
            P(("rep", "shard"), None),
            P(("rep", "shard"), None),
            P("shard", None),
            P("shard", None),
            P("shard", None),
            P("shard", None),
            P("shard", None),
            P("shard", None),
            P("shard", None),
            P(None, "shard"),
            P(None, "shard"),
            P(None, "shard"),
            P("shard"),
        ),
        check_vma=False,
    )
```

```python
import functools

import jax
import jax.numpy as jnp
from jax import lax
from jax.experimental import pallas as pl
from jax.experimental.pallas import tpu as pltpu
from jax.sharding import PartitionSpec as P

D = 1024
H = 16
HD = 64
SEQ = 2048
PAIR = 2 * HD

EPS = 1e-05
NEGATIVE = -1e30
SCALE = HD**-0.5
BLOCK = 512
GELU = 0.7978845608028654
LITTLE = pl.CostEstimate(flops=1000, bytes_accessed=1000, transcendentals=0)


def norm_apply(rows, gain, shift):
    mean_rows = jnp.mean(rows, axis=-1, keepdims=True)
    centered = rows - mean_rows
    inverse = lax.rsqrt(jnp.mean(centered * centered, axis=-1, keepdims=True) + EPS)
    return centered * inverse * gain + shift


def gelu_apply(values):
    return jax.nn.gelu(values, approximate=True)


def column_sums(rows):
    return jnp.sum(rows, axis=0, dtype=jnp.float32)


def low(values):
    return values.astype(jnp.bfloat16)


def dot(left, right):
    return jnp.dot(left, right, preferred_element_type=jnp.float32)


def dot_nt(left, right):
    return lax.dot_general(left, right, (((1,), (1,)), ((), ())), preferred_element_type=jnp.float32)


def dot_tn(left, right):
    return lax.dot_general(left, right, (((0,), (0,)), ((), ())), preferred_element_type=jnp.float32)


def after(value, *earlier):
    return lax.optimization_barrier((value, earlier))[0]


def head_halves(rows, scale=None):
    lane = lax.broadcasted_iota(jnp.int32, rows.shape, 1)
    if scale is not None:
        rows = rows * jnp.asarray(scale, rows.dtype)
    zero = jnp.zeros_like(rows)
    return jnp.where(lane < HD, rows, zero), jnp.where(lane < HD, zero, rows)


def self_forward_kernel(ends, q_ref, k_ref, v_ref, seg_col, seg_row, low_ref, full_ref, lse_ref):
    step = pl.program_id(0)
    rows = q_ref.shape[0]
    queries = head_halves(q_ref[...], SCALE)
    query_seg = seg_col[...]
    last_seg = ends[1, step]

    def piece(index, state, masked, diagonal):
        keys = k_ref[pl.ds(index * rows, rows), :]
        values = v_ref[pl.ds(index * rows, rows), :]
        keep = None
        if masked:
            keep = seg_row[:, pl.ds(index * rows, rows)] == query_seg
            if diagonal:
                key_pos = lax.broadcasted_iota(jnp.int32, (rows, rows), 1)
                query_pos = lax.broadcasted_iota(jnp.int32, (rows, rows), 0)
                keep = keep & (key_pos <= query_pos)
        after = []
        for head in range(2):
            top, total, acc = state[head]
            scores = dot_nt(queries[head], keys)
            if masked:
                scores = jnp.where(keep, scores, NEGATIVE)
            top_new = jnp.maximum(top, jnp.max(scores, axis=1, keepdims=True))
            expo = jnp.exp(scores - top_new)
            fade = jnp.exp(top - top_new)
            after.append(
                (
                    top_new,
                    total * fade + jnp.sum(expo, axis=1, keepdims=True),
                    acc * fade + dot(low(expo), values),
                )
            )
        return tuple(after)

    def before(index, state):
        return lax.cond(
            ends[0, index] == last_seg,
            lambda s: piece(index, s, False, False),
            lambda s: piece(index, s, True, False),
            state,
        )

    blank = (
        jnp.full((rows, 1), NEGATIVE, jnp.float32),
        jnp.zeros((rows, 1), jnp.float32),
        jnp.zeros((rows, PAIR), jnp.float32),
    )
    state = lax.fori_loop(0, step, before, (blank, blank))
    state = piece(step, state, True, True)
    lane = lax.broadcasted_iota(jnp.int32, (rows, PAIR), 1)
    joined = jnp.where(lane < HD, state[0][2] / state[0][1], state[1][2] / state[1][1])
    full_ref[...] = joined
    low_ref[...] = low(joined)
    lse_ref[:, 0:1] = state[0][0] + jnp.log(state[0][1])
    lse_ref[:, 1:2] = state[1][0] + jnp.log(state[1][1])


def block_ends(segments, rows):
    return jnp.stack([segments[::rows], segments[rows - 1 :: rows]])


def self_forward(qkv, segments):
    count = qkv.shape[0]
    rows = BLOCK
    col = segments[:, None]
    row = segments[None, :]
    grid_spec = pltpu.PrefetchScalarGridSpec(
        num_scalar_prefetch=1,
        grid=(count // rows,),
        in_specs=[
            pl.BlockSpec((rows, PAIR), lambda i, e: (i, 0)),
            pl.BlockSpec((count, PAIR), lambda i, e: (0, 1)),
            pl.BlockSpec((count, PAIR), lambda i, e: (0, 2)),
            pl.BlockSpec((rows, 1), lambda i, e: (i, 0)),
            pl.BlockSpec((1, count), lambda i, e: (0, 0)),
        ],
        out_specs=[
            pl.BlockSpec((rows, PAIR), lambda i, e: (i, 0)),
            pl.BlockSpec((rows, PAIR), lambda i, e: (i, 0)),
            pl.BlockSpec((rows, 2), lambda i, e: (i, 0)),
        ],
    )
    return pl.pallas_call(
        self_forward_kernel,
        grid_spec=grid_spec,
        out_shape=(
            jax.ShapeDtypeStruct((count, PAIR), jnp.bfloat16),
            jax.ShapeDtypeStruct((count, PAIR), jnp.float32),
            jax.ShapeDtypeStruct((count, 2), jnp.float32),
        ),
        compiler_params=pltpu.CompilerParams(vmem_limit_bytes=40 * 2**20),
        cost_estimate=LITTLE,
    )(block_ends(segments, rows), qkv, qkv, qkv, col, row)


def self_backward_kernel(
    ends, q_ref, k_ref, v_ref, go_ref, lse_ref, delta_ref, seg_col, seg_row, grad_ref, acc_q, acc_k, acc_v
):
    step = pl.program_id(0)
    blocks = pl.num_programs(0)
    rows = k_ref.shape[0]

    @pl.when(step == 0)
    def _():
        acc_q[...] = jnp.zeros_like(acc_q)

    keys = k_ref[...]
    values = v_ref[...]
    key_halves = head_halves(keys, SCALE)
    key_seg = seg_col[...]
    first_seg = ends[0, step]

    def piece(index, masked, diagonal):
        place = pl.ds(pl.multiple_of(index * rows, rows), rows)
        queries = head_halves(q_ref[place, :], SCALE)
        grads = head_halves(go_ref[place, :])
        keep = None
        if masked:
            keep = seg_row[:, place] == key_seg
            if diagonal:
                key_pos = lax.broadcasted_iota(jnp.int32, (rows, rows), 0)
                query_pos = lax.broadcasted_iota(jnp.int32, (rows, rows), 1)
                keep = keep & (key_pos <= query_pos)
        sum_q = sum_k = sum_v = None
        for head in range(2):
            scores = dot_nt(keys, queries[head])
            probs = jnp.exp(scores - lse_ref[head : head + 1, place])
            if masked:
                probs = jnp.where(keep, probs, 0.0)
            part_v = dot(low(probs), grads[head])
            grad_probs = dot_nt(values, grads[head])
            grad_scores = low(probs * (grad_probs - delta_ref[head : head + 1, place]))
            part_k = dot(grad_scores, queries[head])
            part_q = dot_tn(grad_scores, key_halves[head])
            sum_q = part_q if sum_q is None else sum_q + part_q
            sum_k = part_k if sum_k is None else sum_k + part_k
            sum_v = part_v if sum_v is None else sum_v + part_v
        acc_q[place, :] += sum_q
        if diagonal:
            acc_k[...] = sum_k
            acc_v[...] = sum_v
        else:
            acc_k[...] += sum_k
            acc_v[...] += sum_v

    piece(step, True, True)

    @pl.loop(step + 1, blocks)
    def _(index):
        whole = ends[1, index] == first_seg

        @pl.when(whole)
        def _():
            piece(index, False, False)

        @pl.when(jnp.logical_not(whole))
        def _():
            piece(index, True, False)

    own = pl.ds(pl.multiple_of(step * rows, rows), rows)
    grad_ref[own, 0:PAIR] = low(acc_q[own, :])
    grad_ref[own, PAIR : 2 * PAIR] = low(acc_k[...])
    grad_ref[own, 2 * PAIR : 3 * PAIR] = low(acc_v[...])


def self_backward(qkv, grad_att, lse, delta, segments):
    count = qkv.shape[0]
    rows = BLOCK
    col = segments[:, None]
    row = segments[None, :]
    whole = lambda i, e: (0, 0)
    grid_spec = pltpu.PrefetchScalarGridSpec(
        num_scalar_prefetch=1,
        grid=(count // rows,),
        in_specs=[
            pl.BlockSpec((count, PAIR), whole),
            pl.BlockSpec((rows, PAIR), lambda i, e: (i, 1)),
            pl.BlockSpec((rows, PAIR), lambda i, e: (i, 2)),
            pl.BlockSpec((count, PAIR), whole),
            pl.BlockSpec((2, count), whole),
            pl.BlockSpec((2, count), whole),
            pl.BlockSpec((rows, 1), lambda i, e: (i, 0)),
            pl.BlockSpec((1, count), whole),
        ],
        out_specs=pl.BlockSpec((count, 3 * PAIR), whole),
        scratch_shapes=[
            pltpu.VMEM((count, PAIR), jnp.float32),
            pltpu.VMEM((rows, PAIR), jnp.float32),
            pltpu.VMEM((rows, PAIR), jnp.float32),
        ],
    )
    return pl.pallas_call(
        self_backward_kernel,
        grid_spec=grid_spec,
        out_shape=jax.ShapeDtypeStruct((count, 3 * PAIR), jnp.bfloat16),
        compiler_params=pltpu.CompilerParams(vmem_limit_bytes=40 * 2**20),
        cost_estimate=LITTLE,
    )(block_ends(segments, rows), qkv, qkv, qkv, grad_att, lse, delta, col, row)


def cross_forward_kernel(length, q_ref, m_ref, out_ref):
    queries = head_halves(q_ref[...], SCALE)
    keys = m_ref[:, :PAIR]
    values = m_ref[:, PAIR:]
    shape = (q_ref.shape[0], m_ref.shape[0])
    keep = lax.broadcasted_iota(jnp.int32, shape, 1) < length[0]
    parts = []
    for head in range(2):
        scores = jnp.where(keep, dot_nt(queries[head], keys), NEGATIVE)
        expo = jnp.exp(scores - jnp.max(scores, axis=1, keepdims=True))
        parts.append(dot(low(expo), values) / jnp.sum(expo, axis=1, keepdims=True))
    lane = lax.broadcasted_iota(jnp.int32, parts[0].shape, 1)
    out_ref[...] = low(jnp.where(lane < HD, parts[0], parts[1]))


def cross_forward(queries, memory, length):
    count, states = queries.shape[0], memory.shape[0] // (D // PAIR)
    grid_spec = pltpu.PrefetchScalarGridSpec(
        num_scalar_prefetch=1,
        grid=(D // PAIR,),
        in_specs=[
            pl.BlockSpec((count, PAIR), lambda i, e: (0, i)),
            pl.BlockSpec((states, 2 * PAIR), lambda i, e: (i, 0)),
        ],
        out_specs=pl.BlockSpec((count, PAIR), lambda i, e: (0, i)),
    )
    return pl.pallas_call(
        cross_forward_kernel,
        grid_spec=grid_spec,
        out_shape=jax.ShapeDtypeStruct((count, D), jnp.bfloat16),
        cost_estimate=LITTLE,
    )(length, queries, memory)


def cross_backward_kernel(length, q_ref, m_ref, g_ref, dq_ref, dm_ref):
    queries = head_halves(q_ref[...], SCALE)
    grads = head_halves(g_ref[...])
    keys = m_ref[:, :PAIR]
    values = m_ref[:, PAIR:]
    key_halves = head_halves(keys, SCALE)
    shape = (m_ref.shape[0], q_ref.shape[0])
    keep = lax.broadcasted_iota(jnp.int32, shape, 0) < length[0]
    sum_q = sum_k = sum_v = None
    for head in range(2):
        scores = jnp.where(keep, dot_nt(keys, queries[head]), NEGATIVE)
        expo = jnp.exp(scores - jnp.max(scores, axis=0, keepdims=True))
        probs = expo * (1.0 / jnp.sum(expo, axis=0, keepdims=True))
        part_v = dot(low(probs), grads[head])
        grad_probs = dot_nt(values, grads[head])
        inner = jnp.sum(probs * grad_probs, axis=0, keepdims=True)
        grad_scores = low(probs * (grad_probs - inner))
        part_k = dot(grad_scores, queries[head])
        part_q = dot_tn(grad_scores, key_halves[head])
        sum_q = part_q if sum_q is None else sum_q + part_q
        sum_k = part_k if sum_k is None else sum_k + part_k
        sum_v = part_v if sum_v is None else sum_v + part_v
    dq_ref[...] = low(sum_q)
    dm_ref[:, :PAIR] = low(sum_k)
    dm_ref[:, PAIR:] = low(sum_v)


def cross_backward(queries, memory, grads, length):
    count, states = queries.shape[0], memory.shape[0] // (D // PAIR)
    grid_spec = pltpu.PrefetchScalarGridSpec(
        num_scalar_prefetch=1,
        grid=(D // PAIR,),
        in_specs=[
            pl.BlockSpec((count, PAIR), lambda i, e: (0, i)),
            pl.BlockSpec((states, 2 * PAIR), lambda i, e: (i, 0)),
            pl.BlockSpec((count, PAIR), lambda i, e: (0, i)),
        ],
        out_specs=[
            pl.BlockSpec((count, PAIR), lambda i, e: (0, i)),
            pl.BlockSpec((states, 2 * PAIR), lambda i, e: (i, 0)),
        ],
    )
    return pl.pallas_call(
        cross_backward_kernel,
        grid_spec=grid_spec,
        out_shape=(
            jax.ShapeDtypeStruct((count, D), jnp.bfloat16),
            jax.ShapeDtypeStruct((states * (D // PAIR), 2 * PAIR), jnp.bfloat16),
        ),
        cost_estimate=LITTLE,
    )(length, queries, memory, grads)


def front_kernel(x_ref, e_ref, gain, shift, qkv_w, qkv_b, mem_w, mem_b, one_ref, qkv_ref, enc_ref, mem_ref):
    rows = x_ref[0].astype(jnp.float32)
    centered = rows - jnp.mean(rows, axis=-1, keepdims=True)
    inverse = lax.rsqrt(jnp.mean(centered * centered, axis=-1, keepdims=True) + EPS)
    one = low(centered * inverse * gain[...] + shift[...])
    one_ref[...] = one
    qkv_ref[...] = low(dot(one, qkv_w[...]) + qkv_b[...])
    enc_ref[...] = e_ref[0]
    mem_ref[...] = low(dot(e_ref[0], mem_w[...]) + mem_b[...])


def front(rows_all, row_count, gain, shift, qkv_w, qkv_b, mem_w, mem_b):
    span, both, _ = rows_all.shape
    enc_rows = both - row_count
    whole = lambda i: (0, 0)
    return pl.pallas_call(
        front_kernel,
        grid=(span,),
        in_specs=[
            pl.BlockSpec((1, row_count, D), lambda i: (i, 0, 0)),
            pl.BlockSpec((1, enc_rows, D), lambda i: (i, row_count // enc_rows, 0)),
            pl.BlockSpec((1, D), whole),
            pl.BlockSpec((1, D), whole),
            pl.BlockSpec(qkv_w.shape, whole),
            pl.BlockSpec((1, qkv_w.shape[1]), whole),
            pl.BlockSpec(mem_w.shape, whole),
            pl.BlockSpec((1, mem_w.shape[1]), whole),
        ],
        out_specs=[
            pl.BlockSpec((row_count, D), lambda i: (i, 0)),
            pl.BlockSpec((row_count, qkv_w.shape[1]), lambda i: (i, 0)),
            pl.BlockSpec((enc_rows, D), lambda i: (i, 0)),
            pl.BlockSpec((enc_rows, mem_w.shape[1]), lambda i: (i, 0)),
        ],
        out_shape=(
            jax.ShapeDtypeStruct((span * row_count, D), jnp.bfloat16),
            jax.ShapeDtypeStruct((span * row_count, qkv_w.shape[1]), jnp.bfloat16),
            jax.ShapeDtypeStruct((span * enc_rows, D), jnp.bfloat16),
            jax.ShapeDtypeStruct((span * enc_rows, mem_w.shape[1]), jnp.bfloat16),
        ),
        compiler_params=pltpu.CompilerParams(vmem_limit_bytes=32 * 2**20),
        cost_estimate=LITTLE,
    )(rows_all, rows_all, gain[None], shift[None], qkv_w, qkv_b[None], mem_w, mem_b[None])


def gain_kernel(x_ref, g_ref, out_ref):
    rows = x_ref[0].astype(jnp.float32)
    centered = rows - jnp.mean(rows, axis=-1, keepdims=True)
    inverse = lax.rsqrt(jnp.mean(centered * centered, axis=-1, keepdims=True) + EPS)
    grads = g_ref[...].astype(jnp.float32)

    @pl.when(pl.program_id(0) == 0)
    def _():
        out_ref[...] = jnp.zeros_like(out_ref)

    out_ref[0:1, :] += jnp.sum(grads * (centered * inverse), axis=0, keepdims=True)
    out_ref[1:2, :] += jnp.sum(grads, axis=0, keepdims=True)


def gain_sums(rows_all, row_count, grads):
    span = rows_all.shape[0]
    return pl.pallas_call(
        gain_kernel,
        grid=(span,),
        in_specs=[
            pl.BlockSpec((1, row_count, D), lambda i: (i, 0, 0)),
            pl.BlockSpec((row_count, D), lambda i: (i, 0)),
        ],
        out_specs=pl.BlockSpec((2, D), lambda i: (0, 0)),
        out_shape=jax.ShapeDtypeStruct((2, D), jnp.float32),
        cost_estimate=LITTLE,
    )(rows_all, grads)


def feed_kernel(x_ref, w_ref, b_ref, ga_ref, act_ref, pre_ref, in_ref, sum_ref):
    v = dot(x_ref[...], w_ref[...]) + b_ref[...]
    square = v * v
    half = 0.5 + 0.5 * jnp.tanh(v * (GELU + GELU * 0.044715 * square))
    act_ref[...] = low(v * half)
    slope = half + (v * half) * (1.0 - half) * (2.0 * GELU + 6.0 * GELU * 0.044715 * square)
    grad = low(ga_ref[...] * slope)
    pre_ref[...] = grad
    in_ref[...] = low(dot_nt(grad, w_ref[...]))

    @pl.when(pl.program_id(0) == 0)
    def _():
        sum_ref[...] = jnp.zeros_like(sum_ref)

    sum_ref[...] += jnp.sum(grad.astype(jnp.float32), axis=0, keepdims=True)


def feed(rows, weight, bias, grad_act):
    count, hidden = grad_act.shape
    tile = 256
    whole = lambda i: (0, 0)
    block = lambda i: (i, 0)
    return pl.pallas_call(
        feed_kernel,
        grid=(count // tile,),
        in_specs=[
            pl.BlockSpec((tile, D), block),
            pl.BlockSpec((D, hidden), whole),
            pl.BlockSpec((1, hidden), whole),
            pl.BlockSpec((tile, hidden), block),
        ],
        out_specs=[
            pl.BlockSpec((tile, hidden), block),
            pl.BlockSpec((tile, hidden), block),
            pl.BlockSpec((tile, D), block),
            pl.BlockSpec((1, hidden), whole),
        ],
        out_shape=(
            jax.ShapeDtypeStruct((count, hidden), jnp.bfloat16),
            jax.ShapeDtypeStruct((count, hidden), jnp.bfloat16),
            jax.ShapeDtypeStruct((count, D), jnp.bfloat16),
            jax.ShapeDtypeStruct((1, hidden), jnp.float32),
        ),
        compiler_params=pltpu.CompilerParams(vmem_limit_bytes=58 * 2**20),
        cost_estimate=LITTLE,
    )(rows, weight, bias[None], grad_act)


def rep_send(value, step):
    size = lax.axis_size("rep")
    return lax.ppermute(value, "rep", [(i, i ^ step) for i in range(size)])


def rep_start(value):
    return [value] + [rep_send(value, step) for step in range(1, lax.axis_size("rep"))]


def rep_place(parts, axis):
    size, me = lax.axis_size("rep"), lax.axis_index("rep")
    value = parts[0]
    out = jnp.zeros(value.shape[:axis] + (size,) + value.shape[axis:], value.dtype)
    for step, part in enumerate(parts):
        out = lax.dynamic_update_slice_in_dim(out, jnp.expand_dims(part, axis), me ^ step, axis)
    return out


def spread_kernel(place, *refs):
    out_ref = refs[-1]
    for step, part in enumerate(refs[:-1]):
        out_ref[pl.ds(place[0] ^ step, 1)] = part[...].astype(out_ref.dtype)[None]


def spread(parts, first, last, dtype):
    size, columns = len(parts), parts[0].shape[1]
    rows = last - first
    if rows % 32 or first % rows or parts[0].shape[0] % 16:
        return rep_place([part[first:last] for part in parts], 0).astype(dtype)
    tile = rows // 2
    grid_spec = pltpu.PrefetchScalarGridSpec(
        num_scalar_prefetch=1,
        grid=(2,),
        in_specs=[pl.BlockSpec((tile, columns), lambda i, e: (first // tile + i, 0))] * size,
        out_specs=pl.BlockSpec((size, tile, columns), lambda i, e: (0, i, 0)),
    )
    return pl.pallas_call(
        spread_kernel,
        grid_spec=grid_spec,
        out_shape=jax.ShapeDtypeStruct((size, rows, columns), dtype),
        compiler_params=pltpu.CompilerParams(vmem_limit_bytes=40 * 2**20),
        cost_estimate=LITTLE,
    )(lax.axis_index("rep")[None], *parts)


def rep_gather(value, axis):
    return rep_place(rep_start(value), axis)


def rep_swap(parts):
    return lax.all_to_all(parts, "rep", 0, 0, tiled=True)


def rep_split(parts, axis):
    size, me = lax.axis_size("rep"), lax.axis_index("rep")
    picks = [lax.dynamic_index_in_dim(parts, me ^ step, axis, keepdims=False) for step in range(size)]
    return [picks[0]] + [rep_send(low(picks[step]), step) for step in range(1, size)]


def sum_first(parts):
    return low(jnp.sum(parts.astype(jnp.float32), axis=0))


def add_up(parts):
    total = parts[0].astype(jnp.float32)
    for part in parts[1:]:
        total = total + part.astype(jnp.float32)
    return low(total)


def rep_reduce(parts, axis):
    return add_up(rep_split(parts, axis))


def core_send(value):
    size = lax.axis_size("shard")
    return lax.ppermute(value, "shard", [(i, i ^ 1) for i in range(size)])


def line_send(value, step, group=None):
    size = lax.axis_size("shard")
    group = group or size
    route = [(i, i // group * group + (i + 2 * step) % group) for i in range(size)]
    return lax.ppermute(value, "shard", route)


def line_scatter_start(value, group=None):
    group = group or lax.axis_size("shard")
    core = lax.axis_index("shard") % 2
    value = value.reshape((group // 2, 2, value.shape[0] // group) + value.shape[1:])
    mine = lax.dynamic_index_in_dim(value, core, 1, keepdims=False)
    theirs = lax.dynamic_index_in_dim(value, 1 - core, 1, keepdims=False)
    return [mine, core_send(theirs)]


def line_scatter_middle(both, group=None):
    group = group or lax.axis_size("shard")
    chips = group // 2
    chip = lax.axis_index("shard") % group // 2
    line = add_up(both)
    parts = [lax.dynamic_index_in_dim(line, (chip + step) % chips, 0, keepdims=False) for step in range(chips)]
    return [parts[0]] + [line_send(parts[step], step, group) for step in range(1, chips)]


def columns_kernel(place, *refs):
    out_ref = refs[-1]
    rows = out_ref.shape[1]
    for step, part in enumerate(refs[:-1]):
        for block in range(part.shape[0] // rows):
            wide = part[block * rows : (block + 1) * rows, :].astype(out_ref.dtype)
            out_ref[pl.ds(place[0] ^ step, 1), :, block * D : (block + 1) * D] = wide[None]


def spread_columns(parts, first, blocks, rows):
    size, me = len(parts), lax.axis_index("rep")
    if rows % 16:
        parts = [part[first:].reshape(blocks, rows, -1).transpose(1, 0, 2).reshape(rows, -1) for part in parts]
        return rep_place(parts, 0).astype(jnp.float32).reshape(size * rows, -1)
    halves = 2
    taken = blocks * rows // halves
    grid_spec = pltpu.PrefetchScalarGridSpec(
        num_scalar_prefetch=1,
        grid=(halves,),
        in_specs=[pl.BlockSpec((taken, D), lambda i, e: (first // taken + i, 0))] * size,
        out_specs=pl.BlockSpec((size, rows, blocks * D // halves), lambda i, e: (0, 0, i)),
    )
    out = pl.pallas_call(
        columns_kernel,
        grid_spec=grid_spec,
        out_shape=jax.ShapeDtypeStruct((size, rows, blocks * D), jnp.float32),
        compiler_params=pltpu.CompilerParams(vmem_limit_bytes=40 * 2**20),
        cost_estimate=LITTLE,
    )(me[None], *parts)
    return out.reshape(size * rows, blocks * D)


def heads_kernel(span, place, *refs):
    qkv_ref, memory_ref = refs[-2:]
    rows, width = qkv_ref.shape[1], D // span
    for step, part in enumerate(refs[:-2]):
        take = pl.ds(place[0] ^ step, 1)
        for block in range(span):
            wide = part[block * rows : (block + 1) * rows, :].astype(jnp.float32)[None]
            for kind in range(5):
                out, at = (qkv_ref, kind) if kind < 3 else (memory_ref, kind - 3)
                columns = slice(at * D + block * width, at * D + (block + 1) * width)
                out[take, :, columns] = wide[:, :, kind * width : (kind + 1) * width]


def spread_heads(parts, span, rows, width):
    size, me = len(parts), lax.axis_index("rep")
    if rows % 16:
        full = rep_place([part[: span * rows].reshape(span, rows, 5, width) for part in parts], 0)
        full = full.transpose(0, 2, 3, 1, 4).reshape(size * rows, 5 * D).astype(jnp.float32)
        return full[:, : 3 * D], full[:, 3 * D :]
    grid_spec = pltpu.PrefetchScalarGridSpec(
        num_scalar_prefetch=1,
        grid=(1,),
        in_specs=[pl.BlockSpec((span * rows, 5 * width), lambda i, e: (0, 0))] * size,
        out_specs=[
            pl.BlockSpec((size, rows, 3 * D), lambda i, e: (0, 0, 0)),
            pl.BlockSpec((size, rows, 2 * D), lambda i, e: (0, 0, 0)),
        ],
    )
    qkv, memory = pl.pallas_call(
        functools.partial(heads_kernel, span),
        grid_spec=grid_spec,
        out_shape=(
            jax.ShapeDtypeStruct((size, rows, 3 * D), jnp.float32),
            jax.ShapeDtypeStruct((size, rows, 2 * D), jnp.float32),
        ),
        compiler_params=pltpu.CompilerParams(vmem_limit_bytes=40 * 2**20),
        cost_estimate=LITTLE,
    )(me[None], *parts)
    return qkv.reshape(size * rows, 3 * D), memory.reshape(size * rows, 2 * D)


def weight_line(piece):
    kinds, rows, columns = piece.shape
    chips = lax.axis_size("shard") // 2
    chip = lax.axis_index("shard") // 2
    line = jnp.zeros((kinds, chips, rows, columns), piece.dtype)
    for step in range(chips):
        part = line_send(piece, step) if step else piece
        line = lax.dynamic_update_slice_in_dim(line, part[:, None], (chip - step) % chips, 1)
    return line


def join_kernel(place, *refs):
    outs = refs[-3:]
    parts = refs[:-3]
    size = len(parts) // 2
    for core in range(2):
        side = place[1] ^ core
        for step in range(size):
            for kind in range(3):
                outs[kind][0, pl.ds(side, 1), pl.ds(place[0] ^ step, 1)] = parts[core * size + step][kind][None]


def weight_join(mine, other):
    size = len(mine)
    _, chips, rows, _ = mine[0].shape
    core = lax.axis_index("shard") % 2
    if rows % 16:
        first = core == 0
        plane, next_plane = rep_place(mine, 2), rep_place(other, 2)
        low_core, high_core = jnp.where(first, plane, next_plane), jnp.where(first, next_plane, plane)
        full = jnp.stack([low_core, high_core], axis=2).reshape(3, D, D)
        return full[0], full[1], full[2]
    grid_spec = pltpu.PrefetchScalarGridSpec(
        num_scalar_prefetch=1,
        grid=(chips,),
        in_specs=[pl.BlockSpec((3, 1, rows, D), lambda i, e: (0, i, 0, 0))] * (2 * size),
        out_specs=[pl.BlockSpec((1, 2, size, rows, D), lambda i, e: (i, 0, 0, 0, 0))] * 3,
    )
    outs = pl.pallas_call(
        join_kernel,
        grid_spec=grid_spec,
        out_shape=(jax.ShapeDtypeStruct((chips, 2, size, rows, D), jnp.bfloat16),) * 3,
        compiler_params=pltpu.CompilerParams(vmem_limit_bytes=40 * 2**20),
        cost_estimate=LITTLE,
    )(jnp.stack([lax.axis_index("rep"), core]), *mine, *other)
    return tuple(out.reshape(D, D) for out in outs)


def plain_kernel(core, a_ref, b_ref, c_ref, ga_ref, gb_ref, gc_ref, mine_ref, theirs_ref):
    width = a_ref.shape[1] // 2
    for kind, (left, right) in enumerate(((a_ref, ga_ref), (b_ref, gb_ref), (c_ref, gc_ref))):
        for side, out in enumerate((mine_ref, theirs_ref)):
            place = pl.ds(pl.multiple_of((core[0] ^ side) * width, width), width)
            out[kind, 0] = low(dot_tn(left[:, place], right[...])).reshape(out.shape[2:])


def plain_grads(lefts, rights):
    size, chips = lax.axis_size("rep"), lax.axis_size("shard") // 2
    core = lax.axis_index("shard") % 2
    rows = D // (2 * chips * size)
    if rows % 16:
        stack = jnp.stack([low(dot_tn(left, right)) for left, right in zip(lefts, rights)])
        stack = stack.reshape(3, chips, 2, size, rows, D)
        return [lax.dynamic_index_in_dim(stack, core ^ side, 2, keepdims=False) for side in range(2)]
    count = lefts[0].shape[0]
    grid_spec = pltpu.PrefetchScalarGridSpec(
        num_scalar_prefetch=1,
        grid=(chips,),
        in_specs=[pl.BlockSpec((count, D // chips), lambda i, e: (0, i))] * 3
        + [pl.BlockSpec((count, D), lambda i, e: (0, 0))] * 3,
        out_specs=[pl.BlockSpec((3, 1, size, rows, D), lambda i, e: (0, i, 0, 0, 0))] * 2,
    )
    return pl.pallas_call(
        plain_kernel,
        grid_spec=grid_spec,
        out_shape=(jax.ShapeDtypeStruct((3, chips, size, rows, D), jnp.bfloat16),) * 2,
        compiler_params=pltpu.CompilerParams(vmem_limit_bytes=40 * 2**20),
        cost_estimate=LITTLE,
    )(core[None], *lefts, *rights)


def split_kernel(place, mine_ref, other_ref, *outs):
    for step, out in enumerate(outs):
        take = pl.ds(place[0] ^ step, 1)
        total = mine_ref[:, 0, take].astype(jnp.float32) + other_ref[:, 0, take].astype(jnp.float32)
        out[...] = low(total)


def core_sum_split(mine, other):
    kinds, chips, size, rows, _ = mine.shape
    if rows % 16:
        total = add_up([mine, other])
        me = lax.axis_index("rep")
        return [lax.dynamic_index_in_dim(total, me ^ step, 2, keepdims=False) for step in range(size)]
    grid_spec = pltpu.PrefetchScalarGridSpec(
        num_scalar_prefetch=1,
        grid=(chips,),
        in_specs=[pl.BlockSpec((kinds, 1, size, rows, D), lambda i, e: (0, i, 0, 0, 0))] * 2,
        out_specs=[pl.BlockSpec((kinds, 1, rows, D), lambda i, e: (0, i, 0, 0))] * size,
    )
    return pl.pallas_call(
        split_kernel,
        grid_spec=grid_spec,
        out_shape=(jax.ShapeDtypeStruct((kinds, chips, rows, D), jnp.bfloat16),) * size,
        compiler_params=pltpu.CompilerParams(vmem_limit_bytes=40 * 2**20),
        cost_estimate=LITTLE,
    )(lax.axis_index("rep")[None], mine, other)


def reduce_line(line):
    chips = lax.axis_size("shard") // 2
    chip = lax.axis_index("shard") // 2
    parts = [lax.dynamic_index_in_dim(line, (chip + step) % chips, 1, keepdims=False) for step in range(chips)]
    return [parts[0]] + [line_send(parts[step], step) for step in range(1, chips)]


def shards(
    tokens,
    segments,
    enc_states,
    enc_lengths,
    cotangent,
    self_qkv,
    self_out,
    cross_query,
    cross_memory,
    cross_out,
    expand_weight,
    shrink_weight,
    norm_gain,
    norm_bias,
    proj_bias,
    expand_bias,
):
    row_count, enc_rows = tokens.shape[0], enc_states.shape[0]
    span = SEQ // row_count
    width = D // span
    count = lax.axis_size("shard")
    size = lax.axis_size("rep")
    rep_pos = lax.axis_index("rep")
    shard_pos = lax.axis_index("shard")
    local_pos = shard_pos % span
    local_seq = shard_pos // span
    groups = None
    if count != span:
        groups = [[g * span + i for i in range(span)] for g in range(count // span)]
    weight_rows = self_qkv.shape[0]
    part_rows = weight_rows // size
    hidden = expand_bias.shape[0]
    shard_width = norm_gain.shape[1]

    def gather(value, groups=None):
        return lax.all_gather(value, "shard", axis=0, tiled=True, axis_index_groups=groups)

    def scatter(value, groups=None):
        return lax.psum_scatter(value, "shard", scatter_dimension=0, tiled=True, axis_index_groups=groups)

    def swap(value):
        return lax.all_to_all(value, "shard", 0, 0, tiled=True)

    def own_part(weight):
        return lax.dynamic_slice_in_dim(weight, rep_pos * part_rows, part_rows, axis=0)

    def by_pairs(weight, kinds):
        blocks = weight.reshape(part_rows, kinds, span, width).transpose(2, 0, 1, 3)
        return blocks.reshape(span, part_rows, kinds * width)

    rows_all = gather(jnp.concatenate([tokens, enc_states], axis=0), groups)
    blocks = jnp.concatenate([by_pairs(own_part(self_qkv), 3), by_pairs(own_part(cross_memory), 2)], axis=2)
    blocks = jnp.tile(blocks, (count // span, 1, 1))
    small = jnp.concatenate([norm_gain, norm_bias, proj_bias], axis=0)
    small_count = small.shape[0]
    small_rows = -(-small.size // (5 * width))
    small = jnp.pad(small.reshape(-1), (0, small_rows * 5 * width - small.size)).reshape(small_rows, 5 * width)
    blocks = jnp.concatenate([blocks, jnp.broadcast_to(small, (count,) + small.shape)], axis=1)
    swapped = swap(blocks)
    small_all = swapped[:, part_rows:].reshape(count, small_rows * 5 * width)[:, : small_count * shard_width]
    small_all = small_all.reshape(count, small_count, shard_width)
    small_all = small_all.transpose(1, 0, 2).reshape(small_count, D).astype(jnp.float32)
    gain_rows, shift_rows, bias_rows = small_all[:3], small_all[3:6], small_all[6:]
    head_weight = rep_gather(swapped[:, :part_rows], 1).reshape(D, 5 * width)
    qkv_weight, memory_weight = head_weight[:, : 3 * width], head_weight[:, 3 * width :]
    plain_part = jnp.stack([own_part(self_out), own_part(cross_query), own_part(cross_out)])
    plain_line = weight_line(after(plain_part, swapped))
    rows_all, plain_line, head_weight = lax.optimization_barrier((rows_all, plain_line, head_weight))
    plain_mine = rep_start(plain_line)
    expand_part = own_part(expand_weight).reshape(part_rows, count, hidden).transpose(1, 0, 2)
    expand_swapped = swap(after(expand_part, rows_all))
    grad_all = gather(after(cotangent, rows_all))

    rows_all = rows_all.reshape(span, row_count + enc_rows, D)
    seq_segments = lax.dynamic_slice_in_dim(segments, local_seq * SEQ, SEQ)
    own_bias = lax.dynamic_slice_in_dim(bias_rows, local_pos * width, width, axis=1)
    zero_bias = jnp.zeros((width,), jnp.float32)
    qkv_bias = jnp.concatenate([own_bias[0], zero_bias, own_bias[1]])
    memory_bias = jnp.concatenate([zero_bias, own_bias[4]])
    input_one_all, qkv, enc_all, memory_pair = front(
        rows_all, row_count, gain_rows[0], shift_rows[0], qkv_weight, qkv_bias, memory_weight, memory_bias
    )
    att_low, att_full, lse = self_forward(qkv, seq_segments)
    att_low, expand_swapped = lax.optimization_barrier((att_low, expand_swapped))
    attended = lax.all_to_all(att_low, "shard", 0, 1, tiled=True, axis_index_groups=groups)

    memory_all = gather(after(memory_pair, grad_all, att_low), groups)
    enc_count = lax.dynamic_slice_in_dim(enc_lengths, local_seq, 1)
    plain_other = [core_send(part) for part in plain_mine]

    plain_mine, plain_other = after((plain_mine, plain_other), att_low)
    attn_proj, query_in, cross_proj = weight_join(plain_mine, plain_other)
    attended, attn_proj, query_in, cross_proj = lax.optimization_barrier((attended, attn_proj, query_in, cross_proj))
    expand_parts = rep_start(after(expand_swapped, attended).reshape(count * part_rows, hidden))
    residual_in = tokens.astype(jnp.float32)
    hidden_one = residual_in + dot(attended, attn_proj) + bias_rows[2]
    input_two = low(norm_apply(hidden_one, gain_rows[1], shift_rows[1]))
    cross_q = low(dot(input_two, query_in) + bias_rows[3])
    context = cross_forward(cross_q, memory_all, enc_count)
    hidden_two = hidden_one + dot(context, cross_proj) + bias_rows[5]
    input_three = low(norm_apply(hidden_two, gain_rows[2], shift_rows[2]))

    input_three_all = gather(after(input_three, grad_all))
    expand_parts, grad_all_now = after((expand_parts, grad_all), input_three)
    expand_local = spread(expand_parts, 0, count * part_rows, jnp.bfloat16)
    expand_local = expand_local.reshape(size, count, part_rows, hidden).transpose(1, 0, 2, 3).reshape(D, hidden)
    grad_act = dot_nt(grad_all_now, shrink_weight)
    input_three_all, grad_act, expand_local = lax.optimization_barrier((input_three_all, grad_act, expand_local))
    act, grad_pre, grad_in_three_low, hidden_sums = feed(
        input_three_all, expand_local, expand_bias.astype(jnp.float32), grad_act
    )
    grad_hidden_bias = hidden_sums[0]
    grad_in_three = scatter(grad_in_three_low)

    part_hidden = hidden // size
    grad_expand = low(dot_tn(input_three_all, grad_pre)).reshape(count, size, part_rows, hidden)
    expand_grad_parts = rep_split(grad_expand, 1)
    act_late = after(act, grad_expand)
    grad_shrink = low(dot_tn(act_late, grad_all)).reshape(size, part_hidden, D)
    shrink_parts = rep_split(grad_shrink, 0)
    result_part = low(dot(after(act, grad_shrink), shrink_weight))
    expand_sum = add_up(expand_grad_parts)
    grad_in_three, shrink_parts[0], expand_sum, result_part = lax.optimization_barrier(
        (grad_in_three, shrink_parts[0], expand_sum, result_part)
    )
    own_expand = swap(expand_sum)
    result_sum = scatter(result_part)
    grad_in_three = grad_in_three.astype(jnp.float32)

    grad_out = cotangent.astype(jnp.float32)
    norm_three = jax.vjp(norm_apply, hidden_two, gain_rows[2], shift_rows[2])[1](grad_in_three)
    grad_two = grad_out + norm_three[0]
    grad_two_low = low(grad_two)
    grad_context = low(dot_nt(grad_two_low, cross_proj))
    grad_cross_q, memory_part = cross_backward(cross_q, memory_all, grad_context, enc_count)
    mem_grads = scatter(memory_part, groups)
    grad_in_two = dot_nt(grad_cross_q, query_in)
    norm_two = jax.vjp(norm_apply, hidden_one, gain_rows[1], shift_rows[1])[1](grad_in_two)
    grad_one = grad_two + norm_two[0]
    grad_one_low = low(grad_one)
    grad_attn = low(dot_nt(grad_one_low, attn_proj))
    shrink_sum = add_up(after(shrink_parts, grad_cross_q))
    own_expand = own_expand.reshape(part_hidden, D)
    own_feed = jnp.concatenate([shrink_sum, own_expand], axis=0)
    grad_attn, own_feed = lax.optimization_barrier((grad_attn, own_feed))
    grad_att_heads = lax.all_to_all(grad_attn, "shard", 1, 0, tiled=True, axis_index_groups=groups)
    feed_gather = rep_start(own_feed)

    lefts, rights = after(((attended, input_two, context), (grad_one_low, grad_cross_q, grad_two_low)), grad_attn)
    plain_own, plain_theirs = plain_grads(lefts, rights)
    plain_theirs = core_send(plain_theirs)
    grad_att_heads, plain_own = lax.optimization_barrier((grad_att_heads, plain_own))

    delta = jnp.sum((grad_att_heads.astype(jnp.float32) * att_full).reshape(SEQ, 2, HD), axis=-1).T
    plain_rep = core_sum_split(*after((plain_own, plain_theirs), delta))
    delta, plain_rep = lax.optimization_barrier((delta, list(plain_rep)))
    plain_rep = [plain_rep[0]] + [rep_send(plain_rep[step], step) for step in range(1, size)]
    grad_qkv = self_backward(qkv, grad_att_heads, lse.T, delta, seq_segments)
    grad_in_one_low = low(dot_nt(grad_qkv, qkv_weight))
    grad_in_one = scatter(grad_in_one_low, groups)

    input_one_late, mem_grads_late, grad_qkv_late, rows_late = after(
        (input_one_all, mem_grads, grad_qkv, rows_all), grad_in_one_low
    )
    grad_attn_in = dot_tn(input_one_late, grad_qkv_late)
    grad_memory = dot_tn(enc_all, mem_grads_late)
    heads_grad = low(jnp.concatenate([grad_attn_in, grad_memory], axis=1))
    gain_shift = gain_sums(rows_late, row_count, grad_in_one_low)
    qkv_sums = column_sums(grad_qkv_late)
    zero_row = jnp.zeros((D,), jnp.float32)

    def at_own(values):
        return lax.dynamic_update_slice_in_dim(zero_row, values, local_pos * width, 0)

    small_grads = jnp.stack(
        [
            gain_shift[0],
            norm_two[1],
            norm_three[1],
            gain_shift[1],
            norm_two[2],
            norm_three[2],
            at_own(qkv_sums[:width]),
            at_own(qkv_sums[2 * width :]),
            column_sums(grad_one_low),
            column_sums(grad_cross_q),
            at_own(column_sums(mem_grads_late)[width:]),
            column_sums(grad_two_low),
            column_sums(cotangent),
        ]
    )
    small_grads = small_grads.reshape(small_count, count, shard_width).transpose(1, 0, 2)
    small_grads = small_grads.reshape(count, small_count * shard_width)
    hidden_grads = jnp.zeros((count, hidden), jnp.float32)
    hidden_grads = lax.dynamic_update_slice_in_dim(hidden_grads, grad_hidden_bias[None], shard_pos, 0)
    small_grads = low(jnp.concatenate([small_grads, hidden_grads], axis=1))
    small_size = small_grads.shape[1]
    extra = -(-small_size // (5 * width))
    small_grads = jnp.pad(small_grads, ((0, 0), (0, extra * 5 * width - small_size)))
    small_grads = small_grads.reshape(count, extra, 5 * width)
    heads_parts = heads_grad.reshape(count, size, part_rows, 5 * width).transpose(1, 0, 2, 3)
    heads_sum = sum_first(rep_swap(heads_parts))
    own_heads = swap(jnp.concatenate([heads_sum, small_grads], axis=1))
    own_small = sum_first(own_heads[:, part_rows:])
    own_heads = own_heads[:, :part_rows].reshape(count // span, span, part_rows, 5 * width)
    own_heads = own_heads[0] if count == span else sum_first(own_heads)
    heads_gather = rep_start(jnp.concatenate([own_heads.reshape(span * part_rows, 5 * width), own_small], axis=0))

    plain_line_parts = reduce_line(add_up(after(plain_rep, grad_in_one_low)))
    own_plain = add_up(plain_line_parts).reshape(3 * part_rows, D)
    plain_gather = rep_start(own_plain)
    enc_parts = line_scatter_start(low(dot_nt(mem_grads_late, memory_weight)), span)
    grad_enc = add_up(line_scatter_middle(enc_parts, span)).astype(jnp.float32)
    result = hidden_two + after(result_sum, grad_in_one_low).astype(jnp.float32) + bias_rows[6]

    feed_gather = after(feed_gather, heads_grad)
    total_shrink = spread(feed_gather, 0, part_hidden, jnp.float32)
    total_expand = spread_columns(feed_gather, part_hidden, count, part_rows)
    total_plain = [
        spread(plain_gather, kind * part_rows, (kind + 1) * part_rows, jnp.float32).reshape(weight_rows, D)
        for kind in range(3)
    ]
    total_proj, total_query, total_cross = total_plain
    total_small = sum(part[span * part_rows :].astype(jnp.float32) for part in heads_gather)
    total_small = total_small.reshape(-1)[:small_size]
    total_hidden_bias = total_small[small_count * shard_width :]
    total_small = total_small[: small_count * shard_width].reshape(small_count, shard_width)
    total_qkv, total_memory = spread_heads(heads_gather, span, part_rows, width)

    grad_in_one = grad_in_one.astype(jnp.float32)
    norm_one = jax.vjp(lambda rows: norm_apply(rows, gain_rows[0], shift_rows[0]), residual_in)[1](grad_in_one)
    grad_tokens = grad_one + norm_one[0]

    return (
        low(result),
        grad_tokens,
        grad_enc,
        total_qkv,
        total_proj,
        total_query,
        total_memory,
        total_cross,
        total_expand.reshape(weight_rows, count * hidden).astype(jnp.float32),
        total_shrink.reshape(hidden, D).astype(jnp.float32),
        total_small[:3],
        total_small[3:6],
        total_small[6:],
        total_hidden_bias,
    )


def solution(mesh):
    return jax.shard_map(
        shards,
        mesh=mesh,
        in_specs=(
            P(("rep", "shard"), None),
            P("rep"),
            P(("rep", "shard"), None),
            P("rep"),
            P(("rep", "shard"), None),
            P("shard", None),
            P("shard", None),
            P("shard", None),
            P("shard", None),
            P("shard", None),
            P("shard", None),
            P("shard", None),
            P(None, "shard"),
            P(None, "shard"),
            P(None, "shard"),
            P("shard"),
        ),
        out_specs=(
            P(("rep", "shard"), None),
            P(("rep", "shard"), None),
            P(("rep", "shard"), None),
            P("shard", None),
            P("shard", None),
            P("shard", None),
            P("shard", None),
            P("shard", None),
            P("shard", None),
            P("shard", None),
            P(None, "shard"),
            P(None, "shard"),
            P(None, "shard"),
            P("shard"),
        ),
        check_vma=False,
    )
```

```python
import functools

import jax
import jax.numpy as jnp
from jax import lax
from jax.experimental import pallas as pl
from jax.experimental.pallas import tpu as pltpu
from jax.sharding import PartitionSpec as P

D = 1024
H = 16
HD = 64
SEQ = 2048
PAIR = 2 * HD

EPS = 1e-05
NEGATIVE = -1e30
SCALE = HD**-0.5
BLOCK = 512
GELU = 0.7978845608028654
LITTLE = pl.CostEstimate(flops=1000, bytes_accessed=1000, transcendentals=0)


def norm_apply(rows, gain, shift):
    mean_rows = jnp.mean(rows, axis=-1, keepdims=True)
    centered = rows - mean_rows
    inverse = lax.rsqrt(jnp.mean(centered * centered, axis=-1, keepdims=True) + EPS)
    return centered * inverse * gain + shift


def gelu_apply(values):
    return jax.nn.gelu(values, approximate=True)


def column_sums(rows):
    return jnp.sum(rows, axis=0, dtype=jnp.float32)


def low(values):
    return values.astype(jnp.bfloat16)


def dot(left, right):
    return jnp.dot(left, right, preferred_element_type=jnp.float32)


def dot_nt(left, right):
    return lax.dot_general(left, right, (((1,), (1,)), ((), ())), preferred_element_type=jnp.float32)


def dot_tn(left, right):
    return lax.dot_general(left, right, (((0,), (0,)), ((), ())), preferred_element_type=jnp.float32)


def after(value, *earlier):
    return lax.optimization_barrier((value, earlier))[0]


def head_halves(rows, scale=None):
    lane = lax.broadcasted_iota(jnp.int32, rows.shape, 1)
    if scale is not None:
        rows = rows * jnp.asarray(scale, rows.dtype)
    zero = jnp.zeros_like(rows)
    return jnp.where(lane < HD, rows, zero), jnp.where(lane < HD, zero, rows)


def self_forward_kernel(ends, q_ref, k_ref, v_ref, seg_col, seg_row, low_ref, full_ref, lse_ref):
    step = pl.program_id(0)
    rows = q_ref.shape[0]
    queries = head_halves(q_ref[...], SCALE)
    query_seg = seg_col[...]
    last_seg = ends[1, step]

    def piece(index, state, masked, diagonal):
        keys = k_ref[pl.ds(index * rows, rows), :]
        values = v_ref[pl.ds(index * rows, rows), :]
        keep = None
        if masked:
            keep = seg_row[:, pl.ds(index * rows, rows)] == query_seg
            if diagonal:
                key_pos = lax.broadcasted_iota(jnp.int32, (rows, rows), 1)
                query_pos = lax.broadcasted_iota(jnp.int32, (rows, rows), 0)
                keep = keep & (key_pos <= query_pos)
        after = []
        for head in range(2):
            top, total, acc = state[head]
            scores = dot_nt(queries[head], keys)
            if masked:
                scores = jnp.where(keep, scores, NEGATIVE)
            top_new = jnp.maximum(top, jnp.max(scores, axis=1, keepdims=True))
            expo = jnp.exp(scores - top_new)
            fade = jnp.exp(top - top_new)
            after.append(
                (
                    top_new,
                    total * fade + jnp.sum(expo, axis=1, keepdims=True),
                    acc * fade + dot(low(expo), values),
                )
            )
        return tuple(after)

    def before(index, state):
        return lax.cond(
            ends[0, index] == last_seg,
            lambda s: piece(index, s, False, False),
            lambda s: piece(index, s, True, False),
            state,
        )

    blank = (
        jnp.full((rows, 1), NEGATIVE, jnp.float32),
        jnp.zeros((rows, 1), jnp.float32),
        jnp.zeros((rows, PAIR), jnp.float32),
    )
    state = lax.fori_loop(0, step, before, (blank, blank))
    state = piece(step, state, True, True)
    lane = lax.broadcasted_iota(jnp.int32, (rows, PAIR), 1)
    joined = jnp.where(lane < HD, state[0][2] / state[0][1], state[1][2] / state[1][1])
    full_ref[...] = joined
    low_ref[...] = low(joined)
    lse_ref[:, 0:1] = state[0][0] + jnp.log(state[0][1])
    lse_ref[:, 1:2] = state[1][0] + jnp.log(state[1][1])


def block_ends(segments, rows):
    return jnp.stack([segments[::rows], segments[rows - 1 :: rows]])


def self_forward(qkv, segments):
    count = qkv.shape[0]
    rows = BLOCK
    col = segments[:, None]
    row = segments[None, :]
    grid_spec = pltpu.PrefetchScalarGridSpec(
        num_scalar_prefetch=1,
        grid=(count // rows,),
        in_specs=[
            pl.BlockSpec((rows, PAIR), lambda i, e: (i, 0)),
            pl.BlockSpec((count, PAIR), lambda i, e: (0, 1)),
            pl.BlockSpec((count, PAIR), lambda i, e: (0, 2)),
            pl.BlockSpec((rows, 1), lambda i, e: (i, 0)),
            pl.BlockSpec((1, count), lambda i, e: (0, 0)),
        ],
        out_specs=[
            pl.BlockSpec((rows, PAIR), lambda i, e: (i, 0)),
            pl.BlockSpec((rows, PAIR), lambda i, e: (i, 0)),
            pl.BlockSpec((rows, 2), lambda i, e: (i, 0)),
        ],
    )
    return pl.pallas_call(
        self_forward_kernel,
        grid_spec=grid_spec,
        out_shape=(
            jax.ShapeDtypeStruct((count, PAIR), jnp.bfloat16),
            jax.ShapeDtypeStruct((count, PAIR), jnp.float32),
            jax.ShapeDtypeStruct((count, 2), jnp.float32),
        ),
        compiler_params=pltpu.CompilerParams(vmem_limit_bytes=58 * 2**20),
        cost_estimate=LITTLE,
    )(block_ends(segments, rows), qkv, qkv, qkv, col, row)


def self_backward_kernel(
    ends, q_ref, k_ref, v_ref, go_ref, lse_ref, o_ref, seg_col, seg_row, grad_ref, acc_q, acc_k, acc_v, delta_ref
):
    step = pl.program_id(0)
    blocks = pl.num_programs(0)
    rows = k_ref.shape[0]

    @pl.when(step == 0)
    def _():
        acc_q[...] = jnp.zeros_like(acc_q)
        lane = lax.broadcasted_iota(jnp.int32, (8, PAIR), 1) // HD
        pick = (lane == lax.broadcasted_iota(jnp.int32, (8, PAIR), 0)).astype(jnp.float32)
        delta_ref[...] = lax.dot_general(
            pick,
            go_ref[...].astype(jnp.float32) * o_ref[...],
            (((1,), (1,)), ((), ())),
            precision=lax.Precision.HIGHEST,
            preferred_element_type=jnp.float32,
        )

    keys = k_ref[...]
    values = v_ref[...]
    key_halves = head_halves(keys, SCALE)
    key_seg = seg_col[...]
    first_seg = ends[0, step]

    def piece(index, masked, diagonal):
        place = pl.ds(pl.multiple_of(index * rows, rows), rows)
        queries = head_halves(q_ref[place, :], SCALE)
        grads = head_halves(go_ref[place, :])
        keep = None
        if masked:
            keep = seg_row[:, place] == key_seg
            if diagonal:
                key_pos = lax.broadcasted_iota(jnp.int32, (rows, rows), 0)
                query_pos = lax.broadcasted_iota(jnp.int32, (rows, rows), 1)
                keep = keep & (key_pos <= query_pos)
        sum_q = sum_k = sum_v = None
        for head in range(2):
            scores = dot_nt(keys, queries[head])
            probs = jnp.exp(scores - lse_ref[head : head + 1, place])
            if masked:
                probs = jnp.where(keep, probs, 0.0)
            part_v = dot(low(probs), grads[head])
            grad_probs = dot_nt(values, grads[head])
            grad_scores = low(probs * (grad_probs - delta_ref[head : head + 1, place]))
            part_k = dot(grad_scores, queries[head])
            part_q = dot_tn(grad_scores, key_halves[head])
            sum_q = part_q if sum_q is None else sum_q + part_q
            sum_k = part_k if sum_k is None else sum_k + part_k
            sum_v = part_v if sum_v is None else sum_v + part_v
        acc_q[place, :] += sum_q
        if diagonal:
            acc_k[...] = sum_k
            acc_v[...] = sum_v
        else:
            acc_k[...] += sum_k
            acc_v[...] += sum_v

    piece(step, True, True)

    @pl.loop(step + 1, blocks)
    def _(index):
        whole = ends[1, index] == first_seg

        @pl.when(whole)
        def _():
            piece(index, False, False)

        @pl.when(jnp.logical_not(whole))
        def _():
            piece(index, True, False)

    own = pl.ds(pl.multiple_of(step * rows, rows), rows)
    grad_ref[own, 0:PAIR] = low(acc_q[own, :])
    grad_ref[own, PAIR : 2 * PAIR] = low(acc_k[...])
    grad_ref[own, 2 * PAIR : 3 * PAIR] = low(acc_v[...])


def self_backward(qkv, grad_att, lse, attended, segments):
    count = qkv.shape[0]
    rows = BLOCK
    col = segments[:, None]
    row = segments[None, :]
    whole = lambda i, e: (0, 0)
    grid_spec = pltpu.PrefetchScalarGridSpec(
        num_scalar_prefetch=1,
        grid=(count // rows,),
        in_specs=[
            pl.BlockSpec((count, PAIR), whole),
            pl.BlockSpec((rows, PAIR), lambda i, e: (i, 1)),
            pl.BlockSpec((rows, PAIR), lambda i, e: (i, 2)),
            pl.BlockSpec((count, PAIR), whole),
            pl.BlockSpec((2, count), whole),
            pl.BlockSpec((count, PAIR), whole),
            pl.BlockSpec((rows, 1), lambda i, e: (i, 0)),
            pl.BlockSpec((1, count), whole),
        ],
        out_specs=pl.BlockSpec((count, 3 * PAIR), whole),
        scratch_shapes=[
            pltpu.VMEM((count, PAIR), jnp.float32),
            pltpu.VMEM((rows, PAIR), jnp.float32),
            pltpu.VMEM((rows, PAIR), jnp.float32),
            pltpu.VMEM((8, count), jnp.float32),
        ],
    )
    return pl.pallas_call(
        self_backward_kernel,
        grid_spec=grid_spec,
        out_shape=jax.ShapeDtypeStruct((count, 3 * PAIR), jnp.bfloat16),
        compiler_params=pltpu.CompilerParams(vmem_limit_bytes=58 * 2**20),
        cost_estimate=LITTLE,
    )(block_ends(segments, rows), qkv, qkv, qkv, grad_att, lse, attended, col, row)


def cross_forward_kernel(length, q_ref, m_ref, out_ref):
    queries = head_halves(q_ref[...], SCALE)
    keys = m_ref[:, :PAIR]
    values = m_ref[:, PAIR:]
    shape = (q_ref.shape[0], m_ref.shape[0])
    keep = lax.broadcasted_iota(jnp.int32, shape, 1) < length[0]
    parts = []
    for head in range(2):
        scores = jnp.where(keep, dot_nt(queries[head], keys), NEGATIVE)
        expo = jnp.exp(scores - jnp.max(scores, axis=1, keepdims=True))
        parts.append(dot(low(expo), values) / jnp.sum(expo, axis=1, keepdims=True))
    lane = lax.broadcasted_iota(jnp.int32, parts[0].shape, 1)
    out_ref[...] = low(jnp.where(lane < HD, parts[0], parts[1]))


def cross_forward(queries, memory, length):
    count, states = queries.shape[0], memory.shape[0] // (D // PAIR)
    grid_spec = pltpu.PrefetchScalarGridSpec(
        num_scalar_prefetch=1,
        grid=(D // PAIR,),
        in_specs=[
            pl.BlockSpec((count, PAIR), lambda i, e: (0, i)),
            pl.BlockSpec((states, 2 * PAIR), lambda i, e: (i, 0)),
        ],
        out_specs=pl.BlockSpec((count, PAIR), lambda i, e: (0, i)),
    )
    return pl.pallas_call(
        cross_forward_kernel,
        grid_spec=grid_spec,
        out_shape=jax.ShapeDtypeStruct((count, D), jnp.bfloat16),
        cost_estimate=LITTLE,
    )(length, queries, memory)


def cross_backward_kernel(length, q_ref, m_ref, g_ref, dq_ref, dm_ref):
    queries = head_halves(q_ref[...], SCALE)
    grads = head_halves(g_ref[...])
    keys = m_ref[:, :PAIR]
    values = m_ref[:, PAIR:]
    key_halves = head_halves(keys, SCALE)
    shape = (m_ref.shape[0], q_ref.shape[0])
    keep = lax.broadcasted_iota(jnp.int32, shape, 0) < length[0]
    sum_q = sum_k = sum_v = None
    for head in range(2):
        scores = jnp.where(keep, dot_nt(keys, queries[head]), NEGATIVE)
        expo = jnp.exp(scores - jnp.max(scores, axis=0, keepdims=True))
        probs = expo * (1.0 / jnp.sum(expo, axis=0, keepdims=True))
        part_v = dot(low(probs), grads[head])
        grad_probs = dot_nt(values, grads[head])
        inner = jnp.sum(probs * grad_probs, axis=0, keepdims=True)
        grad_scores = low(probs * (grad_probs - inner))
        part_k = dot(grad_scores, queries[head])
        part_q = dot_tn(grad_scores, key_halves[head])
        sum_q = part_q if sum_q is None else sum_q + part_q
        sum_k = part_k if sum_k is None else sum_k + part_k
        sum_v = part_v if sum_v is None else sum_v + part_v
    dq_ref[...] = low(sum_q)
    dm_ref[:, :PAIR] = low(sum_k)
    dm_ref[:, PAIR:] = low(sum_v)


def cross_backward(queries, memory, grads, length):
    count, states = queries.shape[0], memory.shape[0] // (D // PAIR)
    grid_spec = pltpu.PrefetchScalarGridSpec(
        num_scalar_prefetch=1,
        grid=(D // PAIR,),
        in_specs=[
            pl.BlockSpec((count, PAIR), lambda i, e: (0, i)),
            pl.BlockSpec((states, 2 * PAIR), lambda i, e: (i, 0)),
            pl.BlockSpec((count, PAIR), lambda i, e: (0, i)),
        ],
        out_specs=[
            pl.BlockSpec((count, PAIR), lambda i, e: (0, i)),
            pl.BlockSpec((states, 2 * PAIR), lambda i, e: (i, 0)),
        ],
    )
    return pl.pallas_call(
        cross_backward_kernel,
        grid_spec=grid_spec,
        out_shape=(
            jax.ShapeDtypeStruct((count, D), jnp.bfloat16),
            jax.ShapeDtypeStruct((states * (D // PAIR), 2 * PAIR), jnp.bfloat16),
        ),
        cost_estimate=LITTLE,
    )(length, queries, memory, grads)


def front_kernel(x_ref, e_ref, gain, shift, qkv_w, qkv_b, mem_w, mem_b, one_ref, qkv_ref, enc_ref, mem_ref):
    rows = x_ref[0].astype(jnp.float32)
    centered = rows - jnp.mean(rows, axis=-1, keepdims=True)
    inverse = lax.rsqrt(jnp.mean(centered * centered, axis=-1, keepdims=True) + EPS)
    one = low(centered * inverse * gain[...] + shift[...])
    one_ref[...] = one
    qkv_ref[...] = low(dot(one, qkv_w[...]) + qkv_b[...])
    enc_ref[...] = e_ref[0]
    mem_ref[...] = low(dot(e_ref[0], mem_w[...]) + mem_b[...])


def front(rows_all, row_count, gain, shift, qkv_w, qkv_b, mem_w, mem_b):
    span, both, _ = rows_all.shape
    enc_rows = both - row_count
    whole = lambda i: (0, 0)
    return pl.pallas_call(
        front_kernel,
        grid=(span,),
        in_specs=[
            pl.BlockSpec((1, row_count, D), lambda i: (i, 0, 0)),
            pl.BlockSpec((1, enc_rows, D), lambda i: (i, row_count // enc_rows, 0)),
            pl.BlockSpec((1, D), whole),
            pl.BlockSpec((1, D), whole),
            pl.BlockSpec(qkv_w.shape, whole),
            pl.BlockSpec((1, qkv_w.shape[1]), whole),
            pl.BlockSpec(mem_w.shape, whole),
            pl.BlockSpec((1, mem_w.shape[1]), whole),
        ],
        out_specs=[
            pl.BlockSpec((row_count, D), lambda i: (i, 0)),
            pl.BlockSpec((row_count, qkv_w.shape[1]), lambda i: (i, 0)),
            pl.BlockSpec((enc_rows, D), lambda i: (i, 0)),
            pl.BlockSpec((enc_rows, mem_w.shape[1]), lambda i: (i, 0)),
        ],
        out_shape=(
            jax.ShapeDtypeStruct((span * row_count, D), jnp.bfloat16),
            jax.ShapeDtypeStruct((span * row_count, qkv_w.shape[1]), jnp.bfloat16),
            jax.ShapeDtypeStruct((span * enc_rows, D), jnp.bfloat16),
            jax.ShapeDtypeStruct((span * enc_rows, mem_w.shape[1]), jnp.bfloat16),
        ),
        compiler_params=pltpu.CompilerParams(vmem_limit_bytes=58 * 2**20),
        cost_estimate=LITTLE,
    )(rows_all, rows_all, gain[None], shift[None], qkv_w, qkv_b[None], mem_w, mem_b[None])


def feed_kernel(x_ref, w_ref, b_ref, ga_ref, act_ref, pre_ref, in_ref, sum_ref):
    v = dot(x_ref[...], w_ref[...]) + b_ref[...]
    square = v * v
    half = 0.5 + 0.5 * jnp.tanh(v * (GELU + GELU * 0.044715 * square))
    act_ref[...] = low(v * half)
    slope = half + (v * half) * (1.0 - half) * (2.0 * GELU + 6.0 * GELU * 0.044715 * square)
    grad = low(ga_ref[...] * slope)
    pre_ref[...] = grad
    in_ref[...] = low(dot_nt(grad, w_ref[...]))

    @pl.when(pl.program_id(0) == 0)
    def _():
        sum_ref[...] = jnp.zeros_like(sum_ref)

    sum_ref[...] += jnp.sum(grad.astype(jnp.float32), axis=0, keepdims=True)


def feed(rows, weight, bias, grad_act):
    count, hidden = grad_act.shape
    tile = 512
    whole = lambda i: (0, 0)
    block = lambda i: (i, 0)
    return pl.pallas_call(
        feed_kernel,
        grid=(count // tile,),
        in_specs=[
            pl.BlockSpec((tile, D), block),
            pl.BlockSpec((D, hidden), whole),
            pl.BlockSpec((1, hidden), whole),
            pl.BlockSpec((tile, hidden), block),
        ],
        out_specs=[
            pl.BlockSpec((tile, hidden), block),
            pl.BlockSpec((tile, hidden), block),
            pl.BlockSpec((tile, D), block),
            pl.BlockSpec((1, hidden), whole),
        ],
        out_shape=(
            jax.ShapeDtypeStruct((count, hidden), jnp.bfloat16),
            jax.ShapeDtypeStruct((count, hidden), jnp.bfloat16),
            jax.ShapeDtypeStruct((count, D), jnp.bfloat16),
            jax.ShapeDtypeStruct((1, hidden), jnp.float32),
        ),
        compiler_params=pltpu.CompilerParams(vmem_limit_bytes=58 * 2**20),
        cost_estimate=LITTLE,
    )(rows, weight, bias[None], grad_act)


def expand_kernel(replica, x_ref, g_ref, *refs):
    keep, outs = refs[-1], refs[:-1]
    size, rows = len(outs), outs[0].shape[1]
    owners = x_ref.shape[1] // (size * rows)
    keep[...] = low(dot_tn(x_ref[...], g_ref[...])).reshape(keep.shape)
    step = pl.program_id(0) * owners
    for owner in range(owners):
        for other, out in enumerate(outs):
            out[pl.ds(step + owner, 1)] = keep[owner, pl.ds(replica[0] ^ other, 1)]


def expand_grads(rows_in, grads, owners, part_rows):
    size, me = lax.axis_size("rep"), lax.axis_index("rep")
    count, hidden = grads.shape
    if part_rows % 16:
        full = low(dot_tn(rows_in, grads)).reshape(owners, size, part_rows, hidden)
        return [lax.dynamic_index_in_dim(full, me ^ step, 1, keepdims=False) for step in range(size)]
    tile = 2
    grid_spec = pltpu.PrefetchScalarGridSpec(
        num_scalar_prefetch=1,
        grid=(owners // tile,),
        in_specs=[
            pl.BlockSpec((count, tile * size * part_rows), lambda i, e: (0, i)),
            pl.BlockSpec((count, hidden), lambda i, e: (0, 0)),
        ],
        out_specs=[pl.BlockSpec((owners, part_rows, hidden), lambda i, e: (0, 0, 0))] * size,
        scratch_shapes=[pltpu.VMEM((tile, size, part_rows, hidden), jnp.bfloat16)],
    )
    return pl.pallas_call(
        expand_kernel,
        grid_spec=grid_spec,
        out_shape=(jax.ShapeDtypeStruct((owners, part_rows, hidden), jnp.bfloat16),) * size,
        compiler_params=pltpu.CompilerParams(vmem_limit_bytes=58 * 2**20),
        cost_estimate=LITTLE,
    )(me[None], rows_in, grads)


def shrink_kernel(replica, a_ref, g_ref, *outs):
    for step, out in enumerate(outs):

        @pl.when(pl.program_id(0) == step)
        def _():
            out[...] = low(dot_tn(a_ref[...], g_ref[...]))


def shrink_grads(act, grads):
    size, me = lax.axis_size("rep"), lax.axis_index("rep")
    count, hidden = act.shape
    part = hidden // size
    if part % 128:
        full = low(dot_tn(act, grads)).reshape(size, part, D)
        return [lax.dynamic_index_in_dim(full, me ^ step, 0, keepdims=False) for step in range(size)]
    grid_spec = pltpu.PrefetchScalarGridSpec(
        num_scalar_prefetch=1,
        grid=(size,),
        in_specs=[
            pl.BlockSpec((count, part), lambda i, e: (0, e[0] ^ i)),
            pl.BlockSpec((count, D), lambda i, e: (0, 0)),
        ],
        out_specs=[pl.BlockSpec((part, D), lambda i, e: (0, 0))] * size,
    )
    return pl.pallas_call(
        shrink_kernel,
        grid_spec=grid_spec,
        out_shape=(jax.ShapeDtypeStruct((part, D), jnp.bfloat16),) * size,
        compiler_params=pltpu.CompilerParams(vmem_limit_bytes=58 * 2**20),
        cost_estimate=LITTLE,
    )(me[None], act, grads)


def product_kernel(a_ref, b_ref, out_ref):
    out_ref[...] = low(dot(a_ref[...], b_ref[...]))


def product(left, right):
    count, depth = left.shape
    tile = 512
    return pl.pallas_call(
        product_kernel,
        grid=(count // tile,),
        in_specs=[pl.BlockSpec((tile, depth), lambda i: (i, 0)), pl.BlockSpec(right.shape, lambda i: (0, 0))],
        out_specs=pl.BlockSpec((tile, right.shape[1]), lambda i: (i, 0)),
        out_shape=jax.ShapeDtypeStruct((count, right.shape[1]), jnp.bfloat16),
        compiler_params=pltpu.CompilerParams(vmem_limit_bytes=58 * 2**20),
        cost_estimate=LITTLE,
    )(left, right)


def back_kernel(g_ref, w_ref, one_ref, out_ref, sum_ref, own_ref):
    @pl.when(pl.program_id(0) == 0)
    def _():
        sum_ref[...] = jnp.zeros_like(sum_ref)
        own_ref[...] = jnp.zeros_like(own_ref)

    grads = dot_nt(g_ref[...], w_ref[...])
    out_ref[...] = low(grads)
    sum_ref[0:1, :] += jnp.sum(grads * one_ref[...].astype(jnp.float32), axis=0, keepdims=True)
    sum_ref[1:2, :] += jnp.sum(grads, axis=0, keepdims=True)
    own_ref[...] += jnp.sum(g_ref[...].astype(jnp.float32), axis=0, keepdims=True)


def back(grads, weight, rows_in):
    count, width = grads.shape
    tile = 256
    return pl.pallas_call(
        back_kernel,
        grid=(count // tile,),
        in_specs=[
            pl.BlockSpec((tile, width), lambda i: (i, 0)),
            pl.BlockSpec(weight.shape, lambda i: (0, 0)),
            pl.BlockSpec((tile, D), lambda i: (i, 0)),
        ],
        out_specs=[
            pl.BlockSpec((tile, D), lambda i: (i, 0)),
            pl.BlockSpec((2, D), lambda i: (0, 0)),
            pl.BlockSpec((1, width), lambda i: (0, 0)),
        ],
        out_shape=(
            jax.ShapeDtypeStruct((count, D), jnp.bfloat16),
            jax.ShapeDtypeStruct((2, D), jnp.float32),
            jax.ShapeDtypeStruct((1, width), jnp.float32),
        ),
        compiler_params=pltpu.CompilerParams(vmem_limit_bytes=58 * 2**20),
        cost_estimate=LITTLE,
    )(grads, weight, rows_in)


def heads_grads_kernel(x_ref, g_ref, e_ref, m_ref, out_ref):
    width = g_ref.shape[1]
    shape = out_ref.shape[1:3]
    for owner in range(shape[0]):
        place = slice(owner * x_ref.shape[1] // shape[0], (owner + 1) * x_ref.shape[1] // shape[0])
        left = low(dot_tn(x_ref[:, place], g_ref[...]))
        right = low(dot_tn(e_ref[:, place], m_ref[...]))
        for replica in range(out_ref.shape[0]):
            rows = slice(replica * shape[1], (replica + 1) * shape[1])
            out_ref[replica, owner, :, :width] = left[rows, :]
            out_ref[replica, owner, :, width:] = right[rows, :]


def heads_grads(rows_in, grads, enc, enc_grads, owners, part_rows):
    size = lax.axis_size("rep")
    width, enc_width = grads.shape[1], enc_grads.shape[1]
    if part_rows % 16:
        both = low(jnp.concatenate([dot_tn(rows_in, grads), dot_tn(enc, enc_grads)], axis=1))
        return both.reshape(owners, size, part_rows, width + enc_width).transpose(1, 0, 2, 3)
    tile = 2
    return pl.pallas_call(
        heads_grads_kernel,
        grid=(owners // tile,),
        in_specs=[
            pl.BlockSpec((rows_in.shape[0], tile * size * part_rows), lambda i: (0, i)),
            pl.BlockSpec(grads.shape, lambda i: (0, 0)),
            pl.BlockSpec((enc.shape[0], tile * size * part_rows), lambda i: (0, i)),
            pl.BlockSpec(enc_grads.shape, lambda i: (0, 0)),
        ],
        out_specs=pl.BlockSpec((size, tile, part_rows, width + enc_width), lambda i: (0, i, 0, 0)),
        out_shape=jax.ShapeDtypeStruct((size, owners, part_rows, width + enc_width), jnp.bfloat16),
        compiler_params=pltpu.CompilerParams(vmem_limit_bytes=58 * 2**20),
        cost_estimate=LITTLE,
    )(rows_in, grads, enc, enc_grads)


def last_kernel(x_ref, e_ref, one_ref, gain, out_ref):
    rows = x_ref[...].astype(jnp.float32)
    centered = rows - jnp.mean(rows, axis=-1, keepdims=True)
    inverse = lax.rsqrt(jnp.mean(centered * centered, axis=-1, keepdims=True) + EPS)
    x_hat = centered * inverse
    grads = e_ref[...].astype(jnp.float32) * gain[...]
    inner = jnp.mean(grads * x_hat, axis=-1, keepdims=True)
    out_ref[...] = one_ref[...] + inverse * (grads - jnp.mean(grads, axis=-1, keepdims=True) - x_hat * inner)


def last(rows, grads, grad_one, gain):
    count = rows.shape[0]
    tile = 128
    block = pl.BlockSpec((tile, D), lambda i: (i, 0))
    return pl.pallas_call(
        last_kernel,
        grid=(count // tile,),
        in_specs=[block, block, block, pl.BlockSpec((1, D), lambda i: (0, 0))],
        out_specs=block,
        out_shape=jax.ShapeDtypeStruct((count, D), jnp.float32),
        cost_estimate=LITTLE,
    )(rows, grads, grad_one, gain[None])


def rep_send(value, step):
    size = lax.axis_size("rep")
    return lax.ppermute(value, "rep", [(i, i ^ step) for i in range(size)])


def rep_start(value):
    return [value] + [rep_send(value, step) for step in range(1, lax.axis_size("rep"))]


def rep_place(parts, axis):
    size, me = lax.axis_size("rep"), lax.axis_index("rep")
    value = parts[0]
    out = jnp.zeros(value.shape[:axis] + (size,) + value.shape[axis:], value.dtype)
    for step, part in enumerate(parts):
        out = lax.dynamic_update_slice_in_dim(out, jnp.expand_dims(part, axis), me ^ step, axis)
    return out


def spread_kernel(place, *refs):
    out_ref = refs[-1]
    for step, part in enumerate(refs[:-1]):
        out_ref[pl.ds(place[0] ^ step, 1)] = part[...].astype(out_ref.dtype)[None]


def spread(parts, first, last, dtype):
    size, columns = len(parts), parts[0].shape[1]
    rows = last - first
    if rows % 32 or first % rows or parts[0].shape[0] % 16:
        return rep_place([part[first:last] for part in parts], 0).astype(dtype)
    tile = rows // 2
    grid_spec = pltpu.PrefetchScalarGridSpec(
        num_scalar_prefetch=1,
        grid=(2,),
        in_specs=[pl.BlockSpec((tile, columns), lambda i, e: (first // tile + i, 0))] * size,
        out_specs=pl.BlockSpec((size, tile, columns), lambda i, e: (0, i, 0)),
    )
    return pl.pallas_call(
        spread_kernel,
        grid_spec=grid_spec,
        out_shape=jax.ShapeDtypeStruct((size, rows, columns), dtype),
        compiler_params=pltpu.CompilerParams(vmem_limit_bytes=58 * 2**20),
        cost_estimate=LITTLE,
    )(lax.axis_index("rep")[None], *parts)


def rep_gather(value, axis):
    return rep_place(rep_start(value), axis)


def rep_swap(parts):
    return lax.all_to_all(parts, "rep", 0, 0, tiled=True)


def rep_split(parts, axis):
    size, me = lax.axis_size("rep"), lax.axis_index("rep")
    picks = [lax.dynamic_index_in_dim(parts, me ^ step, axis, keepdims=False) for step in range(size)]
    return [picks[0]] + [rep_send(low(picks[step]), step) for step in range(1, size)]


def sum_first(parts):
    return low(jnp.sum(parts.astype(jnp.float32), axis=0))


def add_up(parts):
    total = parts[0].astype(jnp.float32)
    for part in parts[1:]:
        total = total + part.astype(jnp.float32)
    return low(total)


def rep_reduce(parts, axis):
    return add_up(rep_split(parts, axis))


def core_send(value):
    size = lax.axis_size("shard")
    return lax.ppermute(value, "shard", [(i, i ^ 1) for i in range(size)])


def line_send(value, step, group=None):
    size = lax.axis_size("shard")
    group = group or size
    route = [(i, i // group * group + (i + 2 * step) % group) for i in range(size)]
    return lax.ppermute(value, "shard", route)


def line_scatter_start(value, group=None):
    group = group or lax.axis_size("shard")
    core = lax.axis_index("shard") % 2
    value = value.reshape((group // 2, 2, value.shape[0] // group) + value.shape[1:])
    mine = lax.dynamic_index_in_dim(value, core, 1, keepdims=False)
    theirs = lax.dynamic_index_in_dim(value, 1 - core, 1, keepdims=False)
    return [mine, core_send(theirs)]


def line_scatter_middle(both, group=None):
    group = group or lax.axis_size("shard")
    chips = group // 2
    chip = lax.axis_index("shard") % group // 2
    line = add_up(both)
    parts = [lax.dynamic_index_in_dim(line, (chip + step) % chips, 0, keepdims=False) for step in range(chips)]
    return [parts[0]] + [line_send(parts[step], step, group) for step in range(1, chips)]


def columns_kernel(place, *refs):
    out_ref = refs[-1]
    rows = out_ref.shape[1]
    for step, part in enumerate(refs[:-1]):
        for block in range(part.shape[0] // rows):
            wide = part[block * rows : (block + 1) * rows, :].astype(out_ref.dtype)
            out_ref[pl.ds(place[0] ^ step, 1), :, block * D : (block + 1) * D] = wide[None]


def spread_columns(parts, first, blocks, rows):
    size, me = len(parts), lax.axis_index("rep")
    if rows % 16:
        parts = [part[first:].reshape(blocks, rows, -1).transpose(1, 0, 2).reshape(rows, -1) for part in parts]
        return rep_place(parts, 0).astype(jnp.float32).reshape(size * rows, -1)
    halves = 2
    taken = blocks * rows // halves
    grid_spec = pltpu.PrefetchScalarGridSpec(
        num_scalar_prefetch=1,
        grid=(halves,),
        in_specs=[pl.BlockSpec((taken, D), lambda i, e: (first // taken + i, 0))] * size,
        out_specs=pl.BlockSpec((size, rows, blocks * D // halves), lambda i, e: (0, 0, i)),
    )
    out = pl.pallas_call(
        columns_kernel,
        grid_spec=grid_spec,
        out_shape=jax.ShapeDtypeStruct((size, rows, blocks * D), jnp.float32),
        compiler_params=pltpu.CompilerParams(vmem_limit_bytes=58 * 2**20),
        cost_estimate=LITTLE,
    )(me[None], *parts)
    return out.reshape(size * rows, blocks * D)


def heads_kernel(span, place, *refs):
    qkv_ref, memory_ref = refs[-2:]
    rows, width = qkv_ref.shape[1], D // span
    for step, part in enumerate(refs[:-2]):
        take = pl.ds(place[0] ^ step, 1)
        for block in range(span):
            wide = part[block * rows : (block + 1) * rows, :].astype(jnp.float32)[None]
            for kind in range(5):
                out, at = (qkv_ref, kind) if kind < 3 else (memory_ref, kind - 3)
                columns = slice(at * D + block * width, at * D + (block + 1) * width)
                out[take, :, columns] = wide[:, :, kind * width : (kind + 1) * width]


def spread_heads(parts, span, rows, width):
    size, me = len(parts), lax.axis_index("rep")
    if rows % 16:
        full = rep_place([part[: span * rows].reshape(span, rows, 5, width) for part in parts], 0)
        full = full.transpose(0, 2, 3, 1, 4).reshape(size * rows, 5 * D).astype(jnp.float32)
        return full[:, : 3 * D], full[:, 3 * D :]
    grid_spec = pltpu.PrefetchScalarGridSpec(
        num_scalar_prefetch=1,
        grid=(1,),
        in_specs=[pl.BlockSpec((span * rows, 5 * width), lambda i, e: (0, 0))] * size,
        out_specs=[
            pl.BlockSpec((size, rows, 3 * D), lambda i, e: (0, 0, 0)),
            pl.BlockSpec((size, rows, 2 * D), lambda i, e: (0, 0, 0)),
        ],
    )
    qkv, memory = pl.pallas_call(
        functools.partial(heads_kernel, span),
        grid_spec=grid_spec,
        out_shape=(
            jax.ShapeDtypeStruct((size, rows, 3 * D), jnp.float32),
            jax.ShapeDtypeStruct((size, rows, 2 * D), jnp.float32),
        ),
        compiler_params=pltpu.CompilerParams(vmem_limit_bytes=58 * 2**20),
        cost_estimate=LITTLE,
    )(me[None], *parts)
    return qkv.reshape(size * rows, 3 * D), memory.reshape(size * rows, 2 * D)


def weight_line(piece):
    kinds, rows, columns = piece.shape
    chips = lax.axis_size("shard") // 2
    chip = lax.axis_index("shard") // 2
    line = jnp.zeros((kinds, chips, rows, columns), piece.dtype)
    for step in range(chips):
        part = line_send(piece, step) if step else piece
        line = lax.dynamic_update_slice_in_dim(line, part[:, None], (chip - step) % chips, 1)
    return line


def join_kernel(place, *refs):
    outs = refs[-3:]
    parts = refs[:-3]
    size = len(parts) // 2
    for core in range(2):
        side = place[1] ^ core
        for step in range(size):
            for kind in range(3):
                outs[kind][0, pl.ds(side, 1), pl.ds(place[0] ^ step, 1)] = parts[core * size + step][kind][None]


def weight_join(mine, other):
    size = len(mine)
    _, chips, rows, _ = mine[0].shape
    core = lax.axis_index("shard") % 2
    if rows % 16:
        first = core == 0
        plane, next_plane = rep_place(mine, 2), rep_place(other, 2)
        low_core, high_core = jnp.where(first, plane, next_plane), jnp.where(first, next_plane, plane)
        full = jnp.stack([low_core, high_core], axis=2).reshape(3, D, D)
        return full[0], full[1], full[2]
    grid_spec = pltpu.PrefetchScalarGridSpec(
        num_scalar_prefetch=1,
        grid=(chips,),
        in_specs=[pl.BlockSpec((3, 1, rows, D), lambda i, e: (0, i, 0, 0))] * (2 * size),
        out_specs=[pl.BlockSpec((1, 2, size, rows, D), lambda i, e: (i, 0, 0, 0, 0))] * 3,
    )
    outs = pl.pallas_call(
        join_kernel,
        grid_spec=grid_spec,
        out_shape=(jax.ShapeDtypeStruct((chips, 2, size, rows, D), jnp.bfloat16),) * 3,
        compiler_params=pltpu.CompilerParams(vmem_limit_bytes=58 * 2**20),
        cost_estimate=LITTLE,
    )(jnp.stack([lax.axis_index("rep"), core]), *mine, *other)
    return tuple(out.reshape(D, D) for out in outs)


def plain_kernel(core, a_ref, b_ref, c_ref, ga_ref, gb_ref, gc_ref, mine_ref, theirs_ref):
    width = a_ref.shape[1] // 2
    for kind, (left, right) in enumerate(((a_ref, ga_ref), (b_ref, gb_ref), (c_ref, gc_ref))):
        for side, out in enumerate((mine_ref, theirs_ref)):
            place = pl.ds(pl.multiple_of((core[0] ^ side) * width, width), width)
            out[kind, 0] = low(dot_tn(left[:, place], right[...])).reshape(out.shape[2:])


def plain_grads(lefts, rights):
    size, chips = lax.axis_size("rep"), lax.axis_size("shard") // 2
    core = lax.axis_index("shard") % 2
    rows = D // (2 * chips * size)
    if rows % 16:
        stack = jnp.stack([low(dot_tn(left, right)) for left, right in zip(lefts, rights)])
        stack = stack.reshape(3, chips, 2, size, rows, D)
        return [lax.dynamic_index_in_dim(stack, core ^ side, 2, keepdims=False) for side in range(2)]
    count = lefts[0].shape[0]
    grid_spec = pltpu.PrefetchScalarGridSpec(
        num_scalar_prefetch=1,
        grid=(chips,),
        in_specs=[pl.BlockSpec((count, D // chips), lambda i, e: (0, i))] * 3
        + [pl.BlockSpec((count, D), lambda i, e: (0, 0))] * 3,
        out_specs=[pl.BlockSpec((3, 1, size, rows, D), lambda i, e: (0, i, 0, 0, 0))] * 2,
    )
    return pl.pallas_call(
        plain_kernel,
        grid_spec=grid_spec,
        out_shape=(jax.ShapeDtypeStruct((3, chips, size, rows, D), jnp.bfloat16),) * 2,
        compiler_params=pltpu.CompilerParams(vmem_limit_bytes=58 * 2**20),
        cost_estimate=pl.CostEstimate(flops=6 * count * D * D, bytes_accessed=20 * count * D, transcendentals=0),
    )(core[None], *lefts, *rights)


def split_kernel(place, mine_ref, other_ref, *outs):
    for step, out in enumerate(outs):
        take = pl.ds(place[0] ^ step, 1)
        total = mine_ref[:, 0, take].astype(jnp.float32) + other_ref[:, 0, take].astype(jnp.float32)
        out[...] = low(total)


def core_sum_split(mine, other):
    kinds, chips, size, rows, _ = mine.shape
    if rows % 16:
        total = add_up([mine, other])
        me = lax.axis_index("rep")
        return [lax.dynamic_index_in_dim(total, me ^ step, 2, keepdims=False) for step in range(size)]
    grid_spec = pltpu.PrefetchScalarGridSpec(
        num_scalar_prefetch=1,
        grid=(chips,),
        in_specs=[pl.BlockSpec((kinds, 1, size, rows, D), lambda i, e: (0, i, 0, 0, 0))] * 2,
        out_specs=[pl.BlockSpec((kinds, 1, rows, D), lambda i, e: (0, i, 0, 0))] * size,
    )
    return pl.pallas_call(
        split_kernel,
        grid_spec=grid_spec,
        out_shape=(jax.ShapeDtypeStruct((kinds, chips, rows, D), jnp.bfloat16),) * size,
        compiler_params=pltpu.CompilerParams(vmem_limit_bytes=58 * 2**20),
        cost_estimate=LITTLE,
    )(lax.axis_index("rep")[None], mine, other)


def reduce_line(line):
    chips = lax.axis_size("shard") // 2
    chip = lax.axis_index("shard") // 2
    parts = [lax.dynamic_index_in_dim(line, (chip + step) % chips, 1, keepdims=False) for step in range(chips)]
    return [parts[0]] + [line_send(parts[step], step) for step in range(1, chips)]


def shards(
    tokens,
    segments,
    enc_states,
    enc_lengths,
    cotangent,
    self_qkv,
    self_out,
    cross_query,
    cross_memory,
    cross_out,
    expand_weight,
    shrink_weight,
    norm_gain,
    norm_bias,
    proj_bias,
    expand_bias,
):
    row_count, enc_rows = tokens.shape[0], enc_states.shape[0]
    span = SEQ // row_count
    width = D // span
    count = lax.axis_size("shard")
    size = lax.axis_size("rep")
    rep_pos = lax.axis_index("rep")
    shard_pos = lax.axis_index("shard")
    local_pos = shard_pos % span
    local_seq = shard_pos // span
    groups = None
    if count != span:
        groups = [[g * span + i for i in range(span)] for g in range(count // span)]
    weight_rows = self_qkv.shape[0]
    part_rows = weight_rows // size
    hidden = expand_bias.shape[0]
    shard_width = norm_gain.shape[1]

    def gather(value, groups=None):
        return lax.all_gather(value, "shard", axis=0, tiled=True, axis_index_groups=groups)

    def scatter(value, groups=None):
        return lax.psum_scatter(value, "shard", scatter_dimension=0, tiled=True, axis_index_groups=groups)

    def swap(value):
        return lax.all_to_all(value, "shard", 0, 0, tiled=True)

    def own_part(weight):
        return lax.dynamic_slice_in_dim(weight, rep_pos * part_rows, part_rows, axis=0)

    def by_pairs(weight, kinds):
        blocks = weight.reshape(part_rows, kinds, span, width).transpose(2, 0, 1, 3)
        return blocks.reshape(span, part_rows, kinds * width)

    rows_all = gather(jnp.concatenate([tokens, enc_states], axis=0), groups)
    blocks = jnp.concatenate([by_pairs(own_part(self_qkv), 3), by_pairs(own_part(cross_memory), 2)], axis=2)
    blocks = jnp.tile(blocks, (count // span, 1, 1))
    small = jnp.concatenate([norm_gain, norm_bias, proj_bias], axis=0)
    small_count = small.shape[0]
    small_rows = -(-small.size // (5 * width))
    small = jnp.pad(small.reshape(-1), (0, small_rows * 5 * width - small.size)).reshape(small_rows, 5 * width)
    blocks = jnp.concatenate([blocks, jnp.broadcast_to(small, (count,) + small.shape)], axis=1)
    swapped = swap(blocks)
    small_all = swapped[:, part_rows:].reshape(count, small_rows * 5 * width)[:, : small_count * shard_width]
    small_all = small_all.reshape(count, small_count, shard_width)
    small_all = small_all.transpose(1, 0, 2).reshape(small_count, D).astype(jnp.float32)
    gain_rows, shift_rows, bias_rows = small_all[:3], small_all[3:6], small_all[6:]
    head_weight = rep_gather(swapped[:, :part_rows], 1).reshape(D, 5 * width)
    qkv_weight, memory_weight = head_weight[:, : 3 * width], head_weight[:, 3 * width :]
    plain_part = jnp.stack([own_part(self_out), own_part(cross_query), own_part(cross_out)])
    plain_line = weight_line(after(plain_part, swapped))
    plain_mine = rep_start(plain_line)
    rows_all, head_weight, _ = lax.optimization_barrier((rows_all, head_weight, plain_line))
    expand_part = own_part(expand_weight).reshape(part_rows, count, hidden).transpose(1, 0, 2)
    expand_swapped = swap(after(expand_part, rows_all))

    rows_all = rows_all.reshape(span, row_count + enc_rows, D)
    seq_segments = lax.dynamic_slice_in_dim(segments, local_seq * SEQ, SEQ)
    own_bias = lax.dynamic_slice_in_dim(bias_rows, local_pos * width, width, axis=1)
    zero_bias = jnp.zeros((width,), jnp.float32)
    qkv_bias = jnp.concatenate([own_bias[0], zero_bias, own_bias[1]])
    memory_bias = jnp.concatenate([zero_bias, own_bias[4]])
    input_one_all, qkv, enc_all, memory_pair = front(
        rows_all, row_count, gain_rows[0], shift_rows[0], qkv_weight, qkv_bias, memory_weight, memory_bias
    )
    qkv, plain_mine[1], plain_mine[2] = lax.optimization_barrier((qkv, plain_mine[1], plain_mine[2]))
    att_low, att_full, lse = self_forward(qkv, seq_segments)
    att_low, expand_swapped, plain_mine = lax.optimization_barrier((att_low, expand_swapped, plain_mine))
    attended = lax.all_to_all(att_low, "shard", 0, 1, tiled=True, axis_index_groups=groups)

    memory_all = gather(memory_pair, groups)
    enc_count = lax.dynamic_slice_in_dim(enc_lengths, local_seq, 1)
    plain_other = [core_send(part) for part in plain_mine]

    plain_mine, plain_other = after((plain_mine, plain_other), att_low)
    attn_proj, query_in, cross_proj = weight_join(plain_mine, plain_other)
    attended, attn_proj, query_in, cross_proj = lax.optimization_barrier((attended, attn_proj, query_in, cross_proj))
    grad_all = gather(after(cotangent, memory_all, att_low))
    expand_parts = rep_start(after(expand_swapped, attended).reshape(count * part_rows, hidden))
    residual_in = tokens.astype(jnp.float32)
    hidden_one = residual_in + dot(attended, attn_proj) + bias_rows[2]
    input_two = low(norm_apply(hidden_one, gain_rows[1], shift_rows[1]))
    cross_q = low(dot(input_two, query_in) + bias_rows[3])
    context = cross_forward(cross_q, memory_all, enc_count)
    hidden_two = hidden_one + dot(context, cross_proj) + bias_rows[5]
    input_three = low(norm_apply(hidden_two, gain_rows[2], shift_rows[2]))

    input_three_all = gather(after(input_three, grad_all))
    expand_parts, grad_all_now = after((expand_parts, grad_all), input_three)
    expand_local = spread(expand_parts, 0, count * part_rows, jnp.bfloat16)
    expand_local = expand_local.reshape(size, count, part_rows, hidden).transpose(1, 0, 2, 3).reshape(D, hidden)
    grad_act = dot_nt(grad_all_now, shrink_weight)
    input_three_all, grad_act, expand_local = lax.optimization_barrier((input_three_all, grad_act, expand_local))
    act, grad_pre, grad_in_three_low, hidden_sums = feed(
        input_three_all, expand_local, expand_bias.astype(jnp.float32), grad_act
    )
    grad_hidden_bias = hidden_sums[0]
    grad_in_three = scatter(grad_in_three_low)

    part_hidden = hidden // size

    def send_parts(parts):
        return [parts[0]] + [rep_send(parts[step], step) for step in range(1, size)]

    rows_late, grad_pre_late = after((input_three_all, grad_pre), grad_in_three_low)
    expand_grad_parts = expand_grads(rows_late, grad_pre_late, count, part_rows)
    shrink_parts = send_parts(shrink_grads(after(act, expand_grad_parts[0]), grad_all))
    expand_grad_parts = send_parts(expand_grad_parts)
    result_part = product(after(act, shrink_parts[0]), shrink_weight)
    expand_sum = add_up(expand_grad_parts)
    own_expand = swap(expand_sum)
    grad_in_three, shrink_parts[0], result_part = lax.optimization_barrier(
        (grad_in_three, shrink_parts[0], result_part)
    )
    result_sum = scatter(result_part)
    grad_in_three = grad_in_three.astype(jnp.float32)

    grad_out = cotangent.astype(jnp.float32)
    norm_three = jax.vjp(norm_apply, hidden_two, gain_rows[2], shift_rows[2])[1](grad_in_three)
    grad_two = grad_out + norm_three[0]
    grad_two_low = low(grad_two)
    grad_context = low(dot_nt(grad_two_low, cross_proj))
    grad_context, own_expand = lax.optimization_barrier((grad_context, own_expand))
    grad_cross_q, memory_part = cross_backward(cross_q, memory_all, grad_context, enc_count)
    grad_cross_q, memory_part, shrink_parts = lax.optimization_barrier((grad_cross_q, memory_part, shrink_parts))
    mem_grads = scatter(memory_part, groups)
    grad_in_two = dot_nt(grad_cross_q, query_in)
    norm_two = jax.vjp(norm_apply, hidden_one, gain_rows[1], shift_rows[1])[1](grad_in_two)
    grad_one = grad_two + norm_two[0]
    grad_one_low = low(grad_one)
    grad_attn = low(dot_nt(grad_one_low, attn_proj))
    shrink_sum = add_up(shrink_parts)
    own_expand = own_expand.reshape(part_hidden, D)
    own_feed = jnp.concatenate([shrink_sum, own_expand], axis=0)
    grad_attn, own_feed = lax.optimization_barrier((grad_attn, own_feed))
    grad_att_heads = lax.all_to_all(grad_attn, "shard", 1, 0, tiled=True, axis_index_groups=groups)

    lefts, rights = after(((attended, input_two, context), (grad_one_low, grad_cross_q, grad_two_low)), grad_attn)
    plain_own, plain_theirs = plain_grads(lefts, rights)
    plain_theirs = core_send(plain_theirs)
    grad_att_heads, plain_own = lax.optimization_barrier((grad_att_heads, plain_own))

    feed_gather = rep_start(own_feed)
    grad_qkv = self_backward(qkv, grad_att_heads, lse.T, att_full, seq_segments)
    grad_qkv, feed_gather, plain_theirs = lax.optimization_barrier((grad_qkv, feed_gather, plain_theirs))
    heads_parts = heads_grads(input_one_all, grad_qkv, enc_all, mem_grads, count, part_rows)
    heads_swapped = rep_swap(heads_parts)
    grad_in_one_low, one_sums, qkv_sums = back(after(grad_qkv, heads_parts), qkv_weight, input_one_all)
    plain_rep = send_parts(core_sum_split(*after((plain_own, plain_theirs), heads_parts)))
    grad_in_one_low, heads_swapped, plain_rep[0] = lax.optimization_barrier(
        (grad_in_one_low, heads_swapped, plain_rep[0])
    )
    grad_in_one = scatter(grad_in_one_low, groups)

    mem_grads_late = after(mem_grads, grad_in_one_low)
    qkv_sums = qkv_sums[0]
    gain_shift = [(one_sums[0] - shift_rows[0] * one_sums[1]) / gain_rows[0], one_sums[1]]
    zero_row = jnp.zeros((D,), jnp.float32)

    def at_own(values):
        return lax.dynamic_update_slice_in_dim(zero_row, values, local_pos * width, 0)

    small_grads = jnp.stack(
        [
            gain_shift[0],
            norm_two[1],
            norm_three[1],
            gain_shift[1],
            norm_two[2],
            norm_three[2],
            at_own(qkv_sums[:width]),
            at_own(qkv_sums[2 * width :]),
            column_sums(grad_one_low),
            column_sums(grad_cross_q),
            at_own(column_sums(mem_grads_late)[width:]),
            column_sums(grad_two_low),
            column_sums(cotangent),
        ]
    )
    small_grads = small_grads.reshape(small_count, count, shard_width).transpose(1, 0, 2)
    small_grads = small_grads.reshape(count, small_count * shard_width)
    hidden_grads = jnp.zeros((count, hidden), jnp.float32)
    hidden_grads = lax.dynamic_update_slice_in_dim(hidden_grads, grad_hidden_bias[None], shard_pos, 0)
    small_grads = low(jnp.concatenate([small_grads, hidden_grads], axis=1))
    small_size = small_grads.shape[1]
    extra = -(-small_size // (5 * width))
    small_grads = jnp.pad(small_grads, ((0, 0), (0, extra * 5 * width - small_size)))
    small_grads = small_grads.reshape(count, extra, 5 * width)
    heads_sum = sum_first(after(heads_swapped, grad_in_one_low))
    own_heads = swap(jnp.concatenate([heads_sum, small_grads], axis=1))
    own_small = sum_first(own_heads[:, part_rows:])
    own_heads = own_heads[:, :part_rows].reshape(count // span, span, part_rows, 5 * width)
    own_heads = own_heads[0] if count == span else sum_first(own_heads)
    heads_gather = rep_start(jnp.concatenate([own_heads.reshape(span * part_rows, 5 * width), own_small], axis=0))

    plain_line_parts = reduce_line(add_up(after(plain_rep, own_heads)))
    own_plain = add_up(plain_line_parts).reshape(3 * part_rows, D)
    plain_gather = rep_start(own_plain)
    enc_parts = line_scatter_start(low(dot_nt(mem_grads_late, memory_weight)), span)
    grad_enc = add_up(line_scatter_middle(enc_parts, span)).astype(jnp.float32)
    result = hidden_two + after(result_sum, grad_in_one_low).astype(jnp.float32) + bias_rows[6]

    total_shrink = spread(feed_gather, 0, part_hidden, jnp.float32)
    total_expand = spread_columns(feed_gather, part_hidden, count, part_rows)
    total_plain = [
        spread(plain_gather, kind * part_rows, (kind + 1) * part_rows, jnp.float32).reshape(weight_rows, D)
        for kind in range(3)
    ]
    total_proj, total_query, total_cross = total_plain
    total_small = sum(part[span * part_rows :].astype(jnp.float32) for part in heads_gather)
    total_small = total_small.reshape(-1)[:small_size]
    total_hidden_bias = total_small[small_count * shard_width :]
    total_small = total_small[: small_count * shard_width].reshape(small_count, shard_width)
    total_qkv, total_memory = spread_heads(heads_gather, span, part_rows, width)

    grad_tokens = last(tokens, grad_in_one, grad_one, gain_rows[0])

    return (
        low(result),
        grad_tokens,
        grad_enc,
        total_qkv,
        total_proj,
        total_query,
        total_memory,
        total_cross,
        total_expand.reshape(weight_rows, count * hidden).astype(jnp.float32),
        total_shrink.reshape(hidden, D).astype(jnp.float32),
        total_small[:3],
        total_small[3:6],
        total_small[6:],
        total_hidden_bias,
    )


def solution(mesh):
    return jax.shard_map(
        shards,
        mesh=mesh,
        in_specs=(
            P(("rep", "shard"), None),
            P("rep"),
            P(("rep", "shard"), None),
            P("rep"),
            P(("rep", "shard"), None),
            P("shard", None),
            P("shard", None),
            P("shard", None),
            P("shard", None),
            P("shard", None),
            P("shard", None),
            P("shard", None),
            P(None, "shard"),
            P(None, "shard"),
            P(None, "shard"),
            P("shard"),
        ),
        out_specs=(
            P(("rep", "shard"), None),
            P(("rep", "shard"), None),
            P(("rep", "shard"), None),
            P("shard", None),
            P("shard", None),
            P("shard", None),
            P("shard", None),
            P("shard", None),
            P("shard", None),
            P("shard", None),
            P(None, "shard"),
            P(None, "shard"),
            P(None, "shard"),
            P("shard"),
        ),
        check_vma=False,
    )
```

```python
import functools

import jax
import jax.numpy as jnp
from jax import lax
from jax.experimental import pallas as pl
from jax.experimental.pallas import tpu as pltpu
from jax.sharding import PartitionSpec as P

D = 1024
H = 16
HD = 64
SEQ = 2048
PAIR = 2 * HD

EPS = 1e-05
NEGATIVE = -1e30
SCALE = HD**-0.5
BLOCK = 512
GELU = 0.7978845608028654
LITTLE = pl.CostEstimate(flops=1000, bytes_accessed=1000, transcendentals=0)


def norm_apply(rows, gain, shift):
    mean_rows = jnp.mean(rows, axis=-1, keepdims=True)
    centered = rows - mean_rows
    inverse = lax.rsqrt(jnp.mean(centered * centered, axis=-1, keepdims=True) + EPS)
    return centered * inverse * gain + shift


def gelu_apply(values):
    return jax.nn.gelu(values, approximate=True)


def column_sums(rows):
    return jnp.sum(rows, axis=0, dtype=jnp.float32)


def low(values):
    return values.astype(jnp.bfloat16)


def dot(left, right):
    return jnp.dot(left, right, preferred_element_type=jnp.float32)


def dot_nt(left, right):
    return lax.dot_general(left, right, (((1,), (1,)), ((), ())), preferred_element_type=jnp.float32)


def dot_tn(left, right):
    return lax.dot_general(left, right, (((0,), (0,)), ((), ())), preferred_element_type=jnp.float32)


def after(value, *earlier):
    return lax.optimization_barrier((value, earlier))[0]


def head_halves(rows, scale=None):
    lane = lax.broadcasted_iota(jnp.int32, rows.shape, 1)
    if scale is not None:
        rows = rows * jnp.asarray(scale, rows.dtype)
    zero = jnp.zeros_like(rows)
    return jnp.where(lane < HD, rows, zero), jnp.where(lane < HD, zero, rows)


def self_forward_kernel(ends, q_ref, k_ref, v_ref, seg_col, seg_row, low_ref, full_ref, lse_ref):
    step = pl.program_id(0)
    rows = q_ref.shape[0]
    queries = head_halves(q_ref[...], SCALE)
    query_seg = seg_row[...]
    last_seg = ends[1, step]

    def piece(index, state, masked, diagonal):
        place = pl.ds(pl.multiple_of(index * rows, rows), rows)
        keys = k_ref[place, :]
        values = v_ref[place, :]
        keep = None
        if masked:
            keep = seg_col[place, :] == query_seg
            if diagonal:
                key_pos = lax.broadcasted_iota(jnp.int32, (rows, rows), 0)
                query_pos = lax.broadcasted_iota(jnp.int32, (rows, rows), 1)
                keep = keep & (key_pos <= query_pos)
        after_piece = []
        for head in range(2):
            top, total, acc = state[head]
            scores = dot_nt(keys, queries[head])
            if masked:
                scores = jnp.where(keep, scores, NEGATIVE)
            top_new = jnp.maximum(top, jnp.max(scores, axis=0, keepdims=True))
            expo = jnp.exp(scores - top_new)
            fade = jnp.exp(top - top_new)
            after_piece.append(
                (
                    top_new,
                    total * fade + jnp.sum(expo, axis=0, keepdims=True),
                    acc * fade + dot_tn(values, low(expo)),
                )
            )
        return tuple(after_piece)

    def before(index, state):
        return lax.cond(
            ends[0, index] == last_seg,
            lambda s: piece(index, s, False, False),
            lambda s: piece(index, s, True, False),
            state,
        )

    blank = (
        jnp.full((1, rows), NEGATIVE, jnp.float32),
        jnp.zeros((1, rows), jnp.float32),
        jnp.zeros((PAIR, rows), jnp.float32),
    )
    state = lax.fori_loop(0, step, before, (blank, blank))
    state = piece(step, state, True, True)
    parts = [
        (state[head][2] * (1.0 / state[head][1]))[head * HD : (head + 1) * HD] for head in range(2)
    ]
    joined = jnp.concatenate(parts, axis=0).T
    full_ref[...] = joined
    low_ref[...] = low(joined)
    lse_ref[0:1, :] = state[0][0] + jnp.log(state[0][1])
    lse_ref[1:2, :] = state[1][0] + jnp.log(state[1][1])


def block_ends(segments, rows):
    return jnp.stack([segments[::rows], segments[rows - 1 :: rows]])


def self_forward(qkv, segments):
    count = qkv.shape[0]
    rows = BLOCK
    col = segments[:, None]
    row = segments[None, :]
    grid_spec = pltpu.PrefetchScalarGridSpec(
        num_scalar_prefetch=1,
        grid=(count // rows,),
        in_specs=[
            pl.BlockSpec((rows, PAIR), lambda i, e: (i, 0)),
            pl.BlockSpec((count, PAIR), lambda i, e: (0, 1)),
            pl.BlockSpec((count, PAIR), lambda i, e: (0, 2)),
            pl.BlockSpec((count, 1), lambda i, e: (0, 0)),
            pl.BlockSpec((1, rows), lambda i, e: (0, i)),
        ],
        out_specs=[
            pl.BlockSpec((rows, PAIR), lambda i, e: (i, 0)),
            pl.BlockSpec((rows, PAIR), lambda i, e: (i, 0)),
            pl.BlockSpec((2, rows), lambda i, e: (0, i)),
        ],
    )
    return pl.pallas_call(
        self_forward_kernel,
        grid_spec=grid_spec,
        out_shape=(
            jax.ShapeDtypeStruct((count, PAIR), jnp.bfloat16),
            jax.ShapeDtypeStruct((count, PAIR), jnp.float32),
            jax.ShapeDtypeStruct((2, count), jnp.float32),
        ),
        compiler_params=pltpu.CompilerParams(vmem_limit_bytes=58 * 2**20),
        cost_estimate=LITTLE,
    )(block_ends(segments, rows), qkv, qkv, qkv, col, row)


def self_backward_kernel(
    ends, q_ref, k_ref, v_ref, go_ref, lse_ref, o_ref, seg_col, seg_row, grad_ref, acc_q, acc_k, acc_v, delta_ref
):
    step = pl.program_id(0)
    blocks = pl.num_programs(0)
    rows = k_ref.shape[0]

    @pl.when(step == 0)
    def _():
        acc_q[...] = jnp.zeros_like(acc_q)
        lane = lax.broadcasted_iota(jnp.int32, (8, PAIR), 1) // HD
        pick = (lane == lax.broadcasted_iota(jnp.int32, (8, PAIR), 0)).astype(jnp.float32)
        delta_ref[...] = lax.dot_general(
            pick,
            go_ref[...].astype(jnp.float32) * o_ref[...],
            (((1,), (1,)), ((), ())),
            precision=lax.Precision.HIGHEST,
            preferred_element_type=jnp.float32,
        )

    keys = k_ref[...]
    values = v_ref[...]
    key_halves = head_halves(keys, SCALE)
    key_seg = seg_col[...]
    first_seg = ends[0, step]

    def piece(index, masked, diagonal):
        place = pl.ds(pl.multiple_of(index * rows, rows), rows)
        queries = head_halves(q_ref[place, :], SCALE)
        grads = head_halves(go_ref[place, :])
        keep = None
        if masked:
            keep = seg_row[:, place] == key_seg
            if diagonal:
                key_pos = lax.broadcasted_iota(jnp.int32, (rows, rows), 0)
                query_pos = lax.broadcasted_iota(jnp.int32, (rows, rows), 1)
                keep = keep & (key_pos <= query_pos)
        sum_q = sum_k = sum_v = None
        for head in range(2):
            scores = dot_nt(keys, queries[head])
            probs = jnp.exp(scores - lse_ref[head : head + 1, place])
            if masked:
                probs = jnp.where(keep, probs, 0.0)
            part_v = dot(low(probs), grads[head])
            grad_probs = dot_nt(values, grads[head])
            grad_scores = low(probs * (grad_probs - delta_ref[head : head + 1, place]))
            part_k = dot(grad_scores, queries[head])
            part_q = dot_tn(key_halves[head], grad_scores)
            sum_q = part_q if sum_q is None else sum_q + part_q
            sum_k = part_k if sum_k is None else sum_k + part_k
            sum_v = part_v if sum_v is None else sum_v + part_v
        acc_q[:, place] += sum_q
        if diagonal:
            acc_k[...] = sum_k
            acc_v[...] = sum_v
        else:
            acc_k[...] += sum_k
            acc_v[...] += sum_v

    piece(step, True, True)

    @pl.loop(step + 1, blocks)
    def _(index):
        whole = ends[1, index] == first_seg

        @pl.when(whole)
        def _():
            piece(index, False, False)

        @pl.when(jnp.logical_not(whole))
        def _():
            piece(index, True, False)

    own = pl.ds(pl.multiple_of(step * rows, rows), rows)
    grad_ref[own, 0:PAIR] = low(acc_q[:, own].T)
    grad_ref[own, PAIR : 2 * PAIR] = low(acc_k[...])
    grad_ref[own, 2 * PAIR : 3 * PAIR] = low(acc_v[...])


def self_backward(qkv, grad_att, lse, attended, segments):
    count = qkv.shape[0]
    rows = BLOCK
    col = segments[:, None]
    row = segments[None, :]
    whole = lambda i, e: (0, 0)
    grid_spec = pltpu.PrefetchScalarGridSpec(
        num_scalar_prefetch=1,
        grid=(count // rows,),
        in_specs=[
            pl.BlockSpec((count, PAIR), whole),
            pl.BlockSpec((rows, PAIR), lambda i, e: (i, 1)),
            pl.BlockSpec((rows, PAIR), lambda i, e: (i, 2)),
            pl.BlockSpec((count, PAIR), whole),
            pl.BlockSpec((2, count), whole),
            pl.BlockSpec((count, PAIR), whole),
            pl.BlockSpec((rows, 1), lambda i, e: (i, 0)),
            pl.BlockSpec((1, count), whole),
        ],
        out_specs=pl.BlockSpec((count, 3 * PAIR), whole),
        scratch_shapes=[
            pltpu.VMEM((PAIR, count), jnp.float32),
            pltpu.VMEM((rows, PAIR), jnp.float32),
            pltpu.VMEM((rows, PAIR), jnp.float32),
            pltpu.VMEM((8, count), jnp.float32),
        ],
    )
    return pl.pallas_call(
        self_backward_kernel,
        grid_spec=grid_spec,
        out_shape=jax.ShapeDtypeStruct((count, 3 * PAIR), jnp.bfloat16),
        compiler_params=pltpu.CompilerParams(vmem_limit_bytes=58 * 2**20),
        cost_estimate=LITTLE,
    )(block_ends(segments, rows), qkv, qkv, qkv, grad_att, lse, attended, col, row)


def cross_forward_kernel(length, q_ref, m_ref, out_ref):
    queries = head_halves(q_ref[...], SCALE)
    keys = m_ref[:, :PAIR]
    values = m_ref[:, PAIR:]
    shape = (q_ref.shape[0], m_ref.shape[0])
    keep = lax.broadcasted_iota(jnp.int32, shape, 1) < length[0]
    parts = []
    for head in range(2):
        scores = jnp.where(keep, dot_nt(queries[head], keys), NEGATIVE)
        expo = jnp.exp(scores - jnp.max(scores, axis=1, keepdims=True))
        parts.append(dot(low(expo), values) / jnp.sum(expo, axis=1, keepdims=True))
    lane = lax.broadcasted_iota(jnp.int32, parts[0].shape, 1)
    out_ref[...] = low(jnp.where(lane < HD, parts[0], parts[1]))


def cross_forward(queries, memory, length):
    count, states = queries.shape[0], memory.shape[0] // (D // PAIR)
    grid_spec = pltpu.PrefetchScalarGridSpec(
        num_scalar_prefetch=1,
        grid=(D // PAIR,),
        in_specs=[
            pl.BlockSpec((count, PAIR), lambda i, e: (0, i)),
            pl.BlockSpec((states, 2 * PAIR), lambda i, e: (i, 0)),
        ],
        out_specs=pl.BlockSpec((count, PAIR), lambda i, e: (0, i)),
    )
    return pl.pallas_call(
        cross_forward_kernel,
        grid_spec=grid_spec,
        out_shape=jax.ShapeDtypeStruct((count, D), jnp.bfloat16),
        cost_estimate=LITTLE,
    )(length, queries, memory)


def cross_backward_kernel(length, q_ref, m_ref, g_ref, dq_ref, dm_ref):
    queries = head_halves(q_ref[...], SCALE)
    grads = head_halves(g_ref[...])
    keys = m_ref[:, :PAIR]
    values = m_ref[:, PAIR:]
    key_halves = head_halves(keys, SCALE)
    shape = (m_ref.shape[0], q_ref.shape[0])
    keep = lax.broadcasted_iota(jnp.int32, shape, 0) < length[0]
    sum_q = sum_k = sum_v = None
    for head in range(2):
        scores = jnp.where(keep, dot_nt(keys, queries[head]), NEGATIVE)
        expo = jnp.exp(scores - jnp.max(scores, axis=0, keepdims=True))
        probs = expo * (1.0 / jnp.sum(expo, axis=0, keepdims=True))
        part_v = dot(low(probs), grads[head])
        grad_probs = dot_nt(values, grads[head])
        inner = jnp.sum(probs * grad_probs, axis=0, keepdims=True)
        grad_scores = low(probs * (grad_probs - inner))
        part_k = dot(grad_scores, queries[head])
        part_q = dot_tn(grad_scores, key_halves[head])
        sum_q = part_q if sum_q is None else sum_q + part_q
        sum_k = part_k if sum_k is None else sum_k + part_k
        sum_v = part_v if sum_v is None else sum_v + part_v
    dq_ref[...] = low(sum_q)
    dm_ref[:, :PAIR] = low(sum_k)
    dm_ref[:, PAIR:] = low(sum_v)


def cross_backward(queries, memory, grads, length):
    count, states = queries.shape[0], memory.shape[0] // (D // PAIR)
    grid_spec = pltpu.PrefetchScalarGridSpec(
        num_scalar_prefetch=1,
        grid=(D // PAIR,),
        in_specs=[
            pl.BlockSpec((count, PAIR), lambda i, e: (0, i)),
            pl.BlockSpec((states, 2 * PAIR), lambda i, e: (i, 0)),
            pl.BlockSpec((count, PAIR), lambda i, e: (0, i)),
        ],
        out_specs=[
            pl.BlockSpec((count, PAIR), lambda i, e: (0, i)),
            pl.BlockSpec((states, 2 * PAIR), lambda i, e: (i, 0)),
        ],
    )
    return pl.pallas_call(
        cross_backward_kernel,
        grid_spec=grid_spec,
        out_shape=(
            jax.ShapeDtypeStruct((count, D), jnp.bfloat16),
            jax.ShapeDtypeStruct((states * (D // PAIR), 2 * PAIR), jnp.bfloat16),
        ),
        cost_estimate=LITTLE,
    )(length, queries, memory, grads)


def front_kernel(x_ref, gain, shift, qkv_w, qkv_b, one_ref, qkv_ref):
    rows = x_ref[...].astype(jnp.float32)
    centered = rows - jnp.mean(rows, axis=-1, keepdims=True)
    inverse = lax.rsqrt(jnp.mean(centered * centered, axis=-1, keepdims=True) + EPS)
    one = low(centered * inverse * gain[...] + shift[...])
    one_ref[...] = one
    qkv_ref[...] = low(dot(one, qkv_w[...]) + qkv_b[...])


def front(rows, gain, shift, qkv_w, qkv_b):
    count, tile = rows.shape[0], 256
    whole = lambda i: (0, 0)
    block = lambda i: (i, 0)
    return pl.pallas_call(
        front_kernel,
        grid=(count // tile,),
        in_specs=[
            pl.BlockSpec((tile, D), block),
            pl.BlockSpec((1, D), whole),
            pl.BlockSpec((1, D), whole),
            pl.BlockSpec(qkv_w.shape, whole),
            pl.BlockSpec((1, qkv_w.shape[1]), whole),
        ],
        out_specs=[pl.BlockSpec((tile, D), block), pl.BlockSpec((tile, qkv_w.shape[1]), block)],
        out_shape=(
            jax.ShapeDtypeStruct((count, D), jnp.bfloat16),
            jax.ShapeDtypeStruct((count, qkv_w.shape[1]), jnp.bfloat16),
        ),
        compiler_params=pltpu.CompilerParams(vmem_limit_bytes=58 * 2**20),
        cost_estimate=LITTLE,
    )(rows, gain[None], shift[None], qkv_w, qkv_b[None])


def feed_kernel(x_ref, w_ref, b_ref, ga_ref, act_ref, pre_ref, in_ref, sum_ref):
    v = dot(x_ref[...], w_ref[...]) + b_ref[...]
    square = v * v
    half = 0.5 + 0.5 * jnp.tanh(v * (GELU + GELU * 0.044715 * square))
    act_ref[...] = low(v * half)
    slope = half + (v * half) * (1.0 - half) * (2.0 * GELU + 6.0 * GELU * 0.044715 * square)
    grad = low(ga_ref[...] * slope)
    pre_ref[...] = grad
    in_ref[...] = low(dot_nt(grad, w_ref[...]))

    @pl.when(pl.program_id(0) == 0)
    def _():
        sum_ref[...] = jnp.zeros_like(sum_ref)

    sum_ref[...] += jnp.sum(grad.astype(jnp.float32), axis=0, keepdims=True)


def feed(rows, weight, bias, grad_act):
    count, hidden = grad_act.shape
    tile = 512
    whole = lambda i: (0, 0)
    block = lambda i: (i, 0)
    return pl.pallas_call(
        feed_kernel,
        grid=(count // tile,),
        in_specs=[
            pl.BlockSpec((tile, D), block),
            pl.BlockSpec((D, hidden), whole),
            pl.BlockSpec((1, hidden), whole),
            pl.BlockSpec((tile, hidden), block),
        ],
        out_specs=[
            pl.BlockSpec((tile, hidden), block),
            pl.BlockSpec((tile, hidden), block),
            pl.BlockSpec((tile, D), block),
            pl.BlockSpec((1, hidden), whole),
        ],
        out_shape=(
            jax.ShapeDtypeStruct((count, hidden), jnp.bfloat16),
            jax.ShapeDtypeStruct((count, hidden), jnp.bfloat16),
            jax.ShapeDtypeStruct((count, D), jnp.bfloat16),
            jax.ShapeDtypeStruct((1, hidden), jnp.float32),
        ),
        compiler_params=pltpu.CompilerParams(vmem_limit_bytes=58 * 2**20),
        cost_estimate=LITTLE,
    )(rows, weight, bias[None], grad_act)


def expand_kernel(replica, x_ref, g_ref, *refs):
    keep, outs = refs[-1], refs[:-1]
    size, rows = len(outs), outs[0].shape[1]
    owners = x_ref.shape[1] // (size * rows)
    keep[...] = low(dot_tn(x_ref[...], g_ref[...])).reshape(keep.shape)
    step = pl.program_id(0) * owners
    for owner in range(owners):
        for other, out in enumerate(outs):
            out[pl.ds(step + owner, 1)] = keep[owner, pl.ds(replica[0] ^ other, 1)]


def expand_grads(rows_in, grads, owners, part_rows):
    size, me = lax.axis_size("rep"), lax.axis_index("rep")
    count, hidden = grads.shape
    if part_rows % 16:
        full = low(dot_tn(rows_in, grads)).reshape(owners, size, part_rows, hidden)
        return [lax.dynamic_index_in_dim(full, me ^ step, 1, keepdims=False) for step in range(size)]
    tile = 2
    grid_spec = pltpu.PrefetchScalarGridSpec(
        num_scalar_prefetch=1,
        grid=(owners // tile,),
        in_specs=[
            pl.BlockSpec((count, tile * size * part_rows), lambda i, e: (0, i)),
            pl.BlockSpec((count, hidden), lambda i, e: (0, 0)),
        ],
        out_specs=[pl.BlockSpec((owners, part_rows, hidden), lambda i, e: (0, 0, 0))] * size,
        scratch_shapes=[pltpu.VMEM((tile, size, part_rows, hidden), jnp.bfloat16)],
    )
    return pl.pallas_call(
        expand_kernel,
        grid_spec=grid_spec,
        out_shape=(jax.ShapeDtypeStruct((owners, part_rows, hidden), jnp.bfloat16),) * size,
        compiler_params=pltpu.CompilerParams(vmem_limit_bytes=58 * 2**20),
        cost_estimate=LITTLE,
    )(me[None], rows_in, grads)


def shrink_kernel(replica, a_ref, g_ref, *outs):
    for step, out in enumerate(outs):

        @pl.when(pl.program_id(0) == step)
        def _():
            out[...] = low(dot_tn(a_ref[...], g_ref[...]))


def shrink_grads(act, grads):
    size, me = lax.axis_size("rep"), lax.axis_index("rep")
    count, hidden = act.shape
    part = hidden // size
    if part % 128:
        full = low(dot_tn(act, grads)).reshape(size, part, D)
        return [lax.dynamic_index_in_dim(full, me ^ step, 0, keepdims=False) for step in range(size)]
    grid_spec = pltpu.PrefetchScalarGridSpec(
        num_scalar_prefetch=1,
        grid=(size,),
        in_specs=[
            pl.BlockSpec((count, part), lambda i, e: (0, e[0] ^ i)),
            pl.BlockSpec((count, D), lambda i, e: (0, 0)),
        ],
        out_specs=[pl.BlockSpec((part, D), lambda i, e: (0, 0))] * size,
    )
    return pl.pallas_call(
        shrink_kernel,
        grid_spec=grid_spec,
        out_shape=(jax.ShapeDtypeStruct((part, D), jnp.bfloat16),) * size,
        compiler_params=pltpu.CompilerParams(vmem_limit_bytes=58 * 2**20),
        cost_estimate=LITTLE,
    )(me[None], act, grads)


def product_kernel(a_ref, b_ref, out_ref):
    out_ref[...] = low(dot(a_ref[...], b_ref[...]))


def product(left, right):
    count, depth = left.shape
    tile = 512
    return pl.pallas_call(
        product_kernel,
        grid=(count // tile,),
        in_specs=[pl.BlockSpec((tile, depth), lambda i: (i, 0)), pl.BlockSpec(right.shape, lambda i: (0, 0))],
        out_specs=pl.BlockSpec((tile, right.shape[1]), lambda i: (i, 0)),
        out_shape=jax.ShapeDtypeStruct((count, right.shape[1]), jnp.bfloat16),
        compiler_params=pltpu.CompilerParams(vmem_limit_bytes=58 * 2**20),
        cost_estimate=LITTLE,
    )(left, right)


def back_kernel(g_ref, w_ref, one_ref, out_ref, sum_ref, own_ref):
    @pl.when(pl.program_id(0) == 0)
    def _():
        sum_ref[...] = jnp.zeros_like(sum_ref)
        own_ref[...] = jnp.zeros_like(own_ref)

    grads = dot_nt(g_ref[...], w_ref[...])
    out_ref[...] = low(grads)
    sum_ref[0:1, :] += jnp.sum(grads * one_ref[...].astype(jnp.float32), axis=0, keepdims=True)
    sum_ref[1:2, :] += jnp.sum(grads, axis=0, keepdims=True)
    own_ref[...] += jnp.sum(g_ref[...].astype(jnp.float32), axis=0, keepdims=True)


def back(grads, weight, rows_in):
    count, width = grads.shape
    tile = 256
    return pl.pallas_call(
        back_kernel,
        grid=(count // tile,),
        in_specs=[
            pl.BlockSpec((tile, width), lambda i: (i, 0)),
            pl.BlockSpec(weight.shape, lambda i: (0, 0)),
            pl.BlockSpec((tile, D), lambda i: (i, 0)),
        ],
        out_specs=[
            pl.BlockSpec((tile, D), lambda i: (i, 0)),
            pl.BlockSpec((2, D), lambda i: (0, 0)),
            pl.BlockSpec((1, width), lambda i: (0, 0)),
        ],
        out_shape=(
            jax.ShapeDtypeStruct((count, D), jnp.bfloat16),
            jax.ShapeDtypeStruct((2, D), jnp.float32),
            jax.ShapeDtypeStruct((1, width), jnp.float32),
        ),
        compiler_params=pltpu.CompilerParams(vmem_limit_bytes=58 * 2**20),
        cost_estimate=LITTLE,
    )(grads, weight, rows_in)


def heads_grads_kernel(x_ref, g_ref, e_ref, m_ref, out_ref):
    width = g_ref.shape[1]
    shape = out_ref.shape[1:3]
    for owner in range(shape[0]):
        place = slice(owner * x_ref.shape[1] // shape[0], (owner + 1) * x_ref.shape[1] // shape[0])
        left = low(dot_tn(x_ref[:, place], g_ref[...]))
        right = low(dot_tn(e_ref[:, place], m_ref[...]))
        for replica in range(out_ref.shape[0]):
            rows = slice(replica * shape[1], (replica + 1) * shape[1])
            out_ref[replica, owner, :, :width] = left[rows, :]
            out_ref[replica, owner, :, width:] = right[rows, :]


def heads_grads(rows_in, grads, enc, enc_grads, owners, part_rows):
    size = lax.axis_size("rep")
    width, enc_width = grads.shape[1], enc_grads.shape[1]
    if part_rows % 16:
        both = low(jnp.concatenate([dot_tn(rows_in, grads), dot_tn(enc, enc_grads)], axis=1))
        return both.reshape(owners, size, part_rows, width + enc_width).transpose(1, 0, 2, 3)
    tile = 2
    return pl.pallas_call(
        heads_grads_kernel,
        grid=(owners // tile,),
        in_specs=[
            pl.BlockSpec((rows_in.shape[0], tile * size * part_rows), lambda i: (0, i)),
            pl.BlockSpec(grads.shape, lambda i: (0, 0)),
            pl.BlockSpec((enc.shape[0], tile * size * part_rows), lambda i: (0, i)),
            pl.BlockSpec(enc_grads.shape, lambda i: (0, 0)),
        ],
        out_specs=pl.BlockSpec((size, tile, part_rows, width + enc_width), lambda i: (0, i, 0, 0)),
        out_shape=jax.ShapeDtypeStruct((size, owners, part_rows, width + enc_width), jnp.bfloat16),
        compiler_params=pltpu.CompilerParams(vmem_limit_bytes=58 * 2**20),
        cost_estimate=LITTLE,
    )(rows_in, grads, enc, enc_grads)


def last_kernel(x_ref, e_ref, one_ref, gain, out_ref):
    rows = x_ref[...].astype(jnp.float32)
    centered = rows - jnp.mean(rows, axis=-1, keepdims=True)
    inverse = lax.rsqrt(jnp.mean(centered * centered, axis=-1, keepdims=True) + EPS)
    x_hat = centered * inverse
    grads = e_ref[...].astype(jnp.float32) * gain[...]
    inner = jnp.mean(grads * x_hat, axis=-1, keepdims=True)
    out_ref[...] = one_ref[...] + inverse * (grads - jnp.mean(grads, axis=-1, keepdims=True) - x_hat * inner)


def last(rows, grads, grad_one, gain):
    count = rows.shape[0]
    tile = 128
    block = pl.BlockSpec((tile, D), lambda i: (i, 0))
    return pl.pallas_call(
        last_kernel,
        grid=(count // tile,),
        in_specs=[block, block, block, pl.BlockSpec((1, D), lambda i: (0, 0))],
        out_specs=block,
        out_shape=jax.ShapeDtypeStruct((count, D), jnp.float32),
        cost_estimate=LITTLE,
    )(rows, grads, grad_one, gain[None])


def rep_send(value, step):
    size = lax.axis_size("rep")
    return lax.ppermute(value, "rep", [(i, i ^ step) for i in range(size)])


def rep_start(value):
    return [value] + [rep_send(value, step) for step in range(1, lax.axis_size("rep"))]


def rep_place(parts, axis):
    size, me = lax.axis_size("rep"), lax.axis_index("rep")
    value = parts[0]
    out = jnp.zeros(value.shape[:axis] + (size,) + value.shape[axis:], value.dtype)
    for step, part in enumerate(parts):
        out = lax.dynamic_update_slice_in_dim(out, jnp.expand_dims(part, axis), me ^ step, axis)
    return out


def spread_kernel(place, *refs):
    out_ref = refs[-1]
    for step, part in enumerate(refs[:-1]):
        out_ref[pl.ds(place[0] ^ step, 1)] = part[...].astype(out_ref.dtype)[None]


def spread(parts, first, last, dtype):
    size, columns = len(parts), parts[0].shape[1]
    rows = last - first
    if rows % 32 or first % rows or parts[0].shape[0] % 16:
        return rep_place([part[first:last] for part in parts], 0).astype(dtype)
    tile = rows // 2
    grid_spec = pltpu.PrefetchScalarGridSpec(
        num_scalar_prefetch=1,
        grid=(2,),
        in_specs=[pl.BlockSpec((tile, columns), lambda i, e: (first // tile + i, 0))] * size,
        out_specs=pl.BlockSpec((size, tile, columns), lambda i, e: (0, i, 0)),
    )
    return pl.pallas_call(
        spread_kernel,
        grid_spec=grid_spec,
        out_shape=jax.ShapeDtypeStruct((size, rows, columns), dtype),
        compiler_params=pltpu.CompilerParams(vmem_limit_bytes=58 * 2**20),
        cost_estimate=LITTLE,
    )(lax.axis_index("rep")[None], *parts)


def rep_gather(value, axis):
    return rep_place(rep_start(value), axis)


def rep_swap(parts):
    return lax.all_to_all(parts, "rep", 0, 0, tiled=True)


def rep_split(parts, axis):
    size, me = lax.axis_size("rep"), lax.axis_index("rep")
    picks = [lax.dynamic_index_in_dim(parts, me ^ step, axis, keepdims=False) for step in range(size)]
    return [picks[0]] + [rep_send(low(picks[step]), step) for step in range(1, size)]


def sum_first(parts):
    return low(jnp.sum(parts.astype(jnp.float32), axis=0))


def add_up(parts):
    total = parts[0].astype(jnp.float32)
    for part in parts[1:]:
        total = total + part.astype(jnp.float32)
    return low(total)


def rep_reduce(parts, axis):
    return add_up(rep_split(parts, axis))


def core_send(value):
    size = lax.axis_size("shard")
    return lax.ppermute(value, "shard", [(i, i ^ 1) for i in range(size)])


def line_send(value, step, group=None):
    size = lax.axis_size("shard")
    group = group or size
    route = [(i, i // group * group + (i + 2 * step) % group) for i in range(size)]
    return lax.ppermute(value, "shard", route)


def line_scatter_start(value, group=None):
    group = group or lax.axis_size("shard")
    core = lax.axis_index("shard") % 2
    value = value.reshape((group // 2, 2, value.shape[0] // group) + value.shape[1:])
    mine = lax.dynamic_index_in_dim(value, core, 1, keepdims=False)
    theirs = lax.dynamic_index_in_dim(value, 1 - core, 1, keepdims=False)
    return [mine, core_send(theirs)]


def line_scatter_middle(both, group=None):
    group = group or lax.axis_size("shard")
    chips = group // 2
    chip = lax.axis_index("shard") % group // 2
    line = add_up(both)
    parts = [lax.dynamic_index_in_dim(line, (chip + step) % chips, 0, keepdims=False) for step in range(chips)]
    return [parts[0]] + [line_send(parts[step], step, group) for step in range(1, chips)]


def columns_kernel(place, *refs):
    out_ref = refs[-1]
    rows = out_ref.shape[1]
    for step, part in enumerate(refs[:-1]):
        for block in range(part.shape[0] // rows):
            wide = part[block * rows : (block + 1) * rows, :].astype(out_ref.dtype)
            out_ref[pl.ds(place[0] ^ step, 1), :, block * D : (block + 1) * D] = wide[None]


def spread_columns(parts, first, blocks, rows):
    size, me = len(parts), lax.axis_index("rep")
    if rows % 16:
        parts = [part[first:].reshape(blocks, rows, -1).transpose(1, 0, 2).reshape(rows, -1) for part in parts]
        return rep_place(parts, 0).astype(jnp.float32).reshape(size * rows, -1)
    halves = 2
    taken = blocks * rows // halves
    grid_spec = pltpu.PrefetchScalarGridSpec(
        num_scalar_prefetch=1,
        grid=(halves,),
        in_specs=[pl.BlockSpec((taken, D), lambda i, e: (first // taken + i, 0))] * size,
        out_specs=pl.BlockSpec((size, rows, blocks * D // halves), lambda i, e: (0, 0, i)),
    )
    out = pl.pallas_call(
        columns_kernel,
        grid_spec=grid_spec,
        out_shape=jax.ShapeDtypeStruct((size, rows, blocks * D), jnp.float32),
        compiler_params=pltpu.CompilerParams(vmem_limit_bytes=58 * 2**20),
        cost_estimate=LITTLE,
    )(me[None], *parts)
    return out.reshape(size * rows, blocks * D)


def heads_kernel(span, place, *refs):
    qkv_ref, memory_ref = refs[-2:]
    rows, width = qkv_ref.shape[1], D // span
    for step, part in enumerate(refs[:-2]):
        take = pl.ds(place[0] ^ step, 1)
        for block in range(span):
            wide = part[block * rows : (block + 1) * rows, :].astype(jnp.float32)[None]
            for kind in range(5):
                out, at = (qkv_ref, kind) if kind < 3 else (memory_ref, kind - 3)
                columns = slice(at * D + block * width, at * D + (block + 1) * width)
                out[take, :, columns] = wide[:, :, kind * width : (kind + 1) * width]


def spread_heads(parts, span, rows, width):
    size, me = len(parts), lax.axis_index("rep")
    if rows % 16:
        full = rep_place([part[: span * rows].reshape(span, rows, 5, width) for part in parts], 0)
        full = full.transpose(0, 2, 3, 1, 4).reshape(size * rows, 5 * D).astype(jnp.float32)
        return full[:, : 3 * D], full[:, 3 * D :]
    grid_spec = pltpu.PrefetchScalarGridSpec(
        num_scalar_prefetch=1,
        grid=(1,),
        in_specs=[pl.BlockSpec((span * rows, 5 * width), lambda i, e: (0, 0))] * size,
        out_specs=[
            pl.BlockSpec((size, rows, 3 * D), lambda i, e: (0, 0, 0)),
            pl.BlockSpec((size, rows, 2 * D), lambda i, e: (0, 0, 0)),
        ],
    )
    qkv, memory = pl.pallas_call(
        functools.partial(heads_kernel, span),
        grid_spec=grid_spec,
        out_shape=(
            jax.ShapeDtypeStruct((size, rows, 3 * D), jnp.float32),
            jax.ShapeDtypeStruct((size, rows, 2 * D), jnp.float32),
        ),
        compiler_params=pltpu.CompilerParams(vmem_limit_bytes=58 * 2**20),
        cost_estimate=LITTLE,
    )(me[None], *parts)
    return qkv.reshape(size * rows, 3 * D), memory.reshape(size * rows, 2 * D)


def line_start(piece):
    return [piece] + [line_send(piece, step) for step in range(1, lax.axis_size("shard") // 2)]


def line_place(parts):
    chips, chip = len(parts), lax.axis_index("shard") // 2
    kinds, rows, columns = parts[0].shape
    line = jnp.zeros((kinds, chips, rows, columns), parts[0].dtype)
    for step, part in enumerate(parts):
        line = lax.dynamic_update_slice_in_dim(line, part[:, None], (chip - step) % chips, 1)
    return line


def join_kernel(place, *refs):
    outs = refs[-3:]
    parts = refs[:-3]
    size = len(parts) // 2
    for core in range(2):
        side = place[1] ^ core
        for step in range(size):
            for kind in range(3):
                outs[kind][0, pl.ds(side, 1), pl.ds(place[0] ^ step, 1)] = parts[core * size + step][kind][None]


def weight_join(mine, other):
    size = len(mine)
    _, chips, rows, _ = mine[0].shape
    core = lax.axis_index("shard") % 2
    if rows % 16:
        first = core == 0
        plane, next_plane = rep_place(mine, 2), rep_place(other, 2)
        low_core, high_core = jnp.where(first, plane, next_plane), jnp.where(first, next_plane, plane)
        full = jnp.stack([low_core, high_core], axis=2).reshape(3, D, D)
        return full[0], full[1], full[2]
    grid_spec = pltpu.PrefetchScalarGridSpec(
        num_scalar_prefetch=1,
        grid=(chips,),
        in_specs=[pl.BlockSpec((3, 1, rows, D), lambda i, e: (0, i, 0, 0))] * (2 * size),
        out_specs=[pl.BlockSpec((1, 2, size, rows, D), lambda i, e: (i, 0, 0, 0, 0))] * 3,
    )
    outs = pl.pallas_call(
        join_kernel,
        grid_spec=grid_spec,
        out_shape=(jax.ShapeDtypeStruct((chips, 2, size, rows, D), jnp.bfloat16),) * 3,
        compiler_params=pltpu.CompilerParams(vmem_limit_bytes=58 * 2**20),
        cost_estimate=LITTLE,
    )(jnp.stack([lax.axis_index("rep"), core]), *mine, *other)
    return tuple(out.reshape(D, D) for out in outs)


def plain_kernel(core, a_ref, b_ref, c_ref, ga_ref, gb_ref, gc_ref, mine_ref, theirs_ref):
    width = a_ref.shape[1] // 2
    for kind, (left, right) in enumerate(((a_ref, ga_ref), (b_ref, gb_ref), (c_ref, gc_ref))):
        for side, out in enumerate((mine_ref, theirs_ref)):
            place = pl.ds(pl.multiple_of((core[0] ^ side) * width, width), width)
            out[kind, 0] = low(dot_tn(left[:, place], right[...])).reshape(out.shape[2:])


def plain_grads(lefts, rights):
    size, chips = lax.axis_size("rep"), lax.axis_size("shard") // 2
    core = lax.axis_index("shard") % 2
    rows = D // (2 * chips * size)
    if rows % 16:
        stack = jnp.stack([low(dot_tn(left, right)) for left, right in zip(lefts, rights)])
        stack = stack.reshape(3, chips, 2, size, rows, D)
        return [lax.dynamic_index_in_dim(stack, core ^ side, 2, keepdims=False) for side in range(2)]
    count = lefts[0].shape[0]
    grid_spec = pltpu.PrefetchScalarGridSpec(
        num_scalar_prefetch=1,
        grid=(chips,),
        in_specs=[pl.BlockSpec((count, D // chips), lambda i, e: (0, i))] * 3
        + [pl.BlockSpec((count, D), lambda i, e: (0, 0))] * 3,
        out_specs=[pl.BlockSpec((3, 1, size, rows, D), lambda i, e: (0, i, 0, 0, 0))] * 2,
    )
    return pl.pallas_call(
        plain_kernel,
        grid_spec=grid_spec,
        out_shape=(jax.ShapeDtypeStruct((3, chips, size, rows, D), jnp.bfloat16),) * 2,
        compiler_params=pltpu.CompilerParams(vmem_limit_bytes=58 * 2**20),
        cost_estimate=pl.CostEstimate(flops=6 * count * D * D, bytes_accessed=20 * count * D, transcendentals=0),
    )(core[None], *lefts, *rights)


def split_kernel(place, mine_ref, other_ref, *outs):
    for step, out in enumerate(outs):
        take = pl.ds(place[0] ^ step, 1)
        total = mine_ref[:, 0, take].astype(jnp.float32) + other_ref[:, 0, take].astype(jnp.float32)
        out[...] = low(total)


def core_sum_split(mine, other):
    kinds, chips, size, rows, _ = mine.shape
    if rows % 16:
        total = add_up([mine, other])
        me = lax.axis_index("rep")
        return [lax.dynamic_index_in_dim(total, me ^ step, 2, keepdims=False) for step in range(size)]
    grid_spec = pltpu.PrefetchScalarGridSpec(
        num_scalar_prefetch=1,
        grid=(chips,),
        in_specs=[pl.BlockSpec((kinds, 1, size, rows, D), lambda i, e: (0, i, 0, 0, 0))] * 2,
        out_specs=[pl.BlockSpec((kinds, 1, rows, D), lambda i, e: (0, i, 0, 0))] * size,
    )
    return pl.pallas_call(
        split_kernel,
        grid_spec=grid_spec,
        out_shape=(jax.ShapeDtypeStruct((kinds, chips, rows, D), jnp.bfloat16),) * size,
        compiler_params=pltpu.CompilerParams(vmem_limit_bytes=58 * 2**20),
        cost_estimate=LITTLE,
    )(lax.axis_index("rep")[None], mine, other)


def reduce_line(line):
    chips = lax.axis_size("shard") // 2
    chip = lax.axis_index("shard") // 2
    parts = [lax.dynamic_index_in_dim(line, (chip + step) % chips, 1, keepdims=False) for step in range(chips)]
    return [parts[0]] + [line_send(parts[step], step) for step in range(1, chips)]


def shards(
    tokens,
    segments,
    enc_states,
    enc_lengths,
    cotangent,
    self_qkv,
    self_out,
    cross_query,
    cross_memory,
    cross_out,
    expand_weight,
    shrink_weight,
    norm_gain,
    norm_bias,
    proj_bias,
    expand_bias,
):
    row_count, enc_rows = tokens.shape[0], enc_states.shape[0]
    span = SEQ // row_count
    width = D // span
    count = lax.axis_size("shard")
    size = lax.axis_size("rep")
    rep_pos = lax.axis_index("rep")
    shard_pos = lax.axis_index("shard")
    local_pos = shard_pos % span
    local_seq = shard_pos // span
    groups = None
    if count != span:
        groups = [[g * span + i for i in range(span)] for g in range(count // span)]
    weight_rows = self_qkv.shape[0]
    part_rows = weight_rows // size
    hidden = expand_bias.shape[0]
    shard_width = norm_gain.shape[1]

    def gather(value, groups=None):
        return lax.all_gather(value, "shard", axis=0, tiled=True, axis_index_groups=groups)

    def scatter(value, groups=None):
        return lax.psum_scatter(value, "shard", scatter_dimension=0, tiled=True, axis_index_groups=groups)

    def swap(value):
        return lax.all_to_all(value, "shard", 0, 0, tiled=True)

    def own_part(weight):
        return lax.dynamic_slice_in_dim(weight, rep_pos * part_rows, part_rows, axis=0)

    def by_pairs(weight, kinds):
        blocks = weight.reshape(part_rows, kinds, span, width).transpose(2, 0, 1, 3)
        return blocks.reshape(span, part_rows, kinds * width)

    blocks = jnp.concatenate([by_pairs(own_part(self_qkv), 3), by_pairs(own_part(cross_memory), 2)], axis=2)
    blocks = jnp.tile(blocks, (count // span, 1, 1))
    small = jnp.concatenate([norm_gain, norm_bias, proj_bias], axis=0)
    small_count = small.shape[0]
    small_rows = -(-small.size // (5 * width))
    small = jnp.pad(small.reshape(-1), (0, small_rows * 5 * width - small.size)).reshape(small_rows, 5 * width)
    blocks = jnp.concatenate([blocks, jnp.broadcast_to(small, (count,) + small.shape)], axis=1)
    swapped = swap(blocks)
    plain_parts = line_start(jnp.stack([own_part(self_out), own_part(cross_query), own_part(cross_out)]))
    enc_all = gather(enc_states, groups)
    swapped, plain_parts, enc_all = lax.optimization_barrier((swapped, plain_parts, enc_all))
    rows_all = gather(after(tokens, plain_parts, enc_all), groups)
    small_all = swapped[:, part_rows:].reshape(count, small_rows * 5 * width)[:, : small_count * shard_width]
    small_all = small_all.reshape(count, small_count, shard_width)
    small_all = small_all.transpose(1, 0, 2).reshape(small_count, D).astype(jnp.float32)
    gain_rows, shift_rows, bias_rows = small_all[:3], small_all[3:6], small_all[6:]
    head_weight = rep_gather(swapped[:, :part_rows], 1).reshape(D, 5 * width)
    qkv_weight, memory_weight = head_weight[:, : 3 * width], head_weight[:, 3 * width :]
    qkv_weight, memory_weight = head_weight[:, : 3 * width], head_weight[:, 3 * width :]
    own_bias = lax.dynamic_slice_in_dim(bias_rows, local_pos * width, width, axis=1)
    zero_bias = jnp.zeros((width,), jnp.float32)
    memory_pair = low(dot(enc_all, memory_weight) + jnp.concatenate([zero_bias, own_bias[4]]))
    plain_mine = rep_start(line_place(after(plain_parts, head_weight)))
    rows_all, qkv_weight, memory_weight, plain_mine[1], plain_mine[2] = lax.optimization_barrier(
        (rows_all, qkv_weight, memory_weight, plain_mine[1], plain_mine[2])
    )
    memory_all = gather(after(memory_pair, rows_all), groups)
    expand_part = own_part(after(expand_weight, rows_all)).reshape(part_rows, count, hidden).transpose(1, 0, 2)
    expand_swapped = swap(expand_part)

    seq_segments = lax.dynamic_slice_in_dim(segments, local_seq * SEQ, SEQ)
    qkv_bias = jnp.concatenate([own_bias[0], zero_bias, own_bias[1]])
    input_one_all, qkv = front(rows_all, gain_rows[0], shift_rows[0], qkv_weight, qkv_bias)
    att_low, att_full, lse = self_forward(qkv, seq_segments)
    att_low, memory_all, plain_mine, expand_swapped = lax.optimization_barrier(
        (att_low, memory_all, plain_mine, expand_swapped)
    )
    grad_all = gather(after(cotangent, memory_all))
    plain_other = [core_send(part) for part in plain_mine]
    attn_proj, query_in, cross_proj = weight_join(plain_mine, plain_other)
    attended = lax.all_to_all(att_low, "shard", 0, 1, tiled=True, axis_index_groups=groups)

    enc_count = lax.dynamic_slice_in_dim(enc_lengths, local_seq, 1)

    residual_in = tokens.astype(jnp.float32)
    hidden_one = residual_in + dot(attended, attn_proj) + bias_rows[2]
    input_two = low(norm_apply(hidden_one, gain_rows[1], shift_rows[1]))
    cross_q = low(dot(input_two, query_in) + bias_rows[3])
    context = cross_forward(cross_q, memory_all, enc_count)
    hidden_two = hidden_one + dot(context, cross_proj) + bias_rows[5]
    input_three = low(norm_apply(hidden_two, gain_rows[2], shift_rows[2]))

    input_three_all = gather(input_three)
    expand_parts = rep_start(expand_swapped.reshape(count * part_rows, hidden))
    grad_all_now = after(grad_all, input_three)
    expand_local = spread(expand_parts, 0, count * part_rows, jnp.bfloat16)
    expand_local = expand_local.reshape(size, count, part_rows, hidden).transpose(1, 0, 2, 3).reshape(D, hidden)
    grad_act = dot_nt(grad_all_now, shrink_weight)
    input_three_all, grad_act, expand_local = lax.optimization_barrier((input_three_all, grad_act, expand_local))
    act, grad_pre, grad_in_three_low, hidden_sums = feed(
        input_three_all, expand_local, expand_bias.astype(jnp.float32), grad_act
    )
    grad_hidden_bias = hidden_sums[0]
    grad_in_three = scatter(grad_in_three_low)

    part_hidden = hidden // size

    def send_parts(parts):
        return [parts[0]] + [rep_send(parts[step], step) for step in range(1, size)]

    rows_late, grad_pre_late = after((input_three_all, grad_pre), grad_in_three_low)
    expand_grad_parts = expand_grads(rows_late, grad_pre_late, count, part_rows)
    shrink_parts = send_parts(shrink_grads(after(act, expand_grad_parts[0]), grad_all))
    expand_grad_parts = send_parts(expand_grad_parts)
    result_part = product(after(act, shrink_parts[0]), shrink_weight)
    expand_sum = add_up(expand_grad_parts)
    own_expand = swap(expand_sum)
    grad_in_three, shrink_parts[0], result_part = lax.optimization_barrier(
        (grad_in_three, shrink_parts[0], result_part)
    )
    result_sum = scatter(result_part)
    grad_in_three = grad_in_three.astype(jnp.float32)

    grad_out = cotangent.astype(jnp.float32)
    norm_three = jax.vjp(norm_apply, hidden_two, gain_rows[2], shift_rows[2])[1](grad_in_three)
    grad_two = grad_out + norm_three[0]
    grad_two_low = low(grad_two)
    grad_context = low(dot_nt(grad_two_low, cross_proj))
    grad_context, own_expand = lax.optimization_barrier((grad_context, own_expand))
    grad_cross_q, memory_part = cross_backward(cross_q, memory_all, grad_context, enc_count)
    grad_cross_q, memory_part, shrink_parts = lax.optimization_barrier((grad_cross_q, memory_part, shrink_parts))
    mem_grads = scatter(memory_part, groups)
    grad_in_two = dot_nt(grad_cross_q, query_in)
    norm_two = jax.vjp(norm_apply, hidden_one, gain_rows[1], shift_rows[1])[1](grad_in_two)
    grad_one = grad_two + norm_two[0]
    grad_one_low = low(grad_one)
    grad_attn = low(dot_nt(grad_one_low, attn_proj))
    shrink_sum = add_up(shrink_parts)
    own_expand = own_expand.reshape(part_hidden, D)
    own_feed = jnp.concatenate([shrink_sum, own_expand], axis=0)
    grad_attn, own_feed = lax.optimization_barrier((grad_attn, own_feed))
    grad_att_heads = lax.all_to_all(grad_attn, "shard", 1, 0, tiled=True, axis_index_groups=groups)

    lefts, rights = after(((attended, input_two, context), (grad_one_low, grad_cross_q, grad_two_low)), grad_attn)
    plain_own, plain_theirs = plain_grads(lefts, rights)
    plain_theirs = core_send(plain_theirs)
    grad_att_heads, plain_own = lax.optimization_barrier((grad_att_heads, plain_own))

    feed_gather = rep_start(own_feed)
    grad_qkv = self_backward(qkv, grad_att_heads, lse, att_full, seq_segments)
    grad_qkv, feed_gather, plain_theirs = lax.optimization_barrier((grad_qkv, feed_gather, plain_theirs))
    heads_parts = heads_grads(input_one_all, grad_qkv, enc_all, mem_grads, count, part_rows)
    heads_swapped = rep_swap(heads_parts)
    grad_in_one_low, one_sums, qkv_sums = back(after(grad_qkv, heads_parts), qkv_weight, input_one_all)
    plain_rep = send_parts(core_sum_split(*after((plain_own, plain_theirs), heads_parts)))
    grad_in_one_low, heads_swapped, plain_rep[0] = lax.optimization_barrier(
        (grad_in_one_low, heads_swapped, plain_rep[0])
    )
    grad_in_one = scatter(grad_in_one_low, groups)

    mem_grads_late = after(mem_grads, grad_in_one_low)
    qkv_sums = qkv_sums[0]
    gain_shift = [(one_sums[0] - shift_rows[0] * one_sums[1]) / gain_rows[0], one_sums[1]]
    zero_row = jnp.zeros((D,), jnp.float32)

    def at_own(values):
        return lax.dynamic_update_slice_in_dim(zero_row, values, local_pos * width, 0)

    small_grads = jnp.stack(
        [
            gain_shift[0],
            norm_two[1],
            norm_three[1],
            gain_shift[1],
            norm_two[2],
            norm_three[2],
            at_own(qkv_sums[:width]),
            at_own(qkv_sums[2 * width :]),
            column_sums(grad_one_low),
            column_sums(grad_cross_q),
            at_own(column_sums(mem_grads_late)[width:]),
            column_sums(grad_two_low),
            column_sums(cotangent),
        ]
    )
    small_grads = small_grads.reshape(small_count, count, shard_width).transpose(1, 0, 2)
    small_grads = small_grads.reshape(count, small_count * shard_width)
    hidden_grads = jnp.zeros((count, hidden), jnp.float32)
    hidden_grads = lax.dynamic_update_slice_in_dim(hidden_grads, grad_hidden_bias[None], shard_pos, 0)
    small_grads = low(jnp.concatenate([small_grads, hidden_grads], axis=1))
    small_size = small_grads.shape[1]
    extra = -(-small_size // (5 * width))
    small_grads = jnp.pad(small_grads, ((0, 0), (0, extra * 5 * width - small_size)))
    small_grads = small_grads.reshape(count, extra, 5 * width)
    heads_sum = sum_first(after(heads_swapped, grad_in_one_low))
    own_heads = swap(jnp.concatenate([heads_sum, small_grads], axis=1))
    own_small = sum_first(own_heads[:, part_rows:])
    own_heads = own_heads[:, :part_rows].reshape(count // span, span, part_rows, 5 * width)
    own_heads = own_heads[0] if count == span else sum_first(own_heads)
    heads_gather = rep_start(jnp.concatenate([own_heads.reshape(span * part_rows, 5 * width), own_small], axis=0))

    plain_line_parts = reduce_line(add_up(after(plain_rep, own_heads)))
    own_plain = add_up(plain_line_parts).reshape(3 * part_rows, D)
    plain_gather = rep_start(own_plain)
    enc_parts = line_scatter_start(low(dot_nt(mem_grads_late, memory_weight)), span)
    grad_enc = add_up(line_scatter_middle(enc_parts, span)).astype(jnp.float32)
    result = hidden_two + after(result_sum, grad_in_one_low).astype(jnp.float32) + bias_rows[6]

    total_shrink = spread(feed_gather, 0, part_hidden, jnp.float32)
    total_expand = spread_columns(feed_gather, part_hidden, count, part_rows)
    total_plain = [
        spread(plain_gather, kind * part_rows, (kind + 1) * part_rows, jnp.float32).reshape(weight_rows, D)
        for kind in range(3)
    ]
    total_proj, total_query, total_cross = total_plain
    total_small = sum(part[span * part_rows :].astype(jnp.float32) for part in heads_gather)
    total_small = total_small.reshape(-1)[:small_size]
    total_hidden_bias = total_small[small_count * shard_width :]
    total_small = total_small[: small_count * shard_width].reshape(small_count, shard_width)
    total_qkv, total_memory = spread_heads(heads_gather, span, part_rows, width)

    grad_tokens = last(tokens, grad_in_one, grad_one, gain_rows[0])

    return (
        low(result),
        grad_tokens,
        grad_enc,
        total_qkv,
        total_proj,
        total_query,
        total_memory,
        total_cross,
        total_expand.reshape(weight_rows, count * hidden).astype(jnp.float32),
        total_shrink.reshape(hidden, D).astype(jnp.float32),
        total_small[:3],
        total_small[3:6],
        total_small[6:],
        total_hidden_bias,
    )


def solution(mesh):
    return jax.shard_map(
        shards,
        mesh=mesh,
        in_specs=(
            P(("rep", "shard"), None),
            P("rep"),
            P(("rep", "shard"), None),
            P("rep"),
            P(("rep", "shard"), None),
            P("shard", None),
            P("shard", None),
            P("shard", None),
            P("shard", None),
            P("shard", None),
            P("shard", None),
            P("shard", None),
            P(None, "shard"),
            P(None, "shard"),
            P(None, "shard"),
            P("shard"),
        ),
        out_specs=(
            P(("rep", "shard"), None),
            P(("rep", "shard"), None),
            P(("rep", "shard"), None),
            P("shard", None),
            P("shard", None),
            P("shard", None),
            P("shard", None),
            P("shard", None),
            P("shard", None),
            P("shard", None),
            P(None, "shard"),
            P(None, "shard"),
            P(None, "shard"),
            P("shard"),
        ),
        check_vma=False,
    )
```

```python
import functools

import jax
import jax.numpy as jnp
from jax import lax
from jax.experimental import pallas as pl
from jax.experimental.pallas import tpu as pltpu
from jax.sharding import PartitionSpec as P

D = 1024
H = 16
HD = 64
SEQ = 2048
PAIR = 2 * HD

EPS = 1e-05
NEGATIVE = -1e30
SCALE = HD**-0.5
BLOCK = 512
GELU = 0.7978845608028654
LITTLE = pl.CostEstimate(flops=1000, bytes_accessed=1000, transcendentals=0)


def norm_apply(rows, gain, shift):
    mean_rows = jnp.mean(rows, axis=-1, keepdims=True)
    centered = rows - mean_rows
    inverse = lax.rsqrt(jnp.mean(centered * centered, axis=-1, keepdims=True) + EPS)
    return centered * inverse * gain + shift


def gelu_apply(values):
    return jax.nn.gelu(values, approximate=True)


def column_sums(rows):
    return jnp.sum(rows, axis=0, dtype=jnp.float32)


def low(values):
    return values.astype(jnp.bfloat16)


def dot(left, right):
    return jnp.dot(left, right, preferred_element_type=jnp.float32)


def dot_nt(left, right):
    return lax.dot_general(left, right, (((1,), (1,)), ((), ())), preferred_element_type=jnp.float32)


def dot_tn(left, right):
    return lax.dot_general(left, right, (((0,), (0,)), ((), ())), preferred_element_type=jnp.float32)


def after(value, *earlier):
    return lax.optimization_barrier((value, earlier))[0]


def head_halves(rows, scale=None):
    lane = lax.broadcasted_iota(jnp.int32, rows.shape, 1)
    if scale is not None:
        rows = rows * jnp.asarray(scale, rows.dtype)
    zero = jnp.zeros_like(rows)
    return jnp.where(lane < HD, rows, zero), jnp.where(lane < HD, zero, rows)


def self_forward_kernel(ends, q_ref, k_ref, v_ref, seg_col, seg_row, low_ref, full_ref, lse_ref):
    step = pl.program_id(0)
    rows = q_ref.shape[0]
    queries = head_halves(q_ref[...], SCALE)
    query_seg = seg_row[...]
    last_seg = ends[1, step]

    def piece(index, state, masked, diagonal):
        place = pl.ds(pl.multiple_of(index * rows, rows), rows)
        keys = k_ref[place, :]
        values = v_ref[place, :]
        keep = None
        if masked:
            keep = seg_col[place, :] == query_seg
            if diagonal:
                key_pos = lax.broadcasted_iota(jnp.int32, (rows, rows), 0)
                query_pos = lax.broadcasted_iota(jnp.int32, (rows, rows), 1)
                keep = keep & (key_pos <= query_pos)
        after_piece = []
        for head in range(2):
            top, total, acc = state[head]
            scores = dot_nt(keys, queries[head])
            if masked:
                scores = jnp.where(keep, scores, NEGATIVE)
            top_new = jnp.maximum(top, jnp.max(scores, axis=0, keepdims=True))
            expo = jnp.exp(scores - top_new)
            fade = jnp.exp(top - top_new)
            after_piece.append(
                (
                    top_new,
                    total * fade + jnp.sum(expo, axis=0, keepdims=True),
                    acc * fade + dot_tn(values, low(expo)),
                )
            )
        return tuple(after_piece)

    def before(index, state):
        return lax.cond(
            ends[0, index] == last_seg,
            lambda s: piece(index, s, False, False),
            lambda s: piece(index, s, True, False),
            state,
        )

    blank = (
        jnp.full((1, rows), NEGATIVE, jnp.float32),
        jnp.zeros((1, rows), jnp.float32),
        jnp.zeros((PAIR, rows), jnp.float32),
    )
    state = lax.fori_loop(0, step, before, (blank, blank))
    state = piece(step, state, True, True)
    parts = [
        (state[head][2] * (1.0 / state[head][1]))[head * HD : (head + 1) * HD] for head in range(2)
    ]
    joined = jnp.concatenate(parts, axis=0).T
    full_ref[...] = joined
    low_ref[...] = low(joined)
    lse_ref[0:1, :] = state[0][0] + jnp.log(state[0][1])
    lse_ref[1:2, :] = state[1][0] + jnp.log(state[1][1])


def block_ends(segments, rows):
    return jnp.stack([segments[::rows], segments[rows - 1 :: rows]])


def self_forward(qkv, segments):
    count = qkv.shape[0]
    rows = BLOCK
    col = segments[:, None]
    row = segments[None, :]
    grid_spec = pltpu.PrefetchScalarGridSpec(
        num_scalar_prefetch=1,
        grid=(count // rows,),
        in_specs=[
            pl.BlockSpec((rows, PAIR), lambda i, e: (i, 0)),
            pl.BlockSpec((count, PAIR), lambda i, e: (0, 1)),
            pl.BlockSpec((count, PAIR), lambda i, e: (0, 2)),
            pl.BlockSpec((count, 1), lambda i, e: (0, 0)),
            pl.BlockSpec((1, rows), lambda i, e: (0, i)),
        ],
        out_specs=[
            pl.BlockSpec((rows, PAIR), lambda i, e: (i, 0)),
            pl.BlockSpec((rows, PAIR), lambda i, e: (i, 0)),
            pl.BlockSpec((2, rows), lambda i, e: (0, i)),
        ],
    )
    return pl.pallas_call(
        self_forward_kernel,
        grid_spec=grid_spec,
        out_shape=(
            jax.ShapeDtypeStruct((count, PAIR), jnp.bfloat16),
            jax.ShapeDtypeStruct((count, PAIR), jnp.float32),
            jax.ShapeDtypeStruct((2, count), jnp.float32),
        ),
        compiler_params=pltpu.CompilerParams(vmem_limit_bytes=58 * 2**20),
        cost_estimate=LITTLE,
    )(block_ends(segments, rows), qkv, qkv, qkv, col, row)


def self_backward_kernel(
    ends, q_ref, k_ref, v_ref, go_ref, lse_ref, o_ref, seg_col, seg_row, grad_ref, acc_q, acc_k, acc_v, delta_ref
):
    step = pl.program_id(0)
    blocks = pl.num_programs(0)
    rows = k_ref.shape[0]

    @pl.when(step == 0)
    def _():
        acc_q[...] = jnp.zeros_like(acc_q)
        lane = lax.broadcasted_iota(jnp.int32, (8, PAIR), 1) // HD
        pick = (lane == lax.broadcasted_iota(jnp.int32, (8, PAIR), 0)).astype(jnp.float32)
        delta_ref[...] = lax.dot_general(
            pick,
            go_ref[...].astype(jnp.float32) * o_ref[...],
            (((1,), (1,)), ((), ())),
            precision=lax.Precision.HIGHEST,
            preferred_element_type=jnp.float32,
        )

    keys = k_ref[...]
    values = v_ref[...]
    key_halves = head_halves(keys, SCALE)
    key_seg = seg_col[...]
    first_seg = ends[0, step]

    def piece(index, masked, diagonal):
        place = pl.ds(pl.multiple_of(index * rows, rows), rows)
        queries = head_halves(q_ref[place, :], SCALE)
        grads = head_halves(go_ref[place, :])
        keep = None
        if masked:
            keep = seg_row[:, place] == key_seg
            if diagonal:
                key_pos = lax.broadcasted_iota(jnp.int32, (rows, rows), 0)
                query_pos = lax.broadcasted_iota(jnp.int32, (rows, rows), 1)
                keep = keep & (key_pos <= query_pos)
        sum_q = sum_k = sum_v = None
        for head in range(2):
            scores = dot_nt(keys, queries[head])
            probs = jnp.exp(scores - lse_ref[head : head + 1, place])
            if masked:
                probs = jnp.where(keep, probs, 0.0)
            part_v = dot(low(probs), grads[head])
            grad_probs = dot_nt(values, grads[head])
            grad_scores = low(probs * (grad_probs - delta_ref[head : head + 1, place]))
            part_k = dot(grad_scores, queries[head])
            part_q = dot_tn(key_halves[head], grad_scores)
            sum_q = part_q if sum_q is None else sum_q + part_q
            sum_k = part_k if sum_k is None else sum_k + part_k
            sum_v = part_v if sum_v is None else sum_v + part_v
        acc_q[:, place] += sum_q
        if diagonal:
            acc_k[...] = sum_k
            acc_v[...] = sum_v
        else:
            acc_k[...] += sum_k
            acc_v[...] += sum_v

    piece(step, True, True)

    @pl.loop(step + 1, blocks)
    def _(index):
        whole = ends[1, index] == first_seg

        @pl.when(whole)
        def _():
            piece(index, False, False)

        @pl.when(jnp.logical_not(whole))
        def _():
            piece(index, True, False)

    own = pl.ds(pl.multiple_of(step * rows, rows), rows)
    grad_ref[own, 0:PAIR] = low(acc_q[:, own].T)
    grad_ref[own, PAIR : 2 * PAIR] = low(acc_k[...])
    grad_ref[own, 2 * PAIR : 3 * PAIR] = low(acc_v[...])


def self_backward(qkv, grad_att, lse, attended, segments):
    count = qkv.shape[0]
    rows = BLOCK
    col = segments[:, None]
    row = segments[None, :]
    whole = lambda i, e: (0, 0)
    grid_spec = pltpu.PrefetchScalarGridSpec(
        num_scalar_prefetch=1,
        grid=(count // rows,),
        in_specs=[
            pl.BlockSpec((count, PAIR), whole),
            pl.BlockSpec((rows, PAIR), lambda i, e: (i, 1)),
            pl.BlockSpec((rows, PAIR), lambda i, e: (i, 2)),
            pl.BlockSpec((count, PAIR), whole),
            pl.BlockSpec((2, count), whole),
            pl.BlockSpec((count, PAIR), whole),
            pl.BlockSpec((rows, 1), lambda i, e: (i, 0)),
            pl.BlockSpec((1, count), whole),
        ],
        out_specs=pl.BlockSpec((count, 3 * PAIR), whole),
        scratch_shapes=[
            pltpu.VMEM((PAIR, count), jnp.float32),
            pltpu.VMEM((rows, PAIR), jnp.float32),
            pltpu.VMEM((rows, PAIR), jnp.float32),
            pltpu.VMEM((8, count), jnp.float32),
        ],
    )
    return pl.pallas_call(
        self_backward_kernel,
        grid_spec=grid_spec,
        out_shape=jax.ShapeDtypeStruct((count, 3 * PAIR), jnp.bfloat16),
        compiler_params=pltpu.CompilerParams(vmem_limit_bytes=58 * 2**20),
        cost_estimate=pl.CostEstimate(flops=16 * 10**9, bytes_accessed=4 * 2**20, transcendentals=0),
    )(block_ends(segments, rows), qkv, qkv, qkv, grad_att, lse, attended, col, row)


def cross_forward_kernel(length, q_ref, m_ref, out_ref):
    queries = head_halves(q_ref[...], SCALE)
    keys = m_ref[:, :PAIR]
    values = m_ref[:, PAIR:]
    shape = (q_ref.shape[0], m_ref.shape[0])
    keep = lax.broadcasted_iota(jnp.int32, shape, 1) < length[0]
    parts = []
    for head in range(2):
        scores = jnp.where(keep, dot_nt(queries[head], keys), NEGATIVE)
        expo = jnp.exp(scores - jnp.max(scores, axis=1, keepdims=True))
        parts.append(dot(low(expo), values) / jnp.sum(expo, axis=1, keepdims=True))
    lane = lax.broadcasted_iota(jnp.int32, parts[0].shape, 1)
    out_ref[...] = low(jnp.where(lane < HD, parts[0], parts[1]))


def cross_forward(queries, memory, length):
    count, states = queries.shape[0], memory.shape[0] // (D // PAIR)
    grid_spec = pltpu.PrefetchScalarGridSpec(
        num_scalar_prefetch=1,
        grid=(D // PAIR,),
        in_specs=[
            pl.BlockSpec((count, PAIR), lambda i, e: (0, i)),
            pl.BlockSpec((states, 2 * PAIR), lambda i, e: (i, 0)),
        ],
        out_specs=pl.BlockSpec((count, PAIR), lambda i, e: (0, i)),
    )
    return pl.pallas_call(
        cross_forward_kernel,
        grid_spec=grid_spec,
        out_shape=jax.ShapeDtypeStruct((count, D), jnp.bfloat16),
        cost_estimate=LITTLE,
    )(length, queries, memory)


def cross_backward_kernel(length, q_ref, m_ref, g_ref, dq_ref, dm_ref):
    queries = head_halves(q_ref[...], SCALE)
    grads = head_halves(g_ref[...])
    keys = m_ref[:, :PAIR]
    values = m_ref[:, PAIR:]
    key_halves = head_halves(keys, SCALE)
    shape = (m_ref.shape[0], q_ref.shape[0])
    keep = lax.broadcasted_iota(jnp.int32, shape, 0) < length[0]
    sum_q = sum_k = sum_v = None
    for head in range(2):
        scores = jnp.where(keep, dot_nt(keys, queries[head]), NEGATIVE)
        expo = jnp.exp(scores - jnp.max(scores, axis=0, keepdims=True))
        probs = expo * (1.0 / jnp.sum(expo, axis=0, keepdims=True))
        part_v = dot(low(probs), grads[head])
        grad_probs = dot_nt(values, grads[head])
        inner = jnp.sum(probs * grad_probs, axis=0, keepdims=True)
        grad_scores = low(probs * (grad_probs - inner))
        part_k = dot(grad_scores, queries[head])
        part_q = dot_tn(grad_scores, key_halves[head])
        sum_q = part_q if sum_q is None else sum_q + part_q
        sum_k = part_k if sum_k is None else sum_k + part_k
        sum_v = part_v if sum_v is None else sum_v + part_v
    dq_ref[...] = low(sum_q)
    dm_ref[:, :PAIR] = low(sum_k)
    dm_ref[:, PAIR:] = low(sum_v)


def cross_backward(queries, memory, grads, length):
    count, states = queries.shape[0], memory.shape[0] // (D // PAIR)
    grid_spec = pltpu.PrefetchScalarGridSpec(
        num_scalar_prefetch=1,
        grid=(D // PAIR,),
        in_specs=[
            pl.BlockSpec((count, PAIR), lambda i, e: (0, i)),
            pl.BlockSpec((states, 2 * PAIR), lambda i, e: (i, 0)),
            pl.BlockSpec((count, PAIR), lambda i, e: (0, i)),
        ],
        out_specs=[
            pl.BlockSpec((count, PAIR), lambda i, e: (0, i)),
            pl.BlockSpec((states, 2 * PAIR), lambda i, e: (i, 0)),
        ],
    )
    return pl.pallas_call(
        cross_backward_kernel,
        grid_spec=grid_spec,
        out_shape=(
            jax.ShapeDtypeStruct((count, D), jnp.bfloat16),
            jax.ShapeDtypeStruct((states * (D // PAIR), 2 * PAIR), jnp.bfloat16),
        ),
        cost_estimate=LITTLE,
    )(length, queries, memory, grads)


def front_kernel(x_ref, gain, shift, qkv_w, qkv_b, one_ref, qkv_ref):
    rows = x_ref[...].astype(jnp.float32)
    centered = rows - jnp.mean(rows, axis=-1, keepdims=True)
    inverse = lax.rsqrt(jnp.mean(centered * centered, axis=-1, keepdims=True) + EPS)
    one = low(centered * inverse * gain[...] + shift[...])
    one_ref[...] = one
    qkv_ref[...] = low(dot(one, qkv_w[...]) + qkv_b[...])


def front(rows, gain, shift, qkv_w, qkv_b):
    count, tile = rows.shape[0], 256
    whole = lambda i: (0, 0)
    block = lambda i: (i, 0)
    return pl.pallas_call(
        front_kernel,
        grid=(count // tile,),
        in_specs=[
            pl.BlockSpec((tile, D), block),
            pl.BlockSpec((1, D), whole),
            pl.BlockSpec((1, D), whole),
            pl.BlockSpec(qkv_w.shape, whole),
            pl.BlockSpec((1, qkv_w.shape[1]), whole),
        ],
        out_specs=[pl.BlockSpec((tile, D), block), pl.BlockSpec((tile, qkv_w.shape[1]), block)],
        out_shape=(
            jax.ShapeDtypeStruct((count, D), jnp.bfloat16),
            jax.ShapeDtypeStruct((count, qkv_w.shape[1]), jnp.bfloat16),
        ),
        compiler_params=pltpu.CompilerParams(vmem_limit_bytes=58 * 2**20),
        cost_estimate=LITTLE,
    )(rows, gain[None], shift[None], qkv_w, qkv_b[None])


def feed_kernel(x_ref, w_ref, b_ref, ga_ref, act_ref, pre_ref, in_ref, sum_ref):
    v = dot(x_ref[...], w_ref[...]) + b_ref[...]
    square = v * v
    half = 0.5 + 0.5 * jnp.tanh(v * (GELU + GELU * 0.044715 * square))
    act_ref[...] = low(v * half)
    slope = half + (v * half) * (1.0 - half) * (2.0 * GELU + 6.0 * GELU * 0.044715 * square)
    grad = low(ga_ref[...] * slope)
    pre_ref[...] = grad
    in_ref[...] = low(dot_nt(grad, w_ref[...]))

    @pl.when(pl.program_id(0) == 0)
    def _():
        sum_ref[...] = jnp.zeros_like(sum_ref)

    sum_ref[...] += jnp.sum(grad.astype(jnp.float32), axis=0, keepdims=True)


def feed(rows, weight, bias, grad_act):
    count, hidden = grad_act.shape
    tile = 512
    whole = lambda i: (0, 0)
    block = lambda i: (i, 0)
    return pl.pallas_call(
        feed_kernel,
        grid=(count // tile,),
        in_specs=[
            pl.BlockSpec((tile, D), block),
            pl.BlockSpec((D, hidden), whole),
            pl.BlockSpec((1, hidden), whole),
            pl.BlockSpec((tile, hidden), block),
        ],
        out_specs=[
            pl.BlockSpec((tile, hidden), block),
            pl.BlockSpec((tile, hidden), block),
            pl.BlockSpec((tile, D), block),
            pl.BlockSpec((1, hidden), whole),
        ],
        out_shape=(
            jax.ShapeDtypeStruct((count, hidden), jnp.bfloat16),
            jax.ShapeDtypeStruct((count, hidden), jnp.bfloat16),
            jax.ShapeDtypeStruct((count, D), jnp.bfloat16),
            jax.ShapeDtypeStruct((1, hidden), jnp.float32),
        ),
        compiler_params=pltpu.CompilerParams(vmem_limit_bytes=58 * 2**20),
        cost_estimate=LITTLE,
    )(rows, weight, bias[None], grad_act)


def expand_kernel(replica, x_ref, g_ref, *refs):
    keep, outs = refs[-1], refs[:-1]
    size, rows = len(outs), outs[0].shape[1]
    owners = x_ref.shape[1] // (size * rows)
    keep[...] = low(dot_tn(x_ref[...], g_ref[...])).reshape(keep.shape)
    step = pl.program_id(0) * owners
    for owner in range(owners):
        for other, out in enumerate(outs):
            out[pl.ds(step + owner, 1)] = keep[owner, pl.ds(replica[0] ^ other, 1)]


def expand_grads(rows_in, grads, owners, part_rows):
    size, me = lax.axis_size("rep"), lax.axis_index("rep")
    count, hidden = grads.shape
    if part_rows % 16:
        full = low(dot_tn(rows_in, grads)).reshape(owners, size, part_rows, hidden)
        return [lax.dynamic_index_in_dim(full, me ^ step, 1, keepdims=False) for step in range(size)]
    tile = 2
    grid_spec = pltpu.PrefetchScalarGridSpec(
        num_scalar_prefetch=1,
        grid=(owners // tile,),
        in_specs=[
            pl.BlockSpec((count, tile * size * part_rows), lambda i, e: (0, i)),
            pl.BlockSpec((count, hidden), lambda i, e: (0, 0)),
        ],
        out_specs=[pl.BlockSpec((owners, part_rows, hidden), lambda i, e: (0, 0, 0))] * size,
        scratch_shapes=[pltpu.VMEM((tile, size, part_rows, hidden), jnp.bfloat16)],
    )
    return pl.pallas_call(
        expand_kernel,
        grid_spec=grid_spec,
        out_shape=(jax.ShapeDtypeStruct((owners, part_rows, hidden), jnp.bfloat16),) * size,
        compiler_params=pltpu.CompilerParams(vmem_limit_bytes=58 * 2**20),
        cost_estimate=LITTLE,
    )(me[None], rows_in, grads)


def shrink_kernel(replica, a_ref, g_ref, *outs):
    for step, out in enumerate(outs):

        @pl.when(pl.program_id(0) == step)
        def _():
            out[...] = low(dot_tn(a_ref[...], g_ref[...]))


def shrink_grads(act, grads):
    size, me = lax.axis_size("rep"), lax.axis_index("rep")
    count, hidden = act.shape
    part = hidden // size
    if part % 128:
        full = low(dot_tn(act, grads)).reshape(size, part, D)
        return [lax.dynamic_index_in_dim(full, me ^ step, 0, keepdims=False) for step in range(size)]
    grid_spec = pltpu.PrefetchScalarGridSpec(
        num_scalar_prefetch=1,
        grid=(size,),
        in_specs=[
            pl.BlockSpec((count, part), lambda i, e: (0, e[0] ^ i)),
            pl.BlockSpec((count, D), lambda i, e: (0, 0)),
        ],
        out_specs=[pl.BlockSpec((part, D), lambda i, e: (0, 0))] * size,
    )
    return pl.pallas_call(
        shrink_kernel,
        grid_spec=grid_spec,
        out_shape=(jax.ShapeDtypeStruct((part, D), jnp.bfloat16),) * size,
        compiler_params=pltpu.CompilerParams(vmem_limit_bytes=58 * 2**20),
        cost_estimate=LITTLE,
    )(me[None], act, grads)


def product_kernel(a_ref, b_ref, out_ref):
    out_ref[...] = low(dot(a_ref[...], b_ref[...]))


def product(left, right):
    count, depth = left.shape
    tile = 512
    return pl.pallas_call(
        product_kernel,
        grid=(count // tile,),
        in_specs=[pl.BlockSpec((tile, depth), lambda i: (i, 0)), pl.BlockSpec(right.shape, lambda i: (0, 0))],
        out_specs=pl.BlockSpec((tile, right.shape[1]), lambda i: (i, 0)),
        out_shape=jax.ShapeDtypeStruct((count, right.shape[1]), jnp.bfloat16),
        compiler_params=pltpu.CompilerParams(vmem_limit_bytes=58 * 2**20),
        cost_estimate=LITTLE,
    )(left, right)


def back_kernel(g_ref, w_ref, one_ref, out_ref, sum_ref, own_ref):
    @pl.when(pl.program_id(0) == 0)
    def _():
        sum_ref[...] = jnp.zeros_like(sum_ref)
        own_ref[...] = jnp.zeros_like(own_ref)

    grads = dot_nt(g_ref[...], w_ref[...])
    out_ref[...] = low(grads)
    sum_ref[0:1, :] += jnp.sum(grads * one_ref[...].astype(jnp.float32), axis=0, keepdims=True)
    sum_ref[1:2, :] += jnp.sum(grads, axis=0, keepdims=True)
    own_ref[...] += jnp.sum(g_ref[...].astype(jnp.float32), axis=0, keepdims=True)


def back(grads, weight, rows_in):
    count, width = grads.shape
    tile = 256
    return pl.pallas_call(
        back_kernel,
        grid=(count // tile,),
        in_specs=[
            pl.BlockSpec((tile, width), lambda i: (i, 0)),
            pl.BlockSpec(weight.shape, lambda i: (0, 0)),
            pl.BlockSpec((tile, D), lambda i: (i, 0)),
        ],
        out_specs=[
            pl.BlockSpec((tile, D), lambda i: (i, 0)),
            pl.BlockSpec((2, D), lambda i: (0, 0)),
            pl.BlockSpec((1, width), lambda i: (0, 0)),
        ],
        out_shape=(
            jax.ShapeDtypeStruct((count, D), jnp.bfloat16),
            jax.ShapeDtypeStruct((2, D), jnp.float32),
            jax.ShapeDtypeStruct((1, width), jnp.float32),
        ),
        compiler_params=pltpu.CompilerParams(vmem_limit_bytes=58 * 2**20),
        cost_estimate=LITTLE,
    )(grads, weight, rows_in)


def heads_grads_kernel(x_ref, g_ref, e_ref, m_ref, out_ref):
    width = g_ref.shape[1]
    shape = out_ref.shape[1:3]
    for owner in range(shape[0]):
        place = slice(owner * x_ref.shape[1] // shape[0], (owner + 1) * x_ref.shape[1] // shape[0])
        left = low(dot_tn(x_ref[:, place], g_ref[...]))
        right = low(dot_tn(e_ref[:, place], m_ref[...]))
        for replica in range(out_ref.shape[0]):
            rows = slice(replica * shape[1], (replica + 1) * shape[1])
            out_ref[replica, owner, :, :width] = left[rows, :]
            out_ref[replica, owner, :, width:] = right[rows, :]


def heads_grads(rows_in, grads, enc, enc_grads, owners, part_rows):
    size = lax.axis_size("rep")
    width, enc_width = grads.shape[1], enc_grads.shape[1]
    if part_rows % 16:
        both = low(jnp.concatenate([dot_tn(rows_in, grads), dot_tn(enc, enc_grads)], axis=1))
        return both.reshape(owners, size, part_rows, width + enc_width).transpose(1, 0, 2, 3)
    tile = 2
    return pl.pallas_call(
        heads_grads_kernel,
        grid=(owners // tile,),
        in_specs=[
            pl.BlockSpec((rows_in.shape[0], tile * size * part_rows), lambda i: (0, i)),
            pl.BlockSpec(grads.shape, lambda i: (0, 0)),
            pl.BlockSpec((enc.shape[0], tile * size * part_rows), lambda i: (0, i)),
            pl.BlockSpec(enc_grads.shape, lambda i: (0, 0)),
        ],
        out_specs=pl.BlockSpec((size, tile, part_rows, width + enc_width), lambda i: (0, i, 0, 0)),
        out_shape=jax.ShapeDtypeStruct((size, owners, part_rows, width + enc_width), jnp.bfloat16),
        compiler_params=pltpu.CompilerParams(vmem_limit_bytes=58 * 2**20),
        cost_estimate=LITTLE,
    )(rows_in, grads, enc, enc_grads)


def last_kernel(x_ref, e_ref, one_ref, gain, out_ref):
    rows = x_ref[...].astype(jnp.float32)
    centered = rows - jnp.mean(rows, axis=-1, keepdims=True)
    inverse = lax.rsqrt(jnp.mean(centered * centered, axis=-1, keepdims=True) + EPS)
    x_hat = centered * inverse
    grads = e_ref[...].astype(jnp.float32) * gain[...]
    inner = jnp.mean(grads * x_hat, axis=-1, keepdims=True)
    out_ref[...] = one_ref[...] + inverse * (grads - jnp.mean(grads, axis=-1, keepdims=True) - x_hat * inner)


def last(rows, grads, grad_one, gain):
    count = rows.shape[0]
    tile = 128
    block = pl.BlockSpec((tile, D), lambda i: (i, 0))
    return pl.pallas_call(
        last_kernel,
        grid=(count // tile,),
        in_specs=[block, block, block, pl.BlockSpec((1, D), lambda i: (0, 0))],
        out_specs=block,
        out_shape=jax.ShapeDtypeStruct((count, D), jnp.float32),
        cost_estimate=LITTLE,
    )(rows, grads, grad_one, gain[None])


def rep_send(value, step):
    size = lax.axis_size("rep")
    return lax.ppermute(value, "rep", [(i, i ^ step) for i in range(size)])


def rep_start(value):
    return [value] + [rep_send(value, step) for step in range(1, lax.axis_size("rep"))]


def rep_place(parts, axis):
    size, me = lax.axis_size("rep"), lax.axis_index("rep")
    value = parts[0]
    out = jnp.zeros(value.shape[:axis] + (size,) + value.shape[axis:], value.dtype)
    for step, part in enumerate(parts):
        out = lax.dynamic_update_slice_in_dim(out, jnp.expand_dims(part, axis), me ^ step, axis)
    return out


def spread_kernel(place, *refs):
    out_ref = refs[-1]
    for step, part in enumerate(refs[:-1]):
        out_ref[pl.ds(place[0] ^ step, 1)] = part[...].astype(out_ref.dtype)[None]


def spread(parts, first, last, dtype):
    size, columns = len(parts), parts[0].shape[1]
    rows = last - first
    if rows % 32 or first % rows or parts[0].shape[0] % 16:
        return rep_place([part[first:last] for part in parts], 0).astype(dtype)
    tile = rows // 2
    grid_spec = pltpu.PrefetchScalarGridSpec(
        num_scalar_prefetch=1,
        grid=(2,),
        in_specs=[pl.BlockSpec((tile, columns), lambda i, e: (first // tile + i, 0))] * size,
        out_specs=pl.BlockSpec((size, tile, columns), lambda i, e: (0, i, 0)),
    )
    return pl.pallas_call(
        spread_kernel,
        grid_spec=grid_spec,
        out_shape=jax.ShapeDtypeStruct((size, rows, columns), dtype),
        compiler_params=pltpu.CompilerParams(vmem_limit_bytes=58 * 2**20),
        cost_estimate=LITTLE,
    )(lax.axis_index("rep")[None], *parts)


def rep_gather(value, axis):
    return rep_place(rep_start(value), axis)


def rep_swap(parts):
    return lax.all_to_all(parts, "rep", 0, 0, tiled=True)


def rep_split(parts, axis):
    size, me = lax.axis_size("rep"), lax.axis_index("rep")
    picks = [lax.dynamic_index_in_dim(parts, me ^ step, axis, keepdims=False) for step in range(size)]
    return [picks[0]] + [rep_send(low(picks[step]), step) for step in range(1, size)]


def sum_first(parts):
    return low(jnp.sum(parts.astype(jnp.float32), axis=0))


def add_up(parts):
    total = parts[0].astype(jnp.float32)
    for part in parts[1:]:
        total = total + part.astype(jnp.float32)
    return low(total)


def rep_reduce(parts, axis):
    return add_up(rep_split(parts, axis))


def core_send(value):
    size = lax.axis_size("shard")
    return lax.ppermute(value, "shard", [(i, i ^ 1) for i in range(size)])


def line_send(value, step, group=None):
    size = lax.axis_size("shard")
    group = group or size
    route = [(i, i // group * group + (i + 2 * step) % group) for i in range(size)]
    return lax.ppermute(value, "shard", route)


def line_scatter_start(value, group=None):
    group = group or lax.axis_size("shard")
    core = lax.axis_index("shard") % 2
    value = value.reshape((group // 2, 2, value.shape[0] // group) + value.shape[1:])
    mine = lax.dynamic_index_in_dim(value, core, 1, keepdims=False)
    theirs = lax.dynamic_index_in_dim(value, 1 - core, 1, keepdims=False)
    return [mine, core_send(theirs)]


def line_scatter_middle(both, group=None):
    group = group or lax.axis_size("shard")
    chips = group // 2
    chip = lax.axis_index("shard") % group // 2
    line = add_up(both)
    parts = [lax.dynamic_index_in_dim(line, (chip + step) % chips, 0, keepdims=False) for step in range(chips)]
    return [parts[0]] + [line_send(parts[step], step, group) for step in range(1, chips)]


def kinds_kernel(place, *refs):
    outs = refs[-3:]
    rows = outs[0].shape[1]
    for step, part in enumerate(refs[:-3]):
        for kind, out in enumerate(outs):
            out[pl.ds(place[0] ^ step, 1)] = part[kind * rows : (kind + 1) * rows, :].astype(out.dtype)[None]


def spread_kinds(parts, rows):
    size = len(parts)
    if rows % 16:
        return [rep_place([part[k * rows : (k + 1) * rows] for part in parts], 0).astype(jnp.float32) for k in range(3)]
    whole = lambda i, e: (0, 0)
    grid_spec = pltpu.PrefetchScalarGridSpec(
        num_scalar_prefetch=1,
        grid=(1,),
        in_specs=[pl.BlockSpec(parts[0].shape, whole)] * size,
        out_specs=[pl.BlockSpec((size, rows, D), lambda i, e: (0, 0, 0))] * 3,
    )
    return pl.pallas_call(
        kinds_kernel,
        grid_spec=grid_spec,
        out_shape=(jax.ShapeDtypeStruct((size, rows, D), jnp.float32),) * 3,
        cost_estimate=LITTLE,
    )(lax.axis_index("rep")[None], *parts)


def columns_kernel(place, *refs):
    out_ref = refs[-1]
    rows = out_ref.shape[1]
    for step, part in enumerate(refs[:-1]):
        for block in range(part.shape[0] // rows):
            wide = part[block * rows : (block + 1) * rows, :].astype(out_ref.dtype)
            out_ref[pl.ds(place[0] ^ step, 1), :, block * D : (block + 1) * D] = wide[None]


def spread_columns(parts, first, blocks, rows):
    size, me = len(parts), lax.axis_index("rep")
    if rows % 16:
        parts = [part[first:].reshape(blocks, rows, -1).transpose(1, 0, 2).reshape(rows, -1) for part in parts]
        return rep_place(parts, 0).astype(jnp.float32).reshape(size * rows, -1)
    halves = 2
    taken = blocks * rows // halves
    grid_spec = pltpu.PrefetchScalarGridSpec(
        num_scalar_prefetch=1,
        grid=(halves,),
        in_specs=[pl.BlockSpec((taken, D), lambda i, e: (first // taken + i, 0))] * size,
        out_specs=pl.BlockSpec((size, rows, blocks * D // halves), lambda i, e: (0, 0, i)),
    )
    out = pl.pallas_call(
        columns_kernel,
        grid_spec=grid_spec,
        out_shape=jax.ShapeDtypeStruct((size, rows, blocks * D), jnp.float32),
        compiler_params=pltpu.CompilerParams(vmem_limit_bytes=58 * 2**20),
        cost_estimate=LITTLE,
    )(me[None], *parts)
    return out.reshape(size * rows, blocks * D)


def heads_kernel(span, place, *refs):
    qkv_ref, memory_ref = refs[-2:]
    rows, width = qkv_ref.shape[1], D // span
    for step, part in enumerate(refs[:-2]):
        take = pl.ds(place[0] ^ step, 1)
        for block in range(span):
            wide = part[block * rows : (block + 1) * rows, :].astype(jnp.float32)[None]
            for kind in range(5):
                out, at = (qkv_ref, kind) if kind < 3 else (memory_ref, kind - 3)
                columns = slice(at * D + block * width, at * D + (block + 1) * width)
                out[take, :, columns] = wide[:, :, kind * width : (kind + 1) * width]


def spread_heads(parts, span, rows, width):
    size, me = len(parts), lax.axis_index("rep")
    if rows % 16:
        full = rep_place([part[: span * rows].reshape(span, rows, 5, width) for part in parts], 0)
        full = full.transpose(0, 2, 3, 1, 4).reshape(size * rows, 5 * D).astype(jnp.float32)
        return full[:, : 3 * D], full[:, 3 * D :]
    grid_spec = pltpu.PrefetchScalarGridSpec(
        num_scalar_prefetch=1,
        grid=(1,),
        in_specs=[pl.BlockSpec((span * rows, 5 * width), lambda i, e: (0, 0))] * size,
        out_specs=[
            pl.BlockSpec((size, rows, 3 * D), lambda i, e: (0, 0, 0)),
            pl.BlockSpec((size, rows, 2 * D), lambda i, e: (0, 0, 0)),
        ],
    )
    qkv, memory = pl.pallas_call(
        functools.partial(heads_kernel, span),
        grid_spec=grid_spec,
        out_shape=(
            jax.ShapeDtypeStruct((size, rows, 3 * D), jnp.float32),
            jax.ShapeDtypeStruct((size, rows, 2 * D), jnp.float32),
        ),
        compiler_params=pltpu.CompilerParams(vmem_limit_bytes=58 * 2**20),
        cost_estimate=LITTLE,
    )(me[None], *parts)
    return qkv.reshape(size * rows, 3 * D), memory.reshape(size * rows, 2 * D)


def line_start(piece):
    return [piece] + [line_send(piece, step) for step in range(1, lax.axis_size("shard") // 2)]


def line_place(parts):
    chips, chip = len(parts), lax.axis_index("shard") // 2
    kinds, rows, columns = parts[0].shape
    line = jnp.zeros((kinds, chips, rows, columns), parts[0].dtype)
    for step, part in enumerate(parts):
        line = lax.dynamic_update_slice_in_dim(line, part[:, None], (chip - step) % chips, 1)
    return line


def join_kernel(place, *refs):
    outs = refs[-3:]
    parts = refs[:-3]
    size = len(parts) // 2
    for core in range(2):
        side = place[1] ^ core
        for step in range(size):
            for kind in range(3):
                outs[kind][0, pl.ds(side, 1), pl.ds(place[0] ^ step, 1)] = parts[core * size + step][kind][None]


def weight_join(mine, other):
    size = len(mine)
    _, chips, rows, _ = mine[0].shape
    core = lax.axis_index("shard") % 2
    if rows % 16:
        first = core == 0
        plane, next_plane = rep_place(mine, 2), rep_place(other, 2)
        low_core, high_core = jnp.where(first, plane, next_plane), jnp.where(first, next_plane, plane)
        full = jnp.stack([low_core, high_core], axis=2).reshape(3, D, D)
        return full[0], full[1], full[2]
    grid_spec = pltpu.PrefetchScalarGridSpec(
        num_scalar_prefetch=1,
        grid=(chips,),
        in_specs=[pl.BlockSpec((3, 1, rows, D), lambda i, e: (0, i, 0, 0))] * (2 * size),
        out_specs=[pl.BlockSpec((1, 2, size, rows, D), lambda i, e: (i, 0, 0, 0, 0))] * 3,
    )
    outs = pl.pallas_call(
        join_kernel,
        grid_spec=grid_spec,
        out_shape=(jax.ShapeDtypeStruct((chips, 2, size, rows, D), jnp.bfloat16),) * 3,
        compiler_params=pltpu.CompilerParams(vmem_limit_bytes=58 * 2**20),
        cost_estimate=LITTLE,
    )(jnp.stack([lax.axis_index("rep"), core]), *mine, *other)
    return tuple(out.reshape(D, D) for out in outs)


def plain_kernel(core, a_ref, b_ref, c_ref, ga_ref, gb_ref, gc_ref, mine_ref, theirs_ref):
    width = a_ref.shape[1] // 2
    for kind, (left, right) in enumerate(((a_ref, ga_ref), (b_ref, gb_ref), (c_ref, gc_ref))):
        for side, out in enumerate((mine_ref, theirs_ref)):
            place = pl.ds(pl.multiple_of((core[0] ^ side) * width, width), width)
            out[kind, 0] = low(dot_tn(left[:, place], right[...])).reshape(out.shape[2:])


def plain_grads(lefts, rights):
    size, chips = lax.axis_size("rep"), lax.axis_size("shard") // 2
    core = lax.axis_index("shard") % 2
    rows = D // (2 * chips * size)
    if rows % 16:
        stack = jnp.stack([low(dot_tn(left, right)) for left, right in zip(lefts, rights)])
        stack = stack.reshape(3, chips, 2, size, rows, D)
        return [lax.dynamic_index_in_dim(stack, core ^ side, 2, keepdims=False) for side in range(2)]
    count = lefts[0].shape[0]
    grid_spec = pltpu.PrefetchScalarGridSpec(
        num_scalar_prefetch=1,
        grid=(chips,),
        in_specs=[pl.BlockSpec((count, D // chips), lambda i, e: (0, i))] * 3
        + [pl.BlockSpec((count, D), lambda i, e: (0, 0))] * 3,
        out_specs=[pl.BlockSpec((3, 1, size, rows, D), lambda i, e: (0, i, 0, 0, 0))] * 2,
    )
    return pl.pallas_call(
        plain_kernel,
        grid_spec=grid_spec,
        out_shape=(jax.ShapeDtypeStruct((3, chips, size, rows, D), jnp.bfloat16),) * 2,
        compiler_params=pltpu.CompilerParams(vmem_limit_bytes=58 * 2**20),
        cost_estimate=pl.CostEstimate(flops=6 * count * D * D, bytes_accessed=20 * count * D, transcendentals=0),
    )(core[None], *lefts, *rights)


def split_kernel(place, mine_ref, other_ref, *outs):
    for step, out in enumerate(outs):
        take = pl.ds(place[0] ^ step, 1)
        total = mine_ref[:, 0, take].astype(jnp.float32) + other_ref[:, 0, take].astype(jnp.float32)
        out[...] = low(total)


def core_sum_split(mine, other):
    kinds, chips, size, rows, _ = mine.shape
    if rows % 16:
        total = add_up([mine, other])
        me = lax.axis_index("rep")
        return [lax.dynamic_index_in_dim(total, me ^ step, 2, keepdims=False) for step in range(size)]
    grid_spec = pltpu.PrefetchScalarGridSpec(
        num_scalar_prefetch=1,
        grid=(chips,),
        in_specs=[pl.BlockSpec((kinds, 1, size, rows, D), lambda i, e: (0, i, 0, 0, 0))] * 2,
        out_specs=[pl.BlockSpec((kinds, 1, rows, D), lambda i, e: (0, i, 0, 0))] * size,
    )
    return pl.pallas_call(
        split_kernel,
        grid_spec=grid_spec,
        out_shape=(jax.ShapeDtypeStruct((kinds, chips, rows, D), jnp.bfloat16),) * size,
        compiler_params=pltpu.CompilerParams(vmem_limit_bytes=58 * 2**20),
        cost_estimate=LITTLE,
    )(lax.axis_index("rep")[None], mine, other)


def reduce_line(line):
    chips = lax.axis_size("shard") // 2
    chip = lax.axis_index("shard") // 2
    parts = [lax.dynamic_index_in_dim(line, (chip + step) % chips, 1, keepdims=False) for step in range(chips)]
    return [parts[0]] + [line_send(parts[step], step) for step in range(1, chips)]


def shards(
    tokens,
    segments,
    enc_states,
    enc_lengths,
    cotangent,
    self_qkv,
    self_out,
    cross_query,
    cross_memory,
    cross_out,
    expand_weight,
    shrink_weight,
    norm_gain,
    norm_bias,
    proj_bias,
    expand_bias,
):
    row_count, enc_rows = tokens.shape[0], enc_states.shape[0]
    span = SEQ // row_count
    width = D // span
    count = lax.axis_size("shard")
    size = lax.axis_size("rep")
    rep_pos = lax.axis_index("rep")
    shard_pos = lax.axis_index("shard")
    local_pos = shard_pos % span
    local_seq = shard_pos // span
    groups = None
    if count != span:
        groups = [[g * span + i for i in range(span)] for g in range(count // span)]
    weight_rows = self_qkv.shape[0]
    part_rows = weight_rows // size
    hidden = expand_bias.shape[0]
    shard_width = norm_gain.shape[1]

    def gather(value, groups=None):
        return lax.all_gather(value, "shard", axis=0, tiled=True, axis_index_groups=groups)

    def scatter(value, groups=None):
        return lax.psum_scatter(value, "shard", scatter_dimension=0, tiled=True, axis_index_groups=groups)

    def swap(value):
        return lax.all_to_all(value, "shard", 0, 0, tiled=True)

    def own_part(weight):
        return lax.dynamic_slice_in_dim(weight, rep_pos * part_rows, part_rows, axis=0)

    def by_pairs(weight, kinds):
        blocks = weight.reshape(part_rows, kinds, span, width).transpose(2, 0, 1, 3)
        return blocks.reshape(span, part_rows, kinds * width)

    blocks = jnp.concatenate([by_pairs(own_part(self_qkv), 3), by_pairs(own_part(cross_memory), 2)], axis=2)
    blocks = jnp.tile(blocks, (count // span, 1, 1))
    small = jnp.concatenate([norm_gain, norm_bias, proj_bias], axis=0)
    small_count = small.shape[0]
    small_rows = -(-small.size // (5 * width))
    small = jnp.pad(small.reshape(-1), (0, small_rows * 5 * width - small.size)).reshape(small_rows, 5 * width)
    blocks = jnp.concatenate([blocks, jnp.broadcast_to(small, (count,) + small.shape)], axis=1)
    swapped = swap(blocks)
    plain_parts = line_start(jnp.stack([own_part(self_out), own_part(cross_query), own_part(cross_out)]))
    enc_all = gather(enc_states, groups)
    swapped, plain_parts, enc_all = lax.optimization_barrier((swapped, plain_parts, enc_all))
    rows_all = gather(after(tokens, plain_parts, enc_all), groups)
    small_all = swapped[:, part_rows:].reshape(count, small_rows * 5 * width)[:, : small_count * shard_width]
    small_all = small_all.reshape(count, small_count, shard_width)
    small_all = small_all.transpose(1, 0, 2).reshape(small_count, D).astype(jnp.float32)
    gain_rows, shift_rows, bias_rows = small_all[:3], small_all[3:6], small_all[6:]
    head_weight = rep_gather(swapped[:, :part_rows], 1).reshape(D, 5 * width)
    qkv_weight, memory_weight = head_weight[:, : 3 * width], head_weight[:, 3 * width :]
    qkv_weight, memory_weight = head_weight[:, : 3 * width], head_weight[:, 3 * width :]
    own_bias = lax.dynamic_slice_in_dim(bias_rows, local_pos * width, width, axis=1)
    zero_bias = jnp.zeros((width,), jnp.float32)
    memory_pair = low(dot(enc_all, memory_weight) + jnp.concatenate([zero_bias, own_bias[4]]))
    plain_mine = rep_start(line_place(after(plain_parts, head_weight)))
    rows_all, qkv_weight, memory_weight, plain_mine[1], plain_mine[2] = lax.optimization_barrier(
        (rows_all, qkv_weight, memory_weight, plain_mine[1], plain_mine[2])
    )
    memory_all = gather(after(memory_pair, rows_all), groups)
    expand_part = own_part(after(expand_weight, rows_all)).reshape(part_rows, count, hidden).transpose(1, 0, 2)
    expand_swapped = swap(expand_part)

    seq_segments = lax.dynamic_slice_in_dim(segments, local_seq * SEQ, SEQ)
    qkv_bias = jnp.concatenate([own_bias[0], zero_bias, own_bias[1]])
    input_one_all, qkv = front(rows_all, gain_rows[0], shift_rows[0], qkv_weight, qkv_bias)
    att_low, att_full, lse = self_forward(qkv, seq_segments)
    att_low, memory_all, plain_mine, expand_swapped = lax.optimization_barrier(
        (att_low, memory_all, plain_mine, expand_swapped)
    )
    grad_all = gather(after(cotangent, memory_all))
    plain_other = [core_send(part) for part in plain_mine]
    attn_proj, query_in, cross_proj = weight_join(plain_mine, plain_other)
    attended = lax.all_to_all(att_low, "shard", 0, 1, tiled=True, axis_index_groups=groups)

    enc_count = lax.dynamic_slice_in_dim(enc_lengths, local_seq, 1)

    residual_in = tokens.astype(jnp.float32)
    hidden_one = residual_in + dot(attended, attn_proj) + bias_rows[2]
    input_two = low(norm_apply(hidden_one, gain_rows[1], shift_rows[1]))
    cross_q = low(dot(input_two, query_in) + bias_rows[3])
    context = cross_forward(cross_q, memory_all, enc_count)
    hidden_two = hidden_one + dot(context, cross_proj) + bias_rows[5]
    input_three = low(norm_apply(hidden_two, gain_rows[2], shift_rows[2]))

    input_three_all = gather(input_three)
    expand_parts = rep_start(expand_swapped.reshape(count * part_rows, hidden))
    grad_all_now = after(grad_all, input_three)
    expand_local = spread(expand_parts, 0, count * part_rows, jnp.bfloat16)
    expand_local = expand_local.reshape(size, count, part_rows, hidden).transpose(1, 0, 2, 3).reshape(D, hidden)
    grad_act = dot_nt(grad_all_now, shrink_weight)
    input_three_all, grad_act, expand_local = lax.optimization_barrier((input_three_all, grad_act, expand_local))
    act, grad_pre, grad_in_three_low, hidden_sums = feed(
        input_three_all, expand_local, expand_bias.astype(jnp.float32), grad_act
    )
    grad_hidden_bias = hidden_sums[0]
    grad_in_three = scatter(grad_in_three_low)

    part_hidden = hidden // size

    def send_parts(parts):
        return [parts[0]] + [rep_send(parts[step], step) for step in range(1, size)]

    rows_late, grad_pre_late = after((input_three_all, grad_pre), grad_in_three_low)
    expand_grad_parts = expand_grads(rows_late, grad_pre_late, count, part_rows)
    shrink_parts = send_parts(shrink_grads(after(act, expand_grad_parts[0]), grad_all))
    expand_grad_parts = send_parts(expand_grad_parts)
    result_part = product(after(act, shrink_parts[0]), shrink_weight)
    expand_sum = add_up(expand_grad_parts)
    own_expand = swap(expand_sum)
    grad_in_three, shrink_parts[0], result_part = lax.optimization_barrier(
        (grad_in_three, shrink_parts[0], result_part)
    )
    result_sum = scatter(result_part)
    grad_in_three = grad_in_three.astype(jnp.float32)

    grad_out = cotangent.astype(jnp.float32)
    norm_three = jax.vjp(norm_apply, hidden_two, gain_rows[2], shift_rows[2])[1](grad_in_three)
    grad_two = grad_out + norm_three[0]
    grad_two_low = low(grad_two)
    grad_context = low(dot_nt(grad_two_low, cross_proj))
    grad_context, own_expand = lax.optimization_barrier((grad_context, own_expand))
    grad_cross_q, memory_part = cross_backward(cross_q, memory_all, grad_context, enc_count)
    grad_cross_q, memory_part, shrink_parts = lax.optimization_barrier((grad_cross_q, memory_part, shrink_parts))
    mem_grads = scatter(memory_part, groups)
    grad_in_two = dot_nt(grad_cross_q, query_in)
    norm_two = jax.vjp(norm_apply, hidden_one, gain_rows[1], shift_rows[1])[1](grad_in_two)
    grad_one = grad_two + norm_two[0]
    grad_one_low = low(grad_one)
    grad_attn = low(dot_nt(grad_one_low, attn_proj))
    shrink_sum = add_up(shrink_parts)
    own_expand = own_expand.reshape(part_hidden, D)
    own_feed = jnp.concatenate([shrink_sum, own_expand], axis=0)
    grad_attn, own_feed = lax.optimization_barrier((grad_attn, own_feed))
    grad_att_heads = lax.all_to_all(grad_attn, "shard", 1, 0, tiled=True, axis_index_groups=groups)

    lefts, rights = after(((attended, input_two, context), (grad_one_low, grad_cross_q, grad_two_low)), grad_attn)
    plain_own, plain_theirs = plain_grads(lefts, rights)
    plain_theirs = core_send(plain_theirs)
    grad_att_heads, plain_own = lax.optimization_barrier((grad_att_heads, plain_own))

    feed_gather = rep_start(own_feed)
    grad_qkv = self_backward(qkv, grad_att_heads, lse, att_full, seq_segments)
    heads_parts = heads_grads(input_one_all, grad_qkv, enc_all, mem_grads, count, part_rows)
    heads_swapped = rep_swap(heads_parts)
    grad_in_one_low, one_sums, qkv_sums = back(after(grad_qkv, heads_parts, feed_gather), qkv_weight, input_one_all)
    plain_rep = send_parts(core_sum_split(*after((plain_own, plain_theirs), heads_parts)))
    grad_in_one_low, heads_swapped, plain_rep[0] = lax.optimization_barrier(
        (grad_in_one_low, heads_swapped, plain_rep[0])
    )
    grad_in_one = scatter(grad_in_one_low, groups)

    mem_grads_late = after(mem_grads, grad_in_one_low)
    qkv_sums = qkv_sums[0]
    gain_shift = [(one_sums[0] - shift_rows[0] * one_sums[1]) / gain_rows[0], one_sums[1]]
    zero_row = jnp.zeros((D,), jnp.float32)

    def at_own(values):
        return lax.dynamic_update_slice_in_dim(zero_row, values, local_pos * width, 0)

    small_grads = jnp.stack(
        [
            gain_shift[0],
            norm_two[1],
            norm_three[1],
            gain_shift[1],
            norm_two[2],
            norm_three[2],
            at_own(qkv_sums[:width]),
            at_own(qkv_sums[2 * width :]),
            column_sums(grad_one_low),
            column_sums(grad_cross_q),
            at_own(column_sums(mem_grads_late)[width:]),
            column_sums(grad_two_low),
            column_sums(cotangent),
        ]
    )
    small_grads = small_grads.reshape(small_count, count, shard_width).transpose(1, 0, 2)
    small_grads = small_grads.reshape(count, small_count * shard_width)
    hidden_grads = jnp.zeros((count, hidden), jnp.float32)
    hidden_grads = lax.dynamic_update_slice_in_dim(hidden_grads, grad_hidden_bias[None], shard_pos, 0)
    small_grads = low(jnp.concatenate([small_grads, hidden_grads], axis=1))
    small_size = small_grads.shape[1]
    extra = -(-small_size // (5 * width))
    small_grads = jnp.pad(small_grads, ((0, 0), (0, extra * 5 * width - small_size)))
    small_grads = small_grads.reshape(count, extra, 5 * width)
    heads_sum = sum_first(after(heads_swapped, grad_in_one_low))
    own_heads = swap(jnp.concatenate([heads_sum, small_grads], axis=1))
    own_small = sum_first(own_heads[:, part_rows:])
    own_heads = own_heads[:, :part_rows].reshape(count // span, span, part_rows, 5 * width)
    own_heads = own_heads[0] if count == span else sum_first(own_heads)
    heads_gather = rep_start(jnp.concatenate([own_heads.reshape(span * part_rows, 5 * width), own_small], axis=0))

    plain_line_parts = reduce_line(add_up(after(plain_rep, own_heads)))
    own_plain = add_up(plain_line_parts).reshape(3 * part_rows, D)
    plain_gather = rep_start(own_plain)
    enc_parts = line_scatter_start(low(dot_nt(mem_grads_late, memory_weight)), span)
    grad_enc = add_up(line_scatter_middle(enc_parts, span)).astype(jnp.float32)
    result = hidden_two + after(result_sum, grad_in_one_low).astype(jnp.float32) + bias_rows[6]

    total_shrink = spread(feed_gather, 0, part_hidden, jnp.float32)
    total_expand = spread_columns(feed_gather, part_hidden, count, part_rows)
    total_small = sum(part[span * part_rows :].astype(jnp.float32) for part in heads_gather)
    total_small = total_small.reshape(-1)[:small_size]
    total_hidden_bias = total_small[small_count * shard_width :]
    total_small = total_small[: small_count * shard_width].reshape(small_count, shard_width)
    total_qkv, total_memory = spread_heads(heads_gather, span, part_rows, width)

    grad_tokens = last(tokens, grad_in_one, grad_one, gain_rows[0])
    plain_gather = after(plain_gather, grad_tokens, result)
    total_proj, total_query, total_cross = [part.reshape(weight_rows, D) for part in spread_kinds(plain_gather, part_rows)]

    return (
        low(result),
        grad_tokens,
        grad_enc,
        total_qkv,
        total_proj,
        total_query,
        total_memory,
        total_cross,
        total_expand.reshape(weight_rows, count * hidden).astype(jnp.float32),
        total_shrink.reshape(hidden, D).astype(jnp.float32),
        total_small[:3],
        total_small[3:6],
        total_small[6:],
        total_hidden_bias,
    )


def solution(mesh):
    return jax.shard_map(
        shards,
        mesh=mesh,
        in_specs=(
            P(("rep", "shard"), None),
            P("rep"),
            P(("rep", "shard"), None),
            P("rep"),
            P(("rep", "shard"), None),
            P("shard", None),
            P("shard", None),
            P("shard", None),
            P("shard", None),
            P("shard", None),
            P("shard", None),
            P("shard", None),
            P(None, "shard"),
            P(None, "shard"),
            P(None, "shard"),
            P("shard"),
        ),
        out_specs=(
            P(("rep", "shard"), None),
            P(("rep", "shard"), None),
            P(("rep", "shard"), None),
            P("shard", None),
            P("shard", None),
            P("shard", None),
            P("shard", None),
            P("shard", None),
            P("shard", None),
            P("shard", None),
            P(None, "shard"),
            P(None, "shard"),
            P(None, "shard"),
            P("shard"),
        ),
        check_vma=False,
    )
```

```python
import functools

import jax
import jax.numpy as jnp
from jax import lax
from jax.experimental import pallas as pl
from jax.experimental.pallas import tpu as pltpu
from jax.sharding import PartitionSpec as P

D = 1024
H = 16
HD = 64
SEQ = 2048
PAIR = 2 * HD

EPS = 1e-05
NEGATIVE = -1e30
SCALE = HD**-0.5
BLOCK = 512
GELU = 0.7978845608028654
LITTLE = pl.CostEstimate(flops=1000, bytes_accessed=1000, transcendentals=0)


def norm_apply(rows, gain, shift):
    mean_rows = jnp.mean(rows, axis=-1, keepdims=True)
    centered = rows - mean_rows
    inverse = lax.rsqrt(jnp.mean(centered * centered, axis=-1, keepdims=True) + EPS)
    return centered * inverse * gain + shift


def gelu_apply(values):
    return jax.nn.gelu(values, approximate=True)


def column_sums(rows):
    return jnp.sum(rows, axis=0, dtype=jnp.float32)


def low(values):
    return values.astype(jnp.bfloat16)


def dot(left, right):
    return jnp.dot(left, right, preferred_element_type=jnp.float32)


def dot_nt(left, right):
    return lax.dot_general(left, right, (((1,), (1,)), ((), ())), preferred_element_type=jnp.float32)


def dot_tn(left, right):
    return lax.dot_general(left, right, (((0,), (0,)), ((), ())), preferred_element_type=jnp.float32)


def after(value, *earlier):
    return lax.optimization_barrier((value, earlier))[0]


def head_halves(rows, scale=None):
    lane = lax.broadcasted_iota(jnp.int32, rows.shape, 1)
    if scale is not None:
        rows = rows * jnp.asarray(scale, rows.dtype)
    zero = jnp.zeros_like(rows)
    return jnp.where(lane < HD, rows, zero), jnp.where(lane < HD, zero, rows)


def self_forward_kernel(ends, q_ref, k_ref, v_ref, seg_col, seg_row, low_ref, full_ref, lse_ref):
    step = pl.program_id(0)
    rows = q_ref.shape[0]
    queries = head_halves(q_ref[...], SCALE)
    query_seg = seg_row[...]
    last_seg = ends[1, step]

    def piece(index, state, masked, diagonal):
        place = pl.ds(pl.multiple_of(index * rows, rows), rows)
        keys = k_ref[place, :]
        values = v_ref[place, :]
        keep = None
        if masked:
            keep = seg_col[place, :] == query_seg
            if diagonal:
                key_pos = lax.broadcasted_iota(jnp.int32, (rows, rows), 0)
                query_pos = lax.broadcasted_iota(jnp.int32, (rows, rows), 1)
                keep = keep & (key_pos <= query_pos)
        after_piece = []
        for head in range(2):
            top, total, acc = state[head]
            scores = dot_nt(keys, queries[head])
            if masked:
                scores = jnp.where(keep, scores, NEGATIVE)
            top_new = jnp.maximum(top, jnp.max(scores, axis=0, keepdims=True))
            expo = jnp.exp(scores - top_new)
            fade = jnp.exp(top - top_new)
            after_piece.append(
                (
                    top_new,
                    total * fade + jnp.sum(expo, axis=0, keepdims=True),
                    acc * fade + dot_tn(values, low(expo)),
                )
            )
        return tuple(after_piece)

    def before(index, state):
        return lax.cond(
            ends[0, index] == last_seg,
            lambda s: piece(index, s, False, False),
            lambda s: piece(index, s, True, False),
            state,
        )

    blank = (
        jnp.full((1, rows), NEGATIVE, jnp.float32),
        jnp.zeros((1, rows), jnp.float32),
        jnp.zeros((PAIR, rows), jnp.float32),
    )
    state = lax.fori_loop(0, step, before, (blank, blank))
    state = piece(step, state, True, True)
    parts = [
        (state[head][2] * (1.0 / state[head][1]))[head * HD : (head + 1) * HD] for head in range(2)
    ]
    joined = jnp.concatenate(parts, axis=0).T
    full_ref[...] = joined
    low_ref[...] = low(joined)
    lse_ref[0:1, :] = state[0][0] + jnp.log(state[0][1])
    lse_ref[1:2, :] = state[1][0] + jnp.log(state[1][1])


def block_ends(segments, rows):
    return jnp.stack([segments[::rows], segments[rows - 1 :: rows]])


def self_forward(qkv, segments):
    count = qkv.shape[0]
    rows = BLOCK
    col = segments[:, None]
    row = segments[None, :]
    grid_spec = pltpu.PrefetchScalarGridSpec(
        num_scalar_prefetch=1,
        grid=(count // rows,),
        in_specs=[
            pl.BlockSpec((rows, PAIR), lambda i, e: (i, 0)),
            pl.BlockSpec((count, PAIR), lambda i, e: (0, 1)),
            pl.BlockSpec((count, PAIR), lambda i, e: (0, 2)),
            pl.BlockSpec((count, 1), lambda i, e: (0, 0)),
            pl.BlockSpec((1, rows), lambda i, e: (0, i)),
        ],
        out_specs=[
            pl.BlockSpec((rows, PAIR), lambda i, e: (i, 0)),
            pl.BlockSpec((rows, PAIR), lambda i, e: (i, 0)),
            pl.BlockSpec((2, rows), lambda i, e: (0, i)),
        ],
    )
    return pl.pallas_call(
        self_forward_kernel,
        grid_spec=grid_spec,
        out_shape=(
            jax.ShapeDtypeStruct((count, PAIR), jnp.bfloat16),
            jax.ShapeDtypeStruct((count, PAIR), jnp.float32),
            jax.ShapeDtypeStruct((2, count), jnp.float32),
        ),
        compiler_params=pltpu.CompilerParams(vmem_limit_bytes=58 * 2**20),
        cost_estimate=LITTLE,
    )(block_ends(segments, rows), qkv, qkv, qkv, col, row)


def self_backward_kernel(
    ends, q_ref, k_ref, v_ref, go_ref, lse_ref, o_ref, seg_col, seg_row, grad_ref, acc_q, acc_k, acc_v, delta_ref
):
    step = pl.program_id(0)
    blocks = pl.num_programs(0)
    rows = k_ref.shape[0]

    @pl.when(step == 0)
    def _():
        acc_q[...] = jnp.zeros_like(acc_q)
        lane = lax.broadcasted_iota(jnp.int32, (8, PAIR), 1) // HD
        pick = (lane == lax.broadcasted_iota(jnp.int32, (8, PAIR), 0)).astype(jnp.float32)
        delta_ref[...] = lax.dot_general(
            pick,
            go_ref[...].astype(jnp.float32) * o_ref[...],
            (((1,), (1,)), ((), ())),
            precision=lax.Precision.HIGHEST,
            preferred_element_type=jnp.float32,
        )

    keys = k_ref[...]
    values = v_ref[...]
    key_halves = head_halves(keys, SCALE)
    key_seg = seg_col[...]
    first_seg = ends[0, step]

    def piece(index, masked, diagonal):
        place = pl.ds(pl.multiple_of(index * rows, rows), rows)
        queries = head_halves(q_ref[place, :], SCALE)
        grads = head_halves(go_ref[place, :])
        keep = None
        if masked:
            keep = seg_row[:, place] == key_seg
            if diagonal:
                key_pos = lax.broadcasted_iota(jnp.int32, (rows, rows), 0)
                query_pos = lax.broadcasted_iota(jnp.int32, (rows, rows), 1)
                keep = keep & (key_pos <= query_pos)
        sum_q = sum_k = sum_v = None
        for head in range(2):
            scores = dot_nt(keys, queries[head])
            probs = jnp.exp(scores - lse_ref[head : head + 1, place])
            if masked:
                probs = jnp.where(keep, probs, 0.0)
            part_v = dot(low(probs), grads[head])
            grad_probs = dot_nt(values, grads[head])
            grad_scores = low(probs * (grad_probs - delta_ref[head : head + 1, place]))
            part_k = dot(grad_scores, queries[head])
            part_q = dot_tn(key_halves[head], grad_scores)
            sum_q = part_q if sum_q is None else sum_q + part_q
            sum_k = part_k if sum_k is None else sum_k + part_k
            sum_v = part_v if sum_v is None else sum_v + part_v
        acc_q[:, place] += sum_q
        if diagonal:
            acc_k[...] = sum_k
            acc_v[...] = sum_v
        else:
            acc_k[...] += sum_k
            acc_v[...] += sum_v

    piece(step, True, True)

    @pl.loop(step + 1, blocks)
    def _(index):
        whole = ends[1, index] == first_seg

        @pl.when(whole)
        def _():
            piece(index, False, False)

        @pl.when(jnp.logical_not(whole))
        def _():
            piece(index, True, False)

    own = pl.ds(pl.multiple_of(step * rows, rows), rows)
    grad_ref[own, 0:PAIR] = low(acc_q[:, own].T)
    grad_ref[own, PAIR : 2 * PAIR] = low(acc_k[...])
    grad_ref[own, 2 * PAIR : 3 * PAIR] = low(acc_v[...])


def self_backward(qkv, grad_att, lse, attended, segments):
    count = qkv.shape[0]
    rows = BLOCK
    col = segments[:, None]
    row = segments[None, :]
    whole = lambda i, e: (0, 0)
    grid_spec = pltpu.PrefetchScalarGridSpec(
        num_scalar_prefetch=1,
        grid=(count // rows,),
        in_specs=[
            pl.BlockSpec((count, PAIR), whole),
            pl.BlockSpec((rows, PAIR), lambda i, e: (i, 1)),
            pl.BlockSpec((rows, PAIR), lambda i, e: (i, 2)),
            pl.BlockSpec((count, PAIR), whole),
            pl.BlockSpec((2, count), whole),
            pl.BlockSpec((count, PAIR), whole),
            pl.BlockSpec((rows, 1), lambda i, e: (i, 0)),
            pl.BlockSpec((1, count), whole),
        ],
        out_specs=pl.BlockSpec((count, 3 * PAIR), whole),
        scratch_shapes=[
            pltpu.VMEM((PAIR, count), jnp.float32),
            pltpu.VMEM((rows, PAIR), jnp.float32),
            pltpu.VMEM((rows, PAIR), jnp.float32),
            pltpu.VMEM((8, count), jnp.float32),
        ],
    )
    return pl.pallas_call(
        self_backward_kernel,
        grid_spec=grid_spec,
        out_shape=jax.ShapeDtypeStruct((count, 3 * PAIR), jnp.bfloat16),
        compiler_params=pltpu.CompilerParams(vmem_limit_bytes=58 * 2**20),
        cost_estimate=pl.CostEstimate(flops=16 * 10**9, bytes_accessed=4 * 2**20, transcendentals=0),
    )(block_ends(segments, rows), qkv, qkv, qkv, grad_att, lse, attended, col, row)


def cross_forward_kernel(length, q_ref, m_ref, out_ref):
    queries = head_halves(q_ref[...], SCALE)
    keys = m_ref[:, :PAIR]
    values = m_ref[:, PAIR:]
    shape = (q_ref.shape[0], m_ref.shape[0])
    keep = lax.broadcasted_iota(jnp.int32, shape, 1) < length[0]
    parts = []
    for head in range(2):
        scores = jnp.where(keep, dot_nt(queries[head], keys), NEGATIVE)
        expo = jnp.exp(scores - jnp.max(scores, axis=1, keepdims=True))
        parts.append(dot(low(expo), values) / jnp.sum(expo, axis=1, keepdims=True))
    lane = lax.broadcasted_iota(jnp.int32, parts[0].shape, 1)
    out_ref[...] = low(jnp.where(lane < HD, parts[0], parts[1]))


def cross_forward(queries, memory, length):
    count, states = queries.shape[0], memory.shape[0] // (D // PAIR)
    grid_spec = pltpu.PrefetchScalarGridSpec(
        num_scalar_prefetch=1,
        grid=(D // PAIR,),
        in_specs=[
            pl.BlockSpec((count, PAIR), lambda i, e: (0, i)),
            pl.BlockSpec((states, 2 * PAIR), lambda i, e: (i, 0)),
        ],
        out_specs=pl.BlockSpec((count, PAIR), lambda i, e: (0, i)),
    )
    return pl.pallas_call(
        cross_forward_kernel,
        grid_spec=grid_spec,
        out_shape=jax.ShapeDtypeStruct((count, D), jnp.bfloat16),
        cost_estimate=LITTLE,
    )(length, queries, memory)


def cross_backward_kernel(length, q_ref, m_ref, g_ref, dq_ref, dm_ref):
    queries = head_halves(q_ref[...], SCALE)
    grads = head_halves(g_ref[...])
    keys = m_ref[:, :PAIR]
    values = m_ref[:, PAIR:]
    key_halves = head_halves(keys, SCALE)
    shape = (m_ref.shape[0], q_ref.shape[0])
    keep = lax.broadcasted_iota(jnp.int32, shape, 0) < length[0]
    sum_q = sum_k = sum_v = None
    for head in range(2):
        scores = jnp.where(keep, dot_nt(keys, queries[head]), NEGATIVE)
        expo = jnp.exp(scores - jnp.max(scores, axis=0, keepdims=True))
        probs = expo * (1.0 / jnp.sum(expo, axis=0, keepdims=True))
        part_v = dot(low(probs), grads[head])
        grad_probs = dot_nt(values, grads[head])
        inner = jnp.sum(probs * grad_probs, axis=0, keepdims=True)
        grad_scores = low(probs * (grad_probs - inner))
        part_k = dot(grad_scores, queries[head])
        part_q = dot_tn(grad_scores, key_halves[head])
        sum_q = part_q if sum_q is None else sum_q + part_q
        sum_k = part_k if sum_k is None else sum_k + part_k
        sum_v = part_v if sum_v is None else sum_v + part_v
    dq_ref[...] = low(sum_q)
    dm_ref[:, :PAIR] = low(sum_k)
    dm_ref[:, PAIR:] = low(sum_v)


def cross_backward(queries, memory, grads, length):
    count, states = queries.shape[0], memory.shape[0] // (D // PAIR)
    grid_spec = pltpu.PrefetchScalarGridSpec(
        num_scalar_prefetch=1,
        grid=(D // PAIR,),
        in_specs=[
            pl.BlockSpec((count, PAIR), lambda i, e: (0, i)),
            pl.BlockSpec((states, 2 * PAIR), lambda i, e: (i, 0)),
            pl.BlockSpec((count, PAIR), lambda i, e: (0, i)),
        ],
        out_specs=[
            pl.BlockSpec((count, PAIR), lambda i, e: (0, i)),
            pl.BlockSpec((states, 2 * PAIR), lambda i, e: (i, 0)),
        ],
    )
    return pl.pallas_call(
        cross_backward_kernel,
        grid_spec=grid_spec,
        out_shape=(
            jax.ShapeDtypeStruct((count, D), jnp.bfloat16),
            jax.ShapeDtypeStruct((states * (D // PAIR), 2 * PAIR), jnp.bfloat16),
        ),
        cost_estimate=LITTLE,
    )(length, queries, memory, grads)


def front_kernel(x_ref, gain, shift, qkv_w, qkv_b, one_ref, qkv_ref):
    rows = x_ref[...].astype(jnp.float32)
    centered = rows - jnp.mean(rows, axis=-1, keepdims=True)
    inverse = lax.rsqrt(jnp.mean(centered * centered, axis=-1, keepdims=True) + EPS)
    one = low(centered * inverse * gain[...] + shift[...])
    one_ref[...] = one
    qkv_ref[...] = low(dot(one, qkv_w[...]) + qkv_b[...])


def front(rows, gain, shift, qkv_w, qkv_b):
    count, tile = rows.shape[0], 256
    whole = lambda i: (0, 0)
    block = lambda i: (i, 0)
    return pl.pallas_call(
        front_kernel,
        grid=(count // tile,),
        in_specs=[
            pl.BlockSpec((tile, D), block),
            pl.BlockSpec((1, D), whole),
            pl.BlockSpec((1, D), whole),
            pl.BlockSpec(qkv_w.shape, whole),
            pl.BlockSpec((1, qkv_w.shape[1]), whole),
        ],
        out_specs=[pl.BlockSpec((tile, D), block), pl.BlockSpec((tile, qkv_w.shape[1]), block)],
        out_shape=(
            jax.ShapeDtypeStruct((count, D), jnp.bfloat16),
            jax.ShapeDtypeStruct((count, qkv_w.shape[1]), jnp.bfloat16),
        ),
        compiler_params=pltpu.CompilerParams(vmem_limit_bytes=58 * 2**20),
        cost_estimate=LITTLE,
    )(rows, gain[None], shift[None], qkv_w, qkv_b[None])


def feed_kernel(x_ref, w_ref, b_ref, ga_ref, act_ref, pre_ref, in_ref, sum_ref):
    v = dot(x_ref[...], w_ref[...]) + b_ref[...]
    square = v * v
    half = 0.5 + 0.5 * jnp.tanh(v * (GELU + GELU * 0.044715 * square))
    act_ref[...] = low(v * half)
    slope = half + (v * half) * (1.0 - half) * (2.0 * GELU + 6.0 * GELU * 0.044715 * square)
    grad = low(ga_ref[...] * slope)
    pre_ref[...] = grad
    in_ref[...] = low(dot_nt(grad, w_ref[...]))

    @pl.when(pl.program_id(0) == 0)
    def _():
        sum_ref[...] = jnp.zeros_like(sum_ref)

    sum_ref[...] += jnp.sum(grad.astype(jnp.float32), axis=0, keepdims=True)


def feed(rows, weight, bias, grad_act):
    count, hidden = grad_act.shape
    tile = 512
    whole = lambda i: (0, 0)
    block = lambda i: (i, 0)
    return pl.pallas_call(
        feed_kernel,
        grid=(count // tile,),
        in_specs=[
            pl.BlockSpec((tile, D), block),
            pl.BlockSpec((D, hidden), whole),
            pl.BlockSpec((1, hidden), whole),
            pl.BlockSpec((tile, hidden), block),
        ],
        out_specs=[
            pl.BlockSpec((tile, hidden), block),
            pl.BlockSpec((tile, hidden), block),
            pl.BlockSpec((tile, D), block),
            pl.BlockSpec((1, hidden), whole),
        ],
        out_shape=(
            jax.ShapeDtypeStruct((count, hidden), jnp.bfloat16),
            jax.ShapeDtypeStruct((count, hidden), jnp.bfloat16),
            jax.ShapeDtypeStruct((count, D), jnp.bfloat16),
            jax.ShapeDtypeStruct((1, hidden), jnp.float32),
        ),
        compiler_params=pltpu.CompilerParams(vmem_limit_bytes=58 * 2**20),
        cost_estimate=LITTLE,
    )(rows, weight, bias[None], grad_act)


def expand_kernel(replica, x_ref, g_ref, *refs):
    keep, outs = refs[-1], refs[:-1]
    size, rows = len(outs), outs[0].shape[1]
    owners = x_ref.shape[1] // (size * rows)
    keep[...] = low(dot_tn(x_ref[...], g_ref[...])).reshape(keep.shape)
    step = pl.program_id(0) * owners
    for owner in range(owners):
        for other, out in enumerate(outs):
            out[pl.ds(step + owner, 1)] = keep[owner, pl.ds(replica[0] ^ other, 1)]


def expand_grads(rows_in, grads, owners, part_rows):
    size, me = lax.axis_size("rep"), lax.axis_index("rep")
    count, hidden = grads.shape
    if part_rows % 16:
        full = low(dot_tn(rows_in, grads)).reshape(owners, size, part_rows, hidden)
        return [lax.dynamic_index_in_dim(full, me ^ step, 1, keepdims=False) for step in range(size)]
    tile = 2
    grid_spec = pltpu.PrefetchScalarGridSpec(
        num_scalar_prefetch=1,
        grid=(owners // tile,),
        in_specs=[
            pl.BlockSpec((count, tile * size * part_rows), lambda i, e: (0, i)),
            pl.BlockSpec((count, hidden), lambda i, e: (0, 0)),
        ],
        out_specs=[pl.BlockSpec((owners, part_rows, hidden), lambda i, e: (0, 0, 0))] * size,
        scratch_shapes=[pltpu.VMEM((tile, size, part_rows, hidden), jnp.bfloat16)],
    )
    return pl.pallas_call(
        expand_kernel,
        grid_spec=grid_spec,
        out_shape=(jax.ShapeDtypeStruct((owners, part_rows, hidden), jnp.bfloat16),) * size,
        compiler_params=pltpu.CompilerParams(vmem_limit_bytes=58 * 2**20),
        cost_estimate=LITTLE,
    )(me[None], rows_in, grads)


def shrink_kernel(replica, a_ref, g_ref, *outs):
    for step, out in enumerate(outs):

        @pl.when(pl.program_id(0) == step)
        def _():
            out[...] = low(dot_tn(a_ref[...], g_ref[...]))


def shrink_grads(act, grads):
    size, me = lax.axis_size("rep"), lax.axis_index("rep")
    count, hidden = act.shape
    part = hidden // size
    if part % 128:
        full = low(dot_tn(act, grads)).reshape(size, part, D)
        return [lax.dynamic_index_in_dim(full, me ^ step, 0, keepdims=False) for step in range(size)]
    grid_spec = pltpu.PrefetchScalarGridSpec(
        num_scalar_prefetch=1,
        grid=(size,),
        in_specs=[
            pl.BlockSpec((count, part), lambda i, e: (0, e[0] ^ i)),
            pl.BlockSpec((count, D), lambda i, e: (0, 0)),
        ],
        out_specs=[pl.BlockSpec((part, D), lambda i, e: (0, 0))] * size,
    )
    return pl.pallas_call(
        shrink_kernel,
        grid_spec=grid_spec,
        out_shape=(jax.ShapeDtypeStruct((part, D), jnp.bfloat16),) * size,
        compiler_params=pltpu.CompilerParams(vmem_limit_bytes=58 * 2**20),
        cost_estimate=LITTLE,
    )(me[None], act, grads)


def product_kernel(a_ref, b_ref, out_ref):
    out_ref[...] = low(dot(a_ref[...], b_ref[...]))


def product(left, right):
    count, depth = left.shape
    tile = 512
    return pl.pallas_call(
        product_kernel,
        grid=(count // tile,),
        in_specs=[pl.BlockSpec((tile, depth), lambda i: (i, 0)), pl.BlockSpec(right.shape, lambda i: (0, 0))],
        out_specs=pl.BlockSpec((tile, right.shape[1]), lambda i: (i, 0)),
        out_shape=jax.ShapeDtypeStruct((count, right.shape[1]), jnp.bfloat16),
        compiler_params=pltpu.CompilerParams(vmem_limit_bytes=58 * 2**20),
        cost_estimate=LITTLE,
    )(left, right)


def back_kernel(g_ref, w_ref, one_ref, out_ref, sum_ref, own_ref):
    @pl.when(pl.program_id(0) == 0)
    def _():
        sum_ref[...] = jnp.zeros_like(sum_ref)
        own_ref[...] = jnp.zeros_like(own_ref)

    grads = dot_nt(g_ref[...], w_ref[...])
    out_ref[...] = low(grads)
    sum_ref[0:1, :] += jnp.sum(grads * one_ref[...].astype(jnp.float32), axis=0, keepdims=True)
    sum_ref[1:2, :] += jnp.sum(grads, axis=0, keepdims=True)
    own_ref[...] += jnp.sum(g_ref[...].astype(jnp.float32), axis=0, keepdims=True)


def back(grads, weight, rows_in):
    count, width = grads.shape
    tile = 256
    return pl.pallas_call(
        back_kernel,
        grid=(count // tile,),
        in_specs=[
            pl.BlockSpec((tile, width), lambda i: (i, 0)),
            pl.BlockSpec(weight.shape, lambda i: (0, 0)),
            pl.BlockSpec((tile, D), lambda i: (i, 0)),
        ],
        out_specs=[
            pl.BlockSpec((tile, D), lambda i: (i, 0)),
            pl.BlockSpec((2, D), lambda i: (0, 0)),
            pl.BlockSpec((1, width), lambda i: (0, 0)),
        ],
        out_shape=(
            jax.ShapeDtypeStruct((count, D), jnp.bfloat16),
            jax.ShapeDtypeStruct((2, D), jnp.float32),
            jax.ShapeDtypeStruct((1, width), jnp.float32),
        ),
        compiler_params=pltpu.CompilerParams(vmem_limit_bytes=58 * 2**20),
        cost_estimate=LITTLE,
    )(grads, weight, rows_in)


def heads_grads_kernel(x_ref, g_ref, e_ref, m_ref, out_ref):
    width = g_ref.shape[1]
    shape = out_ref.shape[1:3]
    for owner in range(shape[0]):
        place = slice(owner * x_ref.shape[1] // shape[0], (owner + 1) * x_ref.shape[1] // shape[0])
        left = low(dot_tn(x_ref[:, place], g_ref[...]))
        right = low(dot_tn(e_ref[:, place], m_ref[...]))
        for replica in range(out_ref.shape[0]):
            rows = slice(replica * shape[1], (replica + 1) * shape[1])
            out_ref[replica, owner, :, :width] = left[rows, :]
            out_ref[replica, owner, :, width:] = right[rows, :]


def heads_grads(rows_in, grads, enc, enc_grads, owners, part_rows):
    size = lax.axis_size("rep")
    width, enc_width = grads.shape[1], enc_grads.shape[1]
    if part_rows % 16:
        both = low(jnp.concatenate([dot_tn(rows_in, grads), dot_tn(enc, enc_grads)], axis=1))
        return both.reshape(owners, size, part_rows, width + enc_width).transpose(1, 0, 2, 3)
    tile = 2
    return pl.pallas_call(
        heads_grads_kernel,
        grid=(owners // tile,),
        in_specs=[
            pl.BlockSpec((rows_in.shape[0], tile * size * part_rows), lambda i: (0, i)),
            pl.BlockSpec(grads.shape, lambda i: (0, 0)),
            pl.BlockSpec((enc.shape[0], tile * size * part_rows), lambda i: (0, i)),
            pl.BlockSpec(enc_grads.shape, lambda i: (0, 0)),
        ],
        out_specs=pl.BlockSpec((size, tile, part_rows, width + enc_width), lambda i: (0, i, 0, 0)),
        out_shape=jax.ShapeDtypeStruct((size, owners, part_rows, width + enc_width), jnp.bfloat16),
        compiler_params=pltpu.CompilerParams(vmem_limit_bytes=58 * 2**20),
        cost_estimate=LITTLE,
    )(rows_in, grads, enc, enc_grads)


def last_kernel(x_ref, e_ref, one_ref, gain, out_ref):
    rows = x_ref[...].astype(jnp.float32)
    centered = rows - jnp.mean(rows, axis=-1, keepdims=True)
    inverse = lax.rsqrt(jnp.mean(centered * centered, axis=-1, keepdims=True) + EPS)
    x_hat = centered * inverse
    grads = e_ref[...].astype(jnp.float32) * gain[...]
    inner = jnp.mean(grads * x_hat, axis=-1, keepdims=True)
    out_ref[...] = one_ref[...] + inverse * (grads - jnp.mean(grads, axis=-1, keepdims=True) - x_hat * inner)


def last(rows, grads, grad_one, gain):
    count = rows.shape[0]
    tile = 128
    block = pl.BlockSpec((tile, D), lambda i: (i, 0))
    return pl.pallas_call(
        last_kernel,
        grid=(count // tile,),
        in_specs=[block, block, block, pl.BlockSpec((1, D), lambda i: (0, 0))],
        out_specs=block,
        out_shape=jax.ShapeDtypeStruct((count, D), jnp.float32),
        cost_estimate=LITTLE,
    )(rows, grads, grad_one, gain[None])


def rep_send(value, step):
    size = lax.axis_size("rep")
    return lax.ppermute(value, "rep", [(i, i ^ step) for i in range(size)])


def rep_start(value):
    return [value] + [rep_send(value, step) for step in range(1, lax.axis_size("rep"))]


def rep_place(parts, axis):
    size, me = lax.axis_size("rep"), lax.axis_index("rep")
    value = parts[0]
    out = jnp.zeros(value.shape[:axis] + (size,) + value.shape[axis:], value.dtype)
    for step, part in enumerate(parts):
        out = lax.dynamic_update_slice_in_dim(out, jnp.expand_dims(part, axis), me ^ step, axis)
    return out


def spread_kernel(place, *refs):
    out_ref = refs[-1]
    for step, part in enumerate(refs[:-1]):
        out_ref[pl.ds(place[0] ^ step, 1)] = part[...].astype(out_ref.dtype)[None]


def spread(parts, first, last, dtype):
    size, columns = len(parts), parts[0].shape[1]
    rows = last - first
    if rows % 32 or first % rows or parts[0].shape[0] % 16:
        return rep_place([part[first:last] for part in parts], 0).astype(dtype)
    tile = rows // 2
    grid_spec = pltpu.PrefetchScalarGridSpec(
        num_scalar_prefetch=1,
        grid=(2,),
        in_specs=[pl.BlockSpec((tile, columns), lambda i, e: (first // tile + i, 0))] * size,
        out_specs=pl.BlockSpec((size, tile, columns), lambda i, e: (0, i, 0)),
    )
    return pl.pallas_call(
        spread_kernel,
        grid_spec=grid_spec,
        out_shape=jax.ShapeDtypeStruct((size, rows, columns), dtype),
        compiler_params=pltpu.CompilerParams(vmem_limit_bytes=58 * 2**20),
        cost_estimate=LITTLE,
    )(lax.axis_index("rep")[None], *parts)


def rep_gather(value, axis):
    return rep_place(rep_start(value), axis)


def rep_swap(parts):
    return lax.all_to_all(parts, "rep", 0, 0, tiled=True)


def rep_split(parts, axis):
    size, me = lax.axis_size("rep"), lax.axis_index("rep")
    picks = [lax.dynamic_index_in_dim(parts, me ^ step, axis, keepdims=False) for step in range(size)]
    return [picks[0]] + [rep_send(low(picks[step]), step) for step in range(1, size)]


def sum_first(parts):
    return low(jnp.sum(parts.astype(jnp.float32), axis=0))


def add_up(parts):
    total = parts[0].astype(jnp.float32)
    for part in parts[1:]:
        total = total + part.astype(jnp.float32)
    return low(total)


def rep_reduce(parts, axis):
    return add_up(rep_split(parts, axis))


def core_send(value):
    size = lax.axis_size("shard")
    return lax.ppermute(value, "shard", [(i, i ^ 1) for i in range(size)])


def line_send(value, step, group=None):
    size = lax.axis_size("shard")
    group = group or size
    route = [(i, i // group * group + (i + 2 * step) % group) for i in range(size)]
    return lax.ppermute(value, "shard", route)


def line_scatter_start(value, group=None):
    group = group or lax.axis_size("shard")
    core = lax.axis_index("shard") % 2
    value = value.reshape((group // 2, 2, value.shape[0] // group) + value.shape[1:])
    mine = lax.dynamic_index_in_dim(value, core, 1, keepdims=False)
    theirs = lax.dynamic_index_in_dim(value, 1 - core, 1, keepdims=False)
    return [mine, core_send(theirs)]


def line_scatter_middle(both, group=None):
    group = group or lax.axis_size("shard")
    chips = group // 2
    chip = lax.axis_index("shard") % group // 2
    line = add_up(both)
    parts = [lax.dynamic_index_in_dim(line, (chip + step) % chips, 0, keepdims=False) for step in range(chips)]
    return [parts[0]] + [line_send(parts[step], step, group) for step in range(1, chips)]


def kinds_kernel(place, *refs):
    outs = refs[-3:]
    rows = outs[0].shape[1]
    for step, part in enumerate(refs[:-3]):
        for kind, out in enumerate(outs):
            out[pl.ds(place[0] ^ step, 1)] = part[kind * rows : (kind + 1) * rows, :].astype(out.dtype)[None]


def spread_kinds(parts, rows):
    size = len(parts)
    if rows % 16:
        return [rep_place([part[k * rows : (k + 1) * rows] for part in parts], 0).astype(jnp.float32) for k in range(3)]
    whole = lambda i, e: (0, 0)
    grid_spec = pltpu.PrefetchScalarGridSpec(
        num_scalar_prefetch=1,
        grid=(1,),
        in_specs=[pl.BlockSpec(parts[0].shape, whole)] * size,
        out_specs=[pl.BlockSpec((size, rows, D), lambda i, e: (0, 0, 0))] * 3,
    )
    return pl.pallas_call(
        kinds_kernel,
        grid_spec=grid_spec,
        out_shape=(jax.ShapeDtypeStruct((size, rows, D), jnp.float32),) * 3,
        cost_estimate=LITTLE,
    )(lax.axis_index("rep")[None], *parts)


def columns_kernel(place, *refs):
    out_ref = refs[-1]
    rows = out_ref.shape[1]
    for step, part in enumerate(refs[:-1]):
        for block in range(part.shape[0] // rows):
            wide = part[block * rows : (block + 1) * rows, :].astype(out_ref.dtype)
            out_ref[pl.ds(place[0] ^ step, 1), :, block * D : (block + 1) * D] = wide[None]


def spread_columns(parts, first, blocks, rows):
    size, me = len(parts), lax.axis_index("rep")
    if rows % 16:
        parts = [part[first:].reshape(blocks, rows, -1).transpose(1, 0, 2).reshape(rows, -1) for part in parts]
        return rep_place(parts, 0).astype(jnp.float32).reshape(size * rows, -1)
    halves = 2
    taken = blocks * rows // halves
    grid_spec = pltpu.PrefetchScalarGridSpec(
        num_scalar_prefetch=1,
        grid=(halves,),
        in_specs=[pl.BlockSpec((taken, D), lambda i, e: (first // taken + i, 0))] * size,
        out_specs=pl.BlockSpec((size, rows, blocks * D // halves), lambda i, e: (0, 0, i)),
    )
    out = pl.pallas_call(
        columns_kernel,
        grid_spec=grid_spec,
        out_shape=jax.ShapeDtypeStruct((size, rows, blocks * D), jnp.float32),
        compiler_params=pltpu.CompilerParams(vmem_limit_bytes=58 * 2**20),
        cost_estimate=LITTLE,
    )(me[None], *parts)
    return out.reshape(size * rows, blocks * D)


def heads_kernel(span, place, *refs):
    qkv_ref, memory_ref = refs[-2:]
    rows, width = qkv_ref.shape[1], D // span
    for step, part in enumerate(refs[:-2]):
        take = pl.ds(place[0] ^ step, 1)
        for block in range(span):
            wide = part[block * rows : (block + 1) * rows, :].astype(jnp.float32)[None]
            for kind in range(5):
                out, at = (qkv_ref, kind) if kind < 3 else (memory_ref, kind - 3)
                columns = slice(at * D + block * width, at * D + (block + 1) * width)
                out[take, :, columns] = wide[:, :, kind * width : (kind + 1) * width]


def spread_heads(parts, span, rows, width):
    size, me = len(parts), lax.axis_index("rep")
    if rows % 16:
        full = rep_place([part[: span * rows].reshape(span, rows, 5, width) for part in parts], 0)
        full = full.transpose(0, 2, 3, 1, 4).reshape(size * rows, 5 * D).astype(jnp.float32)
        return full[:, : 3 * D], full[:, 3 * D :]
    grid_spec = pltpu.PrefetchScalarGridSpec(
        num_scalar_prefetch=1,
        grid=(1,),
        in_specs=[pl.BlockSpec((span * rows, 5 * width), lambda i, e: (0, 0))] * size,
        out_specs=[
            pl.BlockSpec((size, rows, 3 * D), lambda i, e: (0, 0, 0)),
            pl.BlockSpec((size, rows, 2 * D), lambda i, e: (0, 0, 0)),
        ],
    )
    qkv, memory = pl.pallas_call(
        functools.partial(heads_kernel, span),
        grid_spec=grid_spec,
        out_shape=(
            jax.ShapeDtypeStruct((size, rows, 3 * D), jnp.float32),
            jax.ShapeDtypeStruct((size, rows, 2 * D), jnp.float32),
        ),
        compiler_params=pltpu.CompilerParams(vmem_limit_bytes=58 * 2**20),
        cost_estimate=LITTLE,
    )(me[None], *parts)
    return qkv.reshape(size * rows, 3 * D), memory.reshape(size * rows, 2 * D)


def line_start(piece):
    return [piece] + [line_send(piece, step) for step in range(1, lax.axis_size("shard") // 2)]


def line_place(parts):
    chips, chip = len(parts), lax.axis_index("shard") // 2
    kinds, rows, columns = parts[0].shape
    line = jnp.zeros((kinds, chips, rows, columns), parts[0].dtype)
    for step, part in enumerate(parts):
        line = lax.dynamic_update_slice_in_dim(line, part[:, None], (chip - step) % chips, 1)
    return line


def join_kernel(place, *refs):
    outs = refs[-3:]
    parts = refs[:-3]
    size = len(parts) // 2
    for core in range(2):
        side = place[1] ^ core
        for step in range(size):
            for kind in range(3):
                outs[kind][0, pl.ds(side, 1), pl.ds(place[0] ^ step, 1)] = parts[core * size + step][kind][None]


def weight_join(mine, other):
    size = len(mine)
    _, chips, rows, _ = mine[0].shape
    core = lax.axis_index("shard") % 2
    if rows % 16:
        first = core == 0
        plane, next_plane = rep_place(mine, 2), rep_place(other, 2)
        low_core, high_core = jnp.where(first, plane, next_plane), jnp.where(first, next_plane, plane)
        full = jnp.stack([low_core, high_core], axis=2).reshape(3, D, D)
        return full[0], full[1], full[2]
    grid_spec = pltpu.PrefetchScalarGridSpec(
        num_scalar_prefetch=1,
        grid=(chips,),
        in_specs=[pl.BlockSpec((3, 1, rows, D), lambda i, e: (0, i, 0, 0))] * (2 * size),
        out_specs=[pl.BlockSpec((1, 2, size, rows, D), lambda i, e: (i, 0, 0, 0, 0))] * 3,
    )
    outs = pl.pallas_call(
        join_kernel,
        grid_spec=grid_spec,
        out_shape=(jax.ShapeDtypeStruct((chips, 2, size, rows, D), jnp.bfloat16),) * 3,
        compiler_params=pltpu.CompilerParams(vmem_limit_bytes=58 * 2**20),
        cost_estimate=LITTLE,
    )(jnp.stack([lax.axis_index("rep"), core]), *mine, *other)
    return tuple(out.reshape(D, D) for out in outs)


def plain_kernel(core, a_ref, b_ref, c_ref, ga_ref, gb_ref, gc_ref, mine_ref, theirs_ref):
    width = a_ref.shape[1] // 2
    for kind, (left, right) in enumerate(((a_ref, ga_ref), (b_ref, gb_ref), (c_ref, gc_ref))):
        for side, out in enumerate((mine_ref, theirs_ref)):
            place = pl.ds(pl.multiple_of((core[0] ^ side) * width, width), width)
            out[kind, 0] = low(dot_tn(left[:, place], right[...])).reshape(out.shape[2:])


def plain_grads(lefts, rights):
    size, chips = lax.axis_size("rep"), lax.axis_size("shard") // 2
    core = lax.axis_index("shard") % 2
    rows = D // (2 * chips * size)
    if rows % 16:
        stack = jnp.stack([low(dot_tn(left, right)) for left, right in zip(lefts, rights)])
        stack = stack.reshape(3, chips, 2, size, rows, D)
        return [lax.dynamic_index_in_dim(stack, core ^ side, 2, keepdims=False) for side in range(2)]
    count = lefts[0].shape[0]
    grid_spec = pltpu.PrefetchScalarGridSpec(
        num_scalar_prefetch=1,
        grid=(chips,),
        in_specs=[pl.BlockSpec((count, D // chips), lambda i, e: (0, i))] * 3
        + [pl.BlockSpec((count, D), lambda i, e: (0, 0))] * 3,
        out_specs=[pl.BlockSpec((3, 1, size, rows, D), lambda i, e: (0, i, 0, 0, 0))] * 2,
    )
    return pl.pallas_call(
        plain_kernel,
        grid_spec=grid_spec,
        out_shape=(jax.ShapeDtypeStruct((3, chips, size, rows, D), jnp.bfloat16),) * 2,
        compiler_params=pltpu.CompilerParams(vmem_limit_bytes=58 * 2**20),
        cost_estimate=pl.CostEstimate(flops=6 * count * D * D, bytes_accessed=20 * count * D, transcendentals=0),
    )(core[None], *lefts, *rights)


def split_kernel(place, mine_ref, other_ref, *outs):
    for step, out in enumerate(outs):
        take = pl.ds(place[0] ^ step, 1)
        total = mine_ref[:, 0, take].astype(jnp.float32) + other_ref[:, 0, take].astype(jnp.float32)
        out[...] = low(total)


def core_sum_split(mine, other):
    kinds, chips, size, rows, _ = mine.shape
    if rows % 16:
        total = add_up([mine, other])
        me = lax.axis_index("rep")
        return [lax.dynamic_index_in_dim(total, me ^ step, 2, keepdims=False) for step in range(size)]
    grid_spec = pltpu.PrefetchScalarGridSpec(
        num_scalar_prefetch=1,
        grid=(chips,),
        in_specs=[pl.BlockSpec((kinds, 1, size, rows, D), lambda i, e: (0, i, 0, 0, 0))] * 2,
        out_specs=[pl.BlockSpec((kinds, 1, rows, D), lambda i, e: (0, i, 0, 0))] * size,
    )
    return pl.pallas_call(
        split_kernel,
        grid_spec=grid_spec,
        out_shape=(jax.ShapeDtypeStruct((kinds, chips, rows, D), jnp.bfloat16),) * size,
        compiler_params=pltpu.CompilerParams(vmem_limit_bytes=58 * 2**20),
        cost_estimate=LITTLE,
    )(lax.axis_index("rep")[None], mine, other)


def reduce_line(line):
    chips = lax.axis_size("shard") // 2
    chip = lax.axis_index("shard") // 2
    parts = [lax.dynamic_index_in_dim(line, (chip + step) % chips, 1, keepdims=False) for step in range(chips)]
    return [parts[0]] + [line_send(parts[step], step) for step in range(1, chips)]


def shards(
    tokens,
    segments,
    enc_states,
    enc_lengths,
    cotangent,
    self_qkv,
    self_out,
    cross_query,
    cross_memory,
    cross_out,
    expand_weight,
    shrink_weight,
    norm_gain,
    norm_bias,
    proj_bias,
    expand_bias,
):
    row_count, enc_rows = tokens.shape[0], enc_states.shape[0]
    span = SEQ // row_count
    width = D // span
    count = lax.axis_size("shard")
    size = lax.axis_size("rep")
    rep_pos = lax.axis_index("rep")
    shard_pos = lax.axis_index("shard")
    local_pos = shard_pos % span
    local_seq = shard_pos // span
    groups = None
    if count != span:
        groups = [[g * span + i for i in range(span)] for g in range(count // span)]
    weight_rows = self_qkv.shape[0]
    part_rows = weight_rows // size
    hidden = expand_bias.shape[0]
    shard_width = norm_gain.shape[1]

    def gather(value, groups=None):
        return lax.all_gather(value, "shard", axis=0, tiled=True, axis_index_groups=groups)

    def scatter(value, groups=None):
        return lax.psum_scatter(value, "shard", scatter_dimension=0, tiled=True, axis_index_groups=groups)

    def swap(value):
        return lax.all_to_all(value, "shard", 0, 0, tiled=True)

    def own_part(weight):
        return lax.dynamic_slice_in_dim(weight, rep_pos * part_rows, part_rows, axis=0)

    def by_pairs(weight, kinds):
        blocks = weight.reshape(part_rows, kinds, span, width).transpose(2, 0, 1, 3)
        return blocks.reshape(span, part_rows, kinds * width)

    blocks = jnp.concatenate([by_pairs(own_part(self_qkv), 3), by_pairs(own_part(cross_memory), 2)], axis=2)
    blocks = jnp.tile(blocks, (count // span, 1, 1))
    small = jnp.concatenate([norm_gain, norm_bias, proj_bias], axis=0)
    small_count = small.shape[0]
    small_rows = -(-small.size // (5 * width))
    small = jnp.pad(small.reshape(-1), (0, small_rows * 5 * width - small.size)).reshape(small_rows, 5 * width)
    blocks = jnp.concatenate([blocks, jnp.broadcast_to(small, (count,) + small.shape)], axis=1)
    swapped = swap(blocks)
    plain_parts = line_start(jnp.stack([own_part(self_out), own_part(cross_query), own_part(cross_out)]))
    enc_all = gather(enc_states, groups)
    rows_all = gather(after(tokens, swapped, enc_all, plain_parts[1], plain_parts[-1]), groups)
    small_all = swapped[:, part_rows:].reshape(count, small_rows * 5 * width)[:, : small_count * shard_width]
    small_all = small_all.reshape(count, small_count, shard_width)
    small_all = small_all.transpose(1, 0, 2).reshape(small_count, D).astype(jnp.float32)
    gain_rows, shift_rows, bias_rows = small_all[:3], small_all[3:6], small_all[6:]
    head_weight = rep_gather(swapped[:, :part_rows], 1).reshape(D, 5 * width)
    qkv_weight, memory_weight = head_weight[:, : 3 * width], head_weight[:, 3 * width :]
    qkv_weight, memory_weight = head_weight[:, : 3 * width], head_weight[:, 3 * width :]
    own_bias = lax.dynamic_slice_in_dim(bias_rows, local_pos * width, width, axis=1)
    zero_bias = jnp.zeros((width,), jnp.float32)
    memory_pair = low(dot(enc_all, memory_weight) + jnp.concatenate([zero_bias, own_bias[4]]))
    plain_mine = rep_start(line_place(after(plain_parts, head_weight)))
    rows_all, qkv_weight, memory_weight, plain_mine[1], plain_mine[2] = lax.optimization_barrier(
        (rows_all, qkv_weight, memory_weight, plain_mine[1], plain_mine[2])
    )
    memory_all = gather(after(memory_pair, rows_all), groups)
    expand_part = own_part(after(expand_weight, rows_all)).reshape(part_rows, count, hidden).transpose(1, 0, 2)
    expand_swapped = swap(expand_part)

    seq_segments = lax.dynamic_slice_in_dim(segments, local_seq * SEQ, SEQ)
    qkv_bias = jnp.concatenate([own_bias[0], zero_bias, own_bias[1]])
    input_one_all, qkv = front(rows_all, gain_rows[0], shift_rows[0], qkv_weight, qkv_bias)
    att_low, att_full, lse = self_forward(qkv, seq_segments)
    att_low, memory_all, plain_mine, expand_swapped = lax.optimization_barrier(
        (att_low, memory_all, plain_mine, expand_swapped)
    )
    grad_all = gather(after(cotangent, memory_all))
    plain_other = [core_send(part) for part in plain_mine]
    attn_proj, query_in, cross_proj = weight_join(plain_mine, plain_other)
    attended = lax.all_to_all(att_low, "shard", 0, 1, tiled=True, axis_index_groups=groups)

    enc_count = lax.dynamic_slice_in_dim(enc_lengths, local_seq, 1)

    residual_in = tokens.astype(jnp.float32)
    hidden_one = residual_in + dot(attended, attn_proj) + bias_rows[2]
    input_two = low(norm_apply(hidden_one, gain_rows[1], shift_rows[1]))
    cross_q = low(dot(input_two, query_in) + bias_rows[3])
    context = cross_forward(cross_q, memory_all, enc_count)
    hidden_two = hidden_one + dot(context, cross_proj) + bias_rows[5]
    input_three = low(norm_apply(hidden_two, gain_rows[2], shift_rows[2]))

    input_three_all = gather(input_three)
    expand_parts = rep_start(expand_swapped.reshape(count * part_rows, hidden))
    grad_all_now = after(grad_all, input_three)
    expand_local = spread(expand_parts, 0, count * part_rows, jnp.bfloat16)
    expand_local = expand_local.reshape(size, count, part_rows, hidden).transpose(1, 0, 2, 3).reshape(D, hidden)
    grad_act = dot_nt(grad_all_now, shrink_weight)
    input_three_all, grad_act, expand_local = lax.optimization_barrier((input_three_all, grad_act, expand_local))
    act, grad_pre, grad_in_three_low, hidden_sums = feed(
        input_three_all, expand_local, expand_bias.astype(jnp.float32), grad_act
    )
    grad_hidden_bias = hidden_sums[0]
    grad_in_three = scatter(grad_in_three_low)

    part_hidden = hidden // size

    def send_parts(parts):
        return [parts[0]] + [rep_send(parts[step], step) for step in range(1, size)]

    rows_late, grad_pre_late = after((input_three_all, grad_pre), grad_in_three_low)
    expand_grad_parts = expand_grads(rows_late, grad_pre_late, count, part_rows)
    shrink_parts = send_parts(shrink_grads(after(act, expand_grad_parts[0]), grad_all))
    expand_grad_parts = send_parts(expand_grad_parts)
    result_part = product(after(act, shrink_parts[0]), shrink_weight)
    expand_sum = add_up(expand_grad_parts)
    own_expand = swap(expand_sum)
    grad_in_three, shrink_parts[0], result_part = lax.optimization_barrier(
        (grad_in_three, shrink_parts[0], result_part)
    )
    result_sum = scatter(result_part)
    grad_in_three = grad_in_three.astype(jnp.float32)

    grad_out = cotangent.astype(jnp.float32)
    norm_three = jax.vjp(norm_apply, hidden_two, gain_rows[2], shift_rows[2])[1](grad_in_three)
    grad_two = grad_out + norm_three[0]
    grad_two_low = low(grad_two)
    grad_context = low(dot_nt(grad_two_low, cross_proj))
    grad_context, own_expand = lax.optimization_barrier((grad_context, own_expand))
    grad_cross_q, memory_part = cross_backward(cross_q, memory_all, grad_context, enc_count)
    grad_cross_q, memory_part, shrink_parts = lax.optimization_barrier((grad_cross_q, memory_part, shrink_parts))
    mem_grads = scatter(memory_part, groups)
    grad_in_two = dot_nt(grad_cross_q, query_in)
    norm_two = jax.vjp(norm_apply, hidden_one, gain_rows[1], shift_rows[1])[1](grad_in_two)
    grad_one = grad_two + norm_two[0]
    grad_one_low = low(grad_one)
    grad_attn = low(dot_nt(grad_one_low, attn_proj))
    shrink_sum = add_up(shrink_parts)
    own_expand = own_expand.reshape(part_hidden, D)
    own_feed = jnp.concatenate([shrink_sum, own_expand], axis=0)
    grad_attn, own_feed = lax.optimization_barrier((grad_attn, own_feed))
    grad_att_heads = lax.all_to_all(grad_attn, "shard", 1, 0, tiled=True, axis_index_groups=groups)

    lefts, rights = after(((attended, input_two, context), (grad_one_low, grad_cross_q, grad_two_low)), grad_attn)
    plain_own, plain_theirs = plain_grads(lefts, rights)
    plain_theirs = core_send(plain_theirs)
    grad_att_heads, plain_own = lax.optimization_barrier((grad_att_heads, plain_own))

    feed_gather = rep_start(own_feed)
    grad_qkv = self_backward(qkv, grad_att_heads, lse, att_full, seq_segments)
    heads_parts = heads_grads(input_one_all, grad_qkv, enc_all, mem_grads, count, part_rows)
    heads_swapped = rep_swap(heads_parts)
    grad_in_one_low, one_sums, qkv_sums = back(after(grad_qkv, heads_parts, feed_gather), qkv_weight, input_one_all)
    plain_rep = send_parts(core_sum_split(*after((plain_own, plain_theirs), heads_parts)))
    grad_in_one_low, heads_swapped, plain_rep[0] = lax.optimization_barrier(
        (grad_in_one_low, heads_swapped, plain_rep[0])
    )
    grad_in_one = scatter(grad_in_one_low, groups)

    mem_grads_late = after(mem_grads, grad_in_one_low)
    qkv_sums = qkv_sums[0]
    gain_shift = [(one_sums[0] - shift_rows[0] * one_sums[1]) / gain_rows[0], one_sums[1]]
    zero_row = jnp.zeros((D,), jnp.float32)

    def at_own(values):
        return lax.dynamic_update_slice_in_dim(zero_row, values, local_pos * width, 0)

    small_grads = jnp.stack(
        [
            gain_shift[0],
            norm_two[1],
            norm_three[1],
            gain_shift[1],
            norm_two[2],
            norm_three[2],
            at_own(qkv_sums[:width]),
            at_own(qkv_sums[2 * width :]),
            column_sums(grad_one_low),
            column_sums(grad_cross_q),
            at_own(column_sums(mem_grads_late)[width:]),
            column_sums(grad_two_low),
            column_sums(cotangent),
        ]
    )
    small_grads = small_grads.reshape(small_count, count, shard_width).transpose(1, 0, 2)
    small_grads = small_grads.reshape(count, small_count * shard_width)
    hidden_grads = jnp.zeros((count, hidden), jnp.float32)
    hidden_grads = lax.dynamic_update_slice_in_dim(hidden_grads, grad_hidden_bias[None], shard_pos, 0)
    small_grads = low(jnp.concatenate([small_grads, hidden_grads], axis=1))
    small_size = small_grads.shape[1]
    extra = -(-small_size // (5 * width))
    small_grads = jnp.pad(small_grads, ((0, 0), (0, extra * 5 * width - small_size)))
    small_grads = small_grads.reshape(count, extra, 5 * width)
    heads_sum = sum_first(after(heads_swapped, grad_in_one_low))
    own_heads = swap(jnp.concatenate([heads_sum, small_grads], axis=1))
    own_small = sum_first(own_heads[:, part_rows:])
    own_heads = own_heads[:, :part_rows].reshape(count // span, span, part_rows, 5 * width)
    own_heads = own_heads[0] if count == span else sum_first(own_heads)
    heads_gather = rep_start(jnp.concatenate([own_heads.reshape(span * part_rows, 5 * width), own_small], axis=0))

    plain_line_parts = reduce_line(add_up(after(plain_rep, own_heads)))
    own_plain = add_up(plain_line_parts).reshape(3 * part_rows, D)
    plain_gather = rep_start(own_plain)
    enc_parts = line_scatter_start(low(dot_nt(mem_grads_late, memory_weight)), span)
    grad_enc = add_up(line_scatter_middle(enc_parts, span)).astype(jnp.float32)
    result = hidden_two + after(result_sum, grad_in_one_low).astype(jnp.float32) + bias_rows[6]

    total_shrink = spread(feed_gather, 0, part_hidden, jnp.float32)
    total_expand = spread_columns(feed_gather, part_hidden, count, part_rows)
    total_small = sum(part[span * part_rows :].astype(jnp.float32) for part in heads_gather)
    total_small = total_small.reshape(-1)[:small_size]
    total_hidden_bias = total_small[small_count * shard_width :]
    total_small = total_small[: small_count * shard_width].reshape(small_count, shard_width)
    total_qkv, total_memory = spread_heads(heads_gather, span, part_rows, width)

    grad_tokens = last(tokens, grad_in_one, grad_one, gain_rows[0])
    plain_gather = after(plain_gather, grad_tokens, result)
    total_proj, total_query, total_cross = [part.reshape(weight_rows, D) for part in spread_kinds(plain_gather, part_rows)]

    return (
        low(result),
        grad_tokens,
        grad_enc,
        total_qkv,
        total_proj,
        total_query,
        total_memory,
        total_cross,
        total_expand.reshape(weight_rows, count * hidden).astype(jnp.float32),
        total_shrink.reshape(hidden, D).astype(jnp.float32),
        total_small[:3],
        total_small[3:6],
        total_small[6:],
        total_hidden_bias,
    )


def solution(mesh):
    return jax.shard_map(
        shards,
        mesh=mesh,
        in_specs=(
            P(("rep", "shard"), None),
            P("rep"),
            P(("rep", "shard"), None),
            P("rep"),
            P(("rep", "shard"), None),
            P("shard", None),
            P("shard", None),
            P("shard", None),
            P("shard", None),
            P("shard", None),
            P("shard", None),
            P("shard", None),
            P(None, "shard"),
            P(None, "shard"),
            P(None, "shard"),
            P("shard"),
        ),
        out_specs=(
            P(("rep", "shard"), None),
            P(("rep", "shard"), None),
            P(("rep", "shard"), None),
            P("shard", None),
            P("shard", None),
            P("shard", None),
            P("shard", None),
            P("shard", None),
            P("shard", None),
            P("shard", None),
            P(None, "shard"),
            P(None, "shard"),
            P(None, "shard"),
            P("shard"),
        ),
        check_vma=False,
    )
```

```python
import functools

import jax
import jax.numpy as jnp
from jax import lax
from jax.experimental import pallas as pl
from jax.experimental.pallas import tpu as pltpu
from jax.sharding import PartitionSpec as P

D = 1024
H = 16
HD = 64
SEQ = 2048
PAIR = 2 * HD

EPS = 1e-05
NEGATIVE = -1e30
SCALE = HD**-0.5
BLOCK = 512
GELU = 0.7978845608028654
LITTLE = pl.CostEstimate(flops=1000, bytes_accessed=1000, transcendentals=0)


def norm_apply(rows, gain, shift):
    mean_rows = jnp.mean(rows, axis=-1, keepdims=True)
    centered = rows - mean_rows
    inverse = lax.rsqrt(jnp.mean(centered * centered, axis=-1, keepdims=True) + EPS)
    return centered * inverse * gain + shift


def gelu_apply(values):
    return jax.nn.gelu(values, approximate=True)


def column_sums(rows):
    return jnp.sum(rows, axis=0, dtype=jnp.float32)


def low(values):
    return values.astype(jnp.bfloat16)


def dot(left, right):
    return jnp.dot(left, right, preferred_element_type=jnp.float32)


def dot_nt(left, right):
    return lax.dot_general(left, right, (((1,), (1,)), ((), ())), preferred_element_type=jnp.float32)


def dot_tn(left, right):
    return lax.dot_general(left, right, (((0,), (0,)), ((), ())), preferred_element_type=jnp.float32)


def after(value, *earlier):
    return lax.optimization_barrier((value, earlier))[0]


def head_halves(rows, scale=None):
    lane = lax.broadcasted_iota(jnp.int32, rows.shape, 1)
    if scale is not None:
        rows = rows * jnp.asarray(scale, rows.dtype)
    zero = jnp.zeros_like(rows)
    return jnp.where(lane < HD, rows, zero), jnp.where(lane < HD, zero, rows)


def self_forward_kernel(ends, q_ref, k_ref, v_ref, seg_col, seg_row, low_ref, full_ref, lse_ref):
    step = pl.program_id(0)
    rows = q_ref.shape[0]
    queries = head_halves(q_ref[...], SCALE)
    query_seg = seg_row[...]
    last_seg = ends[1, step]

    def piece(index, state, masked, diagonal):
        place = pl.ds(pl.multiple_of(index * rows, rows), rows)
        keys = k_ref[place, :]
        values = v_ref[place, :]
        keep = None
        if masked:
            keep = seg_col[place, :] == query_seg
            if diagonal:
                key_pos = lax.broadcasted_iota(jnp.int32, (rows, rows), 0)
                query_pos = lax.broadcasted_iota(jnp.int32, (rows, rows), 1)
                keep = keep & (key_pos <= query_pos)
        after_piece = []
        for head in range(2):
            top, total, acc = state[head]
            scores = dot_nt(keys, queries[head])
            if masked:
                scores = jnp.where(keep, scores, NEGATIVE)
            top_new = jnp.maximum(top, jnp.max(scores, axis=0, keepdims=True))
            expo = jnp.exp(scores - top_new)
            fade = jnp.exp(top - top_new)
            after_piece.append(
                (
                    top_new,
                    total * fade + jnp.sum(expo, axis=0, keepdims=True),
                    acc * fade + dot_tn(values, low(expo)),
                )
            )
        return tuple(after_piece)

    def before(index, state):
        return lax.cond(
            ends[0, index] == last_seg,
            lambda s: piece(index, s, False, False),
            lambda s: piece(index, s, True, False),
            state,
        )

    blank = (
        jnp.full((1, rows), NEGATIVE, jnp.float32),
        jnp.zeros((1, rows), jnp.float32),
        jnp.zeros((PAIR, rows), jnp.float32),
    )
    state = lax.fori_loop(0, step, before, (blank, blank))
    state = piece(step, state, True, True)
    parts = [
        (state[head][2] * (1.0 / state[head][1]))[head * HD : (head + 1) * HD] for head in range(2)
    ]
    joined = jnp.concatenate(parts, axis=0).T
    full_ref[...] = joined
    low_ref[...] = low(joined)
    lse_ref[0:1, :] = state[0][0] + jnp.log(state[0][1])
    lse_ref[1:2, :] = state[1][0] + jnp.log(state[1][1])


def block_ends(segments, rows):
    return jnp.stack([segments[::rows], segments[rows - 1 :: rows]])


def self_forward(qkv, segments):
    count = qkv.shape[0]
    rows = BLOCK
    col = segments[:, None]
    row = segments[None, :]
    grid_spec = pltpu.PrefetchScalarGridSpec(
        num_scalar_prefetch=1,
        grid=(count // rows,),
        in_specs=[
            pl.BlockSpec((rows, PAIR), lambda i, e: (i, 0)),
            pl.BlockSpec((count, PAIR), lambda i, e: (0, 1)),
            pl.BlockSpec((count, PAIR), lambda i, e: (0, 2)),
            pl.BlockSpec((count, 1), lambda i, e: (0, 0)),
            pl.BlockSpec((1, rows), lambda i, e: (0, i)),
        ],
        out_specs=[
            pl.BlockSpec((rows, PAIR), lambda i, e: (i, 0)),
            pl.BlockSpec((rows, PAIR), lambda i, e: (i, 0)),
            pl.BlockSpec((2, rows), lambda i, e: (0, i)),
        ],
    )
    return pl.pallas_call(
        self_forward_kernel,
        grid_spec=grid_spec,
        out_shape=(
            jax.ShapeDtypeStruct((count, PAIR), jnp.bfloat16),
            jax.ShapeDtypeStruct((count, PAIR), jnp.float32),
            jax.ShapeDtypeStruct((2, count), jnp.float32),
        ),
        compiler_params=pltpu.CompilerParams(vmem_limit_bytes=58 * 2**20),
        cost_estimate=LITTLE,
    )(block_ends(segments, rows), qkv, qkv, qkv, col, row)


def self_backward_kernel(
    ends, q_ref, k_ref, v_ref, go_ref, lse_ref, o_ref, seg_col, seg_row, grad_ref, acc_q, acc_k, acc_v, delta_ref
):
    step = pl.program_id(0)
    blocks = pl.num_programs(0)
    rows = k_ref.shape[0]

    @pl.when(step == 0)
    def _():
        acc_q[...] = jnp.zeros_like(acc_q)
        lane = lax.broadcasted_iota(jnp.int32, (8, PAIR), 1) // HD
        pick = (lane == lax.broadcasted_iota(jnp.int32, (8, PAIR), 0)).astype(jnp.float32)
        delta_ref[...] = lax.dot_general(
            pick,
            go_ref[...].astype(jnp.float32) * o_ref[...],
            (((1,), (1,)), ((), ())),
            precision=lax.Precision.HIGHEST,
            preferred_element_type=jnp.float32,
        )

    keys = k_ref[...]
    values = v_ref[...]
    key_halves = head_halves(keys, SCALE)
    key_seg = seg_col[...]
    first_seg = ends[0, step]

    def piece(index, masked, diagonal):
        place = pl.ds(pl.multiple_of(index * rows, rows), rows)
        queries = head_halves(q_ref[place, :], SCALE)
        grads = head_halves(go_ref[place, :])
        keep = None
        if masked:
            keep = seg_row[:, place] == key_seg
            if diagonal:
                key_pos = lax.broadcasted_iota(jnp.int32, (rows, rows), 0)
                query_pos = lax.broadcasted_iota(jnp.int32, (rows, rows), 1)
                keep = keep & (key_pos <= query_pos)
        sum_q = sum_k = sum_v = None
        for head in range(2):
            scores = dot_nt(keys, queries[head])
            probs = jnp.exp(scores - lse_ref[head : head + 1, place])
            if masked:
                probs = jnp.where(keep, probs, 0.0)
            part_v = dot(low(probs), grads[head])
            grad_probs = dot_nt(values, grads[head])
            grad_scores = low(probs * (grad_probs - delta_ref[head : head + 1, place]))
            part_k = dot(grad_scores, queries[head])
            part_q = dot_tn(key_halves[head], grad_scores)
            sum_q = part_q if sum_q is None else sum_q + part_q
            sum_k = part_k if sum_k is None else sum_k + part_k
            sum_v = part_v if sum_v is None else sum_v + part_v
        acc_q[:, place] += sum_q
        if diagonal:
            acc_k[...] = sum_k
            acc_v[...] = sum_v
        else:
            acc_k[...] += sum_k
            acc_v[...] += sum_v

    piece(step, True, True)

    @pl.loop(step + 1, blocks)
    def _(index):
        whole = ends[1, index] == first_seg

        @pl.when(whole)
        def _():
            piece(index, False, False)

        @pl.when(jnp.logical_not(whole))
        def _():
            piece(index, True, False)

    own = pl.ds(pl.multiple_of(step * rows, rows), rows)
    grad_ref[own, 0:PAIR] = low(acc_q[:, own].T)
    grad_ref[own, PAIR : 2 * PAIR] = low(acc_k[...])
    grad_ref[own, 2 * PAIR : 3 * PAIR] = low(acc_v[...])


def self_backward(qkv, grad_att, lse, attended, segments):
    count = qkv.shape[0]
    rows = BLOCK
    col = segments[:, None]
    row = segments[None, :]
    whole = lambda i, e: (0, 0)
    grid_spec = pltpu.PrefetchScalarGridSpec(
        num_scalar_prefetch=1,
        grid=(count // rows,),
        in_specs=[
            pl.BlockSpec((count, PAIR), whole),
            pl.BlockSpec((rows, PAIR), lambda i, e: (i, 1)),
            pl.BlockSpec((rows, PAIR), lambda i, e: (i, 2)),
            pl.BlockSpec((count, PAIR), whole),
            pl.BlockSpec((2, count), whole),
            pl.BlockSpec((count, PAIR), whole),
            pl.BlockSpec((rows, 1), lambda i, e: (i, 0)),
            pl.BlockSpec((1, count), whole),
        ],
        out_specs=pl.BlockSpec((count, 3 * PAIR), whole),
        scratch_shapes=[
            pltpu.VMEM((PAIR, count), jnp.float32),
            pltpu.VMEM((rows, PAIR), jnp.float32),
            pltpu.VMEM((rows, PAIR), jnp.float32),
            pltpu.VMEM((8, count), jnp.float32),
        ],
    )
    return pl.pallas_call(
        self_backward_kernel,
        grid_spec=grid_spec,
        out_shape=jax.ShapeDtypeStruct((count, 3 * PAIR), jnp.bfloat16),
        compiler_params=pltpu.CompilerParams(vmem_limit_bytes=58 * 2**20),
        cost_estimate=pl.CostEstimate(flops=16 * 10**9, bytes_accessed=4 * 2**20, transcendentals=0),
    )(block_ends(segments, rows), qkv, qkv, qkv, grad_att, lse, attended, col, row)


def cross_forward_kernel(length, q_ref, m_ref, out_ref):
    queries = head_halves(q_ref[...], SCALE)
    keys = m_ref[:, :PAIR]
    values = m_ref[:, PAIR:]
    shape = (q_ref.shape[0], m_ref.shape[0])
    keep = lax.broadcasted_iota(jnp.int32, shape, 1) < length[0]
    parts = []
    for head in range(2):
        scores = jnp.where(keep, dot_nt(queries[head], keys), NEGATIVE)
        expo = jnp.exp(scores - jnp.max(scores, axis=1, keepdims=True))
        parts.append(dot(low(expo), values) / jnp.sum(expo, axis=1, keepdims=True))
    lane = lax.broadcasted_iota(jnp.int32, parts[0].shape, 1)
    out_ref[...] = low(jnp.where(lane < HD, parts[0], parts[1]))


def cross_forward(queries, memory, length):
    count, states = queries.shape[0], memory.shape[0] // (D // PAIR)
    grid_spec = pltpu.PrefetchScalarGridSpec(
        num_scalar_prefetch=1,
        grid=(D // PAIR,),
        in_specs=[
            pl.BlockSpec((count, PAIR), lambda i, e: (0, i)),
            pl.BlockSpec((states, 2 * PAIR), lambda i, e: (i, 0)),
        ],
        out_specs=pl.BlockSpec((count, PAIR), lambda i, e: (0, i)),
    )
    return pl.pallas_call(
        cross_forward_kernel,
        grid_spec=grid_spec,
        out_shape=jax.ShapeDtypeStruct((count, D), jnp.bfloat16),
        cost_estimate=LITTLE,
    )(length, queries, memory)


def cross_backward_kernel(length, q_ref, m_ref, g_ref, dq_ref, dm_ref):
    queries = head_halves(q_ref[...], SCALE)
    grads = head_halves(g_ref[...])
    keys = m_ref[:, :PAIR]
    values = m_ref[:, PAIR:]
    key_halves = head_halves(keys, SCALE)
    shape = (m_ref.shape[0], q_ref.shape[0])
    keep = lax.broadcasted_iota(jnp.int32, shape, 0) < length[0]
    sum_q = sum_k = sum_v = None
    for head in range(2):
        scores = jnp.where(keep, dot_nt(keys, queries[head]), NEGATIVE)
        expo = jnp.exp(scores - jnp.max(scores, axis=0, keepdims=True))
        probs = expo * (1.0 / jnp.sum(expo, axis=0, keepdims=True))
        part_v = dot(low(probs), grads[head])
        grad_probs = dot_nt(values, grads[head])
        inner = jnp.sum(probs * grad_probs, axis=0, keepdims=True)
        grad_scores = low(probs * (grad_probs - inner))
        part_k = dot(grad_scores, queries[head])
        part_q = dot_tn(grad_scores, key_halves[head])
        sum_q = part_q if sum_q is None else sum_q + part_q
        sum_k = part_k if sum_k is None else sum_k + part_k
        sum_v = part_v if sum_v is None else sum_v + part_v
    dq_ref[...] = low(sum_q)
    dm_ref[:, :PAIR] = low(sum_k)
    dm_ref[:, PAIR:] = low(sum_v)


def cross_backward(queries, memory, grads, length):
    count, states = queries.shape[0], memory.shape[0] // (D // PAIR)
    grid_spec = pltpu.PrefetchScalarGridSpec(
        num_scalar_prefetch=1,
        grid=(D // PAIR,),
        in_specs=[
            pl.BlockSpec((count, PAIR), lambda i, e: (0, i)),
            pl.BlockSpec((states, 2 * PAIR), lambda i, e: (i, 0)),
            pl.BlockSpec((count, PAIR), lambda i, e: (0, i)),
        ],
        out_specs=[
            pl.BlockSpec((count, PAIR), lambda i, e: (0, i)),
            pl.BlockSpec((states, 2 * PAIR), lambda i, e: (i, 0)),
        ],
    )
    return pl.pallas_call(
        cross_backward_kernel,
        grid_spec=grid_spec,
        out_shape=(
            jax.ShapeDtypeStruct((count, D), jnp.bfloat16),
            jax.ShapeDtypeStruct((states * (D // PAIR), 2 * PAIR), jnp.bfloat16),
        ),
        cost_estimate=LITTLE,
    )(length, queries, memory, grads)


def front_kernel(x_ref, gain, shift, qkv_w, qkv_b, one_ref, qkv_ref):
    rows = x_ref[...].astype(jnp.float32)
    centered = rows - jnp.mean(rows, axis=-1, keepdims=True)
    inverse = lax.rsqrt(jnp.mean(centered * centered, axis=-1, keepdims=True) + EPS)
    one = low(centered * inverse * gain[...] + shift[...])
    one_ref[...] = one
    qkv_ref[...] = low(dot(one, qkv_w[...]) + qkv_b[...])


def front(rows, gain, shift, qkv_w, qkv_b):
    count, tile = rows.shape[0], 256
    whole = lambda i: (0, 0)
    block = lambda i: (i, 0)
    return pl.pallas_call(
        front_kernel,
        grid=(count // tile,),
        in_specs=[
            pl.BlockSpec((tile, D), block),
            pl.BlockSpec((1, D), whole),
            pl.BlockSpec((1, D), whole),
            pl.BlockSpec(qkv_w.shape, whole),
            pl.BlockSpec((1, qkv_w.shape[1]), whole),
        ],
        out_specs=[pl.BlockSpec((tile, D), block), pl.BlockSpec((tile, qkv_w.shape[1]), block)],
        out_shape=(
            jax.ShapeDtypeStruct((count, D), jnp.bfloat16),
            jax.ShapeDtypeStruct((count, qkv_w.shape[1]), jnp.bfloat16),
        ),
        compiler_params=pltpu.CompilerParams(vmem_limit_bytes=58 * 2**20),
        cost_estimate=LITTLE,
    )(rows, gain[None], shift[None], qkv_w, qkv_b[None])


def feed_kernel(x_ref, w_ref, b_ref, ga_ref, act_ref, pre_ref, in_ref, sum_ref):
    v = dot(x_ref[...], w_ref[...]) + b_ref[...]
    square = v * v
    half = 0.5 + 0.5 * jnp.tanh(v * (GELU + GELU * 0.044715 * square))
    act_ref[...] = low(v * half)
    slope = half + (v * half) * (1.0 - half) * (2.0 * GELU + 6.0 * GELU * 0.044715 * square)
    grad = low(ga_ref[...] * slope)
    pre_ref[...] = grad
    in_ref[...] = low(dot_nt(grad, w_ref[...]))

    @pl.when(pl.program_id(0) == 0)
    def _():
        sum_ref[...] = jnp.zeros_like(sum_ref)

    sum_ref[...] += jnp.sum(grad.astype(jnp.float32), axis=0, keepdims=True)


def feed(rows, weight, bias, grad_act):
    count, hidden = grad_act.shape
    tile = 512
    whole = lambda i: (0, 0)
    block = lambda i: (i, 0)
    return pl.pallas_call(
        feed_kernel,
        grid=(count // tile,),
        in_specs=[
            pl.BlockSpec((tile, D), block),
            pl.BlockSpec((D, hidden), whole),
            pl.BlockSpec((1, hidden), whole),
            pl.BlockSpec((tile, hidden), block),
        ],
        out_specs=[
            pl.BlockSpec((tile, hidden), block),
            pl.BlockSpec((tile, hidden), block),
            pl.BlockSpec((tile, D), block),
            pl.BlockSpec((1, hidden), whole),
        ],
        out_shape=(
            jax.ShapeDtypeStruct((count, hidden), jnp.bfloat16),
            jax.ShapeDtypeStruct((count, hidden), jnp.bfloat16),
            jax.ShapeDtypeStruct((count, D), jnp.bfloat16),
            jax.ShapeDtypeStruct((1, hidden), jnp.float32),
        ),
        compiler_params=pltpu.CompilerParams(vmem_limit_bytes=58 * 2**20),
        cost_estimate=LITTLE,
    )(rows, weight, bias[None], grad_act)


def expand_kernel(replica, x_ref, g_ref, *refs):
    keep, outs = refs[-1], refs[:-1]
    size, rows = len(outs), outs[0].shape[1]
    owners = x_ref.shape[1] // (size * rows)
    keep[...] = low(dot_tn(x_ref[...], g_ref[...])).reshape(keep.shape)
    step = pl.program_id(0) * owners
    for owner in range(owners):
        for other, out in enumerate(outs):
            out[pl.ds(step + owner, 1)] = keep[owner, pl.ds(replica[0] ^ other, 1)]


def expand_grads(rows_in, grads, owners, part_rows):
    size, me = lax.axis_size("rep"), lax.axis_index("rep")
    count, hidden = grads.shape
    if part_rows % 16:
        full = low(dot_tn(rows_in, grads)).reshape(owners, size, part_rows, hidden)
        return [lax.dynamic_index_in_dim(full, me ^ step, 1, keepdims=False) for step in range(size)]
    tile = 2
    grid_spec = pltpu.PrefetchScalarGridSpec(
        num_scalar_prefetch=1,
        grid=(owners // tile,),
        in_specs=[
            pl.BlockSpec((count, tile * size * part_rows), lambda i, e: (0, i)),
            pl.BlockSpec((count, hidden), lambda i, e: (0, 0)),
        ],
        out_specs=[pl.BlockSpec((owners, part_rows, hidden), lambda i, e: (0, 0, 0))] * size,
        scratch_shapes=[pltpu.VMEM((tile, size, part_rows, hidden), jnp.bfloat16)],
    )
    return pl.pallas_call(
        expand_kernel,
        grid_spec=grid_spec,
        out_shape=(jax.ShapeDtypeStruct((owners, part_rows, hidden), jnp.bfloat16),) * size,
        compiler_params=pltpu.CompilerParams(vmem_limit_bytes=58 * 2**20),
        cost_estimate=LITTLE,
    )(me[None], rows_in, grads)


def shrink_kernel(replica, a_ref, g_ref, *outs):
    for step, out in enumerate(outs):

        @pl.when(pl.program_id(0) == step)
        def _():
            out[...] = low(dot_tn(a_ref[...], g_ref[...]))


def shrink_grads(act, grads):
    size, me = lax.axis_size("rep"), lax.axis_index("rep")
    count, hidden = act.shape
    part = hidden // size
    if part % 128:
        full = low(dot_tn(act, grads)).reshape(size, part, D)
        return [lax.dynamic_index_in_dim(full, me ^ step, 0, keepdims=False) for step in range(size)]
    grid_spec = pltpu.PrefetchScalarGridSpec(
        num_scalar_prefetch=1,
        grid=(size,),
        in_specs=[
            pl.BlockSpec((count, part), lambda i, e: (0, e[0] ^ i)),
            pl.BlockSpec((count, D), lambda i, e: (0, 0)),
        ],
        out_specs=[pl.BlockSpec((part, D), lambda i, e: (0, 0))] * size,
    )
    return pl.pallas_call(
        shrink_kernel,
        grid_spec=grid_spec,
        out_shape=(jax.ShapeDtypeStruct((part, D), jnp.bfloat16),) * size,
        compiler_params=pltpu.CompilerParams(vmem_limit_bytes=58 * 2**20),
        cost_estimate=LITTLE,
    )(me[None], act, grads)


def product_kernel(a_ref, b_ref, out_ref):
    out_ref[...] = low(dot(a_ref[...], b_ref[...]))


def product(left, right):
    count, depth = left.shape
    tile = 512
    return pl.pallas_call(
        product_kernel,
        grid=(count // tile,),
        in_specs=[pl.BlockSpec((tile, depth), lambda i: (i, 0)), pl.BlockSpec(right.shape, lambda i: (0, 0))],
        out_specs=pl.BlockSpec((tile, right.shape[1]), lambda i: (i, 0)),
        out_shape=jax.ShapeDtypeStruct((count, right.shape[1]), jnp.bfloat16),
        compiler_params=pltpu.CompilerParams(vmem_limit_bytes=58 * 2**20),
        cost_estimate=LITTLE,
    )(left, right)


def back_kernel(g_ref, w_ref, one_ref, out_ref, sum_ref, own_ref):
    @pl.when(pl.program_id(0) == 0)
    def _():
        sum_ref[...] = jnp.zeros_like(sum_ref)
        own_ref[...] = jnp.zeros_like(own_ref)

    grads = dot_nt(g_ref[...], w_ref[...])
    out_ref[...] = low(grads)
    sum_ref[0:1, :] += jnp.sum(grads * one_ref[...].astype(jnp.float32), axis=0, keepdims=True)
    sum_ref[1:2, :] += jnp.sum(grads, axis=0, keepdims=True)
    own_ref[...] += jnp.sum(g_ref[...].astype(jnp.float32), axis=0, keepdims=True)


def back(grads, weight, rows_in):
    count, width = grads.shape
    tile = 256
    return pl.pallas_call(
        back_kernel,
        grid=(count // tile,),
        in_specs=[
            pl.BlockSpec((tile, width), lambda i: (i, 0)),
            pl.BlockSpec(weight.shape, lambda i: (0, 0)),
            pl.BlockSpec((tile, D), lambda i: (i, 0)),
        ],
        out_specs=[
            pl.BlockSpec((tile, D), lambda i: (i, 0)),
            pl.BlockSpec((2, D), lambda i: (0, 0)),
            pl.BlockSpec((1, width), lambda i: (0, 0)),
        ],
        out_shape=(
            jax.ShapeDtypeStruct((count, D), jnp.bfloat16),
            jax.ShapeDtypeStruct((2, D), jnp.float32),
            jax.ShapeDtypeStruct((1, width), jnp.float32),
        ),
        compiler_params=pltpu.CompilerParams(vmem_limit_bytes=58 * 2**20),
        cost_estimate=LITTLE,
    )(grads, weight, rows_in)


def heads_grads_kernel(x_ref, g_ref, e_ref, m_ref, out_ref):
    width = g_ref.shape[1]
    shape = out_ref.shape[1:3]
    for owner in range(shape[0]):
        place = slice(owner * x_ref.shape[1] // shape[0], (owner + 1) * x_ref.shape[1] // shape[0])
        left = low(dot_tn(x_ref[:, place], g_ref[...]))
        right = low(dot_tn(e_ref[:, place], m_ref[...]))
        for replica in range(out_ref.shape[0]):
            rows = slice(replica * shape[1], (replica + 1) * shape[1])
            out_ref[replica, owner, :, :width] = left[rows, :]
            out_ref[replica, owner, :, width:] = right[rows, :]


def heads_grads(rows_in, grads, enc, enc_grads, owners, part_rows):
    size = lax.axis_size("rep")
    width, enc_width = grads.shape[1], enc_grads.shape[1]
    if part_rows % 16:
        both = low(jnp.concatenate([dot_tn(rows_in, grads), dot_tn(enc, enc_grads)], axis=1))
        return both.reshape(owners, size, part_rows, width + enc_width).transpose(1, 0, 2, 3)
    tile = 2
    return pl.pallas_call(
        heads_grads_kernel,
        grid=(owners // tile,),
        in_specs=[
            pl.BlockSpec((rows_in.shape[0], tile * size * part_rows), lambda i: (0, i)),
            pl.BlockSpec(grads.shape, lambda i: (0, 0)),
            pl.BlockSpec((enc.shape[0], tile * size * part_rows), lambda i: (0, i)),
            pl.BlockSpec(enc_grads.shape, lambda i: (0, 0)),
        ],
        out_specs=pl.BlockSpec((size, tile, part_rows, width + enc_width), lambda i: (0, i, 0, 0)),
        out_shape=jax.ShapeDtypeStruct((size, owners, part_rows, width + enc_width), jnp.bfloat16),
        compiler_params=pltpu.CompilerParams(vmem_limit_bytes=58 * 2**20),
        cost_estimate=LITTLE,
    )(rows_in, grads, enc, enc_grads)


def last_kernel(x_ref, e_ref, one_ref, gain, out_ref):
    rows = x_ref[...].astype(jnp.float32)
    centered = rows - jnp.mean(rows, axis=-1, keepdims=True)
    inverse = lax.rsqrt(jnp.mean(centered * centered, axis=-1, keepdims=True) + EPS)
    x_hat = centered * inverse
    grads = e_ref[...].astype(jnp.float32) * gain[...]
    inner = jnp.mean(grads * x_hat, axis=-1, keepdims=True)
    out_ref[...] = one_ref[...] + inverse * (grads - jnp.mean(grads, axis=-1, keepdims=True) - x_hat * inner)


def last(rows, grads, grad_one, gain):
    count = rows.shape[0]
    tile = 128
    block = pl.BlockSpec((tile, D), lambda i: (i, 0))
    return pl.pallas_call(
        last_kernel,
        grid=(count // tile,),
        in_specs=[block, block, block, pl.BlockSpec((1, D), lambda i: (0, 0))],
        out_specs=block,
        out_shape=jax.ShapeDtypeStruct((count, D), jnp.float32),
        cost_estimate=LITTLE,
    )(rows, grads, grad_one, gain[None])


def rep_send(value, step):
    size = lax.axis_size("rep")
    return lax.ppermute(value, "rep", [(i, i ^ step) for i in range(size)])


def rep_start(value):
    return [value] + [rep_send(value, step) for step in range(1, lax.axis_size("rep"))]


def rep_place(parts, axis):
    size, me = lax.axis_size("rep"), lax.axis_index("rep")
    value = parts[0]
    out = jnp.zeros(value.shape[:axis] + (size,) + value.shape[axis:], value.dtype)
    for step, part in enumerate(parts):
        out = lax.dynamic_update_slice_in_dim(out, jnp.expand_dims(part, axis), me ^ step, axis)
    return out


def spread_kernel(place, *refs):
    out_ref = refs[-1]
    for step, part in enumerate(refs[:-1]):
        out_ref[pl.ds(place[0] ^ step, 1)] = part[...].astype(out_ref.dtype)[None]


def spread(parts, first, last, dtype):
    size, columns = len(parts), parts[0].shape[1]
    rows = last - first
    if rows % 32 or first % rows or parts[0].shape[0] % 16:
        return rep_place([part[first:last] for part in parts], 0).astype(dtype)
    tile = rows // 2
    grid_spec = pltpu.PrefetchScalarGridSpec(
        num_scalar_prefetch=1,
        grid=(2,),
        in_specs=[pl.BlockSpec((tile, columns), lambda i, e: (first // tile + i, 0))] * size,
        out_specs=pl.BlockSpec((size, tile, columns), lambda i, e: (0, i, 0)),
    )
    return pl.pallas_call(
        spread_kernel,
        grid_spec=grid_spec,
        out_shape=jax.ShapeDtypeStruct((size, rows, columns), dtype),
        compiler_params=pltpu.CompilerParams(vmem_limit_bytes=58 * 2**20),
        cost_estimate=LITTLE,
    )(lax.axis_index("rep")[None], *parts)


def rep_gather(value, axis):
    return rep_place(rep_start(value), axis)


def rep_swap(parts):
    return lax.all_to_all(parts, "rep", 0, 0, tiled=True)


def rep_split(parts, axis):
    size, me = lax.axis_size("rep"), lax.axis_index("rep")
    picks = [lax.dynamic_index_in_dim(parts, me ^ step, axis, keepdims=False) for step in range(size)]
    return [picks[0]] + [rep_send(low(picks[step]), step) for step in range(1, size)]


def sum_first(parts):
    return low(jnp.sum(parts.astype(jnp.float32), axis=0))


def add_up(parts):
    total = parts[0].astype(jnp.float32)
    for part in parts[1:]:
        total = total + part.astype(jnp.float32)
    return low(total)


def rep_reduce(parts, axis):
    return add_up(rep_split(parts, axis))


def core_send(value):
    size = lax.axis_size("shard")
    return lax.ppermute(value, "shard", [(i, i ^ 1) for i in range(size)])


def line_send(value, step, group=None):
    size = lax.axis_size("shard")
    group = group or size
    route = [(i, i // group * group + (i + 2 * step) % group) for i in range(size)]
    return lax.ppermute(value, "shard", route)


def line_scatter_start(value, group=None):
    group = group or lax.axis_size("shard")
    core = lax.axis_index("shard") % 2
    value = value.reshape((group // 2, 2, value.shape[0] // group) + value.shape[1:])
    mine = lax.dynamic_index_in_dim(value, core, 1, keepdims=False)
    theirs = lax.dynamic_index_in_dim(value, 1 - core, 1, keepdims=False)
    return [mine, core_send(theirs)]


def line_scatter_middle(both, group=None):
    group = group or lax.axis_size("shard")
    chips = group // 2
    chip = lax.axis_index("shard") % group // 2
    line = add_up(both)
    parts = [lax.dynamic_index_in_dim(line, (chip + step) % chips, 0, keepdims=False) for step in range(chips)]
    return [parts[0]] + [line_send(parts[step], step, group) for step in range(1, chips)]


def kinds_kernel(place, *refs):
    outs = refs[-3:]
    rows = outs[0].shape[1]
    for step, part in enumerate(refs[:-3]):
        for kind, out in enumerate(outs):
            out[pl.ds(place[0] ^ step, 1)] = part[kind * rows : (kind + 1) * rows, :].astype(out.dtype)[None]


def spread_kinds(parts, rows):
    size = len(parts)
    if rows % 16:
        return [rep_place([part[k * rows : (k + 1) * rows] for part in parts], 0).astype(jnp.float32) for k in range(3)]
    whole = lambda i, e: (0, 0)
    grid_spec = pltpu.PrefetchScalarGridSpec(
        num_scalar_prefetch=1,
        grid=(1,),
        in_specs=[pl.BlockSpec(parts[0].shape, whole)] * size,
        out_specs=[pl.BlockSpec((size, rows, D), lambda i, e: (0, 0, 0))] * 3,
    )
    return pl.pallas_call(
        kinds_kernel,
        grid_spec=grid_spec,
        out_shape=(jax.ShapeDtypeStruct((size, rows, D), jnp.float32),) * 3,
        cost_estimate=LITTLE,
    )(lax.axis_index("rep")[None], *parts)


def columns_kernel(place, *refs):
    out_ref = refs[-1]
    rows = out_ref.shape[1]
    for step, part in enumerate(refs[:-1]):
        for block in range(part.shape[0] // rows):
            wide = part[block * rows : (block + 1) * rows, :].astype(out_ref.dtype)
            out_ref[pl.ds(place[0] ^ step, 1), :, block * D : (block + 1) * D] = wide[None]


def spread_columns(parts, first, blocks, rows):
    size, me = len(parts), lax.axis_index("rep")
    if rows % 16:
        parts = [part[first:].reshape(blocks, rows, -1).transpose(1, 0, 2).reshape(rows, -1) for part in parts]
        return rep_place(parts, 0).astype(jnp.float32).reshape(size * rows, -1)
    halves = 2
    taken = blocks * rows // halves
    grid_spec = pltpu.PrefetchScalarGridSpec(
        num_scalar_prefetch=1,
        grid=(halves,),
        in_specs=[pl.BlockSpec((taken, D), lambda i, e: (first // taken + i, 0))] * size,
        out_specs=pl.BlockSpec((size, rows, blocks * D // halves), lambda i, e: (0, 0, i)),
    )
    out = pl.pallas_call(
        columns_kernel,
        grid_spec=grid_spec,
        out_shape=jax.ShapeDtypeStruct((size, rows, blocks * D), jnp.float32),
        compiler_params=pltpu.CompilerParams(vmem_limit_bytes=58 * 2**20),
        cost_estimate=LITTLE,
    )(me[None], *parts)
    return out.reshape(size * rows, blocks * D)


def heads_kernel(span, place, *refs):
    qkv_ref, memory_ref = refs[-2:]
    rows, width = qkv_ref.shape[1], D // span
    for step, part in enumerate(refs[:-2]):
        take = pl.ds(place[0] ^ step, 1)
        for block in range(span):
            wide = part[block * rows : (block + 1) * rows, :].astype(jnp.float32)[None]
            for kind in range(5):
                out, at = (qkv_ref, kind) if kind < 3 else (memory_ref, kind - 3)
                columns = slice(at * D + block * width, at * D + (block + 1) * width)
                out[take, :, columns] = wide[:, :, kind * width : (kind + 1) * width]


def spread_heads(parts, span, rows, width):
    size, me = len(parts), lax.axis_index("rep")
    if rows % 16:
        full = rep_place([part[: span * rows].reshape(span, rows, 5, width) for part in parts], 0)
        full = full.transpose(0, 2, 3, 1, 4).reshape(size * rows, 5 * D).astype(jnp.float32)
        return full[:, : 3 * D], full[:, 3 * D :]
    grid_spec = pltpu.PrefetchScalarGridSpec(
        num_scalar_prefetch=1,
        grid=(1,),
        in_specs=[pl.BlockSpec((span * rows, 5 * width), lambda i, e: (0, 0))] * size,
        out_specs=[
            pl.BlockSpec((size, rows, 3 * D), lambda i, e: (0, 0, 0)),
            pl.BlockSpec((size, rows, 2 * D), lambda i, e: (0, 0, 0)),
        ],
    )
    qkv, memory = pl.pallas_call(
        functools.partial(heads_kernel, span),
        grid_spec=grid_spec,
        out_shape=(
            jax.ShapeDtypeStruct((size, rows, 3 * D), jnp.float32),
            jax.ShapeDtypeStruct((size, rows, 2 * D), jnp.float32),
        ),
        compiler_params=pltpu.CompilerParams(vmem_limit_bytes=58 * 2**20),
        cost_estimate=LITTLE,
    )(me[None], *parts)
    return qkv.reshape(size * rows, 3 * D), memory.reshape(size * rows, 2 * D)


def line_start(piece):
    return [piece] + [line_send(piece, step) for step in range(1, lax.axis_size("shard") // 2)]


def line_place(parts):
    chips, chip = len(parts), lax.axis_index("shard") // 2
    kinds, rows, columns = parts[0].shape
    line = jnp.zeros((kinds, chips, rows, columns), parts[0].dtype)
    for step, part in enumerate(parts):
        line = lax.dynamic_update_slice_in_dim(line, part[:, None], (chip - step) % chips, 1)
    return line


def join_kernel(place, *refs):
    outs = refs[-3:]
    parts = refs[:-3]
    size = len(parts) // 2
    for core in range(2):
        side = place[1] ^ core
        for step in range(size):
            for kind in range(3):
                outs[kind][0, pl.ds(side, 1), pl.ds(place[0] ^ step, 1)] = parts[core * size + step][kind][None]


def weight_join(mine, other):
    size = len(mine)
    _, chips, rows, _ = mine[0].shape
    core = lax.axis_index("shard") % 2
    if rows % 16:
        first = core == 0
        plane, next_plane = rep_place(mine, 2), rep_place(other, 2)
        low_core, high_core = jnp.where(first, plane, next_plane), jnp.where(first, next_plane, plane)
        full = jnp.stack([low_core, high_core], axis=2).reshape(3, D, D)
        return full[0], full[1], full[2]
    grid_spec = pltpu.PrefetchScalarGridSpec(
        num_scalar_prefetch=1,
        grid=(chips,),
        in_specs=[pl.BlockSpec((3, 1, rows, D), lambda i, e: (0, i, 0, 0))] * (2 * size),
        out_specs=[pl.BlockSpec((1, 2, size, rows, D), lambda i, e: (i, 0, 0, 0, 0))] * 3,
    )
    outs = pl.pallas_call(
        join_kernel,
        grid_spec=grid_spec,
        out_shape=(jax.ShapeDtypeStruct((chips, 2, size, rows, D), jnp.bfloat16),) * 3,
        compiler_params=pltpu.CompilerParams(vmem_limit_bytes=58 * 2**20),
        cost_estimate=LITTLE,
    )(jnp.stack([lax.axis_index("rep"), core]), *mine, *other)
    return tuple(out.reshape(D, D) for out in outs)


def plain_kernel(core, a_ref, b_ref, c_ref, ga_ref, gb_ref, gc_ref, mine_ref, theirs_ref):
    width = a_ref.shape[1] // 2
    for kind, (left, right) in enumerate(((a_ref, ga_ref), (b_ref, gb_ref), (c_ref, gc_ref))):
        for side, out in enumerate((mine_ref, theirs_ref)):
            place = pl.ds(pl.multiple_of((core[0] ^ side) * width, width), width)
            out[kind, 0] = low(dot_tn(left[:, place], right[...])).reshape(out.shape[2:])


def plain_grads(lefts, rights):
    size, chips = lax.axis_size("rep"), lax.axis_size("shard") // 2
    core = lax.axis_index("shard") % 2
    rows = D // (2 * chips * size)
    if rows % 16:
        stack = jnp.stack([low(dot_tn(left, right)) for left, right in zip(lefts, rights)])
        stack = stack.reshape(3, chips, 2, size, rows, D)
        return [lax.dynamic_index_in_dim(stack, core ^ side, 2, keepdims=False) for side in range(2)]
    count = lefts[0].shape[0]
    grid_spec = pltpu.PrefetchScalarGridSpec(
        num_scalar_prefetch=1,
        grid=(chips,),
        in_specs=[pl.BlockSpec((count, D // chips), lambda i, e: (0, i))] * 3
        + [pl.BlockSpec((count, D), lambda i, e: (0, 0))] * 3,
        out_specs=[pl.BlockSpec((3, 1, size, rows, D), lambda i, e: (0, i, 0, 0, 0))] * 2,
    )
    return pl.pallas_call(
        plain_kernel,
        grid_spec=grid_spec,
        out_shape=(jax.ShapeDtypeStruct((3, chips, size, rows, D), jnp.bfloat16),) * 2,
        compiler_params=pltpu.CompilerParams(vmem_limit_bytes=58 * 2**20),
        cost_estimate=pl.CostEstimate(flops=6 * count * D * D, bytes_accessed=20 * count * D, transcendentals=0),
    )(core[None], *lefts, *rights)


def split_kernel(place, mine_ref, other_ref, *outs):
    for step, out in enumerate(outs):
        take = pl.ds(place[0] ^ step, 1)
        total = mine_ref[:, 0, take].astype(jnp.float32) + other_ref[:, 0, take].astype(jnp.float32)
        out[...] = low(total)


def core_sum_split(mine, other):
    kinds, chips, size, rows, _ = mine.shape
    if rows % 16:
        total = add_up([mine, other])
        me = lax.axis_index("rep")
        return [lax.dynamic_index_in_dim(total, me ^ step, 2, keepdims=False) for step in range(size)]
    grid_spec = pltpu.PrefetchScalarGridSpec(
        num_scalar_prefetch=1,
        grid=(chips,),
        in_specs=[pl.BlockSpec((kinds, 1, size, rows, D), lambda i, e: (0, i, 0, 0, 0))] * 2,
        out_specs=[pl.BlockSpec((kinds, 1, rows, D), lambda i, e: (0, i, 0, 0))] * size,
    )
    return pl.pallas_call(
        split_kernel,
        grid_spec=grid_spec,
        out_shape=(jax.ShapeDtypeStruct((kinds, chips, rows, D), jnp.bfloat16),) * size,
        compiler_params=pltpu.CompilerParams(vmem_limit_bytes=58 * 2**20),
        cost_estimate=LITTLE,
    )(lax.axis_index("rep")[None], mine, other)


def reduce_line(line):
    chips = lax.axis_size("shard") // 2
    chip = lax.axis_index("shard") // 2
    parts = [lax.dynamic_index_in_dim(line, (chip + step) % chips, 1, keepdims=False) for step in range(chips)]
    return [parts[0]] + [line_send(parts[step], step) for step in range(1, chips)]


def shards(
    tokens,
    segments,
    enc_states,
    enc_lengths,
    cotangent,
    self_qkv,
    self_out,
    cross_query,
    cross_memory,
    cross_out,
    expand_weight,
    shrink_weight,
    norm_gain,
    norm_bias,
    proj_bias,
    expand_bias,
):
    row_count, enc_rows = tokens.shape[0], enc_states.shape[0]
    span = SEQ // row_count
    width = D // span
    count = lax.axis_size("shard")
    size = lax.axis_size("rep")
    rep_pos = lax.axis_index("rep")
    shard_pos = lax.axis_index("shard")
    local_pos = shard_pos % span
    local_seq = shard_pos // span
    groups = None
    if count != span:
        groups = [[g * span + i for i in range(span)] for g in range(count // span)]
    weight_rows = self_qkv.shape[0]
    part_rows = weight_rows // size
    hidden = expand_bias.shape[0]
    shard_width = norm_gain.shape[1]

    def gather(value, groups=None):
        return lax.all_gather(value, "shard", axis=0, tiled=True, axis_index_groups=groups)

    def scatter(value, groups=None):
        return lax.psum_scatter(value, "shard", scatter_dimension=0, tiled=True, axis_index_groups=groups)

    def swap(value):
        return lax.all_to_all(value, "shard", 0, 0, tiled=True)

    def own_part(weight):
        return lax.dynamic_slice_in_dim(weight, rep_pos * part_rows, part_rows, axis=0)

    def by_pairs(weight, kinds):
        blocks = weight.reshape(part_rows, kinds, span, width).transpose(2, 0, 1, 3)
        return blocks.reshape(span, part_rows, kinds * width)

    blocks = jnp.concatenate([by_pairs(own_part(self_qkv), 3), by_pairs(own_part(cross_memory), 2)], axis=2)
    blocks = jnp.tile(blocks, (count // span, 1, 1))
    small = jnp.concatenate([norm_gain, norm_bias, proj_bias], axis=0)
    small_count = small.shape[0]
    small_rows = -(-small.size // (5 * width))
    small = jnp.pad(small.reshape(-1), (0, small_rows * 5 * width - small.size)).reshape(small_rows, 5 * width)
    blocks = jnp.concatenate([blocks, jnp.broadcast_to(small, (count,) + small.shape)], axis=1)
    swapped = swap(blocks)
    plain_parts = line_start(jnp.stack([own_part(self_out), own_part(cross_query), own_part(cross_out)]))
    enc_all = gather(enc_states, groups)
    rows_all = gather(after(tokens, swapped, enc_all, plain_parts[1], plain_parts[-1]), groups)
    small_all = swapped[:, part_rows:].reshape(count, small_rows * 5 * width)[:, : small_count * shard_width]
    small_all = small_all.reshape(count, small_count, shard_width)
    small_all = small_all.transpose(1, 0, 2).reshape(small_count, D).astype(jnp.float32)
    gain_rows, shift_rows, bias_rows = small_all[:3], small_all[3:6], small_all[6:]
    head_weight = rep_gather(swapped[:, :part_rows], 1).reshape(D, 5 * width)
    qkv_weight, memory_weight = head_weight[:, : 3 * width], head_weight[:, 3 * width :]
    qkv_weight, memory_weight = head_weight[:, : 3 * width], head_weight[:, 3 * width :]
    own_bias = lax.dynamic_slice_in_dim(bias_rows, local_pos * width, width, axis=1)
    zero_bias = jnp.zeros((width,), jnp.float32)
    memory_pair = low(dot(enc_all, memory_weight) + jnp.concatenate([zero_bias, own_bias[4]]))
    plain_mine = rep_start(line_place(after(plain_parts, head_weight)))
    rows_all, qkv_weight, memory_weight, plain_mine[1], plain_mine[2] = lax.optimization_barrier(
        (rows_all, qkv_weight, memory_weight, plain_mine[1], plain_mine[2])
    )
    memory_all = gather(after(memory_pair, rows_all), groups)
    expand_part = own_part(after(expand_weight, rows_all)).reshape(part_rows, count, hidden).transpose(1, 0, 2)
    expand_swapped = swap(expand_part)

    seq_segments = lax.dynamic_slice_in_dim(segments, local_seq * SEQ, SEQ)
    qkv_bias = jnp.concatenate([own_bias[0], zero_bias, own_bias[1]])
    input_one_all, qkv = front(rows_all, gain_rows[0], shift_rows[0], qkv_weight, qkv_bias)
    att_low, att_full, lse = self_forward(qkv, seq_segments)
    att_low, memory_all, plain_mine, expand_swapped = lax.optimization_barrier(
        (att_low, memory_all, plain_mine, expand_swapped)
    )
    grad_all = gather(after(cotangent, memory_all))
    plain_other = [core_send(part) for part in plain_mine]
    attn_proj, query_in, cross_proj = weight_join(plain_mine, plain_other)
    attended = lax.all_to_all(att_low, "shard", 0, 1, tiled=True, axis_index_groups=groups)

    enc_count = lax.dynamic_slice_in_dim(enc_lengths, local_seq, 1)

    residual_in = tokens.astype(jnp.float32)
    hidden_one = residual_in + dot(attended, attn_proj) + bias_rows[2]
    input_two = low(norm_apply(hidden_one, gain_rows[1], shift_rows[1]))
    cross_q = low(dot(input_two, query_in) + bias_rows[3])
    context = cross_forward(cross_q, memory_all, enc_count)
    hidden_two = hidden_one + dot(context, cross_proj) + bias_rows[5]
    input_three = low(norm_apply(hidden_two, gain_rows[2], shift_rows[2]))

    input_three_all = gather(input_three)
    expand_parts = rep_start(expand_swapped.reshape(count * part_rows, hidden))
    grad_all_now = after(grad_all, input_three)
    expand_local = spread(expand_parts, 0, count * part_rows, jnp.bfloat16)
    expand_local = expand_local.reshape(size, count, part_rows, hidden).transpose(1, 0, 2, 3).reshape(D, hidden)
    grad_act = dot_nt(grad_all_now, shrink_weight)
    input_three_all, grad_act, expand_local = lax.optimization_barrier((input_three_all, grad_act, expand_local))
    act, grad_pre, grad_in_three_low, hidden_sums = feed(
        input_three_all, expand_local, expand_bias.astype(jnp.float32), grad_act
    )
    grad_hidden_bias = hidden_sums[0]
    grad_in_three = scatter(grad_in_three_low)

    part_hidden = hidden // size

    def send_parts(parts):
        return [parts[0]] + [rep_send(parts[step], step) for step in range(1, size)]

    rows_late, grad_pre_late = after((input_three_all, grad_pre), grad_in_three_low)
    expand_grad_parts = expand_grads(rows_late, grad_pre_late, count, part_rows)
    shrink_parts = send_parts(shrink_grads(after(act, expand_grad_parts[0]), grad_all))
    expand_grad_parts = send_parts(expand_grad_parts)
    result_part = product(after(act, shrink_parts[0]), shrink_weight)
    expand_sum = add_up(expand_grad_parts)
    own_expand = swap(expand_sum)
    grad_in_three, shrink_parts[0], result_part = lax.optimization_barrier(
        (grad_in_three, shrink_parts[0], result_part)
    )
    result_sum = scatter(result_part)
    grad_in_three = grad_in_three.astype(jnp.float32)

    grad_out = cotangent.astype(jnp.float32)
    norm_three = jax.vjp(norm_apply, hidden_two, gain_rows[2], shift_rows[2])[1](grad_in_three)
    grad_two = grad_out + norm_three[0]
    grad_two_low = low(grad_two)
    grad_context = low(dot_nt(grad_two_low, cross_proj))
    grad_context, own_expand = lax.optimization_barrier((grad_context, own_expand))
    grad_cross_q, memory_part = cross_backward(cross_q, memory_all, grad_context, enc_count)
    grad_cross_q, memory_part, shrink_parts = lax.optimization_barrier((grad_cross_q, memory_part, shrink_parts))
    mem_grads = scatter(memory_part, groups)
    grad_in_two = dot_nt(grad_cross_q, query_in)
    norm_two = jax.vjp(norm_apply, hidden_one, gain_rows[1], shift_rows[1])[1](grad_in_two)
    grad_one = grad_two + norm_two[0]
    grad_one_low = low(grad_one)
    grad_attn = low(dot_nt(grad_one_low, attn_proj))
    shrink_sum = add_up(after(shrink_parts, grad_attn))
    own_expand = own_expand.reshape(part_hidden, D)
    own_feed = jnp.concatenate([shrink_sum, own_expand], axis=0)
    grad_att_heads = lax.all_to_all(grad_attn, "shard", 1, 0, tiled=True, axis_index_groups=groups)

    lefts, rights = after(((attended, input_two, context), (grad_one_low, grad_cross_q, grad_two_low)), grad_attn)
    plain_own, plain_theirs = plain_grads(lefts, rights)
    plain_theirs = core_send(plain_theirs)
    grad_att_heads, plain_own = lax.optimization_barrier((grad_att_heads, plain_own))

    feed_gather = rep_start(own_feed)
    grad_qkv = self_backward(qkv, grad_att_heads, lse, att_full, seq_segments)
    heads_parts = heads_grads(input_one_all, grad_qkv, enc_all, mem_grads, count, part_rows)
    heads_swapped = rep_swap(heads_parts)
    grad_in_one_low, one_sums, qkv_sums = back(after(grad_qkv, heads_parts), qkv_weight, input_one_all)
    plain_rep = send_parts(core_sum_split(*after((plain_own, plain_theirs), heads_parts)))
    grad_in_one_low, heads_swapped, plain_rep[0], feed_gather = lax.optimization_barrier(
        (grad_in_one_low, heads_swapped, plain_rep[0], feed_gather)
    )
    grad_in_one = scatter(grad_in_one_low, groups)

    mem_grads_late = after(mem_grads, grad_in_one_low)
    qkv_sums = qkv_sums[0]
    gain_shift = [(one_sums[0] - shift_rows[0] * one_sums[1]) / gain_rows[0], one_sums[1]]
    zero_row = jnp.zeros((D,), jnp.float32)

    def at_own(values):
        return lax.dynamic_update_slice_in_dim(zero_row, values, local_pos * width, 0)

    small_grads = jnp.stack(
        [
            gain_shift[0],
            norm_two[1],
            norm_three[1],
            gain_shift[1],
            norm_two[2],
            norm_three[2],
            at_own(qkv_sums[:width]),
            at_own(qkv_sums[2 * width :]),
            column_sums(grad_one_low),
            column_sums(grad_cross_q),
            at_own(column_sums(mem_grads_late)[width:]),
            column_sums(grad_two_low),
            column_sums(cotangent),
        ]
    )
    small_grads = small_grads.reshape(small_count, count, shard_width).transpose(1, 0, 2)
    small_grads = small_grads.reshape(count, small_count * shard_width)
    hidden_grads = jnp.zeros((count, hidden), jnp.float32)
    hidden_grads = lax.dynamic_update_slice_in_dim(hidden_grads, grad_hidden_bias[None], shard_pos, 0)
    small_grads = low(jnp.concatenate([small_grads, hidden_grads], axis=1))
    small_size = small_grads.shape[1]
    extra = -(-small_size // (5 * width))
    small_grads = jnp.pad(small_grads, ((0, 0), (0, extra * 5 * width - small_size)))
    small_grads = small_grads.reshape(count, extra, 5 * width)
    heads_sum = sum_first(after(heads_swapped, grad_in_one_low))
    own_heads = swap(jnp.concatenate([heads_sum, small_grads], axis=1))
    own_small = sum_first(own_heads[:, part_rows:])
    own_heads = own_heads[:, :part_rows].reshape(count // span, span, part_rows, 5 * width)
    own_heads = own_heads[0] if count == span else sum_first(own_heads)
    heads_gather = rep_start(jnp.concatenate([own_heads.reshape(span * part_rows, 5 * width), own_small], axis=0))

    plain_line_parts = reduce_line(add_up(after(plain_rep, own_heads)))
    own_plain = add_up(plain_line_parts).reshape(3 * part_rows, D)
    plain_gather = rep_start(own_plain)
    enc_parts = line_scatter_start(low(dot_nt(mem_grads_late, memory_weight)), span)
    grad_enc = add_up(line_scatter_middle(enc_parts, span)).astype(jnp.float32)
    result = hidden_two + after(result_sum, grad_in_one_low).astype(jnp.float32) + bias_rows[6]

    total_shrink = spread(feed_gather, 0, part_hidden, jnp.float32)
    total_expand = spread_columns(feed_gather, part_hidden, count, part_rows)
    total_small = sum(part[span * part_rows :].astype(jnp.float32) for part in heads_gather)
    total_small = total_small.reshape(-1)[:small_size]
    total_hidden_bias = total_small[small_count * shard_width :]
    total_small = total_small[: small_count * shard_width].reshape(small_count, shard_width)
    total_qkv, total_memory = spread_heads(heads_gather, span, part_rows, width)

    grad_tokens = last(tokens, grad_in_one, grad_one, gain_rows[0])
    plain_gather = after(plain_gather, grad_tokens, result)
    total_proj, total_query, total_cross = [part.reshape(weight_rows, D) for part in spread_kinds(plain_gather, part_rows)]

    return (
        low(result),
        grad_tokens,
        grad_enc,
        total_qkv,
        total_proj,
        total_query,
        total_memory,
        total_cross,
        total_expand.reshape(weight_rows, count * hidden).astype(jnp.float32),
        total_shrink.reshape(hidden, D).astype(jnp.float32),
        total_small[:3],
        total_small[3:6],
        total_small[6:],
        total_hidden_bias,
    )


def solution(mesh):
    return jax.shard_map(
        shards,
        mesh=mesh,
        in_specs=(
            P(("rep", "shard"), None),
            P("rep"),
            P(("rep", "shard"), None),
            P("rep"),
            P(("rep", "shard"), None),
            P("shard", None),
            P("shard", None),
            P("shard", None),
            P("shard", None),
            P("shard", None),
            P("shard", None),
            P("shard", None),
            P(None, "shard"),
            P(None, "shard"),
            P(None, "shard"),
            P("shard"),
        ),
        out_specs=(
            P(("rep", "shard"), None),
            P(("rep", "shard"), None),
            P(("rep", "shard"), None),
            P("shard", None),
            P("shard", None),
            P("shard", None),
            P("shard", None),
            P("shard", None),
            P("shard", None),
            P("shard", None),
            P(None, "shard"),
            P(None, "shard"),
            P(None, "shard"),
            P("shard"),
        ),
        check_vma=False,
    )
```

```python
import functools

import jax
import jax.numpy as jnp
from jax import lax
from jax.experimental import pallas as pl
from jax.experimental.pallas import tpu as pltpu
from jax.sharding import PartitionSpec as P

D = 1024
H = 16
HD = 64
SEQ = 2048
PAIR = 2 * HD

EPS = 1e-05
NEGATIVE = -1e30
SCALE = HD**-0.5
BLOCK = 512
GELU = 0.7978845608028654
LITTLE = pl.CostEstimate(flops=1000, bytes_accessed=1000, transcendentals=0)


def norm_apply(rows, gain, shift):
    mean_rows = jnp.mean(rows, axis=-1, keepdims=True)
    centered = rows - mean_rows
    inverse = lax.rsqrt(jnp.mean(centered * centered, axis=-1, keepdims=True) + EPS)
    return centered * inverse * gain + shift


def gelu_apply(values):
    return jax.nn.gelu(values, approximate=True)


def column_sums(rows):
    return jnp.sum(rows, axis=0, dtype=jnp.float32)


def low(values):
    return values.astype(jnp.bfloat16)


def dot(left, right):
    return jnp.dot(left, right, preferred_element_type=jnp.float32)


def dot_nt(left, right):
    return lax.dot_general(left, right, (((1,), (1,)), ((), ())), preferred_element_type=jnp.float32)


def dot_tn(left, right):
    return lax.dot_general(left, right, (((0,), (0,)), ((), ())), preferred_element_type=jnp.float32)


def after(value, *earlier):
    return lax.optimization_barrier((value, earlier))[0]


def head_halves(rows, scale=None):
    lane = lax.broadcasted_iota(jnp.int32, rows.shape, 1)
    if scale is not None:
        rows = rows * jnp.asarray(scale, rows.dtype)
    zero = jnp.zeros_like(rows)
    return jnp.where(lane < HD, rows, zero), jnp.where(lane < HD, zero, rows)


def self_forward_kernel(ends, q_ref, k_ref, v_ref, seg_col, seg_row, low_ref, full_ref, lse_ref):
    step = pl.program_id(0)
    rows = q_ref.shape[0]
    queries = head_halves(q_ref[...], SCALE)
    query_seg = seg_row[...]
    last_seg = ends[1, step]

    def piece(index, state, masked, diagonal):
        place = pl.ds(pl.multiple_of(index * rows, rows), rows)
        keys = k_ref[place, :]
        values = v_ref[place, :]
        keep = None
        if masked:
            keep = seg_col[place, :] == query_seg
            if diagonal:
                key_pos = lax.broadcasted_iota(jnp.int32, (rows, rows), 0)
                query_pos = lax.broadcasted_iota(jnp.int32, (rows, rows), 1)
                keep = keep & (key_pos <= query_pos)
        after_piece = []
        for head in range(2):
            top, total, acc = state[head]
            scores = dot_nt(keys, queries[head])
            if masked:
                scores = jnp.where(keep, scores, NEGATIVE)
            top_new = jnp.maximum(top, jnp.max(scores, axis=0, keepdims=True))
            expo = jnp.exp(scores - top_new)
            fade = jnp.exp(top - top_new)
            after_piece.append(
                (
                    top_new,
                    total * fade + jnp.sum(expo, axis=0, keepdims=True),
                    acc * fade + dot_tn(values, low(expo)),
                )
            )
        return tuple(after_piece)

    def before(index, state):
        return lax.cond(
            ends[0, index] == last_seg,
            lambda s: piece(index, s, False, False),
            lambda s: piece(index, s, True, False),
            state,
        )

    blank = (
        jnp.full((1, rows), NEGATIVE, jnp.float32),
        jnp.zeros((1, rows), jnp.float32),
        jnp.zeros((PAIR, rows), jnp.float32),
    )
    state = lax.fori_loop(0, step, before, (blank, blank))
    state = piece(step, state, True, True)
    parts = [
        (state[head][2] * (1.0 / state[head][1]))[head * HD : (head + 1) * HD] for head in range(2)
    ]
    joined = jnp.concatenate(parts, axis=0).T
    full_ref[...] = joined
    low_ref[...] = low(joined)
    lse_ref[0:1, :] = state[0][0] + jnp.log(state[0][1])
    lse_ref[1:2, :] = state[1][0] + jnp.log(state[1][1])


def block_ends(segments, rows):
    return jnp.stack([segments[::rows], segments[rows - 1 :: rows]])


def self_forward(qkv, segments):
    count = qkv.shape[0]
    rows = BLOCK
    col = segments[:, None]
    row = segments[None, :]
    grid_spec = pltpu.PrefetchScalarGridSpec(
        num_scalar_prefetch=1,
        grid=(count // rows,),
        in_specs=[
            pl.BlockSpec((rows, PAIR), lambda i, e: (i, 0)),
            pl.BlockSpec((count, PAIR), lambda i, e: (0, 1)),
            pl.BlockSpec((count, PAIR), lambda i, e: (0, 2)),
            pl.BlockSpec((count, 1), lambda i, e: (0, 0)),
            pl.BlockSpec((1, rows), lambda i, e: (0, i)),
        ],
        out_specs=[
            pl.BlockSpec((rows, PAIR), lambda i, e: (i, 0)),
            pl.BlockSpec((rows, PAIR), lambda i, e: (i, 0)),
            pl.BlockSpec((2, rows), lambda i, e: (0, i)),
        ],
    )
    return pl.pallas_call(
        self_forward_kernel,
        grid_spec=grid_spec,
        out_shape=(
            jax.ShapeDtypeStruct((count, PAIR), jnp.bfloat16),
            jax.ShapeDtypeStruct((count, PAIR), jnp.float32),
            jax.ShapeDtypeStruct((2, count), jnp.float32),
        ),
        compiler_params=pltpu.CompilerParams(vmem_limit_bytes=58 * 2**20),
        cost_estimate=LITTLE,
    )(block_ends(segments, rows), qkv, qkv, qkv, col, row)


def self_backward_kernel(
    ends, q_ref, k_ref, v_ref, go_ref, lse_ref, o_ref, seg_col, seg_row, grad_ref, acc_q, acc_k, acc_v, delta_ref
):
    step = pl.program_id(0)
    blocks = pl.num_programs(0)
    rows = k_ref.shape[0]

    @pl.when(step == 0)
    def _():
        acc_q[...] = jnp.zeros_like(acc_q)
        lane = lax.broadcasted_iota(jnp.int32, (8, PAIR), 1) // HD
        pick = (lane == lax.broadcasted_iota(jnp.int32, (8, PAIR), 0)).astype(jnp.float32)
        delta_ref[...] = lax.dot_general(
            pick,
            go_ref[...].astype(jnp.float32) * o_ref[...],
            (((1,), (1,)), ((), ())),
            precision=lax.Precision.HIGHEST,
            preferred_element_type=jnp.float32,
        )

    keys = k_ref[...]
    values = v_ref[...]
    key_halves = head_halves(keys, SCALE)
    key_seg = seg_col[...]
    first_seg = ends[0, step]

    def piece(index, masked, diagonal):
        place = pl.ds(pl.multiple_of(index * rows, rows), rows)
        queries = head_halves(q_ref[place, :], SCALE)
        grads = head_halves(go_ref[place, :])
        keep = None
        if masked:
            keep = seg_row[:, place] == key_seg
            if diagonal:
                key_pos = lax.broadcasted_iota(jnp.int32, (rows, rows), 0)
                query_pos = lax.broadcasted_iota(jnp.int32, (rows, rows), 1)
                keep = keep & (key_pos <= query_pos)
        sum_q = sum_k = sum_v = None
        for head in range(2):
            scores = dot_nt(keys, queries[head])
            probs = jnp.exp(scores - lse_ref[head : head + 1, place])
            if masked:
                probs = jnp.where(keep, probs, 0.0)
            part_v = dot(low(probs), grads[head])
            grad_probs = dot_nt(values, grads[head])
            grad_scores = low(probs * (grad_probs - delta_ref[head : head + 1, place]))
            part_k = dot(grad_scores, queries[head])
            part_q = dot_tn(key_halves[head], grad_scores)
            sum_q = part_q if sum_q is None else sum_q + part_q
            sum_k = part_k if sum_k is None else sum_k + part_k
            sum_v = part_v if sum_v is None else sum_v + part_v
        acc_q[:, place] += sum_q
        if diagonal:
            acc_k[...] = sum_k
            acc_v[...] = sum_v
        else:
            acc_k[...] += sum_k
            acc_v[...] += sum_v

    piece(step, True, True)

    @pl.loop(step + 1, blocks)
    def _(index):
        whole = ends[1, index] == first_seg

        @pl.when(whole)
        def _():
            piece(index, False, False)

        @pl.when(jnp.logical_not(whole))
        def _():
            piece(index, True, False)

    own = pl.ds(pl.multiple_of(step * rows, rows), rows)
    grad_ref[own, 0:PAIR] = low(acc_q[:, own].T)
    grad_ref[own, PAIR : 2 * PAIR] = low(acc_k[...])
    grad_ref[own, 2 * PAIR : 3 * PAIR] = low(acc_v[...])


def self_backward(qkv, grad_att, lse, attended, segments):
    count = qkv.shape[0]
    rows = BLOCK
    col = segments[:, None]
    row = segments[None, :]
    whole = lambda i, e: (0, 0)
    grid_spec = pltpu.PrefetchScalarGridSpec(
        num_scalar_prefetch=1,
        grid=(count // rows,),
        in_specs=[
            pl.BlockSpec((count, PAIR), whole),
            pl.BlockSpec((rows, PAIR), lambda i, e: (i, 1)),
            pl.BlockSpec((rows, PAIR), lambda i, e: (i, 2)),
            pl.BlockSpec((count, PAIR), whole),
            pl.BlockSpec((2, count), whole),
            pl.BlockSpec((count, PAIR), whole),
            pl.BlockSpec((rows, 1), lambda i, e: (i, 0)),
            pl.BlockSpec((1, count), whole),
        ],
        out_specs=pl.BlockSpec((count, 3 * PAIR), whole),
        scratch_shapes=[
            pltpu.VMEM((PAIR, count), jnp.float32),
            pltpu.VMEM((rows, PAIR), jnp.float32),
            pltpu.VMEM((rows, PAIR), jnp.float32),
            pltpu.VMEM((8, count), jnp.float32),
        ],
    )
    return pl.pallas_call(
        self_backward_kernel,
        grid_spec=grid_spec,
        out_shape=jax.ShapeDtypeStruct((count, 3 * PAIR), jnp.bfloat16),
        compiler_params=pltpu.CompilerParams(vmem_limit_bytes=58 * 2**20),
        cost_estimate=pl.CostEstimate(flops=16 * 10**9, bytes_accessed=4 * 2**20, transcendentals=0),
    )(block_ends(segments, rows), qkv, qkv, qkv, grad_att, lse, attended, col, row)


def cross_forward_kernel(length, q_ref, m_ref, out_ref):
    queries = head_halves(q_ref[...], SCALE)
    keys = m_ref[:, :PAIR]
    values = m_ref[:, PAIR:]
    shape = (q_ref.shape[0], m_ref.shape[0])
    keep = lax.broadcasted_iota(jnp.int32, shape, 1) < length[0]
    parts = []
    for head in range(2):
        scores = jnp.where(keep, dot_nt(queries[head], keys), NEGATIVE)
        expo = jnp.exp(scores - jnp.max(scores, axis=1, keepdims=True))
        parts.append(dot(low(expo), values) / jnp.sum(expo, axis=1, keepdims=True))
    lane = lax.broadcasted_iota(jnp.int32, parts[0].shape, 1)
    out_ref[...] = low(jnp.where(lane < HD, parts[0], parts[1]))


def cross_forward(queries, memory, length):
    count, states = queries.shape[0], memory.shape[0] // (D // PAIR)
    grid_spec = pltpu.PrefetchScalarGridSpec(
        num_scalar_prefetch=1,
        grid=(D // PAIR,),
        in_specs=[
            pl.BlockSpec((count, PAIR), lambda i, e: (0, i)),
            pl.BlockSpec((states, 2 * PAIR), lambda i, e: (i, 0)),
        ],
        out_specs=pl.BlockSpec((count, PAIR), lambda i, e: (0, i)),
    )
    return pl.pallas_call(
        cross_forward_kernel,
        grid_spec=grid_spec,
        out_shape=jax.ShapeDtypeStruct((count, D), jnp.bfloat16),
        cost_estimate=LITTLE,
    )(length, queries, memory)


def cross_backward_kernel(length, q_ref, m_ref, g_ref, dq_ref, dm_ref):
    queries = head_halves(q_ref[...], SCALE)
    grads = head_halves(g_ref[...])
    keys = m_ref[:, :PAIR]
    values = m_ref[:, PAIR:]
    key_halves = head_halves(keys, SCALE)
    shape = (m_ref.shape[0], q_ref.shape[0])
    keep = lax.broadcasted_iota(jnp.int32, shape, 0) < length[0]
    sum_q = sum_k = sum_v = None
    for head in range(2):
        scores = jnp.where(keep, dot_nt(keys, queries[head]), NEGATIVE)
        expo = jnp.exp(scores - jnp.max(scores, axis=0, keepdims=True))
        probs = expo * (1.0 / jnp.sum(expo, axis=0, keepdims=True))
        part_v = dot(low(probs), grads[head])
        grad_probs = dot_nt(values, grads[head])
        inner = jnp.sum(probs * grad_probs, axis=0, keepdims=True)
        grad_scores = low(probs * (grad_probs - inner))
        part_k = dot(grad_scores, queries[head])
        part_q = dot_tn(grad_scores, key_halves[head])
        sum_q = part_q if sum_q is None else sum_q + part_q
        sum_k = part_k if sum_k is None else sum_k + part_k
        sum_v = part_v if sum_v is None else sum_v + part_v
    dq_ref[...] = low(sum_q)
    dm_ref[:, :PAIR] = low(sum_k)
    dm_ref[:, PAIR:] = low(sum_v)


def cross_backward(queries, memory, grads, length):
    count, states = queries.shape[0], memory.shape[0] // (D // PAIR)
    grid_spec = pltpu.PrefetchScalarGridSpec(
        num_scalar_prefetch=1,
        grid=(D // PAIR,),
        in_specs=[
            pl.BlockSpec((count, PAIR), lambda i, e: (0, i)),
            pl.BlockSpec((states, 2 * PAIR), lambda i, e: (i, 0)),
            pl.BlockSpec((count, PAIR), lambda i, e: (0, i)),
        ],
        out_specs=[
            pl.BlockSpec((count, PAIR), lambda i, e: (0, i)),
            pl.BlockSpec((states, 2 * PAIR), lambda i, e: (i, 0)),
        ],
    )
    return pl.pallas_call(
        cross_backward_kernel,
        grid_spec=grid_spec,
        out_shape=(
            jax.ShapeDtypeStruct((count, D), jnp.bfloat16),
            jax.ShapeDtypeStruct((states * (D // PAIR), 2 * PAIR), jnp.bfloat16),
        ),
        cost_estimate=LITTLE,
    )(length, queries, memory, grads)


def front_kernel(x_ref, gain, shift, qkv_w, qkv_b, one_ref, qkv_ref):
    rows = x_ref[...].astype(jnp.float32)
    centered = rows - jnp.mean(rows, axis=-1, keepdims=True)
    inverse = lax.rsqrt(jnp.mean(centered * centered, axis=-1, keepdims=True) + EPS)
    one = low(centered * inverse * gain[...] + shift[...])
    one_ref[...] = one
    qkv_ref[...] = low(dot(one, qkv_w[...]) + qkv_b[...])


def front(rows, gain, shift, qkv_w, qkv_b):
    count, tile = rows.shape[0], 256
    whole = lambda i: (0, 0)
    block = lambda i: (i, 0)
    return pl.pallas_call(
        front_kernel,
        grid=(count // tile,),
        in_specs=[
            pl.BlockSpec((tile, D), block),
            pl.BlockSpec((1, D), whole),
            pl.BlockSpec((1, D), whole),
            pl.BlockSpec(qkv_w.shape, whole),
            pl.BlockSpec((1, qkv_w.shape[1]), whole),
        ],
        out_specs=[pl.BlockSpec((tile, D), block), pl.BlockSpec((tile, qkv_w.shape[1]), block)],
        out_shape=(
            jax.ShapeDtypeStruct((count, D), jnp.bfloat16),
            jax.ShapeDtypeStruct((count, qkv_w.shape[1]), jnp.bfloat16),
        ),
        compiler_params=pltpu.CompilerParams(vmem_limit_bytes=58 * 2**20),
        cost_estimate=LITTLE,
    )(rows, gain[None], shift[None], qkv_w, qkv_b[None])


def feed_kernel(x_ref, w_ref, b_ref, ga_ref, act_ref, pre_ref, in_ref, sum_ref):
    v = dot(x_ref[...], w_ref[...]) + b_ref[...]
    square = v * v
    half = 0.5 + 0.5 * jnp.tanh(v * (GELU + GELU * 0.044715 * square))
    act_ref[...] = low(v * half)
    slope = half + (v * half) * (1.0 - half) * (2.0 * GELU + 6.0 * GELU * 0.044715 * square)
    grad = low(ga_ref[...] * slope)
    pre_ref[...] = grad
    in_ref[...] = low(dot_nt(grad, w_ref[...]))

    @pl.when(pl.program_id(0) == 0)
    def _():
        sum_ref[...] = jnp.zeros_like(sum_ref)

    sum_ref[...] += jnp.sum(grad.astype(jnp.float32), axis=0, keepdims=True)


def feed(rows, weight, bias, grad_act):
    count, hidden = grad_act.shape
    tile = 512
    whole = lambda i: (0, 0)
    block = lambda i: (i, 0)
    return pl.pallas_call(
        feed_kernel,
        grid=(count // tile,),
        in_specs=[
            pl.BlockSpec((tile, D), block),
            pl.BlockSpec((D, hidden), whole),
            pl.BlockSpec((1, hidden), whole),
            pl.BlockSpec((tile, hidden), block),
        ],
        out_specs=[
            pl.BlockSpec((tile, hidden), block),
            pl.BlockSpec((tile, hidden), block),
            pl.BlockSpec((tile, D), block),
            pl.BlockSpec((1, hidden), whole),
        ],
        out_shape=(
            jax.ShapeDtypeStruct((count, hidden), jnp.bfloat16),
            jax.ShapeDtypeStruct((count, hidden), jnp.bfloat16),
            jax.ShapeDtypeStruct((count, D), jnp.bfloat16),
            jax.ShapeDtypeStruct((1, hidden), jnp.float32),
        ),
        compiler_params=pltpu.CompilerParams(vmem_limit_bytes=58 * 2**20),
        cost_estimate=LITTLE,
    )(rows, weight, bias[None], grad_act)


def expand_kernel(replica, x_ref, g_ref, *refs):
    keep, outs = refs[-1], refs[:-1]
    size, rows = len(outs), outs[0].shape[1]
    owners = x_ref.shape[1] // (size * rows)
    keep[...] = low(dot_tn(x_ref[...], g_ref[...])).reshape(keep.shape)
    step = pl.program_id(0) * owners
    for owner in range(owners):
        for other, out in enumerate(outs):
            out[pl.ds(step + owner, 1)] = keep[owner, pl.ds(replica[0] ^ other, 1)]


def expand_grads(rows_in, grads, owners, part_rows):
    size, me = lax.axis_size("rep"), lax.axis_index("rep")
    count, hidden = grads.shape
    if part_rows % 16:
        full = low(dot_tn(rows_in, grads)).reshape(owners, size, part_rows, hidden)
        return [lax.dynamic_index_in_dim(full, me ^ step, 1, keepdims=False) for step in range(size)]
    tile = 2
    grid_spec = pltpu.PrefetchScalarGridSpec(
        num_scalar_prefetch=1,
        grid=(owners // tile,),
        in_specs=[
            pl.BlockSpec((count, tile * size * part_rows), lambda i, e: (0, i)),
            pl.BlockSpec((count, hidden), lambda i, e: (0, 0)),
        ],
        out_specs=[pl.BlockSpec((owners, part_rows, hidden), lambda i, e: (0, 0, 0))] * size,
        scratch_shapes=[pltpu.VMEM((tile, size, part_rows, hidden), jnp.bfloat16)],
    )
    return pl.pallas_call(
        expand_kernel,
        grid_spec=grid_spec,
        out_shape=(jax.ShapeDtypeStruct((owners, part_rows, hidden), jnp.bfloat16),) * size,
        compiler_params=pltpu.CompilerParams(vmem_limit_bytes=58 * 2**20),
        cost_estimate=LITTLE,
    )(me[None], rows_in, grads)


def shrink_kernel(replica, a_ref, g_ref, *outs):
    for step, out in enumerate(outs):

        @pl.when(pl.program_id(0) == step)
        def _():
            out[...] = low(dot_tn(a_ref[...], g_ref[...]))


def shrink_grads(act, grads):
    size, me = lax.axis_size("rep"), lax.axis_index("rep")
    count, hidden = act.shape
    part = hidden // size
    if part % 128:
        full = low(dot_tn(act, grads)).reshape(size, part, D)
        return [lax.dynamic_index_in_dim(full, me ^ step, 0, keepdims=False) for step in range(size)]
    grid_spec = pltpu.PrefetchScalarGridSpec(
        num_scalar_prefetch=1,
        grid=(size,),
        in_specs=[
            pl.BlockSpec((count, part), lambda i, e: (0, e[0] ^ i)),
            pl.BlockSpec((count, D), lambda i, e: (0, 0)),
        ],
        out_specs=[pl.BlockSpec((part, D), lambda i, e: (0, 0))] * size,
    )
    return pl.pallas_call(
        shrink_kernel,
        grid_spec=grid_spec,
        out_shape=(jax.ShapeDtypeStruct((part, D), jnp.bfloat16),) * size,
        compiler_params=pltpu.CompilerParams(vmem_limit_bytes=58 * 2**20),
        cost_estimate=LITTLE,
    )(me[None], act, grads)


def product_kernel(a_ref, b_ref, out_ref):
    out_ref[...] = low(dot(a_ref[...], b_ref[...]))


def product(left, right):
    count, depth = left.shape
    tile = 512
    return pl.pallas_call(
        product_kernel,
        grid=(count // tile,),
        in_specs=[pl.BlockSpec((tile, depth), lambda i: (i, 0)), pl.BlockSpec(right.shape, lambda i: (0, 0))],
        out_specs=pl.BlockSpec((tile, right.shape[1]), lambda i: (i, 0)),
        out_shape=jax.ShapeDtypeStruct((count, right.shape[1]), jnp.bfloat16),
        compiler_params=pltpu.CompilerParams(vmem_limit_bytes=58 * 2**20),
        cost_estimate=LITTLE,
    )(left, right)


def back_kernel(g_ref, w_ref, one_ref, out_ref, sum_ref, own_ref):
    @pl.when(pl.program_id(0) == 0)
    def _():
        sum_ref[...] = jnp.zeros_like(sum_ref)
        own_ref[...] = jnp.zeros_like(own_ref)

    grads = dot_nt(g_ref[...], w_ref[...])
    out_ref[...] = low(grads)
    sum_ref[0:1, :] += jnp.sum(grads * one_ref[...].astype(jnp.float32), axis=0, keepdims=True)
    sum_ref[1:2, :] += jnp.sum(grads, axis=0, keepdims=True)
    own_ref[...] += jnp.sum(g_ref[...].astype(jnp.float32), axis=0, keepdims=True)


def back(grads, weight, rows_in):
    count, width = grads.shape
    tile = 256
    return pl.pallas_call(
        back_kernel,
        grid=(count // tile,),
        in_specs=[
            pl.BlockSpec((tile, width), lambda i: (i, 0)),
            pl.BlockSpec(weight.shape, lambda i: (0, 0)),
            pl.BlockSpec((tile, D), lambda i: (i, 0)),
        ],
        out_specs=[
            pl.BlockSpec((tile, D), lambda i: (i, 0)),
            pl.BlockSpec((2, D), lambda i: (0, 0)),
            pl.BlockSpec((1, width), lambda i: (0, 0)),
        ],
        out_shape=(
            jax.ShapeDtypeStruct((count, D), jnp.bfloat16),
            jax.ShapeDtypeStruct((2, D), jnp.float32),
            jax.ShapeDtypeStruct((1, width), jnp.float32),
        ),
        compiler_params=pltpu.CompilerParams(vmem_limit_bytes=58 * 2**20),
        cost_estimate=LITTLE,
    )(grads, weight, rows_in)


def heads_grads_kernel(x_ref, g_ref, e_ref, m_ref, out_ref):
    width = g_ref.shape[1]
    shape = out_ref.shape[1:3]
    for owner in range(shape[0]):
        place = slice(owner * x_ref.shape[1] // shape[0], (owner + 1) * x_ref.shape[1] // shape[0])
        left = low(dot_tn(x_ref[:, place], g_ref[...]))
        right = low(dot_tn(e_ref[:, place], m_ref[...]))
        for replica in range(out_ref.shape[0]):
            rows = slice(replica * shape[1], (replica + 1) * shape[1])
            out_ref[replica, owner, :, :width] = left[rows, :]
            out_ref[replica, owner, :, width:] = right[rows, :]


def heads_grads(rows_in, grads, enc, enc_grads, owners, part_rows):
    size = lax.axis_size("rep")
    width, enc_width = grads.shape[1], enc_grads.shape[1]
    if part_rows % 16:
        both = low(jnp.concatenate([dot_tn(rows_in, grads), dot_tn(enc, enc_grads)], axis=1))
        return both.reshape(owners, size, part_rows, width + enc_width).transpose(1, 0, 2, 3)
    tile = 2
    return pl.pallas_call(
        heads_grads_kernel,
        grid=(owners // tile,),
        in_specs=[
            pl.BlockSpec((rows_in.shape[0], tile * size * part_rows), lambda i: (0, i)),
            pl.BlockSpec(grads.shape, lambda i: (0, 0)),
            pl.BlockSpec((enc.shape[0], tile * size * part_rows), lambda i: (0, i)),
            pl.BlockSpec(enc_grads.shape, lambda i: (0, 0)),
        ],
        out_specs=pl.BlockSpec((size, tile, part_rows, width + enc_width), lambda i: (0, i, 0, 0)),
        out_shape=jax.ShapeDtypeStruct((size, owners, part_rows, width + enc_width), jnp.bfloat16),
        compiler_params=pltpu.CompilerParams(vmem_limit_bytes=58 * 2**20),
        cost_estimate=LITTLE,
    )(rows_in, grads, enc, enc_grads)


def last_kernel(x_ref, e_ref, one_ref, gain, out_ref):
    rows = x_ref[...].astype(jnp.float32)
    centered = rows - jnp.mean(rows, axis=-1, keepdims=True)
    inverse = lax.rsqrt(jnp.mean(centered * centered, axis=-1, keepdims=True) + EPS)
    x_hat = centered * inverse
    grads = e_ref[...].astype(jnp.float32) * gain[...]
    inner = jnp.mean(grads * x_hat, axis=-1, keepdims=True)
    out_ref[...] = one_ref[...] + inverse * (grads - jnp.mean(grads, axis=-1, keepdims=True) - x_hat * inner)


def last(rows, grads, grad_one, gain):
    count = rows.shape[0]
    tile = 128
    block = pl.BlockSpec((tile, D), lambda i: (i, 0))
    return pl.pallas_call(
        last_kernel,
        grid=(count // tile,),
        in_specs=[block, block, block, pl.BlockSpec((1, D), lambda i: (0, 0))],
        out_specs=block,
        out_shape=jax.ShapeDtypeStruct((count, D), jnp.float32),
        cost_estimate=LITTLE,
    )(rows, grads, grad_one, gain[None])


def rep_send(value, step):
    size = lax.axis_size("rep")
    return lax.ppermute(value, "rep", [(i, i ^ step) for i in range(size)])


def rep_start(value):
    return [value] + [rep_send(value, step) for step in range(1, lax.axis_size("rep"))]


def rep_place(parts, axis):
    size, me = lax.axis_size("rep"), lax.axis_index("rep")
    value = parts[0]
    out = jnp.zeros(value.shape[:axis] + (size,) + value.shape[axis:], value.dtype)
    for step, part in enumerate(parts):
        out = lax.dynamic_update_slice_in_dim(out, jnp.expand_dims(part, axis), me ^ step, axis)
    return out


def spread_kernel(place, *refs):
    out_ref = refs[-1]
    for step, part in enumerate(refs[:-1]):
        out_ref[pl.ds(place[0] ^ step, 1)] = part[...].astype(out_ref.dtype)[None]


def spread(parts, first, last, dtype):
    size, columns = len(parts), parts[0].shape[1]
    rows = last - first
    if rows % 32 or first % rows or parts[0].shape[0] % 16:
        return rep_place([part[first:last] for part in parts], 0).astype(dtype)
    tile = rows // 2
    grid_spec = pltpu.PrefetchScalarGridSpec(
        num_scalar_prefetch=1,
        grid=(2,),
        in_specs=[pl.BlockSpec((tile, columns), lambda i, e: (first // tile + i, 0))] * size,
        out_specs=pl.BlockSpec((size, tile, columns), lambda i, e: (0, i, 0)),
    )
    return pl.pallas_call(
        spread_kernel,
        grid_spec=grid_spec,
        out_shape=jax.ShapeDtypeStruct((size, rows, columns), dtype),
        compiler_params=pltpu.CompilerParams(vmem_limit_bytes=58 * 2**20),
        cost_estimate=LITTLE,
    )(lax.axis_index("rep")[None], *parts)


def rep_gather(value, axis):
    return rep_place(rep_start(value), axis)


def rep_swap(parts):
    return lax.all_to_all(parts, "rep", 0, 0, tiled=True)


def rep_split(parts, axis):
    size, me = lax.axis_size("rep"), lax.axis_index("rep")
    picks = [lax.dynamic_index_in_dim(parts, me ^ step, axis, keepdims=False) for step in range(size)]
    return [picks[0]] + [rep_send(low(picks[step]), step) for step in range(1, size)]


def sum_first(parts):
    return low(jnp.sum(parts.astype(jnp.float32), axis=0))


def add_up(parts):
    total = parts[0].astype(jnp.float32)
    for part in parts[1:]:
        total = total + part.astype(jnp.float32)
    return low(total)


def rep_reduce(parts, axis):
    return add_up(rep_split(parts, axis))


def core_send(value):
    size = lax.axis_size("shard")
    return lax.ppermute(value, "shard", [(i, i ^ 1) for i in range(size)])


def line_send(value, step, group=None):
    size = lax.axis_size("shard")
    group = group or size
    route = [(i, i // group * group + (i + 2 * step) % group) for i in range(size)]
    return lax.ppermute(value, "shard", route)


def line_scatter_start(value, group=None):
    group = group or lax.axis_size("shard")
    core = lax.axis_index("shard") % 2
    value = value.reshape((group // 2, 2, value.shape[0] // group) + value.shape[1:])
    mine = lax.dynamic_index_in_dim(value, core, 1, keepdims=False)
    theirs = lax.dynamic_index_in_dim(value, 1 - core, 1, keepdims=False)
    return [mine, core_send(theirs)]


def line_scatter_middle(both, group=None):
    group = group or lax.axis_size("shard")
    chips = group // 2
    chip = lax.axis_index("shard") % group // 2
    line = add_up(both)
    parts = [lax.dynamic_index_in_dim(line, (chip + step) % chips, 0, keepdims=False) for step in range(chips)]
    return [parts[0]] + [line_send(parts[step], step, group) for step in range(1, chips)]


def kinds_kernel(place, *refs):
    outs = refs[-3:]
    rows = outs[0].shape[1]
    for step, part in enumerate(refs[:-3]):
        for kind, out in enumerate(outs):
            out[pl.ds(place[0] ^ step, 1)] = part[kind * rows : (kind + 1) * rows, :].astype(out.dtype)[None]


def spread_kinds(parts, rows):
    size = len(parts)
    if rows % 16:
        return [rep_place([part[k * rows : (k + 1) * rows] for part in parts], 0).astype(jnp.float32) for k in range(3)]
    whole = lambda i, e: (0, 0)
    grid_spec = pltpu.PrefetchScalarGridSpec(
        num_scalar_prefetch=1,
        grid=(1,),
        in_specs=[pl.BlockSpec(parts[0].shape, whole)] * size,
        out_specs=[pl.BlockSpec((size, rows, D), lambda i, e: (0, 0, 0))] * 3,
    )
    return pl.pallas_call(
        kinds_kernel,
        grid_spec=grid_spec,
        out_shape=(jax.ShapeDtypeStruct((size, rows, D), jnp.float32),) * 3,
        cost_estimate=LITTLE,
    )(lax.axis_index("rep")[None], *parts)


def columns_kernel(place, *refs):
    out_ref = refs[-1]
    rows = out_ref.shape[1]
    for step, part in enumerate(refs[:-1]):
        for block in range(part.shape[0] // rows):
            wide = part[block * rows : (block + 1) * rows, :].astype(out_ref.dtype)
            out_ref[pl.ds(place[0] ^ step, 1), :, block * D : (block + 1) * D] = wide[None]


def spread_columns(parts, first, blocks, rows):
    size, me = len(parts), lax.axis_index("rep")
    if rows % 16:
        parts = [part[first:].reshape(blocks, rows, -1).transpose(1, 0, 2).reshape(rows, -1) for part in parts]
        return rep_place(parts, 0).astype(jnp.float32).reshape(size * rows, -1)
    halves = 2
    taken = blocks * rows // halves
    grid_spec = pltpu.PrefetchScalarGridSpec(
        num_scalar_prefetch=1,
        grid=(halves,),
        in_specs=[pl.BlockSpec((taken, D), lambda i, e: (first // taken + i, 0))] * size,
        out_specs=pl.BlockSpec((size, rows, blocks * D // halves), lambda i, e: (0, 0, i)),
    )
    out = pl.pallas_call(
        columns_kernel,
        grid_spec=grid_spec,
        out_shape=jax.ShapeDtypeStruct((size, rows, blocks * D), jnp.float32),
        compiler_params=pltpu.CompilerParams(vmem_limit_bytes=58 * 2**20),
        cost_estimate=LITTLE,
    )(me[None], *parts)
    return out.reshape(size * rows, blocks * D)


def heads_kernel(span, place, *refs):
    qkv_ref, memory_ref = refs[-2:]
    rows, width = qkv_ref.shape[1], D // span
    for step, part in enumerate(refs[:-2]):
        take = pl.ds(place[0] ^ step, 1)
        for block in range(span):
            wide = part[block * rows : (block + 1) * rows, :].astype(jnp.float32)[None]
            for kind in range(5):
                out, at = (qkv_ref, kind) if kind < 3 else (memory_ref, kind - 3)
                columns = slice(at * D + block * width, at * D + (block + 1) * width)
                out[take, :, columns] = wide[:, :, kind * width : (kind + 1) * width]


def spread_heads(parts, span, rows, width):
    size, me = len(parts), lax.axis_index("rep")
    if rows % 16:
        full = rep_place([part[: span * rows].reshape(span, rows, 5, width) for part in parts], 0)
        full = full.transpose(0, 2, 3, 1, 4).reshape(size * rows, 5 * D).astype(jnp.float32)
        return full[:, : 3 * D], full[:, 3 * D :]
    grid_spec = pltpu.PrefetchScalarGridSpec(
        num_scalar_prefetch=1,
        grid=(1,),
        in_specs=[pl.BlockSpec((span * rows, 5 * width), lambda i, e: (0, 0))] * size,
        out_specs=[
            pl.BlockSpec((size, rows, 3 * D), lambda i, e: (0, 0, 0)),
            pl.BlockSpec((size, rows, 2 * D), lambda i, e: (0, 0, 0)),
        ],
    )
    qkv, memory = pl.pallas_call(
        functools.partial(heads_kernel, span),
        grid_spec=grid_spec,
        out_shape=(
            jax.ShapeDtypeStruct((size, rows, 3 * D), jnp.float32),
            jax.ShapeDtypeStruct((size, rows, 2 * D), jnp.float32),
        ),
        compiler_params=pltpu.CompilerParams(vmem_limit_bytes=58 * 2**20),
        cost_estimate=LITTLE,
    )(me[None], *parts)
    return qkv.reshape(size * rows, 3 * D), memory.reshape(size * rows, 2 * D)


def line_start(piece):
    return [piece] + [line_send(piece, step) for step in range(1, lax.axis_size("shard") // 2)]


def line_place(parts):
    chips, chip = len(parts), lax.axis_index("shard") // 2
    kinds, rows, columns = parts[0].shape
    line = jnp.zeros((kinds, chips, rows, columns), parts[0].dtype)
    for step, part in enumerate(parts):
        line = lax.dynamic_update_slice_in_dim(line, part[:, None], (chip - step) % chips, 1)
    return line


def join_kernel(place, *refs):
    outs = refs[-3:]
    parts = refs[:-3]
    size = len(parts) // 2
    for core in range(2):
        side = place[1] ^ core
        for step in range(size):
            for kind in range(3):
                outs[kind][0, pl.ds(side, 1), pl.ds(place[0] ^ step, 1)] = parts[core * size + step][kind][None]


def weight_join(mine, other):
    size = len(mine)
    _, chips, rows, _ = mine[0].shape
    core = lax.axis_index("shard") % 2
    if rows % 16:
        first = core == 0
        plane, next_plane = rep_place(mine, 2), rep_place(other, 2)
        low_core, high_core = jnp.where(first, plane, next_plane), jnp.where(first, next_plane, plane)
        full = jnp.stack([low_core, high_core], axis=2).reshape(3, D, D)
        return full[0], full[1], full[2]
    grid_spec = pltpu.PrefetchScalarGridSpec(
        num_scalar_prefetch=1,
        grid=(chips,),
        in_specs=[pl.BlockSpec((3, 1, rows, D), lambda i, e: (0, i, 0, 0))] * (2 * size),
        out_specs=[pl.BlockSpec((1, 2, size, rows, D), lambda i, e: (i, 0, 0, 0, 0))] * 3,
    )
    outs = pl.pallas_call(
        join_kernel,
        grid_spec=grid_spec,
        out_shape=(jax.ShapeDtypeStruct((chips, 2, size, rows, D), jnp.bfloat16),) * 3,
        compiler_params=pltpu.CompilerParams(vmem_limit_bytes=58 * 2**20),
        cost_estimate=LITTLE,
    )(jnp.stack([lax.axis_index("rep"), core]), *mine, *other)
    return tuple(out.reshape(D, D) for out in outs)


def plain_kernel(core, a_ref, b_ref, c_ref, ga_ref, gb_ref, gc_ref, mine_ref, theirs_ref):
    width = a_ref.shape[1] // 2
    for kind, (left, right) in enumerate(((a_ref, ga_ref), (b_ref, gb_ref), (c_ref, gc_ref))):
        for side, out in enumerate((mine_ref, theirs_ref)):
            place = pl.ds(pl.multiple_of((core[0] ^ side) * width, width), width)
            out[kind, 0] = low(dot_tn(left[:, place], right[...])).reshape(out.shape[2:])


def plain_grads(lefts, rights):
    size, chips = lax.axis_size("rep"), lax.axis_size("shard") // 2
    core = lax.axis_index("shard") % 2
    rows = D // (2 * chips * size)
    if rows % 16:
        stack = jnp.stack([low(dot_tn(left, right)) for left, right in zip(lefts, rights)])
        stack = stack.reshape(3, chips, 2, size, rows, D)
        return [lax.dynamic_index_in_dim(stack, core ^ side, 2, keepdims=False) for side in range(2)]
    count = lefts[0].shape[0]
    grid_spec = pltpu.PrefetchScalarGridSpec(
        num_scalar_prefetch=1,
        grid=(chips,),
        in_specs=[pl.BlockSpec((count, D // chips), lambda i, e: (0, i))] * 3
        + [pl.BlockSpec((count, D), lambda i, e: (0, 0))] * 3,
        out_specs=[pl.BlockSpec((3, 1, size, rows, D), lambda i, e: (0, i, 0, 0, 0))] * 2,
    )
    return pl.pallas_call(
        plain_kernel,
        grid_spec=grid_spec,
        out_shape=(jax.ShapeDtypeStruct((3, chips, size, rows, D), jnp.bfloat16),) * 2,
        compiler_params=pltpu.CompilerParams(vmem_limit_bytes=58 * 2**20),
        cost_estimate=pl.CostEstimate(flops=6 * count * D * D, bytes_accessed=20 * count * D, transcendentals=0),
    )(core[None], *lefts, *rights)


def split_kernel(place, mine_ref, other_ref, *outs):
    for step, out in enumerate(outs):
        take = pl.ds(place[0] ^ step, 1)
        total = mine_ref[:, 0, take].astype(jnp.float32) + other_ref[:, 0, take].astype(jnp.float32)
        out[...] = low(total)


def core_sum_split(mine, other):
    kinds, chips, size, rows, _ = mine.shape
    if rows % 16:
        total = add_up([mine, other])
        me = lax.axis_index("rep")
        return [lax.dynamic_index_in_dim(total, me ^ step, 2, keepdims=False) for step in range(size)]
    grid_spec = pltpu.PrefetchScalarGridSpec(
        num_scalar_prefetch=1,
        grid=(chips,),
        in_specs=[pl.BlockSpec((kinds, 1, size, rows, D), lambda i, e: (0, i, 0, 0, 0))] * 2,
        out_specs=[pl.BlockSpec((kinds, 1, rows, D), lambda i, e: (0, i, 0, 0))] * size,
    )
    return pl.pallas_call(
        split_kernel,
        grid_spec=grid_spec,
        out_shape=(jax.ShapeDtypeStruct((kinds, chips, rows, D), jnp.bfloat16),) * size,
        compiler_params=pltpu.CompilerParams(vmem_limit_bytes=58 * 2**20),
        cost_estimate=LITTLE,
    )(lax.axis_index("rep")[None], mine, other)


def reduce_line(line):
    chips = lax.axis_size("shard") // 2
    chip = lax.axis_index("shard") // 2
    parts = [lax.dynamic_index_in_dim(line, (chip + step) % chips, 1, keepdims=False) for step in range(chips)]
    return [parts[0]] + [line_send(parts[step], step) for step in range(1, chips)]


def shards(
    tokens,
    segments,
    enc_states,
    enc_lengths,
    cotangent,
    self_qkv,
    self_out,
    cross_query,
    cross_memory,
    cross_out,
    expand_weight,
    shrink_weight,
    norm_gain,
    norm_bias,
    proj_bias,
    expand_bias,
):
    row_count, enc_rows = tokens.shape[0], enc_states.shape[0]
    span = SEQ // row_count
    width = D // span
    count = lax.axis_size("shard")
    size = lax.axis_size("rep")
    rep_pos = lax.axis_index("rep")
    shard_pos = lax.axis_index("shard")
    local_pos = shard_pos % span
    local_seq = shard_pos // span
    groups = None
    if count != span:
        groups = [[g * span + i for i in range(span)] for g in range(count // span)]
    weight_rows = self_qkv.shape[0]
    part_rows = weight_rows // size
    hidden = expand_bias.shape[0]
    shard_width = norm_gain.shape[1]

    def gather(value, groups=None):
        return lax.all_gather(value, "shard", axis=0, tiled=True, axis_index_groups=groups)

    def scatter(value, groups=None):
        return lax.psum_scatter(value, "shard", scatter_dimension=0, tiled=True, axis_index_groups=groups)

    def swap(value):
        return lax.all_to_all(value, "shard", 0, 0, tiled=True)

    def own_part(weight):
        return lax.dynamic_slice_in_dim(weight, rep_pos * part_rows, part_rows, axis=0)

    def by_pairs(weight, kinds):
        blocks = weight.reshape(part_rows, kinds, span, width).transpose(2, 0, 1, 3)
        return blocks.reshape(span, part_rows, kinds * width)

    blocks = jnp.concatenate([by_pairs(own_part(self_qkv), 3), by_pairs(own_part(cross_memory), 2)], axis=2)
    blocks = jnp.tile(blocks, (count // span, 1, 1))
    small = jnp.concatenate([norm_gain, norm_bias, proj_bias], axis=0)
    small_count = small.shape[0]
    small_rows = -(-small.size // (5 * width))
    small = jnp.pad(small.reshape(-1), (0, small_rows * 5 * width - small.size)).reshape(small_rows, 5 * width)
    blocks = jnp.concatenate([blocks, jnp.broadcast_to(small, (count,) + small.shape)], axis=1)
    swapped = swap(blocks)
    plain_parts = line_start(jnp.stack([own_part(self_out), own_part(cross_query), own_part(cross_out)]))
    enc_all = gather(enc_states, groups)
    rows_all = gather(after(tokens, swapped, enc_all, plain_parts[1], plain_parts[-1]), groups)
    small_all = swapped[:, part_rows:].reshape(count, small_rows * 5 * width)[:, : small_count * shard_width]
    small_all = small_all.reshape(count, small_count, shard_width)
    small_all = small_all.transpose(1, 0, 2).reshape(small_count, D).astype(jnp.float32)
    gain_rows, shift_rows, bias_rows = small_all[:3], small_all[3:6], small_all[6:]
    head_weight = rep_gather(swapped[:, :part_rows], 1).reshape(D, 5 * width)
    qkv_weight, memory_weight = head_weight[:, : 3 * width], head_weight[:, 3 * width :]
    qkv_weight, memory_weight = head_weight[:, : 3 * width], head_weight[:, 3 * width :]
    own_bias = lax.dynamic_slice_in_dim(bias_rows, local_pos * width, width, axis=1)
    zero_bias = jnp.zeros((width,), jnp.float32)
    memory_pair = low(dot(enc_all, memory_weight) + jnp.concatenate([zero_bias, own_bias[4]]))
    plain_mine = rep_start(line_place(after(plain_parts, head_weight)))
    rows_all, qkv_weight, memory_weight, plain_mine[1], plain_mine[2] = lax.optimization_barrier(
        (rows_all, qkv_weight, memory_weight, plain_mine[1], plain_mine[2])
    )
    memory_all = gather(after(memory_pair, rows_all), groups)
    expand_part = own_part(after(expand_weight, rows_all)).reshape(part_rows, count, hidden).transpose(1, 0, 2)
    expand_swapped = swap(expand_part)

    seq_segments = lax.dynamic_slice_in_dim(segments, local_seq * SEQ, SEQ)
    qkv_bias = jnp.concatenate([own_bias[0], zero_bias, own_bias[1]])
    input_one_all, qkv = front(rows_all, gain_rows[0], shift_rows[0], qkv_weight, qkv_bias)
    att_low, att_full, lse = self_forward(qkv, seq_segments)
    att_low, memory_all, plain_mine, expand_swapped = lax.optimization_barrier(
        (att_low, memory_all, plain_mine, expand_swapped)
    )
    grad_all = gather(after(cotangent, memory_all))
    plain_other = [core_send(part) for part in plain_mine]
    attn_proj, query_in, cross_proj = weight_join(plain_mine, plain_other)
    attended = lax.all_to_all(att_low, "shard", 0, 1, tiled=True, axis_index_groups=groups)

    enc_count = lax.dynamic_slice_in_dim(enc_lengths, local_seq, 1)

    residual_in = tokens.astype(jnp.float32)
    hidden_one = residual_in + dot(attended, attn_proj) + bias_rows[2]
    input_two = low(norm_apply(hidden_one, gain_rows[1], shift_rows[1]))
    cross_q = low(dot(input_two, query_in) + bias_rows[3])
    context = cross_forward(cross_q, memory_all, enc_count)
    hidden_two = hidden_one + dot(context, cross_proj) + bias_rows[5]
    input_three = low(norm_apply(hidden_two, gain_rows[2], shift_rows[2]))

    input_three_all = gather(input_three)
    expand_parts = rep_start(expand_swapped.reshape(count * part_rows, hidden))
    grad_all_now = after(grad_all, input_three)
    expand_local = spread(expand_parts, 0, count * part_rows, jnp.bfloat16)
    expand_local = expand_local.reshape(size, count, part_rows, hidden).transpose(1, 0, 2, 3).reshape(D, hidden)
    grad_act = dot_nt(grad_all_now, shrink_weight)
    input_three_all, grad_act, expand_local = lax.optimization_barrier((input_three_all, grad_act, expand_local))
    act, grad_pre, grad_in_three_low, hidden_sums = feed(
        input_three_all, expand_local, expand_bias.astype(jnp.float32), grad_act
    )
    grad_hidden_bias = hidden_sums[0]
    grad_in_three = scatter(grad_in_three_low)

    part_hidden = hidden // size

    def send_parts(parts):
        return [parts[0]] + [rep_send(parts[step], step) for step in range(1, size)]

    rows_late, grad_pre_late = after((input_three_all, grad_pre), grad_in_three_low)
    expand_grad_parts = expand_grads(rows_late, grad_pre_late, count, part_rows)
    shrink_parts = send_parts(shrink_grads(after(act, expand_grad_parts[0]), grad_all))
    expand_grad_parts = send_parts(expand_grad_parts)
    result_part = product(after(act, shrink_parts[0]), shrink_weight)
    expand_sum = add_up(expand_grad_parts)
    own_expand = swap(expand_sum)
    grad_in_three, shrink_parts[0], result_part = lax.optimization_barrier(
        (grad_in_three, shrink_parts[0], result_part)
    )
    result_sum = scatter(result_part)
    grad_in_three = grad_in_three.astype(jnp.float32)

    grad_out = cotangent.astype(jnp.float32)
    norm_three = jax.vjp(norm_apply, hidden_two, gain_rows[2], shift_rows[2])[1](grad_in_three)
    grad_two = grad_out + norm_three[0]
    grad_two_low = low(grad_two)
    grad_context = low(dot_nt(grad_two_low, cross_proj))
    grad_cross_q, memory_part = cross_backward(cross_q, memory_all, grad_context, enc_count)
    grad_cross_q, memory_part, shrink_parts, own_expand = lax.optimization_barrier(
        (grad_cross_q, memory_part, shrink_parts, own_expand)
    )
    mem_grads = scatter(memory_part, groups)
    grad_in_two = dot_nt(grad_cross_q, query_in)
    norm_two = jax.vjp(norm_apply, hidden_one, gain_rows[1], shift_rows[1])[1](grad_in_two)
    grad_one = grad_two + norm_two[0]
    grad_one_low = low(grad_one)
    grad_attn = low(dot_nt(grad_one_low, attn_proj))
    shrink_sum = add_up(after(shrink_parts, grad_attn))
    own_expand = own_expand.reshape(part_hidden, D)
    own_feed = jnp.concatenate([shrink_sum, own_expand], axis=0)
    grad_att_heads = lax.all_to_all(grad_attn, "shard", 1, 0, tiled=True, axis_index_groups=groups)

    lefts, rights = after(((attended, input_two, context), (grad_one_low, grad_cross_q, grad_two_low)), grad_attn)
    plain_own, plain_theirs = plain_grads(lefts, rights)
    plain_theirs = core_send(plain_theirs)
    grad_att_heads, plain_own = lax.optimization_barrier((grad_att_heads, plain_own))

    feed_gather = rep_start(own_feed)
    grad_qkv = self_backward(qkv, grad_att_heads, lse, att_full, seq_segments)
    heads_parts = heads_grads(input_one_all, grad_qkv, enc_all, mem_grads, count, part_rows)
    heads_swapped = rep_swap(heads_parts)
    grad_in_one_low, one_sums, qkv_sums = back(after(grad_qkv, heads_parts), qkv_weight, input_one_all)
    plain_rep = send_parts(core_sum_split(*after((plain_own, plain_theirs), heads_parts)))
    grad_in_one_low, heads_swapped, plain_rep[0], feed_gather = lax.optimization_barrier(
        (grad_in_one_low, heads_swapped, plain_rep[0], feed_gather)
    )
    grad_in_one = scatter(grad_in_one_low, groups)

    mem_grads_late = after(mem_grads, grad_in_one_low)
    qkv_sums = qkv_sums[0]
    gain_shift = [(one_sums[0] - shift_rows[0] * one_sums[1]) / gain_rows[0], one_sums[1]]
    zero_row = jnp.zeros((D,), jnp.float32)

    def at_own(values):
        return lax.dynamic_update_slice_in_dim(zero_row, values, local_pos * width, 0)

    small_grads = jnp.stack(
        [
            gain_shift[0],
            norm_two[1],
            norm_three[1],
            gain_shift[1],
            norm_two[2],
            norm_three[2],
            at_own(qkv_sums[:width]),
            at_own(qkv_sums[2 * width :]),
            column_sums(grad_one_low),
            column_sums(grad_cross_q),
            at_own(column_sums(mem_grads_late)[width:]),
            column_sums(grad_two_low),
            column_sums(cotangent),
        ]
    )
    small_grads = small_grads.reshape(small_count, count, shard_width).transpose(1, 0, 2)
    small_grads = small_grads.reshape(count, small_count * shard_width)
    hidden_grads = jnp.zeros((count, hidden), jnp.float32)
    hidden_grads = lax.dynamic_update_slice_in_dim(hidden_grads, grad_hidden_bias[None], shard_pos, 0)
    small_grads = low(jnp.concatenate([small_grads, hidden_grads], axis=1))
    small_size = small_grads.shape[1]
    extra = -(-small_size // (5 * width))
    small_grads = jnp.pad(small_grads, ((0, 0), (0, extra * 5 * width - small_size)))
    small_grads = small_grads.reshape(count, extra, 5 * width)
    heads_sum = sum_first(after(heads_swapped, grad_in_one_low))
    own_heads = swap(jnp.concatenate([heads_sum, small_grads], axis=1))
    own_small = sum_first(own_heads[:, part_rows:])
    own_heads = own_heads[:, :part_rows].reshape(count // span, span, part_rows, 5 * width)
    own_heads = own_heads[0] if count == span else sum_first(own_heads)
    heads_gather = rep_start(jnp.concatenate([own_heads.reshape(span * part_rows, 5 * width), own_small], axis=0))

    plain_line_parts = reduce_line(add_up(after(plain_rep, own_heads)))
    own_plain = add_up(plain_line_parts).reshape(3 * part_rows, D)
    plain_gather = rep_start(own_plain)
    enc_parts = line_scatter_start(low(dot_nt(mem_grads_late, memory_weight)), span)
    grad_enc = add_up(line_scatter_middle(enc_parts, span)).astype(jnp.float32)
    result = hidden_two + after(result_sum, grad_in_one_low).astype(jnp.float32) + bias_rows[6]

    total_shrink = spread(feed_gather, 0, part_hidden, jnp.float32)
    total_expand = spread_columns(feed_gather, part_hidden, count, part_rows)
    total_small = sum(part[span * part_rows :].astype(jnp.float32) for part in heads_gather)
    total_small = total_small.reshape(-1)[:small_size]
    total_hidden_bias = total_small[small_count * shard_width :]
    total_small = total_small[: small_count * shard_width].reshape(small_count, shard_width)
    total_qkv, total_memory = spread_heads(heads_gather, span, part_rows, width)

    grad_tokens = last(tokens, grad_in_one, grad_one, gain_rows[0])
    plain_gather = after(plain_gather, grad_tokens, result)
    total_proj, total_query, total_cross = [part.reshape(weight_rows, D) for part in spread_kinds(plain_gather, part_rows)]

    return (
        low(result),
        grad_tokens,
        grad_enc,
        total_qkv,
        total_proj,
        total_query,
        total_memory,
        total_cross,
        total_expand.reshape(weight_rows, count * hidden).astype(jnp.float32),
        total_shrink.reshape(hidden, D).astype(jnp.float32),
        total_small[:3],
        total_small[3:6],
        total_small[6:],
        total_hidden_bias,
    )


def solution(mesh):
    return jax.shard_map(
        shards,
        mesh=mesh,
        in_specs=(
            P(("rep", "shard"), None),
            P("rep"),
            P(("rep", "shard"), None),
            P("rep"),
            P(("rep", "shard"), None),
            P("shard", None),
            P("shard", None),
            P("shard", None),
            P("shard", None),
            P("shard", None),
            P("shard", None),
            P("shard", None),
            P(None, "shard"),
            P(None, "shard"),
            P(None, "shard"),
            P("shard"),
        ),
        out_specs=(
            P(("rep", "shard"), None),
            P(("rep", "shard"), None),
            P(("rep", "shard"), None),
            P("shard", None),
            P("shard", None),
            P("shard", None),
            P("shard", None),
            P("shard", None),
            P("shard", None),
            P("shard", None),
            P(None, "shard"),
            P(None, "shard"),
            P(None, "shard"),
            P("shard"),
        ),
        check_vma=False,
    )
```
